32 devices in a mesh: groups: 2 (over y), fsdp: 4 (over x, core), tensor: 4 (over z).
Axes of the slice: x: 2, y: 2, z: 4, core: 2. Of those that a mesh axis runs over, the one named last changes fastest.
Arguments:
- tokens: bfloat16 [1024, 8192], P(('groups', 'fsdp')), parts along dimension 0, may hold values from -64 to 64
- gate_weight: bfloat16 [8192, 14336], P('fsdp', 'tensor'), may hold values from -0.0625 to 0.0625
- up_weight: bfloat16 [8192, 14336], P('fsdp', 'tensor'), may hold values from -0.0625 to 0.0625
- down_weight: bfloat16 [14336, 8192], P('tensor', 'fsdp'), may hold values from -0.046875 to 0.046875
- right_factor: bfloat16 [64, 128, 128], P('fsdp', 'tensor'), may hold values from -0.5 to 0.5
- left_factor: bfloat16 [128, 64, 64], P('fsdp', 'tensor'), may hold values from -0.75 to 0.75
Outputs:
- grad_right: float32 [128, 128, 128], P(('groups', 'fsdp'), 'tensor'), parts along dimension 0
- grad_left: float32 [256, 64, 64], P(('groups', 'fsdp'), 'tensor'), parts along dimension 0
The draws below stay inside these ranges and needn't reach their ends.
There are 2 independent parts, one for each index of `groups`. The reference program is written for one: setup_inputs(seed, part) draws one part's arguments, and reference() takes and returns one part's arrays. A program takes and returns all parts, laid end to end along the dimension named above; an argument that names none is the same for every part. Nothing has to cross between parts.
All inputs are finite; a program needn't handle non-finite values.
Results may differ from the reference program's by a relative error of at most 0.0055.
Values may be sent and summed in bfloat16 or wider, within the bound.
No kernel may reach another device: no remote copies, remote signals or barrier semaphores. Data moves between devices by JAX's collectives and lax.ppermute only.
A program may use at most 128 MiB of HBM per device.

```python
import math
import jax
import jax.numpy as jnp
from jax import lax

D = 8192
FF = 14336
NBLK = 64
BSZ = 128
TOKENS = 512
FEAT_SHARE = 2048
HIDDEN_SHARE = 3584


def draw_tokens(key, part):
    base_key, row_key, col_key = jax.random.split(jax.random.fold_in(key, 11), 3)
    base = jnp.clip(jax.random.normal(base_key, (TOKENS, D), jnp.float32), -6.0, 6.0)
    row_scale = jnp.exp(jax.random.uniform(row_key, (TOKENS, 1), jnp.float32, -0.1, 0.1))
    col_scale = 0.6 * jnp.exp(jax.random.uniform(col_key, (1, D), jnp.float32, -1.15, 1.15))
    return (base * row_scale * col_scale).astype(jnp.bfloat16)


def levels(stream_key, shape, pieces, smallest, top_value):
    loudness, own = 1.0, jax.random.fold_in(stream_key, 6)
    for position, blocks in pieces:
        draws = jnp.exp(jax.random.uniform(jax.random.fold_in(own, position), (blocks,), jnp.float32, smallest / len(pieces), top_value / len(pieces)))
        loudness = loudness * jnp.repeat(draws, shape[position] // blocks).reshape([-1 if axis == position else 1 for axis in range(len(shape))])
    return loudness


def centred(own_key, extent, spread, limit, cuts=(), dtype=jnp.bfloat16):
    factor_of = levels(own_key, extent, cuts, -0.22, 0.18) if cuts else 1.0
    array = jax.random.normal(own_key, extent, jnp.float32) * spread * factor_of
    return jnp.minimum(jnp.maximum(array, -limit), limit).astype(dtype)


def setup_inputs(seed: int = 0, part: int = 0) -> dict:
    splits = jax.random.split(jax.random.key(seed), 7)
    part_keys = jax.random.split(jax.random.fold_in(splits[6], part), 7)
    tokens = draw_tokens(jax.random.fold_in(jax.random.fold_in(splits[6], part), 71), part)
    gate_weight = centred(splits[1], (D, FF), D ** -0.5, 0.0625, ((0, 4), (1, 4)))
    up_weight = centred(splits[2], (D, FF), D ** -0.5, 0.0625, ((0, 4), (1, 4)))
    down_weight = centred(splits[3], (FF, D), FF ** -0.5, 0.046875, ((0, 4), (1, 4)))
    right_factor = centred(splits[4], (NBLK, BSZ, BSZ), BSZ ** -0.5, 0.5, ((0, 4), (1, 4)))
    left_factor = centred(splits[5], (BSZ, NBLK, NBLK), NBLK ** -0.5, 0.75, ((0, 4), (1, 4)))
    return dict(tokens=tokens, gate_weight=gate_weight, up_weight=up_weight, down_weight=down_weight, right_factor=right_factor, left_factor=left_factor)


def grouped_product(left_parts, right_parts, rows, width):

    def add_group(total, pair):
        product = jnp.dot(pair[0], pair[1], preferred_element_type=jnp.float32)
        rounded = lax.optimization_barrier(product.astype(jnp.bfloat16))
        return (total + rounded.astype(jnp.float32), None)
    start = jnp.zeros((rows, width), jnp.float32)
    return lax.scan(add_group, start, (left_parts, right_parts))[0]

def reference(tokens, gate_weight, up_weight, down_weight, right_factor, left_factor):
    feature_groups = D // FEAT_SHARE
    hidden_groups = FF // HIDDEN_SHARE
    token_parts = jnp.moveaxis(tokens.reshape(TOKENS, feature_groups, FEAT_SHARE), 1, 0)
    gate_sum = grouped_product(token_parts, gate_weight.reshape(feature_groups, FEAT_SHARE, FF), TOKENS, FF)
    up_sum = grouped_product(token_parts, up_weight.reshape(feature_groups, FEAT_SHARE, FF), TOKENS, FF)
    hidden = (jax.nn.silu(gate_sum) * up_sum).astype(jnp.bfloat16)
    hidden_parts = jnp.moveaxis(hidden.reshape(TOKENS, hidden_groups, HIDDEN_SHARE), 1, 0)
    target = grouped_product(hidden_parts, down_weight.reshape(hidden_groups, HIDDEN_SHARE, D), TOKENS, D)
    block_input = tokens.reshape(TOKENS, NBLK, BSZ).astype(jnp.float32)
    mixed = jnp.einsum('nij,ikj->nik', block_input, right_factor.astype(jnp.float32)).astype(jnp.bfloat16)
    left_wide = left_factor.astype(jnp.float32)
    mixed_wide = mixed.astype(jnp.float32)
    student = jnp.einsum('nij,jki->njk', mixed_wide, left_wide)
    out_grad = (student - target.reshape(TOKENS, BSZ, NBLK)) / math.sqrt(TOKENS)
    grad_left = jnp.einsum('njk,nij->jki', out_grad, mixed_wide)
    mixed_grad = jnp.einsum('njk,jki->nij', out_grad, left_wide).astype(jnp.bfloat16)
    grad_right = jnp.einsum('nik,nij->ikj', mixed_grad.astype(jnp.float32), block_input)
    return (grad_right, grad_left)
```

```python
import functools
import math

import jax
import jax.numpy as jnp
from jax import lax
from jax.experimental import pallas as pl
from jax.experimental.pallas import tpu as pltpu
from jax.sharding import PartitionSpec as P

BLK = 256
F32 = jnp.float32
BF16 = jnp.bfloat16


def gate_up_kernel(idx_ref, top_ref, bottom_ref, gate_ref, up_ref, mine_ref, other_ref):
    rows = top_ref.shape[0]
    lhs = jnp.concatenate([top_ref[...], bottom_ref[...]], axis=0)
    for slot, weight_ref in enumerate((gate_ref, up_ref)):
        product = jnp.dot(lhs, weight_ref[...], preferred_element_type=F32).astype(BF16)
        mine_ref[slot] = product[:rows]
        other_ref[slot] = product[rows:]


def gate_up(top, top_block, bottom, gate, up, column, first, width):
    rows, feat = bottom.shape
    if width % BLK or gate.shape[1] % BLK or rows % 16 or feat % 128:
        lhs = jnp.concatenate(
            [lax.dynamic_slice_in_dim(top, top_block * feat, feat, 1), bottom], axis=0
        )
        both = [
            jnp.dot(
                lhs,
                lax.dynamic_slice_in_dim(w, column + first, width, 1),
                preferred_element_type=F32,
            ).astype(BF16)
            for w in (gate, up)
        ]
        both = jnp.stack(both)
        return both[:, :rows], both[:, rows:]
    scalars = jnp.stack([top_block, column // BLK + first // BLK]).astype(jnp.int32)
    weight_spec = pl.BlockSpec((feat, BLK), lambda n, s: (0, s[1] + n))
    out_spec = pl.BlockSpec((2, rows, BLK), lambda n, s: (0, 0, n))
    shape = jax.ShapeDtypeStruct((2, rows, width), BF16)
    return pl.pallas_call(
        gate_up_kernel,
        grid_spec=pltpu.PrefetchScalarGridSpec(
            num_scalar_prefetch=1,
            grid=(width // BLK,),
            in_specs=[
                pl.BlockSpec((rows, feat), lambda n, s: (0, s[0])),
                pl.BlockSpec((rows, feat), lambda n, s: (0, 0)),
                weight_spec,
                weight_spec,
            ],
            out_specs=[out_spec, out_spec],
        ),
        out_shape=[shape, shape],
        compiler_params=pltpu.CompilerParams(vmem_limit_bytes=24 * 2**20),
        cost_estimate=pl.CostEstimate(
            flops=2 * 2 * rows * feat * 2 * width,
            bytes_accessed=2 * feat * 2 * width + 2 * 2 * rows * (feat + 2 * width),
            transcendentals=0,
        ),
        name="gate_up",
    )(scalars, top, bottom, gate, up)


def down_kernel(idx_ref, mine_ref, other_ref, weight_ref, total_ref, out_ref):
    lhs = jnp.concatenate([mine_ref[...], other_ref[...]], axis=0)
    product = jnp.dot(lhs, weight_ref[...], preferred_element_type=F32)

    @pl.when(pl.program_id(0) == 0)
    def _():
        out_ref[...] = total_ref[...] + product

    @pl.when(pl.program_id(0) > 0)
    def _():
        out_ref[...] += product


def down_add(total, mine, other, weight, row):
    rows, width = mine.shape
    outs = weight.shape[1]
    if width % BLK or weight.shape[0] % BLK or rows % 16 or outs % 128:
        lhs = jnp.concatenate([mine, other], axis=0)
        part = lax.dynamic_slice_in_dim(weight, row, width, 0)
        return total + jnp.dot(lhs, part, preferred_element_type=F32)
    scalars = jnp.reshape(row // BLK, (1,)).astype(jnp.int32)
    hidden_spec = pl.BlockSpec((rows, BLK), lambda k, s: (0, k))
    whole = pl.BlockSpec((2 * rows, outs), lambda k, s: (0, 0))
    return pl.pallas_call(
        down_kernel,
        grid_spec=pltpu.PrefetchScalarGridSpec(
            num_scalar_prefetch=1,
            grid=(width // BLK,),
            in_specs=[
                hidden_spec,
                hidden_spec,
                pl.BlockSpec((BLK, outs), lambda k, s: (s[0] + k, 0)),
                whole,
            ],
            out_specs=whole,
        ),
        out_shape=jax.ShapeDtypeStruct((2 * rows, outs), F32),
        compiler_params=pltpu.CompilerParams(vmem_limit_bytes=24 * 2**20),
        cost_estimate=pl.CostEstimate(
            flops=2 * 2 * rows * width * outs,
            bytes_accessed=2 * width * outs + 2 * 2 * rows * width + 16 * rows * outs,
            transcendentals=0,
        ),
        name="down_add",
    )(scalars, mine, other, weight, total)


def body(tokens, gate_weight, up_weight, down_weight, right_factor, left_factor):
    fsdp_count = lax.axis_size("fsdp")
    tensor_count = lax.axis_size("tensor")
    chips = fsdp_count // 2
    rows, model = tokens.shape
    feat, hid = gate_weight.shape
    part = hid // chips
    me = lax.axis_index("fsdp")
    chip, core = me // 2, me % 2
    z = lax.axis_index("tensor")

    def swap(value):
        return lax.ppermute(value, "fsdp", [(i, i ^ 1) for i in range(fsdp_count)])

    def shift(value, hops):
        perm = [(i, (i + 2 * hops) % fsdp_count) for i in range(fsdp_count)]
        return lax.ppermute(value, "fsdp", perm)

    def gather_z(value):
        if tensor_count > 4:
            return lax.all_gather(value, "tensor", axis=0, tiled=True)
        size = value.shape[0]
        whole = jnp.zeros((size * tensor_count,) + value.shape[1:], value.dtype)
        whole = lax.dynamic_update_slice_in_dim(whole, value, z * size, 0)
        for step in range(1, tensor_count):
            perm = [(i, (i + step) % tensor_count) for i in range(tensor_count)]
            got = lax.ppermute(value, "tensor", perm)
            source = lax.rem(z - step + tensor_count, tensor_count)
            whole = lax.dynamic_update_slice_in_dim(whole, got, source * size, 0)
        return whole

    def scatter_z(value):
        if tensor_count > 4:
            return lax.psum_scatter(value, "tensor", scatter_dimension=0, tiled=False)
        total = lax.dynamic_index_in_dim(value, z, 0, keepdims=False)
        for step in range(1, tensor_count):
            target_z = lax.rem(z + step, tensor_count)
            piece = lax.dynamic_index_in_dim(value, target_z, 0, keepdims=False)
            perm = [(i, (i + step) % tensor_count) for i in range(tensor_count)]
            total += lax.ppermute(piece.astype(BF16), "tensor", perm).astype(F32)
        return total

    def columns(value, start, width):
        return lax.dynamic_slice_in_dim(value, start, width, 1)

    pairs = {0: (tokens, me, swap(columns(tokens, (me ^ 1) * feat, feat)))}
    row_share = rows // tensor_count
    own_share = lax.dynamic_slice_in_dim(tokens, z * row_share, row_share, 0)
    gathered = {}
    for dt in range(1, chips):
        for g in range(chips):
            features = (chip - dt + g + chips) % chips * (2 * feat)
            piece = shift(columns(own_share, features, 2 * feat), -dt)
            gathered[dt, g] = gather_z(piece)
        got = gathered[dt, 0]
        pairs[dt] = (
            columns(got, core * feat, feat),
            jnp.int32(0),
            swap(columns(got, (1 - core) * feat, feat)),
        )

    if part % BLK == 0 and part // BLK > 1:
        head = (part // BLK + 1) // 2 * BLK
        chunks = [(0, head), (head, part - head)]
    else:
        chunks = [(0, part)]

    def partial(dt, dp, chunk):
        column = (chip + dp) % chips * part
        top, block, bottom = pairs[dt]
        mine, other = gate_up(top, block, bottom, gate_weight, up_weight, column, *chunk)
        return mine, swap(other)

    kept, got = {}, {}
    for dt in range(chips):
        for dp in list(range(1, chips)) + [0]:
            for n, chunk in enumerate(chunks):
                mine, from_core = partial(dt, dp, chunk)
                if dp:
                    both = (mine.astype(F32) + from_core.astype(F32)).astype(BF16)
                    got[dt, dp, n] = shift(both, dp)
                else:
                    kept[dt, n] = (mine, from_core)

    hidden = {}
    for e in list(range(1, chips)) + [0]:
        for n in range(len(chunks)):
            terms = list(kept[e, n])
            terms += [got[(e + dp) % chips, dp, n] for dp in range(1, chips)]
            total = sum(term.astype(F32) for term in terms)
            value = (jax.nn.silu(total[0]) * total[1]).astype(BF16)
            hidden[e, 0, n] = value
            for d in range(1, chips):
                hidden[e, d, n] = shift(value, d)

    totals = {u: jnp.zeros((2 * rows, down_weight.shape[1]), F32) for u in range(chips)}
    for e in list(range(1, chips)) + [0]:
        for n, (first, width) in enumerate(chunks):
            for d in range(chips):
                u = (e - d + chips) % chips
                mine = hidden[e, d, n]
                row = (chip - d + chips) % chips * part + first
                totals[u] = down_add(totals[u], mine, swap(mine), down_weight, row)

    token_rows = []
    for dt in range(chips):
        if dt == 0:
            full = tokens
        else:
            full = jnp.zeros((rows, model), BF16)
            for g in range(chips):
                features = (chip + g) % chips * (2 * feat)
                full = lax.dynamic_update_slice_in_dim(full, gathered[dt, g], features, 1)
        token_rows += [full, swap(full)]
    inputs = jnp.concatenate(token_rows, axis=0)
    count = inputs.shape[0]

    blocks, share, size = right_factor.shape
    ratio = tensor_count // fsdp_count
    turn = []
    for a in range(fsdp_count):
        for b in range(tensor_count):
            turn.append((a * tensor_count + b, (b // ratio) * tensor_count + a * ratio + b % ratio))
    back = [(b, a) for a, b in turn]
    right_rows = gather_z(lax.ppermute(right_factor, ("fsdp", "tensor"), turn)[None])
    right_rows = right_rows.reshape(fsdp_count, ratio, blocks, share, size)
    right_rows = right_rows.transpose(0, 2, 1, 3, 4).reshape(
        fsdp_count * blocks, ratio * share, size
    )
    left_rows = jnp.moveaxis(gather_z(jnp.moveaxis(left_factor, 1, 0)), 0, 1)

    block_input = inputs.reshape(count, fsdp_count * blocks, size)
    mixed = jnp.einsum(
        "nim,ijm->nij", block_input, right_rows, preferred_element_type=F32
    ).astype(BF16)
    student = jnp.einsum("nij,jki->njk", mixed, left_rows, preferred_element_type=F32)
    target = jnp.concatenate([totals[u] for u in range(chips)], axis=0)
    scale = 1.0 / math.sqrt(count)
    out_grad = (student * (1.0 / tensor_count) - target.reshape(student.shape)) * scale
    out_grad = out_grad.astype(BF16)
    grad_left = jnp.einsum("njk,nij->kji", out_grad, mixed, preferred_element_type=F32)
    mixed_grad = jnp.einsum(
        "njk,jki->nij", out_grad, left_rows, preferred_element_type=F32
    ).astype(BF16)
    grad_right = jnp.einsum(
        "nij,nim->ijm", mixed_grad, block_input, preferred_element_type=F32
    )
    grad_left = scatter_z(
        grad_left.reshape((tensor_count, -1) + grad_left.shape[1:])
    )
    grad_left = jnp.moveaxis(grad_left, 0, 1)
    grad_right = grad_right.reshape(fsdp_count, blocks, ratio, share, size)
    grad_right = grad_right.transpose(0, 2, 1, 3, 4).reshape(
        tensor_count, blocks, share, size
    )
    grad_right = lax.ppermute(scatter_z(grad_right), ("fsdp", "tensor"), back)
    return grad_right, grad_left


def solution(mesh):
    return jax.shard_map(
        body,
        mesh=mesh,
        in_specs=(
            P(("groups", "fsdp"), None),
            P("fsdp", "tensor"),
            P("fsdp", "tensor"),
            P("tensor", "fsdp"),
            P("fsdp", "tensor", None),
            P("fsdp", "tensor", None),
        ),
        out_specs=(P(("groups", "fsdp"), "tensor", None), P(("groups", "fsdp"), "tensor", None)),
        check_vma=False,
    )
```

```python
import functools
import math

import jax
import jax.numpy as jnp
from jax import lax
from jax.experimental import pallas as pl
from jax.experimental.pallas import tpu as pltpu
from jax.sharding import PartitionSpec as P

BLK = 256
F32 = jnp.float32
BF16 = jnp.bfloat16


def gate_up_kernel(idx_ref, top_ref, bottom_ref, gate_ref, up_ref, mine_ref, other_ref):
    rows = top_ref.shape[0]
    lhs = jnp.concatenate([top_ref[...], bottom_ref[...]], axis=0)
    for slot, weight_ref in enumerate((gate_ref, up_ref)):
        product = jnp.dot(lhs, weight_ref[...], preferred_element_type=F32).astype(BF16)
        mine_ref[slot] = product[:rows]
        other_ref[slot] = product[rows:]


def gate_up(top, top_block, bottom, gate, up, column, first, width):
    rows, feat = bottom.shape
    if width % BLK or gate.shape[1] % BLK or rows % 16 or feat % 128:
        lhs = jnp.concatenate(
            [lax.dynamic_slice_in_dim(top, top_block * feat, feat, 1), bottom], axis=0
        )
        both = [
            jnp.dot(
                lhs,
                lax.dynamic_slice_in_dim(w, column + first, width, 1),
                preferred_element_type=F32,
            ).astype(BF16)
            for w in (gate, up)
        ]
        both = jnp.stack(both)
        return both[:, :rows], both[:, rows:]
    scalars = jnp.stack([top_block, lax.div(column, BLK) + first // BLK]).astype(jnp.int32)
    weight_spec = pl.BlockSpec((feat, BLK), lambda n, s: (0, s[1] + n))
    out_spec = pl.BlockSpec((2, rows, BLK), lambda n, s: (0, 0, n))
    shape = jax.ShapeDtypeStruct((2, rows, width), BF16)
    return pl.pallas_call(
        gate_up_kernel,
        grid_spec=pltpu.PrefetchScalarGridSpec(
            num_scalar_prefetch=1,
            grid=(width // BLK,),
            in_specs=[
                pl.BlockSpec((rows, feat), lambda n, s: (0, s[0])),
                pl.BlockSpec((rows, feat), lambda n, s: (0, 0)),
                weight_spec,
                weight_spec,
            ],
            out_specs=[out_spec, out_spec],
        ),
        out_shape=[shape, shape],
        compiler_params=pltpu.CompilerParams(vmem_limit_bytes=50 * 2**20),
        cost_estimate=pl.CostEstimate(
            flops=2 * 2 * rows * feat * 2 * width,
            bytes_accessed=2 * feat * 2 * width + 2 * 2 * rows * (feat + 2 * width),
            transcendentals=0,
        ),
        name="gate_up",
    )(scalars, top, bottom, gate, up)


def down_kernel(idx_ref, mine_ref, other_ref, weight_ref, *refs):
    out_ref = refs[-1]
    lhs = jnp.concatenate([mine_ref[...], other_ref[...]], axis=0)
    product = jnp.dot(lhs, weight_ref[...], preferred_element_type=F32)

    @pl.when(pl.program_id(0) == 0)
    def _():
        out_ref[...] = refs[0][...] + product if len(refs) > 1 else product

    @pl.when(pl.program_id(0) > 0)
    def _():
        out_ref[...] += product


def down_add(total, mine, other, weight, row):
    rows, width = mine.shape
    outs = weight.shape[1]
    if width % BLK or weight.shape[0] % BLK or rows % 16 or outs % 128:
        lhs = jnp.concatenate([mine, other], axis=0)
        part = lax.dynamic_slice_in_dim(weight, row, width, 0)
        product = jnp.dot(lhs, part, preferred_element_type=F32)
        return product if total is None else total + product
    scalars = jnp.reshape(lax.div(row, BLK), (1,)).astype(jnp.int32)
    hidden_spec = pl.BlockSpec((rows, BLK), lambda k, s: (0, k))
    whole = pl.BlockSpec((2 * rows, outs), lambda k, s: (0, 0))
    totals = [] if total is None else [total]
    return pl.pallas_call(
        down_kernel,
        grid_spec=pltpu.PrefetchScalarGridSpec(
            num_scalar_prefetch=1,
            grid=(width // BLK,),
            in_specs=[
                hidden_spec,
                hidden_spec,
                pl.BlockSpec((BLK, outs), lambda k, s: (s[0] + k, 0)),
            ]
            + [whole] * len(totals),
            out_specs=whole,
        ),
        out_shape=jax.ShapeDtypeStruct((2 * rows, outs), F32),
        compiler_params=pltpu.CompilerParams(vmem_limit_bytes=50 * 2**20),
        cost_estimate=pl.CostEstimate(
            flops=2 * 2 * rows * width * outs,
            bytes_accessed=2 * width * outs + 2 * 2 * rows * width + 16 * rows * outs,
            transcendentals=0,
        ),
        name="down_add",
    )(scalars, mine, other, weight, *totals)


def body(tokens, gate_weight, up_weight, down_weight, right_factor, left_factor):
    fsdp_count = lax.axis_size("fsdp")
    tensor_count = lax.axis_size("tensor")
    chips = fsdp_count // 2
    rows, model = tokens.shape
    feat, hid = gate_weight.shape
    part = hid // chips
    me = lax.axis_index("fsdp")
    chip, core = lax.div(me, 2), lax.rem(me, 2)
    z = lax.axis_index("tensor")

    def swap(value):
        return lax.ppermute(value, "fsdp", [(i, i ^ 1) for i in range(fsdp_count)])

    def shift(value, hops):
        perm = [(i, (i + 2 * hops) % fsdp_count) for i in range(fsdp_count)]
        return lax.ppermute(value, "fsdp", perm)

    def gather_z(value):
        if tensor_count > 4:
            return lax.all_gather(value, "tensor", axis=0, tiled=True)
        size = value.shape[0]
        whole = jnp.zeros((size * tensor_count,) + value.shape[1:], value.dtype)
        whole = lax.dynamic_update_slice_in_dim(whole, value, z * size, 0)
        for step in range(1, tensor_count):
            perm = [(i, (i + step) % tensor_count) for i in range(tensor_count)]
            got = lax.ppermute(value, "tensor", perm)
            source = lax.rem(z - step + tensor_count, tensor_count)
            whole = lax.dynamic_update_slice_in_dim(whole, got, source * size, 0)
        return whole

    def scatter_z(value):
        if tensor_count > 4:
            return lax.psum_scatter(value, "tensor", scatter_dimension=0, tiled=False)
        total = lax.dynamic_index_in_dim(value, z, 0, keepdims=False)
        for step in range(1, tensor_count):
            target_z = lax.rem(z + step, tensor_count)
            piece = lax.dynamic_index_in_dim(value, target_z, 0, keepdims=False)
            perm = [(i, (i + step) % tensor_count) for i in range(tensor_count)]
            total += lax.ppermute(piece.astype(BF16), "tensor", perm).astype(F32)
        return total

    def columns(value, start, width):
        return lax.dynamic_slice_in_dim(value, start, width, 1)

    def after(value, *others):
        return lax.optimization_barrier((value,) + others)[0]

    def pair_z(value):
        perm = [(i, i ^ 1) for i in range(tensor_count)]
        got = lax.ppermute(value, "tensor", perm)
        odd = lax.rem(z, 2) == 1
        return jnp.concatenate(
            [jnp.where(odd, got, value), jnp.where(odd, value, got)], axis=0
        )

    if part % BLK == 0 and part // BLK > 1:
        head = (part // BLK + 1) // 2 * BLK
        chunks = [(0, head), (head, part - head)]
    else:
        chunks = [(0, part)]

    half = rows // 2
    own_half = lax.dynamic_slice_in_dim(tokens, lax.rem(z, 2) * half, half, 0)

    def send_tokens(value, dt, g):
        features = lax.rem(chip - dt + g + chips, chips) * (2 * feat)
        return shift(columns(value, features, 2 * feat), -dt)

    def partial(pair, dp, first, width):
        column = lax.rem(chip + dp, chips) * part
        top, block, bottom = pair
        mine, other = gate_up(top, block, bottom, gate_weight, up_weight, column, first, width)
        return mine, swap(other)

    def send_partials(pair, got, dt):
        sums = []
        for dp in range(1, chips):
            pieces = [partial(pair, dp, *chunk) for chunk in chunks]
            for n, (mine, from_core) in enumerate(pieces):
                both = (mine.astype(F32) + from_core.astype(F32)).astype(BF16)
                got[dt, dp, n] = shift(both, dp)
                sums.append(both)
        return sums

    got, kept, gathered = {}, {}, {}
    local = swap(columns(tokens, (me ^ 1) * feat, feat))
    arrived = {dt: send_tokens(own_half, dt, 0) for dt in range(1, chips)}
    sums = send_partials((tokens, me, local), got, 0)
    if sums:
        local = after(local, *sums)
    kept[0] = partial((tokens, me, local), 0, 0, part)
    late_tokens = after(tokens, kept[0][0])
    neighbour_tokens = swap(late_tokens)
    late_half = after(own_half, *sums) if sums else own_half

    for dt in range(1, chips):
        gathered[dt, 0] = pair_z(after(arrived[dt], *sums))
        whole = gathered[dt, 0]
        top = columns(whole, core * feat, feat)
        bottom = swap(columns(whole, (1 - core) * feat, feat))
        pair = (top, jnp.int32(0), bottom)
        sums = send_partials(pair, got, dt)
        pair = (top, jnp.int32(0), after(bottom, *sums))
        kept[dt] = partial(pair, 0, 0, part)
        for g in range(1, chips):
            gathered[dt, g] = pair_z(after(send_tokens(late_half, dt, g), kept[dt][0]))

    def activate(e, first, width, n):
        terms = [lax.slice_in_dim(term, first, first + width, axis=2) for term in kept[e]]
        terms += [got[(e + dp) % chips, dp, n] for dp in range(1, chips)]
        total = sum(term.astype(F32) for term in terms)
        return (jax.nn.silu(total[0]) * total[1]).astype(BF16)

    totals = {u: None for u in range(chips)}
    for e in list(range(1, chips)) + [0]:
        values = [activate(e, *chunk, n) for n, chunk in enumerate(chunks)]
        spans = list(chunks)
        if e:
            values, spans = [jnp.concatenate(values, axis=1)], [(0, part)]
        sent = [[value] + [shift(value, d) for d in range(1, chips)] for value in values]
        for (first, width), copies in zip(spans, sent):
            for d, mine in enumerate(copies):
                u = (e - d + chips) % chips
                row = lax.rem(chip - d + chips, chips) * part + first
                totals[u] = down_add(totals[u], mine, swap(mine), down_weight, row)

    token_rows = []
    for dt in range(chips):
        if dt == 0:
            token_rows += [tokens, neighbour_tokens]
            continue
        else:
            full = jnp.zeros((rows, model), BF16)
            for g in range(chips):
                features = lax.rem(chip + g, chips) * (2 * feat)
                full = lax.dynamic_update_slice_in_dim(full, gathered[dt, g], features, 1)
        token_rows += [full, swap(full)]
    inputs = jnp.concatenate(token_rows, axis=0)
    count = inputs.shape[0]

    blocks, share, size = right_factor.shape
    ratio = tensor_count // fsdp_count
    turn = []
    for a in range(fsdp_count):
        for b in range(tensor_count):
            turn.append((a * tensor_count + b, (b // ratio) * tensor_count + a * ratio + b % ratio))
    back = [(b, a) for a, b in turn]
    right_rows = gather_z(lax.ppermute(right_factor, ("fsdp", "tensor"), turn)[None])
    right_rows = right_rows.reshape(fsdp_count, ratio, blocks, share, size)
    right_rows = right_rows.transpose(0, 2, 1, 3, 4).reshape(
        fsdp_count * blocks, ratio * share, size
    )
    left_rows = jnp.moveaxis(gather_z(jnp.moveaxis(left_factor, 1, 0)), 0, 1)

    block_input = inputs.reshape(count, fsdp_count * blocks, size)
    mixed = jnp.einsum(
        "nim,ijm->nij", block_input, right_rows, preferred_element_type=F32
    ).astype(BF16)
    student = jnp.einsum("nij,jki->njk", mixed, left_rows, preferred_element_type=F32)
    target = jnp.concatenate([totals[u] for u in range(chips)], axis=0)
    scale = 1.0 / math.sqrt(count)
    out_grad = (student * (1.0 / tensor_count) - target.reshape(student.shape)) * scale
    out_grad = out_grad.astype(BF16)
    grad_left = jnp.einsum("njk,nij->kji", out_grad, mixed, preferred_element_type=F32)
    mixed_grad = jnp.einsum(
        "njk,jki->nij", out_grad, left_rows, preferred_element_type=F32
    ).astype(BF16)
    grad_right = jnp.einsum(
        "nij,nim->ijm", mixed_grad, block_input, preferred_element_type=F32
    )
    grad_left = scatter_z(
        grad_left.reshape((tensor_count, -1) + grad_left.shape[1:])
    )
    grad_left = jnp.moveaxis(grad_left, 0, 1)
    grad_right = grad_right.reshape(fsdp_count, blocks, ratio, share, size)
    grad_right = grad_right.transpose(0, 2, 1, 3, 4).reshape(
        tensor_count, blocks, share, size
    )
    grad_right = lax.ppermute(scatter_z(grad_right), ("fsdp", "tensor"), back)
    return grad_right, grad_left


def solution(mesh):
    return jax.shard_map(
        body,
        mesh=mesh,
        in_specs=(
            P(("groups", "fsdp"), None),
            P("fsdp", "tensor"),
            P("fsdp", "tensor"),
            P("tensor", "fsdp"),
            P("fsdp", "tensor", None),
            P("fsdp", "tensor", None),
        ),
        out_specs=(P(("groups", "fsdp"), "tensor", None), P(("groups", "fsdp"), "tensor", None)),
        check_vma=False,
    )
```

```python
import functools
import math

import jax
import jax.numpy as jnp
from jax import lax
from jax.experimental import pallas as pl
from jax.experimental.pallas import tpu as pltpu
from jax.sharding import PartitionSpec as P

BLK = 256
LANES = 128
SMALL = pl.CostEstimate(flops=1, bytes_accessed=1, transcendentals=0)
F32 = jnp.float32
BF16 = jnp.bfloat16


def gate_up_kernel(idx_ref, top_ref, bottom_ref, gate_ref, up_ref, mine_ref, other_ref):
    rows = top_ref.shape[0]
    lhs = jnp.concatenate([top_ref[...], bottom_ref[...]], axis=0)
    for slot, weight_ref in enumerate((gate_ref, up_ref)):
        product = jnp.dot(lhs, weight_ref[...], preferred_element_type=F32).astype(BF16)
        mine_ref[slot] = product[:rows]
        other_ref[slot] = product[rows:]


def gate_up(top, top_block, bottom, gate, up, column, first, width):
    rows, feat = bottom.shape
    if width % BLK or gate.shape[1] % BLK or rows % 16 or feat % 128:
        lhs = jnp.concatenate(
            [lax.dynamic_slice_in_dim(top, top_block * feat, feat, 1), bottom], axis=0
        )
        both = [
            jnp.dot(
                lhs,
                lax.dynamic_slice_in_dim(w, column + first, width, 1),
                preferred_element_type=F32,
            ).astype(BF16)
            for w in (gate, up)
        ]
        both = jnp.stack(both)
        return both[:, :rows], both[:, rows:]
    scalars = jnp.stack([top_block, lax.div(column, BLK) + first // BLK]).astype(jnp.int32)
    weight_spec = pl.BlockSpec((feat, BLK), lambda n, s: (0, s[1] + n))
    out_spec = pl.BlockSpec((2, rows, BLK), lambda n, s: (0, 0, n))
    shape = jax.ShapeDtypeStruct((2, rows, width), BF16)
    return pl.pallas_call(
        gate_up_kernel,
        grid_spec=pltpu.PrefetchScalarGridSpec(
            num_scalar_prefetch=1,
            grid=(width // BLK,),
            in_specs=[
                pl.BlockSpec((rows, feat), lambda n, s: (0, s[0])),
                pl.BlockSpec((rows, feat), lambda n, s: (0, 0)),
                weight_spec,
                weight_spec,
            ],
            out_specs=[out_spec, out_spec],
        ),
        out_shape=[shape, shape],
        compiler_params=pltpu.CompilerParams(vmem_limit_bytes=50 * 2**20),
        cost_estimate=pl.CostEstimate(
            flops=2 * 2 * rows * feat * 2 * width,
            bytes_accessed=2 * feat * 2 * width + 2 * 2 * rows * (feat + 2 * width),
            transcendentals=0,
        ),
        name="gate_up",
    )(scalars, top, bottom, gate, up)


def down_kernel(idx_ref, mine_ref, other_ref, weight_ref, *refs):
    out_ref = refs[-1]
    lhs = jnp.concatenate([mine_ref[...], other_ref[...]], axis=0)
    product = jnp.dot(lhs, weight_ref[...], preferred_element_type=F32)

    @pl.when(pl.program_id(0) == 0)
    def _():
        out_ref[...] = refs[0][...] + product if len(refs) > 1 else product

    @pl.when(pl.program_id(0) > 0)
    def _():
        out_ref[...] += product


def down_add(total, mine, other, weight, row):
    rows, width = mine.shape
    outs = weight.shape[1]
    if width % BLK or weight.shape[0] % BLK or rows % 16 or outs % 128:
        lhs = jnp.concatenate([mine, other], axis=0)
        part = lax.dynamic_slice_in_dim(weight, row, width, 0)
        product = jnp.dot(lhs, part, preferred_element_type=F32)
        return product if total is None else total + product
    scalars = jnp.reshape(lax.div(row, BLK), (1,)).astype(jnp.int32)
    hidden_spec = pl.BlockSpec((rows, BLK), lambda k, s: (0, k))
    whole = pl.BlockSpec((2 * rows, outs), lambda k, s: (0, 0))
    totals = [] if total is None else [total]
    return pl.pallas_call(
        down_kernel,
        grid_spec=pltpu.PrefetchScalarGridSpec(
            num_scalar_prefetch=1,
            grid=(width // BLK,),
            in_specs=[
                hidden_spec,
                hidden_spec,
                pl.BlockSpec((BLK, outs), lambda k, s: (s[0] + k, 0)),
            ]
            + [whole] * len(totals),
            out_specs=whole,
        ),
        out_shape=jax.ShapeDtypeStruct((2 * rows, outs), F32),
        compiler_params=pltpu.CompilerParams(vmem_limit_bytes=50 * 2**20),
        cost_estimate=pl.CostEstimate(
            flops=2 * 2 * rows * width * outs,
            bytes_accessed=2 * width * outs + 2 * 2 * rows * width + 16 * rows * outs,
            transcendentals=0,
        ),
        name="down_add",
    )(scalars, mine, other, weight, *totals)


def general_body(tokens, gate_weight, up_weight, down_weight, right_factor, left_factor):
    fsdp_count = lax.axis_size("fsdp")
    tensor_count = lax.axis_size("tensor")
    chips = fsdp_count // 2
    rows, model = tokens.shape
    feat, hid = gate_weight.shape
    part = hid // chips
    me = lax.axis_index("fsdp")
    chip, core = lax.div(me, 2), lax.rem(me, 2)
    z = lax.axis_index("tensor")

    def swap(value):
        return lax.ppermute(value, "fsdp", [(i, i ^ 1) for i in range(fsdp_count)])

    def shift(value, hops):
        perm = [(i, (i + 2 * hops) % fsdp_count) for i in range(fsdp_count)]
        return lax.ppermute(value, "fsdp", perm)

    def gather_z(value):
        if tensor_count > 4:
            return lax.all_gather(value, "tensor", axis=0, tiled=True)
        size = value.shape[0]
        whole = jnp.zeros((size * tensor_count,) + value.shape[1:], value.dtype)
        whole = lax.dynamic_update_slice_in_dim(whole, value, z * size, 0)
        for step in range(1, tensor_count):
            perm = [(i, (i + step) % tensor_count) for i in range(tensor_count)]
            got = lax.ppermute(value, "tensor", perm)
            source = lax.rem(z - step + tensor_count, tensor_count)
            whole = lax.dynamic_update_slice_in_dim(whole, got, source * size, 0)
        return whole

    def scatter_z(value):
        if tensor_count > 4:
            return lax.psum_scatter(value, "tensor", scatter_dimension=0, tiled=False)
        total = lax.dynamic_index_in_dim(value, z, 0, keepdims=False)
        for step in range(1, tensor_count):
            target_z = lax.rem(z + step, tensor_count)
            piece = lax.dynamic_index_in_dim(value, target_z, 0, keepdims=False)
            perm = [(i, (i + step) % tensor_count) for i in range(tensor_count)]
            total += lax.ppermute(piece.astype(BF16), "tensor", perm).astype(F32)
        return total

    def columns(value, start, width):
        return lax.dynamic_slice_in_dim(value, start, width, 1)

    def after(value, *others):
        return lax.optimization_barrier((value,) + others)[0]

    def pair_z(value):
        perm = [(i, i ^ 1) for i in range(tensor_count)]
        got = lax.ppermute(value, "tensor", perm)
        odd = lax.rem(z, 2) == 1
        return jnp.concatenate(
            [jnp.where(odd, got, value), jnp.where(odd, value, got)], axis=0
        )

    if part % BLK == 0 and part // BLK > 1:
        head = (part // BLK + 1) // 2 * BLK
        chunks = [(0, head), (head, part - head)]
    else:
        chunks = [(0, part)]

    half = rows // 2
    own_half = lax.dynamic_slice_in_dim(tokens, lax.rem(z, 2) * half, half, 0)

    def send_tokens(value, dt, g):
        features = lax.rem(chip - dt + g + chips, chips) * (2 * feat)
        return shift(columns(value, features, 2 * feat), -dt)

    def partial(pair, dp, first, width):
        column = lax.rem(chip + dp, chips) * part
        top, block, bottom = pair
        mine, other = gate_up(top, block, bottom, gate_weight, up_weight, column, first, width)
        return mine, swap(other)

    def send_partials(pair, got, dt):
        sums = []
        for dp in range(1, chips):
            pieces = [partial(pair, dp, *chunk) for chunk in chunks]
            for n, (mine, from_core) in enumerate(pieces):
                both = (mine.astype(F32) + from_core.astype(F32)).astype(BF16)
                got[dt, dp, n] = shift(both, dp)
                sums.append(both)
        return sums

    got, kept, gathered = {}, {}, {}
    local = swap(columns(tokens, (me ^ 1) * feat, feat))
    arrived = {dt: send_tokens(own_half, dt, 0) for dt in range(1, chips)}
    sums = send_partials((tokens, me, local), got, 0)
    if sums:
        local = after(local, *sums)
    kept[0] = partial((tokens, me, local), 0, 0, part)
    late_tokens = after(tokens, kept[0][0])
    neighbour_tokens = swap(late_tokens)
    late_half = after(own_half, *sums) if sums else own_half

    for dt in range(1, chips):
        gathered[dt, 0] = pair_z(after(arrived[dt], *sums))
        whole = gathered[dt, 0]
        top = columns(whole, core * feat, feat)
        bottom = swap(columns(whole, (1 - core) * feat, feat))
        pair = (top, jnp.int32(0), bottom)
        sums = send_partials(pair, got, dt)
        pair = (top, jnp.int32(0), after(bottom, *sums))
        kept[dt] = partial(pair, 0, 0, part)
        for g in range(1, chips):
            gathered[dt, g] = pair_z(after(send_tokens(late_half, dt, g), kept[dt][0]))

    def activate(e, first, width, n):
        terms = [lax.slice_in_dim(term, first, first + width, axis=2) for term in kept[e]]
        terms += [got[(e + dp) % chips, dp, n] for dp in range(1, chips)]
        total = sum(term.astype(F32) for term in terms)
        return (jax.nn.silu(total[0]) * total[1]).astype(BF16)

    totals = {u: None for u in range(chips)}
    for e in list(range(1, chips)) + [0]:
        values = [activate(e, *chunk, n) for n, chunk in enumerate(chunks)]
        spans = list(chunks)
        if e:
            values, spans = [jnp.concatenate(values, axis=1)], [(0, part)]
        sent = [[value] + [shift(value, d) for d in range(1, chips)] for value in values]
        for (first, width), copies in zip(spans, sent):
            for d, mine in enumerate(copies):
                u = (e - d + chips) % chips
                row = lax.rem(chip - d + chips, chips) * part + first
                totals[u] = down_add(totals[u], mine, swap(mine), down_weight, row)

    token_rows = []
    for dt in range(chips):
        if dt == 0:
            token_rows += [tokens, neighbour_tokens]
            continue
        else:
            full = jnp.zeros((rows, model), BF16)
            for g in range(chips):
                features = lax.rem(chip + g, chips) * (2 * feat)
                full = lax.dynamic_update_slice_in_dim(full, gathered[dt, g], features, 1)
        token_rows += [full, swap(full)]
    inputs = jnp.concatenate(token_rows, axis=0)
    count = inputs.shape[0]

    blocks, share, size = right_factor.shape
    ratio = tensor_count // fsdp_count
    turn = []
    for a in range(fsdp_count):
        for b in range(tensor_count):
            turn.append((a * tensor_count + b, (b // ratio) * tensor_count + a * ratio + b % ratio))
    back = [(b, a) for a, b in turn]
    right_rows = gather_z(lax.ppermute(right_factor, ("fsdp", "tensor"), turn)[None])
    right_rows = right_rows.reshape(fsdp_count, ratio, blocks, share, size)
    right_rows = right_rows.transpose(0, 2, 1, 3, 4).reshape(
        fsdp_count * blocks, ratio * share, size
    )
    left_rows = jnp.moveaxis(gather_z(jnp.moveaxis(left_factor, 1, 0)), 0, 1)

    block_input = inputs.reshape(count, fsdp_count * blocks, size)
    mixed = jnp.einsum(
        "nim,ijm->nij", block_input, right_rows, preferred_element_type=F32
    ).astype(BF16)
    student = jnp.einsum("nij,jki->njk", mixed, left_rows, preferred_element_type=F32)
    target = jnp.concatenate([totals[u] for u in range(chips)], axis=0)
    scale = 1.0 / math.sqrt(count)
    out_grad = (student * (1.0 / tensor_count) - target.reshape(student.shape)) * scale
    out_grad = out_grad.astype(BF16)
    grad_left = jnp.einsum("njk,nij->kji", out_grad, mixed, preferred_element_type=F32)
    mixed_grad = jnp.einsum(
        "njk,jki->nij", out_grad, left_rows, preferred_element_type=F32
    ).astype(BF16)
    grad_right = jnp.einsum(
        "nij,nim->ijm", mixed_grad, block_input, preferred_element_type=F32
    )
    grad_left = scatter_z(
        grad_left.reshape((tensor_count, -1) + grad_left.shape[1:])
    )
    grad_left = jnp.moveaxis(grad_left, 0, 1)
    grad_right = grad_right.reshape(fsdp_count, blocks, ratio, share, size)
    grad_right = grad_right.transpose(0, 2, 1, 3, 4).reshape(
        tensor_count, blocks, share, size
    )
    grad_right = lax.ppermute(scatter_z(grad_right), ("fsdp", "tensor"), back)
    return grad_right, grad_left


def pack_kernel(idx_ref, tokens_ref, first_ref, rest_ref, sems):
    half, width = first_ref.shape
    row = pl.multiple_of(idx_ref[0] * half, half)
    copies = []
    for n, out_ref in enumerate((first_ref, rest_ref)):
        column = pl.multiple_of(idx_ref[n + 1] * width, width)
        source = tokens_ref.at[pl.ds(row, half), pl.ds(column, width)]
        copies.append(pltpu.make_async_copy(source, out_ref, sems.at[n]))
    for copy in copies:
        copy.start()
    for copy in copies:
        copy.wait()


def pack_tokens(tokens, half, chip):
    rows, model = tokens.shape
    shape = jax.ShapeDtypeStruct((rows // 2, model // 2), BF16)
    return pl.pallas_call(
        pack_kernel,
        in_specs=[pl.BlockSpec(memory_space=pltpu.SMEM), pl.BlockSpec(memory_space=pl.ANY)],
        out_specs=[pl.BlockSpec(memory_space=pl.ANY)] * 2,
        out_shape=[shape, shape],
        scratch_shapes=[pltpu.SemaphoreType.DMA((2,))],
        cost_estimate=SMALL,
        name="pack_tokens",
    )(jnp.stack([half, 1 - chip, chip]).astype(jnp.int32), tokens)


def products_kernel(sets, idx_ref, *refs):
    pieces, (gate_ref, up_ref, mine_ref, other_ref) = refs[: 4 * sets], refs[4 * sets :]
    lhs = jnp.concatenate([piece[...] for piece in pieces], axis=0)
    rows = mine_ref.shape[2]
    for slot, weight_ref in enumerate((gate_ref, up_ref)):
        product = jnp.dot(lhs, weight_ref[...], preferred_element_type=F32).astype(BF16)
        for u in range(sets):
            mine_ref[u, slot] = product[2 * u * rows : (2 * u + 1) * rows]
            other_ref[u, slot] = product[(2 * u + 1) * rows : (2 * u + 2) * rows]


def products(pieces, scalars, gate, up, first, width):
    feat = gate.shape[0]
    sets = len(pieces) // 4
    half = pieces[0][0].shape[0]
    half = half // 2 if pieces[0][1] is not None else half
    start = first // BLK

    def piece_spec(row, column):
        if row is None:
            return pl.BlockSpec((half, feat), lambda n, s: (0, s[column]))
        return pl.BlockSpec((half, feat), lambda n, s: (s[row], s[column]))

    weight_spec = pl.BlockSpec((feat, BLK), lambda n, s: (0, s[4] + start + n))
    out_spec = pl.BlockSpec((sets, 2, 2 * half, BLK), lambda n, s: (0, 0, 0, n))
    shape = jax.ShapeDtypeStruct((sets, 2, 2 * half, width), BF16)
    return pl.pallas_call(
        functools.partial(products_kernel, sets),
        grid_spec=pltpu.PrefetchScalarGridSpec(
            num_scalar_prefetch=1,
            grid=(width // BLK,),
            in_specs=[piece_spec(row, column) for _, row, column in pieces]
            + [weight_spec, weight_spec],
            out_specs=[out_spec, out_spec],
        ),
        out_shape=[shape, shape],
        compiler_params=pltpu.CompilerParams(vmem_limit_bytes=50 * 2**20),
        cost_estimate=SMALL,
        name="gate_up_products",
    )(scalars, *[piece for piece, _, _ in pieces], gate, up)


def target_kernel(idx_ref, *refs):
    pieces, weight_ref, out_ref = refs[:4], refs[4], refs[-1]
    lhs = jnp.concatenate([piece[...] for piece in pieces], axis=0)
    product = jnp.dot(lhs, weight_ref[...], preferred_element_type=F32)

    @pl.when(pl.program_id(0) == 0)
    def _():
        out_ref[...] = refs[5][...] + product if len(refs) > 6 else product

    @pl.when(pl.program_id(0) > 0)
    def _():
        out_ref[...] += product


def target_add(total, pieces, weight, row, width):
    rows, outs = pieces[0][0].shape[0], weight.shape[1]
    scalars = jnp.reshape(lax.div(row, BLK), (1,)).astype(jnp.int32)

    def piece_spec(first):
        return pl.BlockSpec((rows, BLK), lambda k, s: (0, first // BLK + k))

    whole = pl.BlockSpec((4 * rows, outs), lambda k, s: (0, 0))
    totals = [] if total is None else [total]
    return pl.pallas_call(
        target_kernel,
        grid_spec=pltpu.PrefetchScalarGridSpec(
            num_scalar_prefetch=1,
            grid=(width // BLK,),
            in_specs=[piece_spec(first) for _, first in pieces]
            + [pl.BlockSpec((BLK, outs), lambda k, s: (s[0] + k, 0))]
            + [whole] * len(totals),
            out_specs=whole,
        ),
        out_shape=jax.ShapeDtypeStruct((4 * rows, outs), F32),
        compiler_params=pltpu.CompilerParams(vmem_limit_bytes=50 * 2**20),
        cost_estimate=SMALL,
        name="target_add",
    )(scalars, *[piece for piece, _ in pieces], weight, *totals)


TN = (((0,), (0,)), ((), ()))
NT = (((1,), (1,)), ((), ()))
WIDE = 8


def natural(step, chip, per_chip):
    return lax.rem(chip + step // per_chip, 2) * per_chip + lax.rem(step, per_chip)


def student_kernel(steps, late, tensor_count, idx_ref, *refs):
    count = 12 if late else 4
    tokens, (right_ref, left_ref, mixed_ref, student_ref, scratch) = refs[:-5], refs[-5:]
    step = pl.program_id(0)
    chunk = natural(step, idx_ref[2], steps // 2)
    pairs = right_ref.shape[2]
    size = right_ref.shape[3]

    def mix(pieces):
        for t in range(WIDE):
            rows = [piece[:, t * size : (t + 1) * size] for piece in pieces]
            part = lax.dot_general(
                right_ref[0, t], jnp.concatenate(rows, axis=0), NT, preferred_element_type=F32
            )
            start = pl.multiple_of((chunk * WIDE + t) * pairs, pairs)
            for h in range(scratch.shape[0]):
                scratch[h, pl.ds(start, pairs), :] = part[:, h * LANES : (h + 1) * LANES]

    if late:
        pl.when(step < steps // 2)(lambda: mix(tokens[:4]))
        pl.when(step >= steps // 2)(lambda: mix(tokens[4:]))
    else:
        mix(tokens)

    @pl.when(step == steps - 1)
    def _():
        blocks = steps * WIDE
        for j in range(pairs):
            for h in range(scratch.shape[0]):
                rows = scratch[h, pl.ds(j, blocks, stride=pairs), :]
                mixed_ref[j * blocks : (j + 1) * blocks, h * LANES : (h + 1) * LANES] = (
                    rows.astype(BF16)
                )
        for g in range(left_ref.shape[0]):
            span = slice(g * BLK, (g + 1) * BLK)
            student_ref[:, span] = lax.dot_general(
                mixed_ref[span, :], left_ref[g], TN, preferred_element_type=F32
            ) * (1.0 / tensor_count)


def token_specs(half, width, steps, begin, own):
    def chunk(n, s):
        step = jnp.maximum(n - begin, 0)
        return natural(step, s[2], steps // 2)

    if own:
        return [
            pl.BlockSpec((half, width), lambda n, s, p=p: (s[p % 2], chunk(n, s)))
            for p in range(4)
        ]
    near = pl.BlockSpec(
        (half, width), lambda n, s: (0, jnp.clip(n - begin, 0, steps // 2 - 1))
    )
    far = pl.BlockSpec(
        (half, width),
        lambda n, s: (0, jnp.clip(n - begin - steps // 2, 0, steps // 2 - 1)),
    )
    return [near] * 4 + [far] * 4


def student_part(tokens, late, scalars, right_rows, left_diag, tensor_count):
    per_owner, pairs, size = right_rows.shape[1:]
    blocks = right_rows.shape[0] * per_owner
    steps = blocks // WIDE
    half = tokens[0].shape[0] if late else tokens[0].shape[0] // 2
    halves = per_owner // WIDE

    def right_block(n, s):
        chunk = natural(n, s[2], steps // 2)
        return (s[3] ^ (chunk // halves), lax.rem(chunk, halves), 0, 0)

    outs = left_diag.shape[0] * BLK
    return pl.pallas_call(
        functools.partial(student_kernel, steps, late, tensor_count),
        grid_spec=pltpu.PrefetchScalarGridSpec(
            num_scalar_prefetch=1,
            grid=(steps,),
            in_specs=token_specs(half, WIDE * size, steps, 0, not late)
            + [
                pl.BlockSpec((1, WIDE, pairs, size), right_block),
                pl.BlockSpec(left_diag.shape, lambda n, s: (0, 0, 0)),
            ],
            out_specs=[
                pl.BlockSpec((pairs * blocks, 4 * half), lambda n, s: (0, 0)),
                pl.BlockSpec((4 * half, outs), lambda n, s: (0, 0)),
            ],
            scratch_shapes=[pltpu.VMEM((4 * half // LANES, pairs * blocks, LANES), F32)],
        ),
        out_shape=[
            jax.ShapeDtypeStruct((pairs * blocks, 4 * half), BF16),
            jax.ShapeDtypeStruct((4 * half, outs), F32),
        ],
        compiler_params=pltpu.CompilerParams(vmem_limit_bytes=50 * 2**20),
        cost_estimate=SMALL,
        name="student_part",
    )(scalars, *tokens, right_rows, left_diag)


def grads_kernel(groups, steps, scale, idx_ref, *refs):
    total_ref, student0, student1, mixed0, mixed1, left_ref = refs[:6]
    own, near, far = refs[6:10], refs[10:14], refs[14:18]
    out_ref, scratch = refs[18:]
    step = pl.program_id(0)
    z = idx_ref[3]
    parts, size = out_ref.shape[0], out_ref.shape[2]
    pairs = scratch.shape[1] // (steps * WIDE)
    blocks = steps * WIDE
    per_part = blocks // parts

    def place(owner):
        far_bits = z ^ owner
        return lax.rem(far_bits, 2) * 2 + far_bits // 2

    @pl.when(step < groups)
    def _():
        student = jnp.concatenate([student0[...], student1[...]], axis=0)
        out_grad = ((student - total_ref[...]) * scale).astype(BF16)
        mixed = jnp.concatenate([mixed0[...], mixed1[...]], axis=1)
        left = jnp.dot(mixed, out_grad, preferred_element_type=F32).T
        row = pl.multiple_of(step * BLK, BLK)
        back = lax.dot_general(left_ref[0], out_grad, NT, preferred_element_type=F32)
        for h in range(scratch.shape[0]):
            scratch[h, pl.ds(row, BLK), :] = back[:, h * LANES : (h + 1) * LANES]
        low = lax.broadcasted_iota(jnp.int32, (blocks, size), 1) < blocks
        share = blocks // parts
        for pair in range(BLK // size):
            lanes = slice(pair * size, (pair + 1) * size)
            top = left[pair * size : pair * size + blocks, lanes]
            bottom = left[pair * size + blocks : (pair + 1) * size, lanes]
            both = jnp.where(low, top, bottom).astype(BF16)
            begin = per_part * pairs + (step * (BLK // size) + pair) * share
            begin = pl.multiple_of(begin, share)
            for owner in range(parts):
                out_ref[place(owner), pl.ds(begin, share), :] = both[
                    owner * share : (owner + 1) * share
                ]

    def right(later):
        chunk = natural(step - groups, idx_ref[2], steps // 2)
        for t in range(WIDE):
            block = chunk * WIDE + t
            rows = [piece[:, t * size : (t + 1) * size] for piece in own + later]
            lhs = [
                scratch[h, pl.ds(block, pairs, stride=blocks), :]
                for h in range(scratch.shape[0])
            ]
            lhs = jnp.concatenate(lhs, axis=1).astype(BF16)
            value = jnp.dot(
                lhs, jnp.concatenate(rows, axis=0), preferred_element_type=F32
            )
            begin = pl.multiple_of(lax.rem(block, per_part) * pairs, pairs)
            out_ref[place(block // per_part), pl.ds(begin, pairs), :] = value.astype(BF16)

    pl.when((step >= groups) & (step < groups + steps // 2))(lambda: right(near))
    pl.when(step >= groups + steps // 2)(lambda: right(far))


def factor_grads(total, students, mixed, left_diag, own, late, scalars, parts, size, scale):
    groups, count = left_diag.shape[0], total.shape[0]
    rows = mixed[0].shape[0]
    half = late[0].shape[0]
    steps = own[0].shape[1] // (WIDE * size)
    pairs = rows // (steps * WIDE)

    def group(n):
        return jnp.minimum(n, groups - 1)

    out_rows = (rows + pairs * (steps * WIDE) * (steps * WIDE) // size) // parts
    return pl.pallas_call(
        functools.partial(grads_kernel, groups, steps, scale),
        grid_spec=pltpu.PrefetchScalarGridSpec(
            num_scalar_prefetch=1,
            grid=(groups + steps,),
            in_specs=[pl.BlockSpec((count, BLK), lambda n, s: (0, group(n)))]
            + [pl.BlockSpec((count // 2, BLK), lambda n, s: (0, group(n)))] * 2
            + [pl.BlockSpec((BLK, count // 2), lambda n, s: (group(n), 0))] * 2
            + [pl.BlockSpec((1, BLK, BLK), lambda n, s: (group(n), 0, 0))]
            + token_specs(half, WIDE * size, steps, groups, True)
            + token_specs(half, WIDE * size, steps, groups, False),
            out_specs=pl.BlockSpec((parts, out_rows, size), lambda n, s: (0, 0, 0)),
            scratch_shapes=[pltpu.VMEM((count // LANES, rows, LANES), F32)],
        ),
        out_shape=jax.ShapeDtypeStruct((parts, out_rows, size), BF16),
        compiler_params=pltpu.CompilerParams(vmem_limit_bytes=50 * 2**20),
        cost_estimate=SMALL,
        name="factor_grads",
    )(scalars, total, *students, *mixed, left_diag, *own, *late)


def tiled_body(tokens, gate_weight, up_weight, down_weight, right_factor, left_factor):
    fsdp_count = lax.axis_size("fsdp")
    tensor_count = lax.axis_size("tensor")
    rows, model = tokens.shape
    part = gate_weight.shape[1] // 2
    me, z = lax.axis_index("fsdp"), lax.axis_index("tensor")
    chip, core, odd = lax.div(me, 2), lax.rem(me, 2), lax.rem(z, 2)
    both_axes = ("fsdp", "tensor")

    def swap(value):
        return lax.ppermute(value, "fsdp", [(i, i ^ 1) for i in range(fsdp_count)])

    def across(value):
        return lax.ppermute(value, "fsdp", [(i, i ^ 2) for i in range(fsdp_count)])

    def along(value, bit):
        return lax.ppermute(value, "tensor", [(i, i ^ bit) for i in range(tensor_count)])

    def turn(value, bit):
        perm = []
        for f in range(fsdp_count):
            for t in range(tensor_count):
                perm.append((f * tensor_count + t, (t ^ bit) * tensor_count + f))
        return lax.ppermute(value, both_axes, perm)

    def after(value, *others):
        return lax.optimization_barrier((value,) + others)[0]

    def gather(value):
        value = value[None]
        for bit in (1, 2):
            value = jnp.concatenate([value, along(value, bit)], axis=0)
        return value

    def add(*terms):
        return sum(term.astype(F32) for term in terms)

    head = (part // BLK + 1) // 2 * BLK
    chunks = [(0, head), (head, part - head)]

    near_tokens = swap(tokens)
    first, rest = pack_tokens(tokens, odd, chip)
    arrived = across(first)
    base = jnp.stack([odd, 1 - odd])
    mine_block = lax.div(part, BLK) * chip
    other_block = lax.div(part, BLK) * (1 - chip)

    def scalars(block):
        return jnp.concatenate([base, jnp.stack([me, core, block])]).astype(jnp.int32)

    own_pieces = [(t, row, 2) for t in (tokens, near_tokens) for row in (0, 1)]
    got = {}

    def send(e, pieces, order):
        values = [
            products(pieces, order, gate_weight, up_weight, *chunk) for chunk in chunks
        ]
        swapped = [swap(other[0]) for _, other in values]
        sums = [add(mine[0], s).astype(BF16) for (mine, _), s in zip(values, swapped)]
        got[e] = [across(value) for value in sums]
        return values, sums

    values, sums = send(0, own_pieces, scalars(other_block))
    last = values[-1][0]

    right_rows = gather(turn(after(right_factor, first), 0))
    left_rows = gather(after(left_factor, last))
    for axis, bit in ((0, 2), (1, 1)):
        split = left_rows.reshape((2, 2) + left_rows.shape[1:])
        split = jnp.where(lax.rem(lax.div(z, bit), 2) == 1, jnp.flip(split, axis), split)
        left_rows = split.reshape(left_rows.shape)
    left_rows = left_rows.transpose(1, 3, 0, 2)
    pairs, blocks = left_rows.shape[:2]
    left_rows = left_rows.reshape(-1, BLK // blocks, blocks, 1, blocks)
    eye = jnp.eye(BLK // blocks, dtype=jnp.bool_)[None, :, None, :, None]
    left_diag = jnp.where(eye, left_rows, jnp.zeros((), BF16)).reshape(-1, BLK, BLK)

    arrived = after(arrived, last)
    partner = along(arrived, 1)
    near_arrived = swap(arrived)
    late_first = across(after(rest, *sums))
    order = jnp.concatenate([base, jnp.stack([chip, z])]).astype(jnp.int32)
    own = [tokens, tokens, near_tokens, near_tokens]
    mixed0, student0 = student_part(
        [after(tokens, *sums)] + own[1:], False, order, right_rows, left_diag, tensor_count
    )
    partner = after(partner, mixed0)
    late = [arrived, partner, near_arrived, swap(partner)]
    late_pieces = [(t, None, 3) for t in late]
    values, sums = send(1, late_pieces, scalars(other_block))

    kept, other = products(
        own_pieces + late_pieces,
        after(scalars(mine_block), *sums),
        gate_weight,
        up_weight,
        0,
        part,
    )
    kept_other = swap(other)
    late_first = after(late_first, kept)
    late_partner = along(late_first, 1)
    late_rest = [late_first, late_partner, swap(late_first), swap(late_partner)]

    def activate(u, span, term):
        begin, width = span
        terms = [value[u, :, :, begin : begin + width] for value in (kept, kept_other)]
        total = add(*terms, term)
        return (jax.nn.silu(total[0]) * total[1]).astype(BF16)

    hidden_late = jnp.concatenate(
        [activate(1, span, term) for span, term in zip(chunks, got[0])], axis=1
    )
    got_late = across(hidden_late)
    near_hidden_late = swap(hidden_late)
    mixed1, student1 = student_part(
        late + late_rest, True, order, right_rows, left_diag, tensor_count
    )
    near_got_late = swap(got_late)
    total = None
    hidden = [activate(0, span, term) for span, term in zip(chunks, got[1])]
    got_hidden = [across(value) for value in hidden]
    for span, value in zip(chunks, hidden):
        begin, width = span
        pieces = [(value, 0), (swap(value), 0), (hidden_late, begin), (near_hidden_late, begin)]
        total = target_add(total, pieces, down_weight, chip * part + begin, width)
    for span, value in zip(chunks, got_hidden):
        begin, width = span
        pieces = [(got_late, begin), (near_got_late, begin), (value, 0), (swap(value), 0)]
        total = target_add(total, pieces, down_weight, (1 - chip) * part + begin, width)

    grads = factor_grads(
        total,
        (student0, student1),
        (mixed0, mixed1),
        left_diag,
        own,
        late + late_rest,
        order,
        tensor_count,
        right_factor.shape[2],
        1.0 / math.sqrt(rows * fsdp_count),
    )
    summed = add(grads[:2], along(grads[2:], 1)).astype(BF16)
    right_shape = right_factor.shape
    cut = right_shape[0] * right_shape[1]
    grad_right = add(turn(summed[0, :cut], 0), turn(summed[1, :cut], 2))
    grad_left = add(summed[0, cut:], along(summed[1, cut:], 2))
    grad_left = grad_left.reshape(pairs // 2, -1, 2, blocks).transpose(0, 2, 1, 3)
    return grad_right.reshape(right_shape), grad_left.reshape(left_factor.shape)


def body(*args):
    tokens, gate_weight, _, _, right_factor, left_factor = args
    counts = (lax.axis_size("fsdp"), lax.axis_size("tensor"))
    feat, hid = gate_weight.shape
    per_owner, share, size = right_factor.shape
    blocks = left_factor.shape[2]
    fits = hid % (2 * BLK) == 0
    fits = fits and counts == (4, 4) and tokens.shape[0] == 128
    fits = fits and hid >= 4 * BLK and feat % BLK == 0
    fits = fits and size == 128 and 2 * blocks == size and per_owner % WIDE == 0
    fits = fits and left_factor.shape[0] == share and share % 16 == 0
    return (tiled_body if fits else general_body)(*args)


def solution(mesh):
    return jax.shard_map(
        body,
        mesh=mesh,
        in_specs=(
            P(("groups", "fsdp"), None),
            P("fsdp", "tensor"),
            P("fsdp", "tensor"),
            P("tensor", "fsdp"),
            P("fsdp", "tensor", None),
            P("fsdp", "tensor", None),
        ),
        out_specs=(P(("groups", "fsdp"), "tensor", None), P(("groups", "fsdp"), "tensor", None)),
        check_vma=False,
    )
```

```python
import functools
import math

import jax
import jax.numpy as jnp
from jax import lax
from jax.experimental import pallas as pl
from jax.experimental.pallas import tpu as pltpu
from jax.sharding import PartitionSpec as P

BLK = 256
LANES = 128
SMALL = pl.CostEstimate(flops=1, bytes_accessed=1, transcendentals=0)
F32 = jnp.float32
BF16 = jnp.bfloat16


def gate_up_kernel(idx_ref, top_ref, bottom_ref, gate_ref, up_ref, mine_ref, other_ref):
    rows = top_ref.shape[0]
    lhs = jnp.concatenate([top_ref[...], bottom_ref[...]], axis=0)
    for slot, weight_ref in enumerate((gate_ref, up_ref)):
        product = jnp.dot(lhs, weight_ref[...], preferred_element_type=F32).astype(BF16)
        mine_ref[slot] = product[:rows]
        other_ref[slot] = product[rows:]


def gate_up(top, top_block, bottom, gate, up, column, first, width):
    rows, feat = bottom.shape
    if width % BLK or gate.shape[1] % BLK or rows % 16 or feat % 128:
        lhs = jnp.concatenate(
            [lax.dynamic_slice_in_dim(top, top_block * feat, feat, 1), bottom], axis=0
        )
        both = [
            jnp.dot(
                lhs,
                lax.dynamic_slice_in_dim(w, column + first, width, 1),
                preferred_element_type=F32,
            ).astype(BF16)
            for w in (gate, up)
        ]
        both = jnp.stack(both)
        return both[:, :rows], both[:, rows:]
    scalars = jnp.stack([top_block, lax.div(column, BLK) + first // BLK]).astype(jnp.int32)
    weight_spec = pl.BlockSpec((feat, BLK), lambda n, s: (0, s[1] + n))
    out_spec = pl.BlockSpec((2, rows, BLK), lambda n, s: (0, 0, n))
    shape = jax.ShapeDtypeStruct((2, rows, width), BF16)
    return pl.pallas_call(
        gate_up_kernel,
        grid_spec=pltpu.PrefetchScalarGridSpec(
            num_scalar_prefetch=1,
            grid=(width // BLK,),
            in_specs=[
                pl.BlockSpec((rows, feat), lambda n, s: (0, s[0])),
                pl.BlockSpec((rows, feat), lambda n, s: (0, 0)),
                weight_spec,
                weight_spec,
            ],
            out_specs=[out_spec, out_spec],
        ),
        out_shape=[shape, shape],
        compiler_params=pltpu.CompilerParams(vmem_limit_bytes=50 * 2**20),
        cost_estimate=pl.CostEstimate(
            flops=2 * 2 * rows * feat * 2 * width,
            bytes_accessed=2 * feat * 2 * width + 2 * 2 * rows * (feat + 2 * width),
            transcendentals=0,
        ),
        name="gate_up",
    )(scalars, top, bottom, gate, up)


def down_kernel(idx_ref, mine_ref, other_ref, weight_ref, *refs):
    out_ref = refs[-1]
    lhs = jnp.concatenate([mine_ref[...], other_ref[...]], axis=0)
    product = jnp.dot(lhs, weight_ref[...], preferred_element_type=F32)

    @pl.when(pl.program_id(0) == 0)
    def _():
        out_ref[...] = refs[0][...] + product if len(refs) > 1 else product

    @pl.when(pl.program_id(0) > 0)
    def _():
        out_ref[...] += product


def down_add(total, mine, other, weight, row):
    rows, width = mine.shape
    outs = weight.shape[1]
    if width % BLK or weight.shape[0] % BLK or rows % 16 or outs % 128:
        lhs = jnp.concatenate([mine, other], axis=0)
        part = lax.dynamic_slice_in_dim(weight, row, width, 0)
        product = jnp.dot(lhs, part, preferred_element_type=F32)
        return product if total is None else total + product
    scalars = jnp.reshape(lax.div(row, BLK), (1,)).astype(jnp.int32)
    hidden_spec = pl.BlockSpec((rows, BLK), lambda k, s: (0, k))
    whole = pl.BlockSpec((2 * rows, outs), lambda k, s: (0, 0))
    totals = [] if total is None else [total]
    return pl.pallas_call(
        down_kernel,
        grid_spec=pltpu.PrefetchScalarGridSpec(
            num_scalar_prefetch=1,
            grid=(width // BLK,),
            in_specs=[
                hidden_spec,
                hidden_spec,
                pl.BlockSpec((BLK, outs), lambda k, s: (s[0] + k, 0)),
            ]
            + [whole] * len(totals),
            out_specs=whole,
        ),
        out_shape=jax.ShapeDtypeStruct((2 * rows, outs), F32),
        compiler_params=pltpu.CompilerParams(vmem_limit_bytes=50 * 2**20),
        cost_estimate=pl.CostEstimate(
            flops=2 * 2 * rows * width * outs,
            bytes_accessed=2 * width * outs + 2 * 2 * rows * width + 16 * rows * outs,
            transcendentals=0,
        ),
        name="down_add",
    )(scalars, mine, other, weight, *totals)


def general_body(tokens, gate_weight, up_weight, down_weight, right_factor, left_factor):
    fsdp_count = lax.axis_size("fsdp")
    tensor_count = lax.axis_size("tensor")
    chips = fsdp_count // 2
    rows, model = tokens.shape
    feat, hid = gate_weight.shape
    part = hid // chips
    me = lax.axis_index("fsdp")
    chip, core = lax.div(me, 2), lax.rem(me, 2)
    z = lax.axis_index("tensor")

    def swap(value):
        return lax.ppermute(value, "fsdp", [(i, i ^ 1) for i in range(fsdp_count)])

    def shift(value, hops):
        perm = [(i, (i + 2 * hops) % fsdp_count) for i in range(fsdp_count)]
        return lax.ppermute(value, "fsdp", perm)

    def gather_z(value):
        if tensor_count > 4:
            return lax.all_gather(value, "tensor", axis=0, tiled=True)
        size = value.shape[0]
        whole = jnp.zeros((size * tensor_count,) + value.shape[1:], value.dtype)
        whole = lax.dynamic_update_slice_in_dim(whole, value, z * size, 0)
        for step in range(1, tensor_count):
            perm = [(i, (i + step) % tensor_count) for i in range(tensor_count)]
            got = lax.ppermute(value, "tensor", perm)
            source = lax.rem(z - step + tensor_count, tensor_count)
            whole = lax.dynamic_update_slice_in_dim(whole, got, source * size, 0)
        return whole

    def scatter_z(value):
        if tensor_count > 4:
            return lax.psum_scatter(value, "tensor", scatter_dimension=0, tiled=False)
        total = lax.dynamic_index_in_dim(value, z, 0, keepdims=False)
        for step in range(1, tensor_count):
            target_z = lax.rem(z + step, tensor_count)
            piece = lax.dynamic_index_in_dim(value, target_z, 0, keepdims=False)
            perm = [(i, (i + step) % tensor_count) for i in range(tensor_count)]
            total += lax.ppermute(piece.astype(BF16), "tensor", perm).astype(F32)
        return total

    def columns(value, start, width):
        return lax.dynamic_slice_in_dim(value, start, width, 1)

    def after(value, *others):
        return lax.optimization_barrier((value,) + others)[0]

    def pair_z(value):
        perm = [(i, i ^ 1) for i in range(tensor_count)]
        got = lax.ppermute(value, "tensor", perm)
        odd = lax.rem(z, 2) == 1
        return jnp.concatenate(
            [jnp.where(odd, got, value), jnp.where(odd, value, got)], axis=0
        )

    if part % BLK == 0 and part // BLK > 1:
        head = (part // BLK + 1) // 2 * BLK
        chunks = [(0, head), (head, part - head)]
    else:
        chunks = [(0, part)]

    half = rows // 2
    own_half = lax.dynamic_slice_in_dim(tokens, lax.rem(z, 2) * half, half, 0)

    def send_tokens(value, dt, g):
        features = lax.rem(chip - dt + g + chips, chips) * (2 * feat)
        return shift(columns(value, features, 2 * feat), -dt)

    def partial(pair, dp, first, width):
        column = lax.rem(chip + dp, chips) * part
        top, block, bottom = pair
        mine, other = gate_up(top, block, bottom, gate_weight, up_weight, column, first, width)
        return mine, swap(other)

    def send_partials(pair, got, dt):
        sums = []
        for dp in range(1, chips):
            pieces = [partial(pair, dp, *chunk) for chunk in chunks]
            for n, (mine, from_core) in enumerate(pieces):
                both = (mine.astype(F32) + from_core.astype(F32)).astype(BF16)
                got[dt, dp, n] = shift(both, dp)
                sums.append(both)
        return sums

    got, kept, gathered = {}, {}, {}
    local = swap(columns(tokens, (me ^ 1) * feat, feat))
    arrived = {dt: send_tokens(own_half, dt, 0) for dt in range(1, chips)}
    sums = send_partials((tokens, me, local), got, 0)
    if sums:
        local = after(local, *sums)
    kept[0] = partial((tokens, me, local), 0, 0, part)
    late_tokens = after(tokens, kept[0][0])
    neighbour_tokens = swap(late_tokens)
    late_half = after(own_half, *sums) if sums else own_half

    for dt in range(1, chips):
        gathered[dt, 0] = pair_z(after(arrived[dt], *sums))
        whole = gathered[dt, 0]
        top = columns(whole, core * feat, feat)
        bottom = swap(columns(whole, (1 - core) * feat, feat))
        pair = (top, jnp.int32(0), bottom)
        sums = send_partials(pair, got, dt)
        pair = (top, jnp.int32(0), after(bottom, *sums))
        kept[dt] = partial(pair, 0, 0, part)
        for g in range(1, chips):
            gathered[dt, g] = pair_z(after(send_tokens(late_half, dt, g), kept[dt][0]))

    def activate(e, first, width, n):
        terms = [lax.slice_in_dim(term, first, first + width, axis=2) for term in kept[e]]
        terms += [got[(e + dp) % chips, dp, n] for dp in range(1, chips)]
        total = sum(term.astype(F32) for term in terms)
        return (jax.nn.silu(total[0]) * total[1]).astype(BF16)

    totals = {u: None for u in range(chips)}
    for e in list(range(1, chips)) + [0]:
        values = [activate(e, *chunk, n) for n, chunk in enumerate(chunks)]
        spans = list(chunks)
        if e:
            values, spans = [jnp.concatenate(values, axis=1)], [(0, part)]
        sent = [[value] + [shift(value, d) for d in range(1, chips)] for value in values]
        for (first, width), copies in zip(spans, sent):
            for d, mine in enumerate(copies):
                u = (e - d + chips) % chips
                row = lax.rem(chip - d + chips, chips) * part + first
                totals[u] = down_add(totals[u], mine, swap(mine), down_weight, row)

    token_rows = []
    for dt in range(chips):
        if dt == 0:
            token_rows += [tokens, neighbour_tokens]
            continue
        else:
            full = jnp.zeros((rows, model), BF16)
            for g in range(chips):
                features = lax.rem(chip + g, chips) * (2 * feat)
                full = lax.dynamic_update_slice_in_dim(full, gathered[dt, g], features, 1)
        token_rows += [full, swap(full)]
    inputs = jnp.concatenate(token_rows, axis=0)
    count = inputs.shape[0]

    blocks, share, size = right_factor.shape
    ratio = tensor_count // fsdp_count
    turn = []
    for a in range(fsdp_count):
        for b in range(tensor_count):
            turn.append((a * tensor_count + b, (b // ratio) * tensor_count + a * ratio + b % ratio))
    back = [(b, a) for a, b in turn]
    right_rows = gather_z(lax.ppermute(right_factor, ("fsdp", "tensor"), turn)[None])
    right_rows = right_rows.reshape(fsdp_count, ratio, blocks, share, size)
    right_rows = right_rows.transpose(0, 2, 1, 3, 4).reshape(
        fsdp_count * blocks, ratio * share, size
    )
    left_rows = jnp.moveaxis(gather_z(jnp.moveaxis(left_factor, 1, 0)), 0, 1)

    block_input = inputs.reshape(count, fsdp_count * blocks, size)
    mixed = jnp.einsum(
        "nim,ijm->nij", block_input, right_rows, preferred_element_type=F32
    ).astype(BF16)
    student = jnp.einsum("nij,jki->njk", mixed, left_rows, preferred_element_type=F32)
    target = jnp.concatenate([totals[u] for u in range(chips)], axis=0)
    scale = 1.0 / math.sqrt(count)
    out_grad = (student * (1.0 / tensor_count) - target.reshape(student.shape)) * scale
    out_grad = out_grad.astype(BF16)
    grad_left = jnp.einsum("njk,nij->kji", out_grad, mixed, preferred_element_type=F32)
    mixed_grad = jnp.einsum(
        "njk,jki->nij", out_grad, left_rows, preferred_element_type=F32
    ).astype(BF16)
    grad_right = jnp.einsum(
        "nij,nim->ijm", mixed_grad, block_input, preferred_element_type=F32
    )
    grad_left = scatter_z(
        grad_left.reshape((tensor_count, -1) + grad_left.shape[1:])
    )
    grad_left = jnp.moveaxis(grad_left, 0, 1)
    grad_right = grad_right.reshape(fsdp_count, blocks, ratio, share, size)
    grad_right = grad_right.transpose(0, 2, 1, 3, 4).reshape(
        tensor_count, blocks, share, size
    )
    grad_right = lax.ppermute(scatter_z(grad_right), ("fsdp", "tensor"), back)
    return grad_right, grad_left


def cut_kernel(idx_ref, first_in, rest_in, first_ref, rest_ref):
    first_ref[...] = first_in[...]
    rest_ref[...] = rest_in[...]


def cut_tokens(tokens, half, chip):
    rows, model = tokens.shape
    block = (rows // 2, model // 2)
    shape = jax.ShapeDtypeStruct(block, BF16)
    whole = pl.BlockSpec(block, lambda n, s: (0, 0))
    return pl.pallas_call(
        cut_kernel,
        grid_spec=pltpu.PrefetchScalarGridSpec(
            num_scalar_prefetch=1,
            grid=(1,),
            in_specs=[
                pl.BlockSpec(block, lambda n, s: (s[0], s[1])),
                pl.BlockSpec(block, lambda n, s: (s[0], s[2])),
            ],
            out_specs=[whole, whole],
        ),
        out_shape=[shape, shape],
        cost_estimate=SMALL,
        name="cut_tokens",
    )(jnp.stack([half, 1 - chip, chip]).astype(jnp.int32), tokens, tokens)


def products_kernel(sets, idx_ref, *refs):
    pieces, (gate_ref, up_ref, mine_ref, other_ref) = refs[: 4 * sets], refs[4 * sets :]
    lhs = jnp.concatenate([piece[...] for piece in pieces], axis=0)
    rows = mine_ref.shape[2]
    for slot, weight_ref in enumerate((gate_ref, up_ref)):
        product = jnp.dot(lhs, weight_ref[...], preferred_element_type=F32).astype(BF16)
        for u in range(sets):
            mine_ref[u, slot] = product[2 * u * rows : (2 * u + 1) * rows]
            other_ref[u, slot] = product[(2 * u + 1) * rows : (2 * u + 2) * rows]


def products(pieces, scalars, gate, up, first, width):
    feat = gate.shape[0]
    sets = len(pieces) // 4
    half = pieces[0][0].shape[0]
    half = half // 2 if pieces[0][1] is not None else half
    start = first // BLK

    def piece_spec(row, column):
        if row is None:
            return pl.BlockSpec((half, feat), lambda n, s: (0, s[column]))
        return pl.BlockSpec((half, feat), lambda n, s: (s[row], s[column]))

    weight_spec = pl.BlockSpec((feat, BLK), lambda n, s: (0, s[4] + start + n))
    out_spec = pl.BlockSpec((sets, 2, 2 * half, BLK), lambda n, s: (0, 0, 0, n))
    shape = jax.ShapeDtypeStruct((sets, 2, 2 * half, width), BF16)
    return pl.pallas_call(
        functools.partial(products_kernel, sets),
        grid_spec=pltpu.PrefetchScalarGridSpec(
            num_scalar_prefetch=1,
            grid=(width // BLK,),
            in_specs=[piece_spec(row, column) for _, row, column in pieces]
            + [weight_spec, weight_spec],
            out_specs=[out_spec, out_spec],
        ),
        out_shape=[shape, shape],
        compiler_params=pltpu.CompilerParams(vmem_limit_bytes=50 * 2**20),
        cost_estimate=SMALL,
        name="gate_up_products",
    )(scalars, *[piece for piece, _, _ in pieces], gate, up)


def fill_rows(lhs, sets):
    row = 0
    for group in sets:
        column = 0
        for piece in group:
            rows, width = piece.shape
            lhs[row : row + rows, column : column + width] = piece[...]
            column += width
        row += group[0].shape[0]


def split_sets(refs, counts):
    sets, start = [], 0
    for count in counts:
        sets.append(refs[start : start + count])
        start += count
    return sets, refs[start:]


def whole_spec(array):
    return pl.BlockSpec(array.shape, lambda n, s: (0,) * array.ndim)


def target_kernel(counts, idx_ref, *refs):
    sets, (weight_ref, out_ref, lhs) = split_sets(refs, counts)
    pl.when(pl.program_id(0) == 0)(lambda: fill_rows(lhs, sets))
    out_ref[...] = jnp.dot(lhs[...], weight_ref[...], preferred_element_type=F32)


def target_part(sets, weight, chip):
    pieces = [piece for group in sets for piece in group]
    width = sum(piece.shape[1] for piece in sets[0])
    rows = sum(group[0].shape[0] for group in sets)
    outs = weight.shape[1]
    return pl.pallas_call(
        functools.partial(target_kernel, [len(group) for group in sets]),
        grid_spec=pltpu.PrefetchScalarGridSpec(
            num_scalar_prefetch=1,
            grid=(outs // BLK,),
            in_specs=[whole_spec(piece) for piece in pieces]
            + [pl.BlockSpec((width, BLK), lambda n, s: (s[0], n))],
            out_specs=pl.BlockSpec((rows, BLK), lambda n, s: (0, n)),
            scratch_shapes=[pltpu.VMEM((rows, width), BF16)],
        ),
        out_shape=jax.ShapeDtypeStruct((rows, outs), F32),
        compiler_params=pltpu.CompilerParams(vmem_limit_bytes=50 * 2**20),
        cost_estimate=SMALL,
        name="target_part",
    )(jnp.reshape(chip, (1,)).astype(jnp.int32), *pieces, weight)


TN = (((0,), (0,)), ((), ()))
NT = (((1,), (1,)), ((), ()))
WIDE = 8


def natural(step, chip, per_chip):
    return lax.rem(chip + step // per_chip, 2) * per_chip + lax.rem(step, per_chip)


def spread_kernel(left_ref, out_ref, scratch):
    groups, fold = out_ref.shape[0], BLK // left_ref.shape[1]
    blocks = left_ref.shape[1]
    scratch[...] = jnp.zeros_like(scratch)
    zeros = jnp.zeros((blocks, blocks), F32)
    for g in range(groups):
        for a in range(fold):
            value = left_ref[g * fold + a].astype(F32)
            pair = [value, zeros] if a % 2 == 0 else [zeros, value]
            wide = jnp.concatenate(pair, axis=1)
            lanes = slice(a // 2 * LANES, (a // 2 + 1) * LANES)
            for c in range(blocks // WIDE):
                row = (c * fold + a) * WIDE
                scratch[row : row + WIDE, lanes] = wide[c * WIDE : (c + 1) * WIDE]
        out_ref[g] = scratch[...].astype(BF16)


def spread_left(left):
    pairs, blocks, _ = left.shape
    return pl.pallas_call(
        spread_kernel,
        out_shape=jax.ShapeDtypeStruct((pairs * blocks // BLK, BLK, BLK), BF16),
        scratch_shapes=[pltpu.VMEM((BLK, BLK), F32)],
        cost_estimate=SMALL,
        name="spread_left",
    )(left)


def student_kernel(steps, late, tensor_count, idx_ref, *refs):
    tokens, (right_ref, left_ref, mixed_ref, student_ref, spread) = refs[:-5], refs[-5:]
    step = pl.program_id(0)
    chunk = natural(step, idx_ref[2], steps // 2)
    groups = left_ref.shape[0]
    pairs = right_ref.shape[2]
    share = BLK // groups

    @pl.when(step == 0)
    def _():
        spread[...] = jnp.zeros_like(spread)

    for t in range(WIDE):
        spread[t, pl.ds(t, pairs, stride=WIDE), :] = right_ref[0, t].astype(F32)
    factor = jnp.concatenate([spread[t] for t in range(WIDE)], axis=1).astype(BF16)

    def mix(pieces):
        rows = jnp.concatenate([piece[...] for piece in pieces], axis=0)
        part = lax.dot_general(factor, rows, NT, preferred_element_type=F32).astype(BF16)
        start = pl.multiple_of(chunk * share, share)
        for g in range(groups):
            mixed_ref[g, pl.ds(start, share), :] = part[g * share : (g + 1) * share]

    if late:
        pl.when(step < steps // 2)(lambda: mix(tokens[:4]))
        pl.when(step >= steps // 2)(lambda: mix(tokens[4:]))
    else:
        mix(tokens)

    @pl.when(step == steps - 1)
    def _():
        for g in range(groups):
            student_ref[:, g * BLK : (g + 1) * BLK] = lax.dot_general(
                mixed_ref[g], left_ref[g], TN, preferred_element_type=F32
            ) * (1.0 / tensor_count)


def token_specs(half, width, steps, begin, own):
    def chunk(n, s):
        step = jnp.maximum(n - begin, 0)
        return natural(step, s[2], steps // 2)

    if own:
        return [
            pl.BlockSpec((half, width), lambda n, s, p=p: (s[p % 2], chunk(n, s)))
            for p in range(4)
        ]
    near = pl.BlockSpec(
        (half, width), lambda n, s: (0, jnp.clip(n - begin, 0, steps // 2 - 1))
    )
    far = pl.BlockSpec(
        (half, width),
        lambda n, s: (0, jnp.clip(n - begin - steps // 2, 0, steps // 2 - 1)),
    )
    return [near] * 4 + [far] * 4


def student_part(tokens, late, scalars, right_rows, left_diag, tensor_count):
    per_owner, pairs, size = right_rows.shape[1:]
    blocks = right_rows.shape[0] * per_owner
    steps = blocks // WIDE
    half = tokens[0].shape[0] if late else tokens[0].shape[0] // 2
    halves = per_owner // WIDE

    def right_block(n, s):
        chunk = natural(n, s[2], steps // 2)
        return (s[3] ^ (chunk // halves), lax.rem(chunk, halves), 0, 0)

    groups = left_diag.shape[0]
    return pl.pallas_call(
        functools.partial(student_kernel, steps, late, tensor_count),
        grid_spec=pltpu.PrefetchScalarGridSpec(
            num_scalar_prefetch=1,
            grid=(steps,),
            in_specs=token_specs(half, WIDE * size, steps, 0, not late)
            + [
                pl.BlockSpec((1, WIDE, pairs, size), right_block),
                whole_spec(left_diag),
            ],
            out_specs=[
                pl.BlockSpec((groups, BLK, 4 * half), lambda n, s: (0, 0, 0)),
                pl.BlockSpec((4 * half, groups * BLK), lambda n, s: (0, 0)),
            ],
            scratch_shapes=[pltpu.VMEM((WIDE, pairs * WIDE, size), F32)],
        ),
        out_shape=[
            jax.ShapeDtypeStruct((groups, BLK, 4 * half), BF16),
            jax.ShapeDtypeStruct((4 * half, groups * BLK), F32),
        ],
        compiler_params=pltpu.CompilerParams(vmem_limit_bytes=50 * 2**20),
        cost_estimate=pl.CostEstimate(
            flops=10**10, bytes_accessed=10**7, transcendentals=0
        ),
        name="student_part",
    )(scalars, *tokens, right_rows, left_diag)


def grads_kernel(groups, steps, scale, counts, idx_ref, *refs):
    sets, refs = split_sets(refs, counts)
    weight_ref, total_ref, student0, student1, mixed0, mixed1, left_ref = refs[:7]
    own, near, far = refs[7:11], refs[11:15], refs[15:19]
    out_ref, lhs, back, wide = refs[19:]
    step = pl.program_id(0)
    z = idx_ref[3]
    parts, size = out_ref.shape[0], out_ref.shape[2]
    blocks = steps * WIDE
    per_part = blocks // parts
    share = BLK // steps
    pairs = groups * share // WIDE
    fold = BLK // blocks

    def place(owner):
        bits = z ^ owner
        return lax.rem(bits, 2) * 2 + bits // 2

    pl.when(step == 0)(lambda: fill_rows(lhs, sets))

    @pl.when(step < groups)
    def _():
        target = total_ref[...] + jnp.dot(
            lhs[...], weight_ref[...], preferred_element_type=F32
        )
        student = jnp.concatenate([student0[...], student1[...]], axis=0)
        out_grad = ((student - target) * scale).astype(BF16)
        mixed = jnp.concatenate([mixed0[0], mixed1[0]], axis=1)
        left = jnp.dot(mixed, out_grad, preferred_element_type=F32)
        value = lax.dot_general(
            left_ref[0], out_grad, NT, preferred_element_type=F32
        ).astype(BF16)
        row = pl.multiple_of(step * share, share)
        for c in range(steps):
            back[c, pl.ds(row, share), :] = value[c * share : (c + 1) * share]
        low = lax.broadcasted_iota(jnp.int32, (blocks, size), 1) < blocks
        rows = blocks // parts
        for pair in range(fold // 2):
            lanes = slice(pair * size, (pair + 1) * size)
            picked = []
            for a in (2 * pair, 2 * pair + 1):
                for c in range(steps):
                    begin = (c * fold + a) * WIDE
                    picked.append(left[begin : begin + WIDE, lanes])
            turned = jnp.concatenate(picked, axis=0).T
            both = jnp.where(low, turned[:blocks], turned[blocks:]).astype(BF16)
            begin = per_part * pairs + (step * (fold // 2) + pair) * rows
            begin = pl.multiple_of(begin, rows)
            for owner in range(parts):
                out_ref[place(owner), pl.ds(begin, rows), :] = both[
                    owner * rows : (owner + 1) * rows
                ]

    def right(later):
        chunk = natural(step - groups, idx_ref[2], steps // 2)
        rows = jnp.concatenate([piece[...] for piece in own + later], axis=0)
        value = jnp.dot(back[chunk], rows, preferred_element_type=F32)
        for t in range(WIDE):
            wide[t] = value[:, t * size : (t + 1) * size]
        for t in range(WIDE):
            block = chunk * WIDE + t
            begin = pl.multiple_of(lax.rem(block, per_part) * pairs, pairs)
            out_ref[place(block // per_part), pl.ds(begin, pairs), :] = wide[
                t, pl.ds(t, pairs, stride=WIDE), :
            ].astype(BF16)

    pl.when((step >= groups) & (step < groups + steps // 2))(lambda: right(near))
    pl.when(step >= groups + steps // 2)(lambda: right(far))


def factor_grads(
    sets, weight, total, students, mixed, left_diag, own, late, scalars, parts, size, scale
):
    pieces = [piece for group in sets for piece in group]
    groups, count = left_diag.shape[0], total.shape[0]
    width = weight.shape[0] // 2
    half = late[0].shape[0]
    steps = own[0].shape[1] // (WIDE * size)
    blocks = steps * WIDE
    pairs = groups * BLK // blocks

    def group(n):
        return jnp.minimum(n, groups - 1)

    out_rows = (pairs * blocks + pairs * blocks * blocks // size) // parts
    return pl.pallas_call(
        functools.partial(grads_kernel, groups, steps, scale, [len(g) for g in sets]),
        grid_spec=pltpu.PrefetchScalarGridSpec(
            num_scalar_prefetch=1,
            grid=(groups + steps,),
            in_specs=[whole_spec(piece) for piece in pieces]
            + [pl.BlockSpec((width, BLK), lambda n, s: (1 - s[2], group(n)))]
            + [pl.BlockSpec((count, BLK), lambda n, s: (0, group(n)))]
            + [pl.BlockSpec((count // 2, BLK), lambda n, s: (0, group(n)))] * 2
            + [pl.BlockSpec((1, BLK, count // 2), lambda n, s: (group(n), 0, 0))] * 2
            + [pl.BlockSpec((1, BLK, BLK), lambda n, s: (group(n), 0, 0))]
            + token_specs(half, WIDE * size, steps, groups, True)
            + token_specs(half, WIDE * size, steps, groups, False),
            out_specs=pl.BlockSpec((parts, out_rows, size), lambda n, s: (0, 0, 0)),
            scratch_shapes=[
                pltpu.VMEM((count, width), BF16),
                pltpu.VMEM((steps, groups * (BLK // steps), count), BF16),
                pltpu.VMEM((WIDE, pairs * WIDE, size), F32),
            ],
        ),
        out_shape=jax.ShapeDtypeStruct((parts, out_rows, size), BF16),
        compiler_params=pltpu.CompilerParams(vmem_limit_bytes=50 * 2**20),
        cost_estimate=SMALL,
        name="factor_grads",
    )(scalars, *pieces, weight, total, *students, *mixed, left_diag, *own, *late)


def tiled_body(tokens, gate_weight, up_weight, down_weight, right_factor, left_factor):
    fsdp_count = lax.axis_size("fsdp")
    tensor_count = lax.axis_size("tensor")
    rows, model = tokens.shape
    part = gate_weight.shape[1] // 2
    me, z = lax.axis_index("fsdp"), lax.axis_index("tensor")
    chip, core, odd = lax.div(me, 2), lax.rem(me, 2), lax.rem(z, 2)
    both_axes = ("fsdp", "tensor")

    def swap(value):
        return lax.ppermute(value, "fsdp", [(i, i ^ 1) for i in range(fsdp_count)])

    def across(value):
        return lax.ppermute(value, "fsdp", [(i, i ^ 2) for i in range(fsdp_count)])

    def along(value, bit):
        return lax.ppermute(value, "tensor", [(i, i ^ bit) for i in range(tensor_count)])

    def turn(value, bit):
        perm = []
        for f in range(fsdp_count):
            for t in range(tensor_count):
                perm.append((f * tensor_count + t, (t ^ bit) * tensor_count + f))
        return lax.ppermute(value, both_axes, perm)

    def after(value, *others):
        return lax.optimization_barrier((value,) + others)[0]

    def double(value, bit):
        return jnp.concatenate([value, along(value, bit)], axis=0)

    def add(*terms):
        return sum(term.astype(F32) for term in terms)

    head = (part // BLK + 1) // 2 * BLK
    chunks = [(0, head), (head, part - head)]

    near_tokens = swap(tokens)
    first, rest = cut_tokens(tokens, odd, chip)
    arrived = across(first)
    base = jnp.stack([odd, 1 - odd])
    mine_block = lax.div(part, BLK) * chip
    other_block = lax.div(part, BLK) * (1 - chip)

    def scalars(block):
        return jnp.concatenate([base, jnp.stack([me, core, block])]).astype(jnp.int32)

    own_pieces = [(t, row, 2) for t in (tokens, near_tokens) for row in (0, 1)]
    mine, other = products(
        own_pieces, scalars(other_block), gate_weight, up_weight, 0, part
    )
    early = mine
    sums = add(mine[0], swap(other[0])).astype(BF16)
    got_early = across(sums)

    right_rows = turn(after(right_factor, first), 0)[None]
    left_rows = along(after(left_factor, first), 1)[None]
    left_rows = jnp.concatenate([left_factor[None], left_rows], axis=0)
    right_rows = double(double(after(right_rows, early), 1), 2)
    left_rows = double(after(left_rows, early), 2)
    for axis, bit in ((0, 2), (1, 1)):
        split = left_rows.reshape((2, 2) + left_rows.shape[1:])
        split = jnp.where(lax.rem(lax.div(z, bit), 2) == 1, jnp.flip(split, axis), split)
        left_rows = split.reshape(left_rows.shape)
    pairs, blocks = left_rows.shape[1], left_rows.shape[3]
    left_rows = left_rows.transpose(1, 3, 0, 2).reshape(pairs, blocks, blocks)
    left_diag = spread_left(after(left_rows, early))

    arrived = after(arrived, early)
    partner = along(arrived, 1)
    near_arrived = swap(arrived)
    late_first = across(after(rest, sums))
    order = jnp.concatenate([base, jnp.stack([chip, z])]).astype(jnp.int32)
    own = [tokens, tokens, near_tokens, near_tokens]
    mixed0, student0 = student_part(
        [after(tokens, sums)] + own[1:], False, order, right_rows, left_diag, tensor_count
    )
    partner = after(partner, mixed0)
    late = [arrived, partner, near_arrived, swap(partner)]
    late_pieces = [(t, None, 3) for t in late]

    kept, other = products(
        own_pieces + late_pieces,
        after(scalars(mine_block), mixed0, sums),
        gate_weight,
        up_weight,
        0,
        part,
    )
    kept_other = swap(after(other, got_early, late_first))
    late_order = after(scalars(other_block), kept)
    value0, other0 = products(late_pieces, late_order, gate_weight, up_weight, *chunks[0])
    near0 = swap(other0[0])

    def activate(u, span, term):
        begin, width = span
        terms = [value[u, :, :, begin : begin + width] for value in (kept, kept_other)]
        total = add(*terms, term)
        return (jax.nn.silu(total[0]) * total[1]).astype(BF16)

    hidden_late = activate(1, (0, part), after(got_early, value0))
    got_late = across(hidden_late)
    late_order = after(late_order, value0, hidden_late)
    value1, other1 = products(late_pieces, late_order, gate_weight, up_weight, *chunks[1])
    got0 = across(add(value0[0], after(near0, value1)).astype(BF16))
    near1 = swap(after(other1[0], got_late))
    got1 = across(add(value1[0], near1).astype(BF16))

    near_hidden_late = swap(hidden_late)
    late_first = after(late_first, value1)
    late_partner = along(late_first, 1)
    late_rest = [late_first, late_partner, swap(late_first), swap(late_partner)]
    mixed1, student1 = student_part(
        late + late_rest, True, order, right_rows, left_diag, tensor_count
    )
    near_got_late = swap(got_late)
    hidden = [activate(0, span, term) for span, term in zip(chunks, (got0, got1))]
    got_hidden = [across(value) for value in hidden]
    sets = [hidden, [swap(value) for value in hidden], [hidden_late], [near_hidden_late]]
    total = target_part(sets, down_weight, chip)
    near_hidden = [swap(value) for value in got_hidden]
    sets = [[got_late], [near_got_late], got_hidden, near_hidden]

    grads = factor_grads(
        sets,
        down_weight,
        total,
        (student0, student1),
        (mixed0, mixed1),
        left_diag,
        own,
        late + late_rest,
        order,
        tensor_count,
        right_factor.shape[2],
        1.0 / math.sqrt(rows * fsdp_count),
    )
    summed = add(grads[:2], along(grads[2:], 1)).astype(BF16)
    right_shape = right_factor.shape
    cut = right_shape[0] * right_shape[1]
    grad_right = add(turn(summed[0, :cut], 0), turn(summed[1, :cut], 2))
    grad_left = add(summed[0, cut:], along(summed[1, cut:], 2))
    grad_left = grad_left.reshape(pairs // 2, -1, 2, blocks).transpose(0, 2, 1, 3)
    return grad_right.reshape(right_shape), grad_left.reshape(left_factor.shape)


def body(*args):
    tokens, gate_weight, _, _, right_factor, left_factor = args
    counts = (lax.axis_size("fsdp"), lax.axis_size("tensor"))
    feat, hid = gate_weight.shape
    per_owner, share, size = right_factor.shape
    blocks = left_factor.shape[2]
    fits = hid % (2 * BLK) == 0
    fits = fits and counts == (4, 4) and tokens.shape[0] == 128
    fits = fits and hid >= 4 * BLK and feat % BLK == 0
    fits = fits and size == 128 and 2 * blocks == size and per_owner % WIDE == 0
    fits = fits and left_factor.shape[0] == share and share % 16 == 0
    return (tiled_body if fits else general_body)(*args)


def solution(mesh):
    return jax.shard_map(
        body,
        mesh=mesh,
        in_specs=(
            P(("groups", "fsdp"), None),
            P("fsdp", "tensor"),
            P("fsdp", "tensor"),
            P("tensor", "fsdp"),
            P("fsdp", "tensor", None),
            P("fsdp", "tensor", None),
        ),
        out_specs=(P(("groups", "fsdp"), "tensor", None), P(("groups", "fsdp"), "tensor", None)),
        check_vma=False,
    )
```

```python
import functools
import math

import jax
import jax.numpy as jnp
from jax import lax
from jax.experimental import pallas as pl
from jax.experimental.pallas import tpu as pltpu
from jax.sharding import PartitionSpec as P

BLK = 256
LANES = 128
SMALL = pl.CostEstimate(flops=1, bytes_accessed=1, transcendentals=0)
F32 = jnp.float32
BF16 = jnp.bfloat16


def gate_up_kernel(idx_ref, top_ref, bottom_ref, gate_ref, up_ref, mine_ref, other_ref):
    rows = top_ref.shape[0]
    lhs = jnp.concatenate([top_ref[...], bottom_ref[...]], axis=0)
    for slot, weight_ref in enumerate((gate_ref, up_ref)):
        product = jnp.dot(lhs, weight_ref[...], preferred_element_type=F32).astype(BF16)
        mine_ref[slot] = product[:rows]
        other_ref[slot] = product[rows:]


def gate_up(top, top_block, bottom, gate, up, column, first, width):
    rows, feat = bottom.shape
    if width % BLK or gate.shape[1] % BLK or rows % 16 or feat % 128:
        lhs = jnp.concatenate(
            [lax.dynamic_slice_in_dim(top, top_block * feat, feat, 1), bottom], axis=0
        )
        both = [
            jnp.dot(
                lhs,
                lax.dynamic_slice_in_dim(w, column + first, width, 1),
                preferred_element_type=F32,
            ).astype(BF16)
            for w in (gate, up)
        ]
        both = jnp.stack(both)
        return both[:, :rows], both[:, rows:]
    scalars = jnp.stack([top_block, lax.div(column, BLK) + first // BLK]).astype(jnp.int32)
    weight_spec = pl.BlockSpec((feat, BLK), lambda n, s: (0, s[1] + n))
    out_spec = pl.BlockSpec((2, rows, BLK), lambda n, s: (0, 0, n))
    shape = jax.ShapeDtypeStruct((2, rows, width), BF16)
    return pl.pallas_call(
        gate_up_kernel,
        grid_spec=pltpu.PrefetchScalarGridSpec(
            num_scalar_prefetch=1,
            grid=(width // BLK,),
            in_specs=[
                pl.BlockSpec((rows, feat), lambda n, s: (0, s[0])),
                pl.BlockSpec((rows, feat), lambda n, s: (0, 0)),
                weight_spec,
                weight_spec,
            ],
            out_specs=[out_spec, out_spec],
        ),
        out_shape=[shape, shape],
        compiler_params=pltpu.CompilerParams(vmem_limit_bytes=50 * 2**20),
        cost_estimate=pl.CostEstimate(
            flops=2 * 2 * rows * feat * 2 * width,
            bytes_accessed=2 * feat * 2 * width + 2 * 2 * rows * (feat + 2 * width),
            transcendentals=0,
        ),
        name="gate_up",
    )(scalars, top, bottom, gate, up)


def down_kernel(idx_ref, mine_ref, other_ref, weight_ref, *refs):
    out_ref = refs[-1]
    lhs = jnp.concatenate([mine_ref[...], other_ref[...]], axis=0)
    product = jnp.dot(lhs, weight_ref[...], preferred_element_type=F32)

    @pl.when(pl.program_id(0) == 0)
    def _():
        out_ref[...] = refs[0][...] + product if len(refs) > 1 else product

    @pl.when(pl.program_id(0) > 0)
    def _():
        out_ref[...] += product


def down_add(total, mine, other, weight, row):
    rows, width = mine.shape
    outs = weight.shape[1]
    if width % BLK or weight.shape[0] % BLK or rows % 16 or outs % 128:
        lhs = jnp.concatenate([mine, other], axis=0)
        part = lax.dynamic_slice_in_dim(weight, row, width, 0)
        product = jnp.dot(lhs, part, preferred_element_type=F32)
        return product if total is None else total + product
    scalars = jnp.reshape(lax.div(row, BLK), (1,)).astype(jnp.int32)
    hidden_spec = pl.BlockSpec((rows, BLK), lambda k, s: (0, k))
    whole = pl.BlockSpec((2 * rows, outs), lambda k, s: (0, 0))
    totals = [] if total is None else [total]
    return pl.pallas_call(
        down_kernel,
        grid_spec=pltpu.PrefetchScalarGridSpec(
            num_scalar_prefetch=1,
            grid=(width // BLK,),
            in_specs=[
                hidden_spec,
                hidden_spec,
                pl.BlockSpec((BLK, outs), lambda k, s: (s[0] + k, 0)),
            ]
            + [whole] * len(totals),
            out_specs=whole,
        ),
        out_shape=jax.ShapeDtypeStruct((2 * rows, outs), F32),
        compiler_params=pltpu.CompilerParams(vmem_limit_bytes=50 * 2**20),
        cost_estimate=pl.CostEstimate(
            flops=2 * 2 * rows * width * outs,
            bytes_accessed=2 * width * outs + 2 * 2 * rows * width + 16 * rows * outs,
            transcendentals=0,
        ),
        name="down_add",
    )(scalars, mine, other, weight, *totals)


def general_body(tokens, gate_weight, up_weight, down_weight, right_factor, left_factor):
    fsdp_count = lax.axis_size("fsdp")
    tensor_count = lax.axis_size("tensor")
    chips = fsdp_count // 2
    rows, model = tokens.shape
    feat, hid = gate_weight.shape
    part = hid // chips
    me = lax.axis_index("fsdp")
    chip, core = lax.div(me, 2), lax.rem(me, 2)
    z = lax.axis_index("tensor")

    def swap(value):
        return lax.ppermute(value, "fsdp", [(i, i ^ 1) for i in range(fsdp_count)])

    def shift(value, hops):
        perm = [(i, (i + 2 * hops) % fsdp_count) for i in range(fsdp_count)]
        return lax.ppermute(value, "fsdp", perm)

    def gather_z(value):
        if tensor_count > 4:
            return lax.all_gather(value, "tensor", axis=0, tiled=True)
        size = value.shape[0]
        whole = jnp.zeros((size * tensor_count,) + value.shape[1:], value.dtype)
        whole = lax.dynamic_update_slice_in_dim(whole, value, z * size, 0)
        for step in range(1, tensor_count):
            perm = [(i, (i + step) % tensor_count) for i in range(tensor_count)]
            got = lax.ppermute(value, "tensor", perm)
            source = lax.rem(z - step + tensor_count, tensor_count)
            whole = lax.dynamic_update_slice_in_dim(whole, got, source * size, 0)
        return whole

    def scatter_z(value):
        if tensor_count > 4:
            return lax.psum_scatter(value, "tensor", scatter_dimension=0, tiled=False)
        total = lax.dynamic_index_in_dim(value, z, 0, keepdims=False)
        for step in range(1, tensor_count):
            target_z = lax.rem(z + step, tensor_count)
            piece = lax.dynamic_index_in_dim(value, target_z, 0, keepdims=False)
            perm = [(i, (i + step) % tensor_count) for i in range(tensor_count)]
            total += lax.ppermute(piece.astype(BF16), "tensor", perm).astype(F32)
        return total

    def columns(value, start, width):
        return lax.dynamic_slice_in_dim(value, start, width, 1)

    def after(value, *others):
        return lax.optimization_barrier((value,) + others)[0]

    def pair_z(value):
        perm = [(i, i ^ 1) for i in range(tensor_count)]
        got = lax.ppermute(value, "tensor", perm)
        odd = lax.rem(z, 2) == 1
        return jnp.concatenate(
            [jnp.where(odd, got, value), jnp.where(odd, value, got)], axis=0
        )

    if part % BLK == 0 and part // BLK > 1:
        head = (part // BLK + 1) // 2 * BLK
        chunks = [(0, head), (head, part - head)]
    else:
        chunks = [(0, part)]

    half = rows // 2
    own_half = lax.dynamic_slice_in_dim(tokens, lax.rem(z, 2) * half, half, 0)

    def send_tokens(value, dt, g):
        features = lax.rem(chip - dt + g + chips, chips) * (2 * feat)
        return shift(columns(value, features, 2 * feat), -dt)

    def partial(pair, dp, first, width):
        column = lax.rem(chip + dp, chips) * part
        top, block, bottom = pair
        mine, other = gate_up(top, block, bottom, gate_weight, up_weight, column, first, width)
        return mine, swap(other)

    def send_partials(pair, got, dt):
        sums = []
        for dp in range(1, chips):
            pieces = [partial(pair, dp, *chunk) for chunk in chunks]
            for n, (mine, from_core) in enumerate(pieces):
                both = (mine.astype(F32) + from_core.astype(F32)).astype(BF16)
                got[dt, dp, n] = shift(both, dp)
                sums.append(both)
        return sums

    got, kept, gathered = {}, {}, {}
    local = swap(columns(tokens, (me ^ 1) * feat, feat))
    arrived = {dt: send_tokens(own_half, dt, 0) for dt in range(1, chips)}
    sums = send_partials((tokens, me, local), got, 0)
    if sums:
        local = after(local, *sums)
    kept[0] = partial((tokens, me, local), 0, 0, part)
    late_tokens = after(tokens, kept[0][0])
    neighbour_tokens = swap(late_tokens)
    late_half = after(own_half, *sums) if sums else own_half

    for dt in range(1, chips):
        gathered[dt, 0] = pair_z(after(arrived[dt], *sums))
        whole = gathered[dt, 0]
        top = columns(whole, core * feat, feat)
        bottom = swap(columns(whole, (1 - core) * feat, feat))
        pair = (top, jnp.int32(0), bottom)
        sums = send_partials(pair, got, dt)
        pair = (top, jnp.int32(0), after(bottom, *sums))
        kept[dt] = partial(pair, 0, 0, part)
        for g in range(1, chips):
            gathered[dt, g] = pair_z(after(send_tokens(late_half, dt, g), kept[dt][0]))

    def activate(e, first, width, n):
        terms = [lax.slice_in_dim(term, first, first + width, axis=2) for term in kept[e]]
        terms += [got[(e + dp) % chips, dp, n] for dp in range(1, chips)]
        total = sum(term.astype(F32) for term in terms)
        return (jax.nn.silu(total[0]) * total[1]).astype(BF16)

    totals = {u: None for u in range(chips)}
    for e in list(range(1, chips)) + [0]:
        values = [activate(e, *chunk, n) for n, chunk in enumerate(chunks)]
        spans = list(chunks)
        if e:
            values, spans = [jnp.concatenate(values, axis=1)], [(0, part)]
        sent = [[value] + [shift(value, d) for d in range(1, chips)] for value in values]
        for (first, width), copies in zip(spans, sent):
            for d, mine in enumerate(copies):
                u = (e - d + chips) % chips
                row = lax.rem(chip - d + chips, chips) * part + first
                totals[u] = down_add(totals[u], mine, swap(mine), down_weight, row)

    token_rows = []
    for dt in range(chips):
        if dt == 0:
            token_rows += [tokens, neighbour_tokens]
            continue
        else:
            full = jnp.zeros((rows, model), BF16)
            for g in range(chips):
                features = lax.rem(chip + g, chips) * (2 * feat)
                full = lax.dynamic_update_slice_in_dim(full, gathered[dt, g], features, 1)
        token_rows += [full, swap(full)]
    inputs = jnp.concatenate(token_rows, axis=0)
    count = inputs.shape[0]

    blocks, share, size = right_factor.shape
    ratio = tensor_count // fsdp_count
    turn = []
    for a in range(fsdp_count):
        for b in range(tensor_count):
            turn.append((a * tensor_count + b, (b // ratio) * tensor_count + a * ratio + b % ratio))
    back = [(b, a) for a, b in turn]
    right_rows = gather_z(lax.ppermute(right_factor, ("fsdp", "tensor"), turn)[None])
    right_rows = right_rows.reshape(fsdp_count, ratio, blocks, share, size)
    right_rows = right_rows.transpose(0, 2, 1, 3, 4).reshape(
        fsdp_count * blocks, ratio * share, size
    )
    left_rows = jnp.moveaxis(gather_z(jnp.moveaxis(left_factor, 1, 0)), 0, 1)

    block_input = inputs.reshape(count, fsdp_count * blocks, size)
    mixed = jnp.einsum(
        "nim,ijm->nij", block_input, right_rows, preferred_element_type=F32
    ).astype(BF16)
    student = jnp.einsum("nij,jki->njk", mixed, left_rows, preferred_element_type=F32)
    target = jnp.concatenate([totals[u] for u in range(chips)], axis=0)
    scale = 1.0 / math.sqrt(count)
    out_grad = (student * (1.0 / tensor_count) - target.reshape(student.shape)) * scale
    out_grad = out_grad.astype(BF16)
    grad_left = jnp.einsum("njk,nij->kji", out_grad, mixed, preferred_element_type=F32)
    mixed_grad = jnp.einsum(
        "njk,jki->nij", out_grad, left_rows, preferred_element_type=F32
    ).astype(BF16)
    grad_right = jnp.einsum(
        "nij,nim->ijm", mixed_grad, block_input, preferred_element_type=F32
    )
    grad_left = scatter_z(
        grad_left.reshape((tensor_count, -1) + grad_left.shape[1:])
    )
    grad_left = jnp.moveaxis(grad_left, 0, 1)
    grad_right = grad_right.reshape(fsdp_count, blocks, ratio, share, size)
    grad_right = grad_right.transpose(0, 2, 1, 3, 4).reshape(
        tensor_count, blocks, share, size
    )
    grad_right = lax.ppermute(scatter_z(grad_right), ("fsdp", "tensor"), back)
    return grad_right, grad_left


def cut_kernel(idx_ref, first_in, rest_in, first_ref, rest_ref):
    first_ref[...] = first_in[...]
    rest_ref[...] = rest_in[...]


def cut_tokens(tokens, half, chip):
    rows, model = tokens.shape
    block = (rows // 2, model // 2)
    shape = jax.ShapeDtypeStruct(block, BF16)
    whole = pl.BlockSpec(block, lambda n, s: (0, 0))
    return pl.pallas_call(
        cut_kernel,
        grid_spec=pltpu.PrefetchScalarGridSpec(
            num_scalar_prefetch=1,
            grid=(1,),
            in_specs=[
                pl.BlockSpec(block, lambda n, s: (s[0], s[1])),
                pl.BlockSpec(block, lambda n, s: (s[0], s[2])),
            ],
            out_specs=[whole, whole],
        ),
        out_shape=[shape, shape],
        cost_estimate=SMALL,
        name="cut_tokens",
    )(jnp.stack([half, 1 - chip, chip]).astype(jnp.int32), tokens, tokens)


def products_kernel(sets, idx_ref, *refs):
    pieces, (gate_ref, up_ref, mine_ref, other_ref) = refs[: 4 * sets], refs[4 * sets :]
    lhs = jnp.concatenate([piece[...] for piece in pieces], axis=0)
    rows = mine_ref.shape[2]
    for slot, weight_ref in enumerate((gate_ref, up_ref)):
        product = jnp.dot(lhs, weight_ref[...], preferred_element_type=F32).astype(BF16)
        for u in range(sets):
            mine_ref[u, slot] = product[2 * u * rows : (2 * u + 1) * rows]
            other_ref[u, slot] = product[(2 * u + 1) * rows : (2 * u + 2) * rows]


def products(pieces, scalars, gate, up, first, width):
    feat = gate.shape[0]
    sets = len(pieces) // 4
    half = pieces[0][0].shape[0]
    half = half // 2 if pieces[0][1] is not None else half
    start = first // BLK

    def piece_spec(row, column):
        if row is None:
            return pl.BlockSpec((half, feat), lambda n, s: (0, s[column]))
        return pl.BlockSpec((half, feat), lambda n, s: (s[row], s[column]))

    weight_spec = pl.BlockSpec((feat, BLK), lambda n, s: (0, s[4] + start + n))
    out_spec = pl.BlockSpec((sets, 2, 2 * half, BLK), lambda n, s: (0, 0, 0, n))
    shape = jax.ShapeDtypeStruct((sets, 2, 2 * half, width), BF16)
    return pl.pallas_call(
        functools.partial(products_kernel, sets),
        grid_spec=pltpu.PrefetchScalarGridSpec(
            num_scalar_prefetch=1,
            grid=(width // BLK,),
            in_specs=[piece_spec(row, column) for _, row, column in pieces]
            + [weight_spec, weight_spec],
            out_specs=[out_spec, out_spec],
        ),
        out_shape=[shape, shape],
        compiler_params=pltpu.CompilerParams(vmem_limit_bytes=50 * 2**20),
        cost_estimate=SMALL,
        name="gate_up_products",
    )(scalars, *[piece for piece, _, _ in pieces], gate, up)


def fill_rows(lhs, sets):
    row = 0
    for group in sets:
        column = 0
        for piece in group:
            rows, width = piece.shape
            lhs[row : row + rows, column : column + width] = piece[...]
            column += width
        row += group[0].shape[0]


def split_sets(refs, counts):
    sets, start = [], 0
    for count in counts:
        sets.append(refs[start : start + count])
        start += count
    return sets, refs[start:]


def whole_spec(array):
    return pl.BlockSpec(array.shape, lambda n, s: (0,) * array.ndim)


def target_kernel(counts, tiles, idx_ref, *refs):
    sets, refs = split_sets(refs, counts)
    weights, terms, (out_ref, lhs) = refs[:tiles], refs[tiles:-2], refs[-2:]
    pl.when(pl.program_id(0) == 0)(lambda: fill_rows(lhs, sets))
    weight = jnp.concatenate([ref[...] for ref in weights], axis=0)
    product = jnp.dot(lhs[...], weight, preferred_element_type=F32)
    out_ref[...] = sum((ref[...] for ref in terms), product)


def target_part(terms, sets, weight, row, width):
    counts = [1] * len(sets)
    rows = sum(piece.shape[0] for piece, _ in sets)
    outs = weight.shape[1]
    tiles = width // BLK

    def piece_spec(piece, first):
        return pl.BlockSpec((piece.shape[0], width), lambda n, s: (0, first // width))

    pieces = []
    for piece, first in sets:
        if first % width:
            piece, first = lax.slice_in_dim(piece, first, first + width, axis=1), 0
        pieces.append((piece, first))
    return pl.pallas_call(
        functools.partial(target_kernel, counts, tiles),
        grid_spec=pltpu.PrefetchScalarGridSpec(
            num_scalar_prefetch=1,
            grid=(outs // BLK,),
            in_specs=[piece_spec(*piece) for piece in pieces]
            + [pl.BlockSpec((BLK, BLK), lambda n, s, k=k: (s[0] + k, n)) for k in range(tiles)]
            + [pl.BlockSpec((term.shape[0], BLK), lambda n, s: (0, n)) for term in terms],
            out_specs=pl.BlockSpec((rows, BLK), lambda n, s: (0, n)),
            scratch_shapes=[pltpu.VMEM((rows, width), BF16)],
        ),
        out_shape=jax.ShapeDtypeStruct((rows, outs), F32),
        compiler_params=pltpu.CompilerParams(vmem_limit_bytes=50 * 2**20),
        cost_estimate=SMALL,
        name="target_part",
    )(
        jnp.reshape(lax.div(row, BLK), (1,)).astype(jnp.int32),
        *[piece for piece, _ in pieces],
        *[weight] * tiles,
        *terms,
    )


TN = (((0,), (0,)), ((), ()))
NT = (((1,), (1,)), ((), ()))
WIDE = 8


def natural(step, chip, per_chip):
    return lax.rem(chip + step // per_chip, 2) * per_chip + lax.rem(step, per_chip)


def spread_kernel(left_ref, out_ref, scratch):
    groups, fold = out_ref.shape[0], BLK // left_ref.shape[1]
    blocks = left_ref.shape[1]
    scratch[...] = jnp.zeros_like(scratch)
    zeros = jnp.zeros((blocks, blocks), F32)
    for g in range(groups):
        for a in range(fold):
            value = left_ref[g * fold + a].astype(F32)
            pair = [value, zeros] if a % 2 == 0 else [zeros, value]
            wide = jnp.concatenate(pair, axis=1)
            lanes = slice(a // 2 * LANES, (a // 2 + 1) * LANES)
            for c in range(blocks // WIDE):
                row = (c * fold + a) * WIDE
                scratch[row : row + WIDE, lanes] = wide[c * WIDE : (c + 1) * WIDE]
        out_ref[g] = scratch[...].astype(BF16)


def spread_left(left):
    pairs, blocks, _ = left.shape
    return pl.pallas_call(
        spread_kernel,
        out_shape=jax.ShapeDtypeStruct((pairs * blocks // BLK, BLK, BLK), BF16),
        scratch_shapes=[pltpu.VMEM((BLK, BLK), F32)],
        cost_estimate=SMALL,
        name="spread_left",
    )(left)


def student_kernel(steps, late, tensor_count, idx_ref, *refs):
    tokens, refs = refs[:-6], refs[-6:]
    right_ref, left_ref, target_ref, mixed_ref, rest_ref, spread = refs
    step = pl.program_id(0)
    chunk = natural(step, idx_ref[2], steps // 2)
    groups = left_ref.shape[0]
    pairs = right_ref.shape[2]
    share = BLK // groups

    @pl.when(step == 0)
    def _():
        spread[...] = jnp.zeros_like(spread)

    for t in range(WIDE):
        spread[t, pl.ds(t, pairs, stride=WIDE), :] = right_ref[0, t].astype(F32)
    factor = jnp.concatenate([spread[t] for t in range(WIDE)], axis=1).astype(BF16)

    def mix(pieces):
        rows = jnp.concatenate([piece[...] for piece in pieces], axis=0)
        part = lax.dot_general(factor, rows, NT, preferred_element_type=F32).astype(BF16)
        start = pl.multiple_of(chunk * share, share)
        for g in range(groups):
            mixed_ref[g, pl.ds(start, share), :] = part[g * share : (g + 1) * share]

    if late:
        pl.when(step < steps // 2)(lambda: mix(tokens[:4]))
        pl.when(step >= steps // 2)(lambda: mix(tokens[4:]))
    else:
        mix(tokens)

    @pl.when(step == steps - 1)
    def _():
        for g in range(groups):
            span = slice(g * BLK, (g + 1) * BLK)
            student = lax.dot_general(
                mixed_ref[g], left_ref[g], TN, preferred_element_type=F32
            )
            rest_ref[:, span] = student * (1.0 / tensor_count) - target_ref[:, span]


def token_specs(half, width, steps, begin, own):
    def chunk(n, s):
        step = jnp.maximum(n - begin, 0)
        return natural(step, s[2], steps // 2)

    if own:
        return [
            pl.BlockSpec((half, width), lambda n, s, p=p: (s[p % 2], chunk(n, s)))
            for p in range(4)
        ]
    near = pl.BlockSpec(
        (half, width), lambda n, s: (0, jnp.clip(n - begin, 0, steps // 2 - 1))
    )
    far = pl.BlockSpec(
        (half, width),
        lambda n, s: (0, jnp.clip(n - begin - steps // 2, 0, steps // 2 - 1)),
    )
    return [near] * 4 + [far] * 4


def student_part(tokens, late, scalars, right_rows, left_diag, target, tensor_count):
    per_owner, pairs, size = right_rows.shape[1:]
    blocks = right_rows.shape[0] * per_owner
    steps = blocks // WIDE
    half = tokens[0].shape[0] if late else tokens[0].shape[0] // 2
    halves = per_owner // WIDE

    def right_block(n, s):
        chunk = natural(n, s[2], steps // 2)
        return (s[3] ^ (chunk // halves), lax.rem(chunk, halves), 0, 0)

    groups = left_diag.shape[0]
    return pl.pallas_call(
        functools.partial(student_kernel, steps, late, tensor_count),
        grid_spec=pltpu.PrefetchScalarGridSpec(
            num_scalar_prefetch=1,
            grid=(steps,),
            in_specs=token_specs(half, WIDE * size, steps, 0, not late)
            + [
                pl.BlockSpec((1, WIDE, pairs, size), right_block),
                whole_spec(left_diag),
                pl.BlockSpec((4 * half, groups * BLK), lambda n, s: (int(late), 0)),
            ],
            out_specs=[
                pl.BlockSpec((groups, BLK, 4 * half), lambda n, s: (0, 0, 0)),
                pl.BlockSpec((4 * half, groups * BLK), lambda n, s: (0, 0)),
            ],
            scratch_shapes=[pltpu.VMEM((WIDE, pairs * WIDE, size), F32)],
        ),
        out_shape=[
            jax.ShapeDtypeStruct((groups, BLK, 4 * half), BF16),
            jax.ShapeDtypeStruct((4 * half, groups * BLK), F32),
        ],
        compiler_params=pltpu.CompilerParams(vmem_limit_bytes=50 * 2**20),
        cost_estimate=pl.CostEstimate(
            flops=10**10, bytes_accessed=10**7, transcendentals=0
        ),
        name="student_part",
    )(scalars, *tokens, right_rows, left_diag, target)


def grads_kernel(groups, steps, scale, counts, idx_ref, *refs):
    sets, refs = split_sets(refs, counts)
    weight_ref, rest0, rest1, mixed0, mixed1, left_ref = refs[:6]
    own, near, far = refs[6:10], refs[10:14], refs[14:18]
    out_ref, lhs, back, wide = refs[18:]
    step = pl.program_id(0)
    z = idx_ref[3]
    parts, size = out_ref.shape[0], out_ref.shape[2]
    blocks = steps * WIDE
    per_part = blocks // parts
    share = BLK // steps
    pairs = groups * share // WIDE
    fold = BLK // blocks

    def place(owner):
        bits = z ^ owner
        return lax.rem(bits, 2) * 2 + bits // 2

    pl.when(step == 0)(lambda: fill_rows(lhs, sets))

    @pl.when(step < groups)
    def _():
        target = jnp.dot(lhs[...], weight_ref[...], preferred_element_type=F32)
        rest = jnp.concatenate([rest0[...], rest1[...]], axis=0)
        out_grad = ((rest - target) * scale).astype(BF16)
        mixed = jnp.concatenate([mixed0[0], mixed1[0]], axis=1)
        left = jnp.dot(mixed, out_grad, preferred_element_type=F32)
        value = lax.dot_general(
            left_ref[0], out_grad, NT, preferred_element_type=F32
        ).astype(BF16)
        row = pl.multiple_of(step * share, share)
        for c in range(steps):
            back[c, pl.ds(row, share), :] = value[c * share : (c + 1) * share]
        low = lax.broadcasted_iota(jnp.int32, (blocks, size), 1) < blocks
        rows = blocks // parts
        for pair in range(fold // 2):
            lanes = slice(pair * size, (pair + 1) * size)
            picked = []
            for a in (2 * pair, 2 * pair + 1):
                for c in range(steps):
                    begin = (c * fold + a) * WIDE
                    picked.append(left[begin : begin + WIDE, lanes])
            turned = jnp.concatenate(picked, axis=0).T
            both = jnp.where(low, turned[:blocks], turned[blocks:]).astype(BF16)
            begin = per_part * pairs + (step * (fold // 2) + pair) * rows
            begin = pl.multiple_of(begin, rows)
            for owner in range(parts):
                out_ref[place(owner), pl.ds(begin, rows), :] = both[
                    owner * rows : (owner + 1) * rows
                ]

    def right(later):
        chunk = natural(step - groups, idx_ref[2], steps // 2)
        rows = jnp.concatenate([piece[...] for piece in own + later], axis=0)
        value = jnp.dot(back[chunk], rows, preferred_element_type=F32)
        for t in range(WIDE):
            wide[t] = value[:, t * size : (t + 1) * size]
        for t in range(WIDE):
            block = chunk * WIDE + t
            begin = pl.multiple_of(lax.rem(block, per_part) * pairs, pairs)
            out_ref[place(block // per_part), pl.ds(begin, pairs), :] = wide[
                t, pl.ds(t, pairs, stride=WIDE), :
            ].astype(BF16)

    pl.when((step >= groups) & (step < groups + steps // 2))(lambda: right(near))
    pl.when(step >= groups + steps // 2)(lambda: right(far))


def factor_grads(
    sets, weight, rest, mixed, left_diag, own, late, scalars, parts, size, scale
):
    pieces = [piece for group in sets for piece in group]
    groups, count = left_diag.shape[0], 2 * rest[0].shape[0]
    width = weight.shape[0] // 2
    half = late[0].shape[0]
    steps = own[0].shape[1] // (WIDE * size)
    blocks = steps * WIDE
    pairs = groups * BLK // blocks

    def group(n):
        return jnp.minimum(n, groups - 1)

    out_rows = (pairs * blocks + pairs * blocks * blocks // size) // parts
    return pl.pallas_call(
        functools.partial(grads_kernel, groups, steps, scale, [len(g) for g in sets]),
        grid_spec=pltpu.PrefetchScalarGridSpec(
            num_scalar_prefetch=1,
            grid=(groups + steps,),
            in_specs=[whole_spec(piece) for piece in pieces]
            + [pl.BlockSpec((width, BLK), lambda n, s: (1 - s[2], group(n)))]
            + [pl.BlockSpec((count // 2, BLK), lambda n, s: (0, group(n)))] * 2
            + [pl.BlockSpec((1, BLK, count // 2), lambda n, s: (group(n), 0, 0))] * 2
            + [pl.BlockSpec((1, BLK, BLK), lambda n, s: (group(n), 0, 0))]
            + token_specs(half, WIDE * size, steps, groups, True)
            + token_specs(half, WIDE * size, steps, groups, False),
            out_specs=pl.BlockSpec((parts, out_rows, size), lambda n, s: (0, 0, 0)),
            scratch_shapes=[
                pltpu.VMEM((count, width), BF16),
                pltpu.VMEM((steps, groups * (BLK // steps), count), BF16),
                pltpu.VMEM((WIDE, pairs * WIDE, size), F32),
            ],
        ),
        out_shape=jax.ShapeDtypeStruct((parts, out_rows, size), BF16),
        compiler_params=pltpu.CompilerParams(vmem_limit_bytes=50 * 2**20),
        cost_estimate=SMALL,
        name="factor_grads",
    )(scalars, *pieces, weight, *rest, *mixed, left_diag, *own, *late)


def tiled_body(tokens, gate_weight, up_weight, down_weight, right_factor, left_factor):
    fsdp_count = lax.axis_size("fsdp")
    tensor_count = lax.axis_size("tensor")
    rows, model = tokens.shape
    part = gate_weight.shape[1] // 2
    me, z = lax.axis_index("fsdp"), lax.axis_index("tensor")
    chip, core, odd = lax.div(me, 2), lax.rem(me, 2), lax.rem(z, 2)
    both_axes = ("fsdp", "tensor")

    def swap(value):
        return lax.ppermute(value, "fsdp", [(i, i ^ 1) for i in range(fsdp_count)])

    def across(value):
        return lax.ppermute(value, "fsdp", [(i, i ^ 2) for i in range(fsdp_count)])

    def along(value, bit):
        return lax.ppermute(value, "tensor", [(i, i ^ bit) for i in range(tensor_count)])

    def turn(value, bit):
        perm = []
        for f in range(fsdp_count):
            for t in range(tensor_count):
                perm.append((f * tensor_count + t, (t ^ bit) * tensor_count + f))
        return lax.ppermute(value, both_axes, perm)

    def after(value, *others):
        return lax.optimization_barrier((value,) + others)[0]

    def double(value, bit):
        return jnp.concatenate([value, along(value, bit)], axis=0)

    def add(*terms):
        return sum(term.astype(F32) for term in terms)

    head = (part // BLK + 1) // 2 * BLK
    chunks = [(0, head), (head, part - head)]

    near_tokens = swap(tokens)
    first, rest = cut_tokens(tokens, odd, chip)
    arrived = across(first)
    base = jnp.stack([odd, 1 - odd])
    mine_block = lax.div(part, BLK) * chip
    other_block = lax.div(part, BLK) * (1 - chip)

    def scalars(block):
        return jnp.concatenate([base, jnp.stack([me, core, block])]).astype(jnp.int32)

    own_pieces = [(t, row, 2) for t in (tokens, near_tokens) for row in (0, 1)]
    mine, other = products(
        own_pieces, scalars(other_block), gate_weight, up_weight, 0, part
    )
    early = mine
    sums = add(mine[0], swap(after(other[0], arrived))).astype(BF16)
    got_early = across(sums)

    arrived = after(arrived, early)
    partner = along(arrived, 1)
    near_arrived = swap(arrived)
    late_first = across(after(rest, sums))
    order = jnp.concatenate([base, jnp.stack([chip, z])]).astype(jnp.int32)
    own = [tokens, tokens, near_tokens, near_tokens]
    late = [arrived, partner, near_arrived, swap(partner)]
    late_pieces = [(t, None, 3) for t in late]

    pairs, blocks = left_factor.shape[0], left_factor.shape[2]
    right_rows = turn(after(right_factor, sums), 0)[None]
    left_own = left_factor.reshape(1, -1, LANES)
    left_rows = double(after(left_own, sums), 1)

    late_order = after(scalars(other_block), sums, right_rows, left_rows)
    value0, other0 = products(late_pieces, late_order, gate_weight, up_weight, *chunks[0])
    near0 = swap(after(other0[0], got_early))
    late_order = after(late_order, value0)
    value1, other1 = products(late_pieces, late_order, gate_weight, up_weight, *chunks[1])
    near1 = swap(other1[0])
    sums0 = add(value0[0], after(near0, value1)).astype(BF16)
    got0 = across(sums0)
    mine_order = after(scalars(mine_block), value1, sums0)
    right_rows, left_rows = after(right_rows, value1), after(left_rows, value1)
    more_right, more_left = along(right_rows, 1), along(left_rows, 2)
    kept, other = products(
        own_pieces + late_pieces, mine_order, gate_weight, up_weight, 0, part
    )
    kept_other = swap(after(other, got0, late_first, near1, more_right, more_left))
    right_rows = jnp.concatenate([right_rows, after(more_right, kept)], axis=0)
    left_rows = jnp.concatenate([left_rows, after(more_left, kept)], axis=0)
    right_rows = double(right_rows, 2)
    sums1 = add(value1[0], after(near1, kept)).astype(BF16)
    got1 = across(sums1)

    left_rows = left_rows.reshape((tensor_count,) + left_factor.shape)
    for axis, bit in ((0, 2), (1, 1)):
        split = left_rows.reshape((2, 2) + left_rows.shape[1:])
        split = jnp.where(lax.rem(lax.div(z, bit), 2) == 1, jnp.flip(split, axis), split)
        left_rows = split.reshape(left_rows.shape)
    left_rows = left_rows.transpose(1, 3, 0, 2).reshape(pairs, blocks, blocks)

    def activate(u, span, term):
        begin, width = span
        terms = [value[u, :, :, begin : begin + width] for value in (kept, kept_other)]
        total = add(*terms, term)
        return (jax.nn.silu(total[0]) * total[1]).astype(BF16)

    hidden_late = activate(1, (0, part), got_early)
    got_late = across(hidden_late)
    near_hidden_late = swap(hidden_late)
    hidden0 = activate(0, chunks[0], after(got0, hidden_late))
    got_hidden0 = across(hidden0)
    left_diag = spread_left(after(left_rows, hidden0))
    late_partner = along(after(late_first, kept), 1)

    def target(term, span, value):
        sets = [(value, 0), (swap(value), 0)]
        sets += [(hidden_late, span[0]), (near_hidden_late, span[0])]
        return target_part(term, sets, down_weight, chip * part + span[0], span[1])

    total = target([], chunks[0], after(hidden0, sums1))
    hidden1 = activate(0, chunks[1], after(got1, total, got_late))
    got_hidden1 = across(hidden1)
    total = target([total], chunks[1], hidden1)
    got_late, got_hidden0 = after(got_late, total), after(got_hidden0, total)
    late_partner = after(late_partner, total)
    late_rest = [late_first, late_partner, swap(late_first), swap(late_partner)]
    near_got_late = swap(got_late)
    near_got0 = swap(got_hidden0)
    mixed0, rest0 = student_part(
        own, False, order, right_rows, left_diag, total, tensor_count
    )
    got_hidden1 = after(got_hidden1, mixed0)
    mixed1, rest1 = student_part(
        late + [after(late_rest[0], mixed0)] + late_rest[1:],
        True,
        order,
        right_rows,
        left_diag,
        total,
        tensor_count,
    )
    got_hidden = [got_hidden0, got_hidden1]
    sets = [[got_late], [near_got_late], got_hidden, [near_got0, swap(got_hidden1)]]

    grads = factor_grads(
        sets,
        down_weight,
        (rest0, rest1),
        (mixed0, mixed1),
        left_diag,
        own,
        late + late_rest,
        order,
        tensor_count,
        right_factor.shape[2],
        1.0 / math.sqrt(rows * fsdp_count),
    )
    summed = add(grads[:2], along(grads[2:], 1)).astype(BF16)
    right_shape = right_factor.shape
    cut = right_shape[0] * right_shape[1]
    grad_right = add(turn(summed[0, :cut], 0), turn(summed[1, :cut], 2))
    grad_left = add(summed[0, cut:], along(summed[1, cut:], 2))
    grad_left = grad_left.reshape(pairs // 2, -1, 2, blocks).transpose(0, 2, 1, 3)
    return grad_right.reshape(right_shape), grad_left.reshape(left_factor.shape)


def body(*args):
    tokens, gate_weight, _, _, right_factor, left_factor = args
    counts = (lax.axis_size("fsdp"), lax.axis_size("tensor"))
    feat, hid = gate_weight.shape
    per_owner, share, size = right_factor.shape
    blocks = left_factor.shape[2]
    fits = hid % (2 * BLK) == 0
    fits = fits and counts == (4, 4) and tokens.shape[0] == 128
    fits = fits and hid >= 4 * BLK and feat % BLK == 0
    fits = fits and size == 128 and 2 * blocks == size and per_owner % WIDE == 0
    fits = fits and left_factor.shape[0] == share and share % 16 == 0
    return (tiled_body if fits else general_body)(*args)


def solution(mesh):
    return jax.shard_map(
        body,
        mesh=mesh,
        in_specs=(
            P(("groups", "fsdp"), None),
            P("fsdp", "tensor"),
            P("fsdp", "tensor"),
            P("tensor", "fsdp"),
            P("fsdp", "tensor", None),
            P("fsdp", "tensor", None),
        ),
        out_specs=(P(("groups", "fsdp"), "tensor", None), P(("groups", "fsdp"), "tensor", None)),
        check_vma=False,
    )
```

```python
import functools
import math

import jax
import jax.numpy as jnp
from jax import lax
from jax.experimental import pallas as pl
from jax.experimental.pallas import tpu as pltpu
from jax.sharding import PartitionSpec as P

BLK = 256
LANES = 128
SMALL = pl.CostEstimate(flops=1, bytes_accessed=1, transcendentals=0)
F32 = jnp.float32
BF16 = jnp.bfloat16


def gate_up_kernel(idx_ref, top_ref, bottom_ref, gate_ref, up_ref, mine_ref, other_ref):
    rows = top_ref.shape[0]
    lhs = jnp.concatenate([top_ref[...], bottom_ref[...]], axis=0)
    for slot, weight_ref in enumerate((gate_ref, up_ref)):
        product = jnp.dot(lhs, weight_ref[...], preferred_element_type=F32).astype(BF16)
        mine_ref[slot] = product[:rows]
        other_ref[slot] = product[rows:]


def gate_up(top, top_block, bottom, gate, up, column, first, width):
    rows, feat = bottom.shape
    if width % BLK or gate.shape[1] % BLK or rows % 16 or feat % 128:
        lhs = jnp.concatenate(
            [lax.dynamic_slice_in_dim(top, top_block * feat, feat, 1), bottom], axis=0
        )
        both = [
            jnp.dot(
                lhs,
                lax.dynamic_slice_in_dim(w, column + first, width, 1),
                preferred_element_type=F32,
            ).astype(BF16)
            for w in (gate, up)
        ]
        both = jnp.stack(both)
        return both[:, :rows], both[:, rows:]
    scalars = jnp.stack([top_block, lax.div(column, BLK) + first // BLK]).astype(jnp.int32)
    weight_spec = pl.BlockSpec((feat, BLK), lambda n, s: (0, s[1] + n))
    out_spec = pl.BlockSpec((2, rows, BLK), lambda n, s: (0, 0, n))
    shape = jax.ShapeDtypeStruct((2, rows, width), BF16)
    return pl.pallas_call(
        gate_up_kernel,
        grid_spec=pltpu.PrefetchScalarGridSpec(
            num_scalar_prefetch=1,
            grid=(width // BLK,),
            in_specs=[
                pl.BlockSpec((rows, feat), lambda n, s: (0, s[0])),
                pl.BlockSpec((rows, feat), lambda n, s: (0, 0)),
                weight_spec,
                weight_spec,
            ],
            out_specs=[out_spec, out_spec],
        ),
        out_shape=[shape, shape],
        compiler_params=pltpu.CompilerParams(vmem_limit_bytes=50 * 2**20),
        cost_estimate=pl.CostEstimate(
            flops=2 * 2 * rows * feat * 2 * width,
            bytes_accessed=2 * feat * 2 * width + 2 * 2 * rows * (feat + 2 * width),
            transcendentals=0,
        ),
        name="gate_up",
    )(scalars, top, bottom, gate, up)


def down_kernel(idx_ref, mine_ref, other_ref, weight_ref, *refs):
    out_ref = refs[-1]
    lhs = jnp.concatenate([mine_ref[...], other_ref[...]], axis=0)
    product = jnp.dot(lhs, weight_ref[...], preferred_element_type=F32)

    @pl.when(pl.program_id(0) == 0)
    def _():
        out_ref[...] = refs[0][...] + product if len(refs) > 1 else product

    @pl.when(pl.program_id(0) > 0)
    def _():
        out_ref[...] += product


def down_add(total, mine, other, weight, row):
    rows, width = mine.shape
    outs = weight.shape[1]
    if width % BLK or weight.shape[0] % BLK or rows % 16 or outs % 128:
        lhs = jnp.concatenate([mine, other], axis=0)
        part = lax.dynamic_slice_in_dim(weight, row, width, 0)
        product = jnp.dot(lhs, part, preferred_element_type=F32)
        return product if total is None else total + product
    scalars = jnp.reshape(lax.div(row, BLK), (1,)).astype(jnp.int32)
    hidden_spec = pl.BlockSpec((rows, BLK), lambda k, s: (0, k))
    whole = pl.BlockSpec((2 * rows, outs), lambda k, s: (0, 0))
    totals = [] if total is None else [total]
    return pl.pallas_call(
        down_kernel,
        grid_spec=pltpu.PrefetchScalarGridSpec(
            num_scalar_prefetch=1,
            grid=(width // BLK,),
            in_specs=[
                hidden_spec,
                hidden_spec,
                pl.BlockSpec((BLK, outs), lambda k, s: (s[0] + k, 0)),
            ]
            + [whole] * len(totals),
            out_specs=whole,
        ),
        out_shape=jax.ShapeDtypeStruct((2 * rows, outs), F32),
        compiler_params=pltpu.CompilerParams(vmem_limit_bytes=50 * 2**20),
        cost_estimate=pl.CostEstimate(
            flops=2 * 2 * rows * width * outs,
            bytes_accessed=2 * width * outs + 2 * 2 * rows * width + 16 * rows * outs,
            transcendentals=0,
        ),
        name="down_add",
    )(scalars, mine, other, weight, *totals)


def general_body(tokens, gate_weight, up_weight, down_weight, right_factor, left_factor):
    fsdp_count = lax.axis_size("fsdp")
    tensor_count = lax.axis_size("tensor")
    chips = fsdp_count // 2
    rows, model = tokens.shape
    feat, hid = gate_weight.shape
    part = hid // chips
    me = lax.axis_index("fsdp")
    chip, core = lax.div(me, 2), lax.rem(me, 2)
    z = lax.axis_index("tensor")

    def swap(value):
        return lax.ppermute(value, "fsdp", [(i, i ^ 1) for i in range(fsdp_count)])

    def shift(value, hops):
        perm = [(i, (i + 2 * hops) % fsdp_count) for i in range(fsdp_count)]
        return lax.ppermute(value, "fsdp", perm)

    def gather_z(value):
        if tensor_count > 4:
            return lax.all_gather(value, "tensor", axis=0, tiled=True)
        size = value.shape[0]
        whole = jnp.zeros((size * tensor_count,) + value.shape[1:], value.dtype)
        whole = lax.dynamic_update_slice_in_dim(whole, value, z * size, 0)
        for step in range(1, tensor_count):
            perm = [(i, (i + step) % tensor_count) for i in range(tensor_count)]
            got = lax.ppermute(value, "tensor", perm)
            source = lax.rem(z - step + tensor_count, tensor_count)
            whole = lax.dynamic_update_slice_in_dim(whole, got, source * size, 0)
        return whole

    def scatter_z(value):
        if tensor_count > 4:
            return lax.psum_scatter(value, "tensor", scatter_dimension=0, tiled=False)
        total = lax.dynamic_index_in_dim(value, z, 0, keepdims=False)
        for step in range(1, tensor_count):
            target_z = lax.rem(z + step, tensor_count)
            piece = lax.dynamic_index_in_dim(value, target_z, 0, keepdims=False)
            perm = [(i, (i + step) % tensor_count) for i in range(tensor_count)]
            total += lax.ppermute(piece.astype(BF16), "tensor", perm).astype(F32)
        return total

    def columns(value, start, width):
        return lax.dynamic_slice_in_dim(value, start, width, 1)

    def after(value, *others):
        return lax.optimization_barrier((value,) + others)[0]

    def pair_z(value):
        perm = [(i, i ^ 1) for i in range(tensor_count)]
        got = lax.ppermute(value, "tensor", perm)
        odd = lax.rem(z, 2) == 1
        return jnp.concatenate(
            [jnp.where(odd, got, value), jnp.where(odd, value, got)], axis=0
        )

    if part % BLK == 0 and part // BLK > 1:
        head = (part // BLK + 1) // 2 * BLK
        chunks = [(0, head), (head, part - head)]
    else:
        chunks = [(0, part)]

    half = rows // 2
    own_half = lax.dynamic_slice_in_dim(tokens, lax.rem(z, 2) * half, half, 0)

    def send_tokens(value, dt, g):
        features = lax.rem(chip - dt + g + chips, chips) * (2 * feat)
        return shift(columns(value, features, 2 * feat), -dt)

    def partial(pair, dp, first, width):
        column = lax.rem(chip + dp, chips) * part
        top, block, bottom = pair
        mine, other = gate_up(top, block, bottom, gate_weight, up_weight, column, first, width)
        return mine, swap(other)

    def send_partials(pair, got, dt):
        sums = []
        for dp in range(1, chips):
            pieces = [partial(pair, dp, *chunk) for chunk in chunks]
            for n, (mine, from_core) in enumerate(pieces):
                both = (mine.astype(F32) + from_core.astype(F32)).astype(BF16)
                got[dt, dp, n] = shift(both, dp)
                sums.append(both)
        return sums

    got, kept, gathered = {}, {}, {}
    local = swap(columns(tokens, (me ^ 1) * feat, feat))
    arrived = {dt: send_tokens(own_half, dt, 0) for dt in range(1, chips)}
    sums = send_partials((tokens, me, local), got, 0)
    if sums:
        local = after(local, *sums)
    kept[0] = partial((tokens, me, local), 0, 0, part)
    late_tokens = after(tokens, kept[0][0])
    neighbour_tokens = swap(late_tokens)
    late_half = after(own_half, *sums) if sums else own_half

    for dt in range(1, chips):
        gathered[dt, 0] = pair_z(after(arrived[dt], *sums))
        whole = gathered[dt, 0]
        top = columns(whole, core * feat, feat)
        bottom = swap(columns(whole, (1 - core) * feat, feat))
        pair = (top, jnp.int32(0), bottom)
        sums = send_partials(pair, got, dt)
        pair = (top, jnp.int32(0), after(bottom, *sums))
        kept[dt] = partial(pair, 0, 0, part)
        for g in range(1, chips):
            gathered[dt, g] = pair_z(after(send_tokens(late_half, dt, g), kept[dt][0]))

    def activate(e, first, width, n):
        terms = [lax.slice_in_dim(term, first, first + width, axis=2) for term in kept[e]]
        terms += [got[(e + dp) % chips, dp, n] for dp in range(1, chips)]
        total = sum(term.astype(F32) for term in terms)
        return (jax.nn.silu(total[0]) * total[1]).astype(BF16)

    totals = {u: None for u in range(chips)}
    for e in list(range(1, chips)) + [0]:
        values = [activate(e, *chunk, n) for n, chunk in enumerate(chunks)]
        spans = list(chunks)
        if e:
            values, spans = [jnp.concatenate(values, axis=1)], [(0, part)]
        sent = [[value] + [shift(value, d) for d in range(1, chips)] for value in values]
        for (first, width), copies in zip(spans, sent):
            for d, mine in enumerate(copies):
                u = (e - d + chips) % chips
                row = lax.rem(chip - d + chips, chips) * part + first
                totals[u] = down_add(totals[u], mine, swap(mine), down_weight, row)

    token_rows = []
    for dt in range(chips):
        if dt == 0:
            token_rows += [tokens, neighbour_tokens]
            continue
        else:
            full = jnp.zeros((rows, model), BF16)
            for g in range(chips):
                features = lax.rem(chip + g, chips) * (2 * feat)
                full = lax.dynamic_update_slice_in_dim(full, gathered[dt, g], features, 1)
        token_rows += [full, swap(full)]
    inputs = jnp.concatenate(token_rows, axis=0)
    count = inputs.shape[0]

    blocks, share, size = right_factor.shape
    ratio = tensor_count // fsdp_count
    turn = []
    for a in range(fsdp_count):
        for b in range(tensor_count):
            turn.append((a * tensor_count + b, (b // ratio) * tensor_count + a * ratio + b % ratio))
    back = [(b, a) for a, b in turn]
    right_rows = gather_z(lax.ppermute(right_factor, ("fsdp", "tensor"), turn)[None])
    right_rows = right_rows.reshape(fsdp_count, ratio, blocks, share, size)
    right_rows = right_rows.transpose(0, 2, 1, 3, 4).reshape(
        fsdp_count * blocks, ratio * share, size
    )
    left_rows = jnp.moveaxis(gather_z(jnp.moveaxis(left_factor, 1, 0)), 0, 1)

    block_input = inputs.reshape(count, fsdp_count * blocks, size)
    mixed = jnp.einsum(
        "nim,ijm->nij", block_input, right_rows, preferred_element_type=F32
    ).astype(BF16)
    student = jnp.einsum("nij,jki->njk", mixed, left_rows, preferred_element_type=F32)
    target = jnp.concatenate([totals[u] for u in range(chips)], axis=0)
    scale = 1.0 / math.sqrt(count)
    out_grad = (student * (1.0 / tensor_count) - target.reshape(student.shape)) * scale
    out_grad = out_grad.astype(BF16)
    grad_left = jnp.einsum("njk,nij->kji", out_grad, mixed, preferred_element_type=F32)
    mixed_grad = jnp.einsum(
        "njk,jki->nij", out_grad, left_rows, preferred_element_type=F32
    ).astype(BF16)
    grad_right = jnp.einsum(
        "nij,nim->ijm", mixed_grad, block_input, preferred_element_type=F32
    )
    grad_left = scatter_z(
        grad_left.reshape((tensor_count, -1) + grad_left.shape[1:])
    )
    grad_left = jnp.moveaxis(grad_left, 0, 1)
    grad_right = grad_right.reshape(fsdp_count, blocks, ratio, share, size)
    grad_right = grad_right.transpose(0, 2, 1, 3, 4).reshape(
        tensor_count, blocks, share, size
    )
    grad_right = lax.ppermute(scatter_z(grad_right), ("fsdp", "tensor"), back)
    return grad_right, grad_left


def cut_kernel(idx_ref, first_in, rest_in, first_ref, rest_ref):
    first_ref[...] = first_in[...]
    rest_ref[...] = rest_in[...]


def cut_tokens(tokens, half, chip):
    rows, model = tokens.shape
    block = (rows // 2, model // 2)
    shape = jax.ShapeDtypeStruct(block, BF16)
    whole = pl.BlockSpec(block, lambda n, s: (0, 0))
    return pl.pallas_call(
        cut_kernel,
        grid_spec=pltpu.PrefetchScalarGridSpec(
            num_scalar_prefetch=1,
            grid=(1,),
            in_specs=[
                pl.BlockSpec(block, lambda n, s: (s[0], s[1])),
                pl.BlockSpec(block, lambda n, s: (s[0], s[2])),
            ],
            out_specs=[whole, whole],
        ),
        out_shape=[shape, shape],
        cost_estimate=SMALL,
        name="cut_tokens",
    )(jnp.stack([half, 1 - chip, chip]).astype(jnp.int32), tokens, tokens)


def products_kernel(sets, idx_ref, *refs):
    pieces, (gate_ref, up_ref, mine_ref, other_ref) = refs[: 4 * sets], refs[4 * sets :]
    lhs = jnp.concatenate([piece[...] for piece in pieces], axis=0)
    rows = mine_ref.shape[2]
    for slot, weight_ref in enumerate((gate_ref, up_ref)):
        product = jnp.dot(lhs, weight_ref[...], preferred_element_type=F32).astype(BF16)
        for u in range(sets):
            mine_ref[u, slot] = product[2 * u * rows : (2 * u + 1) * rows]
            other_ref[u, slot] = product[(2 * u + 1) * rows : (2 * u + 2) * rows]


def products(pieces, scalars, gate, up, first, width):
    feat = gate.shape[0]
    sets = len(pieces) // 4
    half = pieces[0][0].shape[0]
    half = half // 2 if pieces[0][1] is not None else half
    start = first // BLK

    def piece_spec(row, column):
        if row is None:
            return pl.BlockSpec((half, feat), lambda n, s: (0, s[column]))
        return pl.BlockSpec((half, feat), lambda n, s: (s[row], s[column]))

    weight_spec = pl.BlockSpec(
        (feat, BLK), lambda n, s: (0, s[4] + start + n), pipeline_mode=pl.Buffered(2)
    )
    out_spec = pl.BlockSpec((sets, 2, 2 * half, BLK), lambda n, s: (0, 0, 0, n))
    shape = jax.ShapeDtypeStruct((sets, 2, 2 * half, width), BF16)
    return pl.pallas_call(
        functools.partial(products_kernel, sets),
        grid_spec=pltpu.PrefetchScalarGridSpec(
            num_scalar_prefetch=1,
            grid=(width // BLK,),
            in_specs=[piece_spec(row, column) for _, row, column in pieces]
            + [weight_spec, weight_spec],
            out_specs=[out_spec, out_spec],
        ),
        out_shape=[shape, shape],
        compiler_params=pltpu.CompilerParams(vmem_limit_bytes=50 * 2**20),
        cost_estimate=SMALL,
        name="gate_up_products",
    )(scalars, *[piece for piece, _, _ in pieces], gate, up)


def fill_rows(lhs, pieces, chip):
    own, near, got, near_got = pieces
    rows, width = own.shape[1:]
    for u in range(2):
        for part, (mine, other) in enumerate(((own, near), (got, near_got))):
            begin = pl.multiple_of(lax.rem(chip + part, 2) * width, LANES)
            which = u if part == 0 else 1 - u
            lhs[2 * u * rows : (2 * u + 1) * rows, pl.ds(begin, width)] = mine[which]
            lhs[(2 * u + 1) * rows : (2 * u + 2) * rows, pl.ds(begin, width)] = other[which]


def whole_spec(array):
    return pl.BlockSpec(array.shape, lambda n, s: (0,) * array.ndim)


TN = (((0,), (0,)), ((), ()))
NT = (((1,), (1,)), ((), ()))
WIDE = 8


def natural(step, chip, per_chip):
    return lax.rem(chip + step // per_chip, 2) * per_chip + lax.rem(step, per_chip)


def spread_kernel(left_ref, out_ref, scratch):
    groups, fold = out_ref.shape[0], BLK // left_ref.shape[1]
    blocks = left_ref.shape[1]
    scratch[...] = jnp.zeros_like(scratch)
    zeros = jnp.zeros((blocks, blocks), F32)
    for g in range(groups):
        for a in range(fold):
            value = left_ref[g * fold + a].astype(F32)
            pair = [value, zeros] if a % 2 == 0 else [zeros, value]
            wide = jnp.concatenate(pair, axis=1)
            lanes = slice(a // 2 * LANES, (a // 2 + 1) * LANES)
            for c in range(blocks // WIDE):
                row = (c * fold + a) * WIDE
                scratch[row : row + WIDE, lanes] = wide[c * WIDE : (c + 1) * WIDE]
        out_ref[g] = scratch[...].astype(BF16)


def spread_left(left):
    pairs, blocks, _ = left.shape
    return pl.pallas_call(
        spread_kernel,
        out_shape=jax.ShapeDtypeStruct((pairs * blocks // BLK, BLK, BLK), BF16),
        scratch_shapes=[pltpu.VMEM((BLK, BLK), F32)],
        cost_estimate=SMALL,
        name="spread_left",
    )(left)


def student_kernel(steps, late, tensor_count, idx_ref, *refs):
    tokens, (right_ref, left_ref, mixed_ref, student_ref, spread) = refs[:-5], refs[-5:]
    step = pl.program_id(0)
    chunk = natural(step, idx_ref[2], steps // 2)
    groups = left_ref.shape[0]
    pairs = right_ref.shape[2]
    share = BLK // groups

    @pl.when(step == 0)
    def _():
        spread[...] = jnp.zeros_like(spread)

    for t in range(WIDE):
        spread[t, pl.ds(t, pairs, stride=WIDE), :] = right_ref[0, t].astype(F32)
    factor = jnp.concatenate([spread[t] for t in range(WIDE)], axis=1).astype(BF16)

    def mix(pieces):
        rows = jnp.concatenate([piece[...] for piece in pieces], axis=0)
        part = lax.dot_general(factor, rows, NT, preferred_element_type=F32).astype(BF16)
        start = pl.multiple_of(chunk * share, share)
        for g in range(groups):
            mixed_ref[g, pl.ds(start, share), :] = part[g * share : (g + 1) * share]

    if late:
        pl.when(step < steps // 2)(lambda: mix(tokens[:4]))
        pl.when(step >= steps // 2)(lambda: mix(tokens[4:]))
    else:
        mix(tokens)

    @pl.when(step == steps - 1)
    def _():
        for g in range(groups):
            span = slice(g * BLK, (g + 1) * BLK)
            student = lax.dot_general(
                mixed_ref[g], left_ref[g], TN, preferred_element_type=F32
            )
            student_ref[:, span] = student * (1.0 / tensor_count)


def token_specs(half, width, steps, begin, own):
    def chunk(n, s):
        step = jnp.maximum(n - begin, 0)
        return natural(step, s[2], steps // 2)

    if own:
        return [
            pl.BlockSpec(
                (half, width),
                lambda n, s, p=p: (s[p % 2], chunk(n, s)),
                pipeline_mode=pl.Buffered(2),
            )
            for p in range(4)
        ]
    near = pl.BlockSpec(
        (half, width),
        lambda n, s: (0, jnp.clip(n - begin, 0, steps // 2 - 1)),
        pipeline_mode=pl.Buffered(2),
    )
    far = pl.BlockSpec(
        (half, width),
        lambda n, s: (0, jnp.clip(n - begin - steps // 2, 0, steps // 2 - 1)),
        pipeline_mode=pl.Buffered(2),
    )
    return [near] * 4 + [far] * 4


def student_part(tokens, late, scalars, right_rows, left_diag, tensor_count):
    per_owner, pairs, size = right_rows.shape[1:]
    blocks = right_rows.shape[0] * per_owner
    steps = blocks // WIDE
    half = tokens[0].shape[0] if late else tokens[0].shape[0] // 2
    halves = per_owner // WIDE

    def right_block(n, s):
        chunk = natural(n, s[2], steps // 2)
        return (s[3] ^ (chunk // halves), lax.rem(chunk, halves), 0, 0)

    groups = left_diag.shape[0]
    return pl.pallas_call(
        functools.partial(student_kernel, steps, late, tensor_count),
        grid_spec=pltpu.PrefetchScalarGridSpec(
            num_scalar_prefetch=1,
            grid=(steps,),
            in_specs=token_specs(half, WIDE * size, steps, 0, not late)
            + [
                pl.BlockSpec((1, WIDE, pairs, size), right_block),
                whole_spec(left_diag),
            ],
            out_specs=[
                pl.BlockSpec((groups, BLK, 4 * half), lambda n, s: (0, 0, 0)),
                pl.BlockSpec((4 * half, groups * BLK), lambda n, s: (0, 0)),
            ],
            scratch_shapes=[pltpu.VMEM((WIDE, pairs * WIDE, size), F32)],
        ),
        out_shape=[
            jax.ShapeDtypeStruct((groups, BLK, 4 * half), BF16),
            jax.ShapeDtypeStruct((4 * half, groups * BLK), F32),
        ],
        compiler_params=pltpu.CompilerParams(vmem_limit_bytes=50 * 2**20),
        cost_estimate=pl.CostEstimate(
            flops=10**10, bytes_accessed=10**7, transcendentals=0
        ),
        name="student_part",
    )(scalars, *tokens, right_rows, left_diag)


def grads_kernel(groups, steps, scale, idx_ref, *refs):
    hidden, refs = refs[:4], refs[4:]
    weight_ref, student0, student1, mixed0, mixed1, left_ref = refs[:6]
    own, near, far = refs[6:10], refs[10:14], refs[14:18]
    out_ref, lhs, back, wide = refs[18:]
    step = pl.program_id(0)
    z = idx_ref[3]
    parts, size = out_ref.shape[0], out_ref.shape[2]
    blocks = steps * WIDE
    per_part = blocks // parts
    share = BLK // steps
    pairs = groups * share // WIDE
    fold = BLK // blocks

    def place(owner):
        bits = z ^ owner
        return lax.rem(bits, 2) * 2 + bits // 2

    pl.when(step == 0)(lambda: fill_rows(lhs, hidden, idx_ref[2]))

    @pl.when(step < groups)
    def _():
        target = jnp.dot(lhs[...], weight_ref[...], preferred_element_type=F32)
        student = jnp.concatenate([student0[...], student1[...]], axis=0)
        out_grad = ((student - target) * scale).astype(BF16)
        mixed = jnp.concatenate([mixed0[0], mixed1[0]], axis=1)
        left = jnp.dot(mixed, out_grad, preferred_element_type=F32)
        value = lax.dot_general(
            left_ref[0], out_grad, NT, preferred_element_type=F32
        ).astype(BF16)
        row = pl.multiple_of(step * share, share)
        for c in range(steps):
            back[c, pl.ds(row, share), :] = value[c * share : (c + 1) * share]
        low = lax.broadcasted_iota(jnp.int32, (blocks, size), 1) < blocks
        rows = blocks // parts
        for pair in range(fold // 2):
            lanes = slice(pair * size, (pair + 1) * size)
            picked = []
            for a in (2 * pair, 2 * pair + 1):
                for c in range(steps):
                    begin = (c * fold + a) * WIDE
                    picked.append(left[begin : begin + WIDE, lanes])
            turned = jnp.concatenate(picked, axis=0).T
            both = jnp.where(low, turned[:blocks], turned[blocks:]).astype(BF16)
            begin = per_part * pairs + (step * (fold // 2) + pair) * rows
            begin = pl.multiple_of(begin, rows)
            for owner in range(parts):
                out_ref[place(owner), pl.ds(begin, rows), :] = both[
                    owner * rows : (owner + 1) * rows
                ]

    def right(later):
        chunk = natural(step - groups, idx_ref[2], steps // 2)
        rows = jnp.concatenate([piece[...] for piece in own + later], axis=0)
        value = jnp.dot(back[chunk], rows, preferred_element_type=F32)
        for t in range(WIDE):
            wide[t] = value[:, t * size : (t + 1) * size]
        for t in range(WIDE):
            block = chunk * WIDE + t
            begin = pl.multiple_of(lax.rem(block, per_part) * pairs, pairs)
            out_ref[place(block // per_part), pl.ds(begin, pairs), :] = wide[
                t, pl.ds(t, pairs, stride=WIDE), :
            ].astype(BF16)

    pl.when((step >= groups) & (step < groups + steps // 2))(lambda: right(near))
    pl.when(step >= groups + steps // 2)(lambda: right(far))


def factor_grads(
    hidden, weight, students, mixed, left_diag, own, late, scalars, parts, size, scale
):
    groups, count = left_diag.shape[0], 2 * students[0].shape[0]
    width = weight.shape[0]
    half = late[0].shape[0]
    steps = own[0].shape[1] // (WIDE * size)
    blocks = steps * WIDE
    pairs = groups * BLK // blocks
    deep = pl.Buffered(2)

    def group(n):
        return jnp.minimum(n, groups - 1)

    column = pl.BlockSpec((count // 2, BLK), lambda n, s: (0, group(n)), pipeline_mode=deep)
    slab = pl.BlockSpec((1, BLK, count // 2), lambda n, s: (group(n), 0, 0), pipeline_mode=deep)
    out_rows = (pairs * blocks + pairs * blocks * blocks // size) // parts
    return pl.pallas_call(
        functools.partial(grads_kernel, groups, steps, scale),
        grid_spec=pltpu.PrefetchScalarGridSpec(
            num_scalar_prefetch=1,
            grid=(groups + steps,),
            in_specs=[whole_spec(piece) for piece in hidden]
            + [pl.BlockSpec((width, BLK), lambda n, s: (0, group(n)), pipeline_mode=deep)]
            + [column, column, slab, slab]
            + [
                pl.BlockSpec(
                    (1, BLK, BLK), lambda n, s: (group(n), 0, 0), pipeline_mode=deep
                )
            ]
            + token_specs(half, WIDE * size, steps, groups, True)
            + token_specs(half, WIDE * size, steps, groups, False),
            out_specs=pl.BlockSpec((parts, out_rows, size), lambda n, s: (0, 0, 0)),
            scratch_shapes=[
                pltpu.VMEM((count, width), BF16),
                pltpu.VMEM((steps, groups * (BLK // steps), count), BF16),
                pltpu.VMEM((WIDE, pairs * WIDE, size), F32),
            ],
        ),
        out_shape=jax.ShapeDtypeStruct((parts, out_rows, size), BF16),
        compiler_params=pltpu.CompilerParams(vmem_limit_bytes=50 * 2**20),
        cost_estimate=SMALL,
        name="factor_grads",
    )(scalars, *hidden, weight, *students, *mixed, left_diag, *own, *late)


def tiled_body(tokens, gate_weight, up_weight, down_weight, right_factor, left_factor):
    fsdp_count = lax.axis_size("fsdp")
    tensor_count = lax.axis_size("tensor")
    rows, model = tokens.shape
    part = gate_weight.shape[1] // 2
    me, z = lax.axis_index("fsdp"), lax.axis_index("tensor")
    chip, core, odd = lax.div(me, 2), lax.rem(me, 2), lax.rem(z, 2)
    both_axes = ("fsdp", "tensor")

    def swap(value):
        return lax.ppermute(value, "fsdp", [(i, i ^ 1) for i in range(fsdp_count)])

    def across(value):
        return lax.ppermute(value, "fsdp", [(i, i ^ 2) for i in range(fsdp_count)])

    def along(value, bit):
        return lax.ppermute(value, "tensor", [(i, i ^ bit) for i in range(tensor_count)])

    def turn(value, bit):
        perm = []
        for f in range(fsdp_count):
            for t in range(tensor_count):
                perm.append((f * tensor_count + t, (t ^ bit) * tensor_count + f))
        return lax.ppermute(value, both_axes, perm)

    def after(value, *others):
        return lax.optimization_barrier((value,) + others)[0]

    def double(value, bit):
        return jnp.concatenate([value, along(value, bit)], axis=0)

    def add(*terms):
        return sum(term.astype(F32) for term in terms)

    near_tokens = swap(tokens)
    first, rest = cut_tokens(tokens, odd, chip)
    arrived = across(first)
    base = jnp.stack([odd, 1 - odd])
    mine_block = lax.div(part, BLK) * chip
    other_block = lax.div(part, BLK) * (1 - chip)

    def scalars(block):
        return jnp.concatenate([base, jnp.stack([me, core, block])]).astype(jnp.int32)

    own_pieces = [(t, row, 2) for t in (tokens, near_tokens) for row in (0, 1)]
    mine, other = products(
        own_pieces, scalars(other_block), gate_weight, up_weight, 0, part
    )
    early = mine
    sums = add(mine[0], swap(after(other[0], arrived))).astype(BF16)
    got_early = across(sums)

    arrived = after(arrived, early)
    partner = along(arrived, 1)
    near_arrived = swap(arrived)
    late_first = across(after(rest, sums))
    order = jnp.concatenate([base, jnp.stack([chip, z])]).astype(jnp.int32)
    own = [tokens, tokens, near_tokens, near_tokens]
    late = [arrived, partner, near_arrived, swap(partner)]
    late_pieces = [(t, None, 3) for t in late]

    pairs, blocks = left_factor.shape[0], left_factor.shape[2]
    right_rows = turn(after(right_factor, sums), 0)[None]
    left_own = left_factor.reshape(1, -1, LANES)
    left_rows = double(after(left_own, sums), 1)

    late_order = after(scalars(other_block), sums, right_rows, left_rows)
    mine, other = products(late_pieces, late_order, gate_weight, up_weight, 0, part)
    near = swap(after(other[0], got_early, late_first))
    right_rows, left_rows = after(right_rows, mine), after(left_rows, mine)
    more_right, more_left = along(right_rows, 1), along(left_rows, 2)
    sums = add(mine[0], near).astype(BF16)
    got = across(sums)
    mine_order = after(scalars(mine_block), sums)
    kept, other = products(
        own_pieces + late_pieces, mine_order, gate_weight, up_weight, 0, part
    )
    right_rows = jnp.concatenate([right_rows, after(more_right, kept)], axis=0)
    left_rows = jnp.concatenate([left_rows, after(more_left, kept)], axis=0)

    left_rows = left_rows.reshape((tensor_count,) + left_factor.shape)
    for axis, bit in ((0, 2), (1, 1)):
        split = left_rows.reshape((2, 2) + left_rows.shape[1:])
        split = jnp.where(lax.rem(lax.div(z, bit), 2) == 1, jnp.flip(split, axis), split)
        left_rows = split.reshape(left_rows.shape)
    left_rows = left_rows.transpose(1, 3, 0, 2).reshape(pairs, blocks, blocks)

    left_diag = spread_left(left_rows)
    near_kept = swap(after(other, got, right_rows, left_diag))
    more_right = along(right_rows, 2)
    late_partner = along(after(late_first, kept), 1)
    hidden = []
    for u, term in enumerate((got, got_early)):
        total = add(kept[u], near_kept[u], term)
        hidden.append((jax.nn.silu(total[0]) * total[1]).astype(BF16))
    hidden = jnp.stack(hidden)
    got_hidden = across(hidden)
    near_hidden = swap(hidden)
    more_right, late_partner = after(more_right, hidden), after(late_partner, hidden)
    right_rows = jnp.concatenate([right_rows, more_right], axis=0)
    mixed0, student0 = student_part(
        [after(tokens, hidden)] + own[1:], False, order, right_rows, left_diag, tensor_count
    )
    late_rest = [late_first, late_partner, swap(late_first), swap(late_partner)]
    mixed1, student1 = student_part(
        late + [after(late_rest[0], mixed0)] + late_rest[1:],
        True,
        order,
        right_rows,
        left_diag,
        tensor_count,
    )
    got_hidden = after(got_hidden, mixed1)
    hidden = [hidden, near_hidden, got_hidden, swap(got_hidden)]

    grads = factor_grads(
        hidden,
        down_weight,
        (student0, student1),
        (mixed0, mixed1),
        left_diag,
        own,
        late + late_rest,
        order,
        tensor_count,
        right_factor.shape[2],
        1.0 / math.sqrt(rows * fsdp_count),
    )
    summed = add(grads[:2], along(grads[2:], 1)).astype(BF16)
    right_shape = right_factor.shape
    cut = right_shape[0] * right_shape[1]
    grad_right = add(turn(summed[0, :cut], 0), turn(summed[1, :cut], 2))
    grad_left = add(summed[0, cut:], along(summed[1, cut:], 2))
    grad_left = grad_left.reshape(pairs // 2, -1, 2, blocks).transpose(0, 2, 1, 3)
    return grad_right.reshape(right_shape), grad_left.reshape(left_factor.shape)


def body(*args):
    tokens, gate_weight, _, _, right_factor, left_factor = args
    counts = (lax.axis_size("fsdp"), lax.axis_size("tensor"))
    feat, hid = gate_weight.shape
    per_owner, share, size = right_factor.shape
    blocks = left_factor.shape[2]
    fits = hid % (2 * BLK) == 0
    fits = fits and counts == (4, 4) and tokens.shape[0] == 128
    fits = fits and hid >= 4 * BLK and feat % BLK == 0
    fits = fits and size == 128 and 2 * blocks == size and per_owner % WIDE == 0
    fits = fits and left_factor.shape[0] == share and share % 16 == 0
    return (tiled_body if fits else general_body)(*args)


def solution(mesh):
    return jax.shard_map(
        body,
        mesh=mesh,
        in_specs=(
            P(("groups", "fsdp"), None),
            P("fsdp", "tensor"),
            P("fsdp", "tensor"),
            P("tensor", "fsdp"),
            P("fsdp", "tensor", None),
            P("fsdp", "tensor", None),
        ),
        out_specs=(P(("groups", "fsdp"), "tensor", None), P(("groups", "fsdp"), "tensor", None)),
        check_vma=False,
    )
```

```python
import functools
import math

import jax
import jax.numpy as jnp
from jax import lax
from jax.experimental import pallas as pl
from jax.experimental.pallas import tpu as pltpu
from jax.sharding import PartitionSpec as P

BLK = 256
LANES = 128
SMALL = pl.CostEstimate(flops=1, bytes_accessed=1, transcendentals=0)
F32 = jnp.float32
BF16 = jnp.bfloat16


def gate_up_kernel(idx_ref, top_ref, bottom_ref, gate_ref, up_ref, mine_ref, other_ref):
    rows = top_ref.shape[0]
    lhs = jnp.concatenate([top_ref[...], bottom_ref[...]], axis=0)
    for slot, weight_ref in enumerate((gate_ref, up_ref)):
        product = jnp.dot(lhs, weight_ref[...], preferred_element_type=F32).astype(BF16)
        mine_ref[slot] = product[:rows]
        other_ref[slot] = product[rows:]


def gate_up(top, top_block, bottom, gate, up, column, first, width):
    rows, feat = bottom.shape
    if width % BLK or gate.shape[1] % BLK or rows % 16 or feat % 128:
        lhs = jnp.concatenate(
            [lax.dynamic_slice_in_dim(top, top_block * feat, feat, 1), bottom], axis=0
        )
        both = [
            jnp.dot(
                lhs,
                lax.dynamic_slice_in_dim(w, column + first, width, 1),
                preferred_element_type=F32,
            ).astype(BF16)
            for w in (gate, up)
        ]
        both = jnp.stack(both)
        return both[:, :rows], both[:, rows:]
    scalars = jnp.stack([top_block, lax.div(column, BLK) + first // BLK]).astype(jnp.int32)
    weight_spec = pl.BlockSpec((feat, BLK), lambda n, s: (0, s[1] + n))
    out_spec = pl.BlockSpec((2, rows, BLK), lambda n, s: (0, 0, n))
    shape = jax.ShapeDtypeStruct((2, rows, width), BF16)
    return pl.pallas_call(
        gate_up_kernel,
        grid_spec=pltpu.PrefetchScalarGridSpec(
            num_scalar_prefetch=1,
            grid=(width // BLK,),
            in_specs=[
                pl.BlockSpec((rows, feat), lambda n, s: (0, s[0])),
                pl.BlockSpec((rows, feat), lambda n, s: (0, 0)),
                weight_spec,
                weight_spec,
            ],
            out_specs=[out_spec, out_spec],
        ),
        out_shape=[shape, shape],
        compiler_params=pltpu.CompilerParams(vmem_limit_bytes=50 * 2**20),
        cost_estimate=pl.CostEstimate(
            flops=2 * 2 * rows * feat * 2 * width,
            bytes_accessed=2 * feat * 2 * width + 2 * 2 * rows * (feat + 2 * width),
            transcendentals=0,
        ),
        name="gate_up",
    )(scalars, top, bottom, gate, up)


def down_kernel(idx_ref, mine_ref, other_ref, weight_ref, *refs):
    out_ref = refs[-1]
    lhs = jnp.concatenate([mine_ref[...], other_ref[...]], axis=0)
    product = jnp.dot(lhs, weight_ref[...], preferred_element_type=F32)

    @pl.when(pl.program_id(0) == 0)
    def _():
        out_ref[...] = refs[0][...] + product if len(refs) > 1 else product

    @pl.when(pl.program_id(0) > 0)
    def _():
        out_ref[...] += product


def down_add(total, mine, other, weight, row):
    rows, width = mine.shape
    outs = weight.shape[1]
    if width % BLK or weight.shape[0] % BLK or rows % 16 or outs % 128:
        lhs = jnp.concatenate([mine, other], axis=0)
        part = lax.dynamic_slice_in_dim(weight, row, width, 0)
        product = jnp.dot(lhs, part, preferred_element_type=F32)
        return product if total is None else total + product
    scalars = jnp.reshape(lax.div(row, BLK), (1,)).astype(jnp.int32)
    hidden_spec = pl.BlockSpec((rows, BLK), lambda k, s: (0, k))
    whole = pl.BlockSpec((2 * rows, outs), lambda k, s: (0, 0))
    totals = [] if total is None else [total]
    return pl.pallas_call(
        down_kernel,
        grid_spec=pltpu.PrefetchScalarGridSpec(
            num_scalar_prefetch=1,
            grid=(width // BLK,),
            in_specs=[
                hidden_spec,
                hidden_spec,
                pl.BlockSpec((BLK, outs), lambda k, s: (s[0] + k, 0)),
            ]
            + [whole] * len(totals),
            out_specs=whole,
        ),
        out_shape=jax.ShapeDtypeStruct((2 * rows, outs), F32),
        compiler_params=pltpu.CompilerParams(vmem_limit_bytes=50 * 2**20),
        cost_estimate=pl.CostEstimate(
            flops=2 * 2 * rows * width * outs,
            bytes_accessed=2 * width * outs + 2 * 2 * rows * width + 16 * rows * outs,
            transcendentals=0,
        ),
        name="down_add",
    )(scalars, mine, other, weight, *totals)


def general_body(tokens, gate_weight, up_weight, down_weight, right_factor, left_factor):
    fsdp_count = lax.axis_size("fsdp")
    tensor_count = lax.axis_size("tensor")
    chips = fsdp_count // 2
    rows, model = tokens.shape
    feat, hid = gate_weight.shape
    part = hid // chips
    me = lax.axis_index("fsdp")
    chip, core = lax.div(me, 2), lax.rem(me, 2)
    z = lax.axis_index("tensor")

    def swap(value):
        return lax.ppermute(value, "fsdp", [(i, i ^ 1) for i in range(fsdp_count)])

    def shift(value, hops):
        perm = [(i, (i + 2 * hops) % fsdp_count) for i in range(fsdp_count)]
        return lax.ppermute(value, "fsdp", perm)

    def gather_z(value):
        if tensor_count > 4:
            return lax.all_gather(value, "tensor", axis=0, tiled=True)
        size = value.shape[0]
        whole = jnp.zeros((size * tensor_count,) + value.shape[1:], value.dtype)
        whole = lax.dynamic_update_slice_in_dim(whole, value, z * size, 0)
        for step in range(1, tensor_count):
            perm = [(i, (i + step) % tensor_count) for i in range(tensor_count)]
            got = lax.ppermute(value, "tensor", perm)
            source = lax.rem(z - step + tensor_count, tensor_count)
            whole = lax.dynamic_update_slice_in_dim(whole, got, source * size, 0)
        return whole

    def scatter_z(value):
        if tensor_count > 4:
            return lax.psum_scatter(value, "tensor", scatter_dimension=0, tiled=False)
        total = lax.dynamic_index_in_dim(value, z, 0, keepdims=False)
        for step in range(1, tensor_count):
            target_z = lax.rem(z + step, tensor_count)
            piece = lax.dynamic_index_in_dim(value, target_z, 0, keepdims=False)
            perm = [(i, (i + step) % tensor_count) for i in range(tensor_count)]
            total += lax.ppermute(piece.astype(BF16), "tensor", perm).astype(F32)
        return total

    def columns(value, start, width):
        return lax.dynamic_slice_in_dim(value, start, width, 1)

    def after(value, *others):
        return lax.optimization_barrier((value,) + others)[0]

    def pair_z(value):
        perm = [(i, i ^ 1) for i in range(tensor_count)]
        got = lax.ppermute(value, "tensor", perm)
        odd = lax.rem(z, 2) == 1
        return jnp.concatenate(
            [jnp.where(odd, got, value), jnp.where(odd, value, got)], axis=0
        )

    if part % BLK == 0 and part // BLK > 1:
        head = (part // BLK + 1) // 2 * BLK
        chunks = [(0, head), (head, part - head)]
    else:
        chunks = [(0, part)]

    half = rows // 2
    own_half = lax.dynamic_slice_in_dim(tokens, lax.rem(z, 2) * half, half, 0)

    def send_tokens(value, dt, g):
        features = lax.rem(chip - dt + g + chips, chips) * (2 * feat)
        return shift(columns(value, features, 2 * feat), -dt)

    def partial(pair, dp, first, width):
        column = lax.rem(chip + dp, chips) * part
        top, block, bottom = pair
        mine, other = gate_up(top, block, bottom, gate_weight, up_weight, column, first, width)
        return mine, swap(other)

    def send_partials(pair, got, dt):
        sums = []
        for dp in range(1, chips):
            pieces = [partial(pair, dp, *chunk) for chunk in chunks]
            for n, (mine, from_core) in enumerate(pieces):
                both = (mine.astype(F32) + from_core.astype(F32)).astype(BF16)
                got[dt, dp, n] = shift(both, dp)
                sums.append(both)
        return sums

    got, kept, gathered = {}, {}, {}
    local = swap(columns(tokens, (me ^ 1) * feat, feat))
    arrived = {dt: send_tokens(own_half, dt, 0) for dt in range(1, chips)}
    sums = send_partials((tokens, me, local), got, 0)
    if sums:
        local = after(local, *sums)
    kept[0] = partial((tokens, me, local), 0, 0, part)
    late_tokens = after(tokens, kept[0][0])
    neighbour_tokens = swap(late_tokens)
    late_half = after(own_half, *sums) if sums else own_half

    for dt in range(1, chips):
        gathered[dt, 0] = pair_z(after(arrived[dt], *sums))
        whole = gathered[dt, 0]
        top = columns(whole, core * feat, feat)
        bottom = swap(columns(whole, (1 - core) * feat, feat))
        pair = (top, jnp.int32(0), bottom)
        sums = send_partials(pair, got, dt)
        pair = (top, jnp.int32(0), after(bottom, *sums))
        kept[dt] = partial(pair, 0, 0, part)
        for g in range(1, chips):
            gathered[dt, g] = pair_z(after(send_tokens(late_half, dt, g), kept[dt][0]))

    def activate(e, first, width, n):
        terms = [lax.slice_in_dim(term, first, first + width, axis=2) for term in kept[e]]
        terms += [got[(e + dp) % chips, dp, n] for dp in range(1, chips)]
        total = sum(term.astype(F32) for term in terms)
        return (jax.nn.silu(total[0]) * total[1]).astype(BF16)

    totals = {u: None for u in range(chips)}
    for e in list(range(1, chips)) + [0]:
        values = [activate(e, *chunk, n) for n, chunk in enumerate(chunks)]
        spans = list(chunks)
        if e:
            values, spans = [jnp.concatenate(values, axis=1)], [(0, part)]
        sent = [[value] + [shift(value, d) for d in range(1, chips)] for value in values]
        for (first, width), copies in zip(spans, sent):
            for d, mine in enumerate(copies):
                u = (e - d + chips) % chips
                row = lax.rem(chip - d + chips, chips) * part + first
                totals[u] = down_add(totals[u], mine, swap(mine), down_weight, row)

    token_rows = []
    for dt in range(chips):
        if dt == 0:
            token_rows += [tokens, neighbour_tokens]
            continue
        else:
            full = jnp.zeros((rows, model), BF16)
            for g in range(chips):
                features = lax.rem(chip + g, chips) * (2 * feat)
                full = lax.dynamic_update_slice_in_dim(full, gathered[dt, g], features, 1)
        token_rows += [full, swap(full)]
    inputs = jnp.concatenate(token_rows, axis=0)
    count = inputs.shape[0]

    blocks, share, size = right_factor.shape
    ratio = tensor_count // fsdp_count
    turn = []
    for a in range(fsdp_count):
        for b in range(tensor_count):
            turn.append((a * tensor_count + b, (b // ratio) * tensor_count + a * ratio + b % ratio))
    back = [(b, a) for a, b in turn]
    right_rows = gather_z(lax.ppermute(right_factor, ("fsdp", "tensor"), turn)[None])
    right_rows = right_rows.reshape(fsdp_count, ratio, blocks, share, size)
    right_rows = right_rows.transpose(0, 2, 1, 3, 4).reshape(
        fsdp_count * blocks, ratio * share, size
    )
    left_rows = jnp.moveaxis(gather_z(jnp.moveaxis(left_factor, 1, 0)), 0, 1)

    block_input = inputs.reshape(count, fsdp_count * blocks, size)
    mixed = jnp.einsum(
        "nim,ijm->nij", block_input, right_rows, preferred_element_type=F32
    ).astype(BF16)
    student = jnp.einsum("nij,jki->njk", mixed, left_rows, preferred_element_type=F32)
    target = jnp.concatenate([totals[u] for u in range(chips)], axis=0)
    scale = 1.0 / math.sqrt(count)
    out_grad = (student * (1.0 / tensor_count) - target.reshape(student.shape)) * scale
    out_grad = out_grad.astype(BF16)
    grad_left = jnp.einsum("njk,nij->kji", out_grad, mixed, preferred_element_type=F32)
    mixed_grad = jnp.einsum(
        "njk,jki->nij", out_grad, left_rows, preferred_element_type=F32
    ).astype(BF16)
    grad_right = jnp.einsum(
        "nij,nim->ijm", mixed_grad, block_input, preferred_element_type=F32
    )
    grad_left = scatter_z(
        grad_left.reshape((tensor_count, -1) + grad_left.shape[1:])
    )
    grad_left = jnp.moveaxis(grad_left, 0, 1)
    grad_right = grad_right.reshape(fsdp_count, blocks, ratio, share, size)
    grad_right = grad_right.transpose(0, 2, 1, 3, 4).reshape(
        tensor_count, blocks, share, size
    )
    grad_right = lax.ppermute(scatter_z(grad_right), ("fsdp", "tensor"), back)
    return grad_right, grad_left


def cut_kernel(idx_ref, first_in, rest_in, first_ref, rest_ref):
    first_ref[...] = first_in[...]
    rest_ref[...] = rest_in[...]


def cut_tokens(tokens, half, chip):
    rows, model = tokens.shape
    first, rest = (rows, model // 2), (rows // 2, model // 2)
    return pl.pallas_call(
        cut_kernel,
        grid_spec=pltpu.PrefetchScalarGridSpec(
            num_scalar_prefetch=1,
            grid=(1,),
            in_specs=[
                pl.BlockSpec(first, lambda n, s: (0, s[1])),
                pl.BlockSpec(rest, lambda n, s: (s[0], s[2])),
            ],
            out_specs=[
                pl.BlockSpec(first, lambda n, s: (0, 0)),
                pl.BlockSpec(rest, lambda n, s: (0, 0)),
            ],
        ),
        out_shape=[jax.ShapeDtypeStruct(first, BF16), jax.ShapeDtypeStruct(rest, BF16)],
        cost_estimate=SMALL,
        name="cut_tokens",
    )(jnp.stack([half, 1 - chip, chip]).astype(jnp.int32), tokens, tokens)


def products_kernel(sets, idx_ref, *refs):
    pieces, (gate_ref, up_ref, mine_ref, other_ref) = refs[: 4 * sets], refs[4 * sets :]
    lhs = jnp.concatenate([piece[...] for piece in pieces], axis=0)
    rows = mine_ref.shape[2]
    for slot, weight_ref in enumerate((gate_ref, up_ref)):
        product = jnp.dot(lhs, weight_ref[...], preferred_element_type=F32).astype(BF16)
        for u in range(sets):
            mine_ref[u, slot] = product[2 * u * rows : (2 * u + 1) * rows]
            other_ref[u, slot] = product[(2 * u + 1) * rows : (2 * u + 2) * rows]


def products(pieces, scalars, gate, up, first, width):
    feat = gate.shape[0]
    sets = len(pieces) // 4
    half = pieces[0][0].shape[0] // 2
    start = first // BLK

    def piece_spec(row, column):
        return pl.BlockSpec((half, feat), lambda n, s: (s[row], s[column]))

    weight_spec = pl.BlockSpec(
        (feat, BLK), lambda n, s: (0, s[4] + start + n)
    )
    out_spec = pl.BlockSpec((sets, 2, 2 * half, BLK), lambda n, s: (0, 0, 0, n))
    shape = jax.ShapeDtypeStruct((sets, 2, 2 * half, width), BF16)
    return pl.pallas_call(
        functools.partial(products_kernel, sets),
        grid_spec=pltpu.PrefetchScalarGridSpec(
            num_scalar_prefetch=1,
            grid=(width // BLK,),
            in_specs=[piece_spec(row, column) for _, row, column in pieces]
            + [weight_spec, weight_spec],
            out_specs=[out_spec, out_spec],
        ),
        out_shape=[shape, shape],
        compiler_params=pltpu.CompilerParams(vmem_limit_bytes=50 * 2**20),
        cost_estimate=SMALL,
        name="gate_up_products",
    )(scalars, *[piece for piece, _, _ in pieces], gate, up)


def fill_rows(lhs, pieces, chip):
    rows, width = pieces[0].shape
    for u in range(2):
        for part in range(2):
            begin = pl.multiple_of(lax.rem(chip + part, 2) * width, LANES)
            which = 4 * part + (u if part == 0 else 1 - u)
            for core in range(2):
                row = (2 * u + core) * rows
                lhs[row : row + rows, pl.ds(begin, width)] = pieces[which + 2 * core][...]


def whole_spec(array):
    return pl.BlockSpec(array.shape, lambda n, s: (0,) * array.ndim)


TN = (((0,), (0,)), ((), ()))
NT = (((1,), (1,)), ((), ()))
WIDE = 8


def natural(step, chip, per_chip):
    return lax.rem(chip + step // per_chip, 2) * per_chip + lax.rem(step, per_chip)


def spread_kernel(idx_ref, rows_ref, out_ref, scratch):
    groups = out_ref.shape[0]
    parts, _, size = rows_ref.shape
    blocks = size // 2
    share = blocks // parts
    fold = BLK // blocks
    begin = rows_ref.shape[1] - groups * fold // 2 * share
    scratch[...] = jnp.zeros_like(scratch)
    low = lax.broadcasted_iota(jnp.int32, (blocks, size), 1) < blocks
    for g in range(groups):
        for pair in range(fold // 2):
            row = begin + (g * (fold // 2) + pair) * share
            picked = [
                rows_ref[idx_ref[3] ^ owner, row : row + share, :] for owner in range(parts)
            ]
            turned = jnp.concatenate(picked + picked, axis=0).astype(F32).T
            for a in range(2):
                value = turned[a * blocks : (a + 1) * blocks]
                value = jnp.where(low if a == 0 else ~low, value, 0.0)
                lanes = slice(pair * size, (pair + 1) * size)
                for c in range(blocks // WIDE):
                    row = (c * fold + 2 * pair + a) * WIDE
                    scratch[row : row + WIDE, lanes] = value[c * WIDE : (c + 1) * WIDE]
        out_ref[g] = scratch[...].astype(BF16)


def spread_left(scalars, rows, groups):
    return pl.pallas_call(
        spread_kernel,
        grid_spec=pltpu.PrefetchScalarGridSpec(
            num_scalar_prefetch=1,
            grid=(1,),
            in_specs=[whole_spec(rows)],
            out_specs=pl.BlockSpec((groups, BLK, BLK), lambda n, s: (0, 0, 0)),
            scratch_shapes=[pltpu.VMEM((BLK, BLK), F32)],
        ),
        out_shape=jax.ShapeDtypeStruct((groups, BLK, BLK), BF16),
        cost_estimate=SMALL,
        name="spread_left",
    )(scalars, rows)


def student_kernel(steps, late, tensor_count, idx_ref, *refs):
    tokens, refs = refs[:-6], refs[-6:]
    rights, (left_ref, mixed_ref, student_ref, spread) = refs[:2], refs[2:]
    step = pl.program_id(0)
    pair = natural(step, idx_ref[2], steps // 2)
    groups = left_ref.shape[0]
    size = spread.shape[2]
    pairs = spread.shape[1] // WIDE
    share = BLK // groups

    @pl.when(step == 0)
    def _():
        spread[...] = jnp.zeros_like(spread)

    def mix(pieces):
        for half, right_ref in enumerate(rights):
            for t in range(WIDE):
                value = right_ref[0, t * pairs : (t + 1) * pairs, :].astype(F32)
                spread[t, pl.ds(t, pairs, stride=WIDE), :] = value
            factor = jnp.concatenate([spread[t] for t in range(WIDE)], axis=1).astype(BF16)
            lanes = slice(half * WIDE * size, (half + 1) * WIDE * size)
            rows = jnp.concatenate([piece[:, lanes] for piece in pieces], axis=0)
            part = lax.dot_general(factor, rows, NT, preferred_element_type=F32).astype(BF16)
            start = pl.multiple_of((2 * pair + half) * share, share)
            for g in range(groups):
                mixed_ref[g, pl.ds(start, share), :] = part[g * share : (g + 1) * share]

    if late:
        pl.when(step < steps // 2)(lambda: mix(tokens[:4]))
        pl.when(step >= steps // 2)(lambda: mix(tokens[4:]))
    else:
        mix(tokens)

    @pl.when(step == steps - 1)
    def _():
        for g in range(groups):
            span = slice(g * BLK, (g + 1) * BLK)
            student = lax.dot_general(
                mixed_ref[g], left_ref[g], TN, preferred_element_type=F32
            )
            student_ref[:, span] = student * (1.0 / tensor_count)


def token_specs(half, width, steps, begin, own):
    def chunk(n, s):
        step = jnp.maximum(n - begin, 0)
        return natural(step, s[2], steps // 2)

    def near(n, s):
        return jnp.clip(n - begin, 0, steps // 2 - 1)

    def far(n, s):
        return jnp.clip(n - begin - steps // 2, 0, steps // 2 - 1)

    def specs(place):
        return [
            pl.BlockSpec((half, width), lambda n, s, p=p: (s[p % 2], place(n, s)))
            for p in range(4)
        ]

    if own:
        return specs(chunk)
    whole = pl.BlockSpec((half, width), lambda n, s: (0, far(n, s)))
    return specs(near) + [whole] * 4


def student_part(tokens, late, scalars, factors, left_diag, pairs, tensor_count):
    parts, _, size = factors.shape
    half = tokens[0].shape[0] // 2
    groups = left_diag.shape[0]
    blocks = groups * BLK // pairs
    steps = blocks // (2 * WIDE)

    def right_spec(half):
        return pl.BlockSpec(
            (1, WIDE * pairs, size),
            lambda n, s: (s[3] ^ natural(n, s[2], steps // 2), half, 0),
        )

    return pl.pallas_call(
        functools.partial(student_kernel, steps, late, tensor_count),
        grid_spec=pltpu.PrefetchScalarGridSpec(
            num_scalar_prefetch=1,
            grid=(steps,),
            in_specs=token_specs(half, 2 * WIDE * size, steps, 0, not late)
            + [right_spec(0), right_spec(1), whole_spec(left_diag)],
            out_specs=[
                pl.BlockSpec((groups, BLK, 4 * half), lambda n, s: (0, 0, 0)),
                pl.BlockSpec((4 * half, groups * BLK), lambda n, s: (0, 0)),
            ],
            scratch_shapes=[pltpu.VMEM((WIDE, pairs * WIDE, size), F32)],
        ),
        out_shape=[
            jax.ShapeDtypeStruct((groups, BLK, 4 * half), BF16),
            jax.ShapeDtypeStruct((4 * half, groups * BLK), F32),
        ],
        compiler_params=pltpu.CompilerParams(vmem_limit_bytes=50 * 2**20),
        cost_estimate=pl.CostEstimate(
            flops=10**10, bytes_accessed=10**7, transcendentals=0
        ),
        name="student_part",
    )(scalars, *tokens, factors, factors, left_diag)


def grads_kernel(groups, steps, scale, idx_ref, *refs):
    hidden, refs = refs[:8], refs[8:]
    weight_ref, student0, student1, mixed0, mixed1, left_ref = refs[:6]
    own, near, far = refs[6:10], refs[10:14], refs[14:18]
    out_ref, lhs, back, wide = refs[18:]
    step = pl.program_id(0)
    z = idx_ref[3]
    parts, size = out_ref.shape[0], out_ref.shape[2]
    chunks = 2 * steps
    blocks = chunks * WIDE
    per_part = blocks // parts
    share = BLK // chunks
    pairs = groups * share // WIDE
    fold = BLK // blocks

    def place(owner):
        bits = z ^ owner
        return lax.rem(bits, 2) * 2 + bits // 2

    pl.when(step == 0)(lambda: fill_rows(lhs, hidden, idx_ref[2]))

    @pl.when(step < groups)
    def _():
        target = jnp.dot(lhs[...], weight_ref[...], preferred_element_type=F32)
        student = jnp.concatenate([student0[...], student1[...]], axis=0)
        out_grad = ((student - target) * scale).astype(BF16)
        mixed = jnp.concatenate([mixed0[0], mixed1[0]], axis=1)
        left = jnp.dot(mixed, out_grad, preferred_element_type=F32)
        value = lax.dot_general(
            left_ref[0], out_grad, NT, preferred_element_type=F32
        ).astype(BF16)
        row = pl.multiple_of(step * share, share)
        for c in range(chunks):
            back[c, pl.ds(row, share), :] = value[c * share : (c + 1) * share]
        low = lax.broadcasted_iota(jnp.int32, (blocks, size), 1) < blocks
        rows = blocks // parts
        for pair in range(fold // 2):
            lanes = slice(pair * size, (pair + 1) * size)
            picked = []
            for a in (2 * pair, 2 * pair + 1):
                for c in range(chunks):
                    begin = (c * fold + a) * WIDE
                    picked.append(left[begin : begin + WIDE, lanes])
            turned = jnp.concatenate(picked, axis=0).T
            both = jnp.where(low, turned[:blocks], turned[blocks:]).astype(BF16)
            begin = per_part * pairs + (step * (fold // 2) + pair) * rows
            begin = pl.multiple_of(begin, rows)
            for owner in range(parts):
                out_ref[place(owner), pl.ds(begin, rows), :] = both[
                    owner * rows : (owner + 1) * rows
                ]

    def right(later):
        pair = natural(step - groups, idx_ref[2], steps // 2)
        for half in range(2):
            chunk = 2 * pair + half
            lanes = slice(half * WIDE * size, (half + 1) * WIDE * size)
            rows = jnp.concatenate([piece[:, lanes] for piece in own + later], axis=0)
            value = jnp.dot(back[chunk], rows, preferred_element_type=F32)
            for t in range(WIDE):
                wide[t] = value[:, t * size : (t + 1) * size]
            for t in range(WIDE):
                block = chunk * WIDE + t
                begin = pl.multiple_of(lax.rem(block, per_part) * pairs, pairs)
                out_ref[place(block // per_part), pl.ds(begin, pairs), :] = wide[
                    t, pl.ds(t, pairs, stride=WIDE), :
                ].astype(BF16)

    pl.when((step >= groups) & (step < groups + steps // 2))(lambda: right(near))
    pl.when(step >= groups + steps // 2)(lambda: right(far))


def factor_grads(
    hidden, weight, students, mixed, left_diag, own, late, scalars, parts, size, scale
):
    groups, count = left_diag.shape[0], 2 * students[0].shape[0]
    width = weight.shape[0]
    half = own[0].shape[0] // 2
    steps = own[0].shape[1] // (2 * WIDE * size)
    blocks = 2 * steps * WIDE
    pairs = groups * BLK // blocks

    def group(n):
        return jnp.minimum(n, groups - 1)

    column = pl.BlockSpec((count // 2, BLK), lambda n, s: (0, group(n)))
    slab = pl.BlockSpec((1, BLK, count // 2), lambda n, s: (group(n), 0, 0))
    out_rows = (pairs * blocks + pairs * blocks * blocks // size) // parts
    return pl.pallas_call(
        functools.partial(grads_kernel, groups, steps, scale),
        grid_spec=pltpu.PrefetchScalarGridSpec(
            num_scalar_prefetch=1,
            grid=(groups + steps,),
            in_specs=[whole_spec(piece) for piece in hidden]
            + [pl.BlockSpec((width, BLK), lambda n, s: (0, group(n)))]
            + [column, column, slab, slab]
            + [
                pl.BlockSpec(
                    (1, BLK, BLK), lambda n, s: (group(n), 0, 0)
                )
            ]
            + token_specs(half, 2 * WIDE * size, steps, groups, True)
            + token_specs(half, 2 * WIDE * size, steps, groups, False),
            out_specs=pl.BlockSpec((parts, out_rows, size), lambda n, s: (0, 0, 0)),
            scratch_shapes=[
                pltpu.VMEM((count, width), BF16),
                pltpu.VMEM((2 * steps, groups * BLK // (2 * steps), count), BF16),
                pltpu.VMEM((WIDE, pairs * WIDE, size), F32),
            ],
        ),
        out_shape=jax.ShapeDtypeStruct((parts, out_rows, size), BF16),
        compiler_params=pltpu.CompilerParams(vmem_limit_bytes=50 * 2**20),
        cost_estimate=SMALL,
        name="factor_grads",
    )(scalars, *hidden, weight, *students, *mixed, left_diag, *own, *late)


def tiled_body(tokens, gate_weight, up_weight, down_weight, right_factor, left_factor):
    fsdp_count = lax.axis_size("fsdp")
    tensor_count = lax.axis_size("tensor")
    rows, model = tokens.shape
    part = gate_weight.shape[1] // 2
    me, z = lax.axis_index("fsdp"), lax.axis_index("tensor")
    chip, core, odd = lax.div(me, 2), lax.rem(me, 2), lax.rem(z, 2)
    both_axes = ("fsdp", "tensor")

    def swap(value):
        return lax.ppermute(value, "fsdp", [(i, i ^ 1) for i in range(fsdp_count)])

    def across(value):
        return lax.ppermute(value, "fsdp", [(i, i ^ 2) for i in range(fsdp_count)])

    def along(value, bit):
        return lax.ppermute(value, "tensor", [(i, i ^ bit) for i in range(tensor_count)])

    def turn(value, bit):
        perm = []
        for f in range(fsdp_count):
            for t in range(tensor_count):
                perm.append((f * tensor_count + t, (t ^ bit) * tensor_count + f))
        return lax.ppermute(value, both_axes, perm)

    def after(value, *others):
        return lax.optimization_barrier((value,) + others)[0]

    def add(*terms):
        return sum(term.astype(F32) for term in terms)

    near_tokens = swap(tokens)
    first, rest = cut_tokens(tokens, odd, chip)
    arrived = across(first)
    base = jnp.stack([odd, 1 - odd])
    mine_block = lax.div(part, BLK) * chip
    other_block = lax.div(part, BLK) * (1 - chip)

    def scalars(block):
        return jnp.concatenate([base, jnp.stack([me, core, block])]).astype(jnp.int32)

    own_pieces = [(t, row, 2) for t in (tokens, near_tokens) for row in (0, 1)]
    mine, other = products(
        own_pieces, after(scalars(other_block), first), gate_weight, up_weight, 0, part
    )
    sums = add(mine[0], after(swap(other[0]), arrived)).astype(BF16)
    got_early = across(sums)
    late_first = across(after(rest, sums))

    pairs, blocks = left_factor.shape[0], left_factor.shape[2]
    left_rows = left_factor.reshape(pairs // 2, 2, -1, blocks).transpose(0, 2, 1, 3)
    factors = turn(after(right_factor, first), 0)
    factors = jnp.concatenate(
        [factors.reshape(-1, LANES), left_rows.reshape(-1, LANES)], axis=0
    )
    factors = after(factors, sums)[None]
    more = along(factors, 1)

    order = jnp.concatenate([base, jnp.stack([chip, z])]).astype(jnp.int32)
    own = [tokens, tokens, near_tokens, near_tokens]
    near_arrived = swap(arrived)
    late_pieces = [(t, row, 3) for t in (arrived, near_arrived) for row in (0, 1)]
    late_order = after(scalars(other_block), sums)
    mine, other = products(late_pieces, late_order, gate_weight, up_weight, 0, part)
    near = swap(other[0])
    factors = after(jnp.concatenate([factors, more], axis=0), mine)
    more = along(factors, 2)
    mine_order = after(scalars(mine_block), mine)
    kept, other = products(
        own_pieces + late_pieces, mine_order, gate_weight, up_weight, 0, part
    )
    near_kept = swap(after(other, got_early, late_first, more))
    sums = add(mine[0], after(near, kept)).astype(BF16)
    got = across(sums)

    factors = jnp.concatenate([factors, after(more, kept)], axis=0)
    left_diag = spread_left(order, factors, pairs * blocks // BLK)

    def activate(u, term):
        total = add(kept[u], near_kept[u], term)
        return (jax.nn.silu(total[0]) * total[1]).astype(BF16)

    hidden1 = activate(1, got_early)
    got1 = across(hidden1)
    near1 = swap(hidden1)
    late_partner = along(after(late_first, kept), 1)
    mixed0, student0 = student_part(
        [after(tokens, hidden1, sums)] + own[1:],
        False,
        order,
        factors,
        left_diag,
        pairs,
        tensor_count,
    )
    hidden0 = activate(0, after(got, mixed0))
    got0 = across(hidden0)
    near0 = swap(hidden0)
    late_partner = after(late_partner, mixed0)
    late = [arrived, arrived, near_arrived, near_arrived]
    late += [late_first, late_partner, swap(late_first), swap(late_partner)]
    mixed1, student1 = student_part(
        [after(arrived, hidden0)] + late[1:],
        True,
        order,
        factors,
        left_diag,
        pairs,
        tensor_count,
    )
    got1, got0 = after(got1, mixed1), after(got0, mixed1)
    hidden = [hidden0, hidden1, near0, near1, got0, got1, swap(got0), swap(got1)]

    grads = factor_grads(
        hidden,
        down_weight,
        (student0, student1),
        (mixed0, mixed1),
        left_diag,
        own,
        late,
        order,
        tensor_count,
        right_factor.shape[2],
        1.0 / math.sqrt(rows * fsdp_count),
    )
    summed = add(grads[:2], along(grads[2:], 1)).astype(BF16)
    right_shape = right_factor.shape
    cut = right_shape[0] * right_shape[1]
    grad_right = add(turn(summed[0, :cut], 0), turn(summed[1, :cut], 2))
    grad_left = add(summed[0, cut:], along(summed[1, cut:], 2))
    grad_left = grad_left.reshape(pairs // 2, -1, 2, blocks).transpose(0, 2, 1, 3)
    return grad_right.reshape(right_shape), grad_left.reshape(left_factor.shape)


def body(*args):
    tokens, gate_weight, _, _, right_factor, left_factor = args
    counts = (lax.axis_size("fsdp"), lax.axis_size("tensor"))
    feat, hid = gate_weight.shape
    per_owner, share, size = right_factor.shape
    blocks = left_factor.shape[2]
    fits = hid % (2 * BLK) == 0
    fits = fits and counts == (4, 4) and tokens.shape[0] == 128
    fits = fits and hid >= 4 * BLK and feat % BLK == 0
    fits = fits and size == 128 and 2 * blocks == size and per_owner % WIDE == 0
    fits = fits and left_factor.shape[0] == share and share % 16 == 0
    return (tiled_body if fits else general_body)(*args)


def solution(mesh):
    return jax.shard_map(
        body,
        mesh=mesh,
        in_specs=(
            P(("groups", "fsdp"), None),
            P("fsdp", "tensor"),
            P("fsdp", "tensor"),
            P("tensor", "fsdp"),
            P("fsdp", "tensor", None),
            P("fsdp", "tensor", None),
        ),
        out_specs=(P(("groups", "fsdp"), "tensor", None), P(("groups", "fsdp"), "tensor", None)),
        check_vma=False,
    )
```

```python
import functools
import math

import jax
import jax.numpy as jnp
from jax import lax
from jax.experimental import pallas as pl
from jax.experimental.pallas import tpu as pltpu
from jax.sharding import PartitionSpec as P

BLK = 256
LANES = 128
SMALL = pl.CostEstimate(flops=1, bytes_accessed=1, transcendentals=0)
LARGE = pl.CostEstimate(flops=10**10, bytes_accessed=10**7, transcendentals=0)
F32 = jnp.float32
BF16 = jnp.bfloat16


def gate_up_kernel(idx_ref, top_ref, bottom_ref, gate_ref, up_ref, mine_ref, other_ref):
    rows = top_ref.shape[0]
    lhs = jnp.concatenate([top_ref[...], bottom_ref[...]], axis=0)
    for slot, weight_ref in enumerate((gate_ref, up_ref)):
        product = jnp.dot(lhs, weight_ref[...], preferred_element_type=F32).astype(BF16)
        mine_ref[slot] = product[:rows]
        other_ref[slot] = product[rows:]


def gate_up(top, top_block, bottom, gate, up, column, first, width):
    rows, feat = bottom.shape
    if width % BLK or gate.shape[1] % BLK or rows % 16 or feat % 128:
        lhs = jnp.concatenate(
            [lax.dynamic_slice_in_dim(top, top_block * feat, feat, 1), bottom], axis=0
        )
        both = [
            jnp.dot(
                lhs,
                lax.dynamic_slice_in_dim(w, column + first, width, 1),
                preferred_element_type=F32,
            ).astype(BF16)
            for w in (gate, up)
        ]
        both = jnp.stack(both)
        return both[:, :rows], both[:, rows:]
    scalars = jnp.stack([top_block, lax.div(column, BLK) + first // BLK]).astype(jnp.int32)
    weight_spec = pl.BlockSpec((feat, BLK), lambda n, s: (0, s[1] + n))
    out_spec = pl.BlockSpec((2, rows, BLK), lambda n, s: (0, 0, n))
    shape = jax.ShapeDtypeStruct((2, rows, width), BF16)
    return pl.pallas_call(
        gate_up_kernel,
        grid_spec=pltpu.PrefetchScalarGridSpec(
            num_scalar_prefetch=1,
            grid=(width // BLK,),
            in_specs=[
                pl.BlockSpec((rows, feat), lambda n, s: (0, s[0])),
                pl.BlockSpec((rows, feat), lambda n, s: (0, 0)),
                weight_spec,
                weight_spec,
            ],
            out_specs=[out_spec, out_spec],
        ),
        out_shape=[shape, shape],
        compiler_params=pltpu.CompilerParams(vmem_limit_bytes=50 * 2**20),
        cost_estimate=pl.CostEstimate(
            flops=2 * 2 * rows * feat * 2 * width,
            bytes_accessed=2 * feat * 2 * width + 2 * 2 * rows * (feat + 2 * width),
            transcendentals=0,
        ),
        name="gate_up",
    )(scalars, top, bottom, gate, up)


def down_kernel(idx_ref, mine_ref, other_ref, weight_ref, *refs):
    out_ref = refs[-1]
    lhs = jnp.concatenate([mine_ref[...], other_ref[...]], axis=0)
    product = jnp.dot(lhs, weight_ref[...], preferred_element_type=F32)

    @pl.when(pl.program_id(0) == 0)
    def _():
        out_ref[...] = refs[0][...] + product if len(refs) > 1 else product

    @pl.when(pl.program_id(0) > 0)
    def _():
        out_ref[...] += product


def down_add(total, mine, other, weight, row):
    rows, width = mine.shape
    outs = weight.shape[1]
    if width % BLK or weight.shape[0] % BLK or rows % 16 or outs % 128:
        lhs = jnp.concatenate([mine, other], axis=0)
        part = lax.dynamic_slice_in_dim(weight, row, width, 0)
        product = jnp.dot(lhs, part, preferred_element_type=F32)
        return product if total is None else total + product
    scalars = jnp.reshape(lax.div(row, BLK), (1,)).astype(jnp.int32)
    hidden_spec = pl.BlockSpec((rows, BLK), lambda k, s: (0, k))
    whole = pl.BlockSpec((2 * rows, outs), lambda k, s: (0, 0))
    totals = [] if total is None else [total]
    return pl.pallas_call(
        down_kernel,
        grid_spec=pltpu.PrefetchScalarGridSpec(
            num_scalar_prefetch=1,
            grid=(width // BLK,),
            in_specs=[
                hidden_spec,
                hidden_spec,
                pl.BlockSpec((BLK, outs), lambda k, s: (s[0] + k, 0)),
            ]
            + [whole] * len(totals),
            out_specs=whole,
        ),
        out_shape=jax.ShapeDtypeStruct((2 * rows, outs), F32),
        compiler_params=pltpu.CompilerParams(vmem_limit_bytes=50 * 2**20),
        cost_estimate=pl.CostEstimate(
            flops=2 * 2 * rows * width * outs,
            bytes_accessed=2 * width * outs + 2 * 2 * rows * width + 16 * rows * outs,
            transcendentals=0,
        ),
        name="down_add",
    )(scalars, mine, other, weight, *totals)


def general_body(tokens, gate_weight, up_weight, down_weight, right_factor, left_factor):
    fsdp_count = lax.axis_size("fsdp")
    tensor_count = lax.axis_size("tensor")
    chips = fsdp_count // 2
    rows, model = tokens.shape
    feat, hid = gate_weight.shape
    part = hid // chips
    me = lax.axis_index("fsdp")
    chip, core = lax.div(me, 2), lax.rem(me, 2)
    z = lax.axis_index("tensor")

    def swap(value):
        return lax.ppermute(value, "fsdp", [(i, i ^ 1) for i in range(fsdp_count)])

    def shift(value, hops):
        perm = [(i, (i + 2 * hops) % fsdp_count) for i in range(fsdp_count)]
        return lax.ppermute(value, "fsdp", perm)

    def gather_z(value):
        if tensor_count > 4:
            return lax.all_gather(value, "tensor", axis=0, tiled=True)
        size = value.shape[0]
        whole = jnp.zeros((size * tensor_count,) + value.shape[1:], value.dtype)
        whole = lax.dynamic_update_slice_in_dim(whole, value, z * size, 0)
        for step in range(1, tensor_count):
            perm = [(i, (i + step) % tensor_count) for i in range(tensor_count)]
            got = lax.ppermute(value, "tensor", perm)
            source = lax.rem(z - step + tensor_count, tensor_count)
            whole = lax.dynamic_update_slice_in_dim(whole, got, source * size, 0)
        return whole

    def scatter_z(value):
        if tensor_count > 4:
            return lax.psum_scatter(value, "tensor", scatter_dimension=0, tiled=False)
        total = lax.dynamic_index_in_dim(value, z, 0, keepdims=False)
        for step in range(1, tensor_count):
            target_z = lax.rem(z + step, tensor_count)
            piece = lax.dynamic_index_in_dim(value, target_z, 0, keepdims=False)
            perm = [(i, (i + step) % tensor_count) for i in range(tensor_count)]
            total += lax.ppermute(piece.astype(BF16), "tensor", perm).astype(F32)
        return total

    def columns(value, start, width):
        return lax.dynamic_slice_in_dim(value, start, width, 1)

    def after(value, *others):
        return lax.optimization_barrier((value,) + others)[0]

    def pair_z(value):
        perm = [(i, i ^ 1) for i in range(tensor_count)]
        got = lax.ppermute(value, "tensor", perm)
        odd = lax.rem(z, 2) == 1
        return jnp.concatenate(
            [jnp.where(odd, got, value), jnp.where(odd, value, got)], axis=0
        )

    if part % BLK == 0 and part // BLK > 1:
        head = (part // BLK + 1) // 2 * BLK
        chunks = [(0, head), (head, part - head)]
    else:
        chunks = [(0, part)]

    half = rows // 2
    own_half = lax.dynamic_slice_in_dim(tokens, lax.rem(z, 2) * half, half, 0)

    def send_tokens(value, dt, g):
        features = lax.rem(chip - dt + g + chips, chips) * (2 * feat)
        return shift(columns(value, features, 2 * feat), -dt)

    def partial(pair, dp, first, width):
        column = lax.rem(chip + dp, chips) * part
        top, block, bottom = pair
        mine, other = gate_up(top, block, bottom, gate_weight, up_weight, column, first, width)
        return mine, swap(other)

    def send_partials(pair, got, dt):
        sums = []
        for dp in range(1, chips):
            pieces = [partial(pair, dp, *chunk) for chunk in chunks]
            for n, (mine, from_core) in enumerate(pieces):
                both = (mine.astype(F32) + from_core.astype(F32)).astype(BF16)
                got[dt, dp, n] = shift(both, dp)
                sums.append(both)
        return sums

    got, kept, gathered = {}, {}, {}
    local = swap(columns(tokens, (me ^ 1) * feat, feat))
    arrived = {dt: send_tokens(own_half, dt, 0) for dt in range(1, chips)}
    sums = send_partials((tokens, me, local), got, 0)
    if sums:
        local = after(local, *sums)
    kept[0] = partial((tokens, me, local), 0, 0, part)
    late_tokens = after(tokens, kept[0][0])
    neighbour_tokens = swap(late_tokens)
    late_half = after(own_half, *sums) if sums else own_half

    for dt in range(1, chips):
        gathered[dt, 0] = pair_z(after(arrived[dt], *sums))
        whole = gathered[dt, 0]
        top = columns(whole, core * feat, feat)
        bottom = swap(columns(whole, (1 - core) * feat, feat))
        pair = (top, jnp.int32(0), bottom)
        sums = send_partials(pair, got, dt)
        pair = (top, jnp.int32(0), after(bottom, *sums))
        kept[dt] = partial(pair, 0, 0, part)
        for g in range(1, chips):
            gathered[dt, g] = pair_z(after(send_tokens(late_half, dt, g), kept[dt][0]))

    def activate(e, first, width, n):
        terms = [lax.slice_in_dim(term, first, first + width, axis=2) for term in kept[e]]
        terms += [got[(e + dp) % chips, dp, n] for dp in range(1, chips)]
        total = sum(term.astype(F32) for term in terms)
        return (jax.nn.silu(total[0]) * total[1]).astype(BF16)

    totals = {u: None for u in range(chips)}
    for e in list(range(1, chips)) + [0]:
        values = [activate(e, *chunk, n) for n, chunk in enumerate(chunks)]
        spans = list(chunks)
        if e:
            values, spans = [jnp.concatenate(values, axis=1)], [(0, part)]
        sent = [[value] + [shift(value, d) for d in range(1, chips)] for value in values]
        for (first, width), copies in zip(spans, sent):
            for d, mine in enumerate(copies):
                u = (e - d + chips) % chips
                row = lax.rem(chip - d + chips, chips) * part + first
                totals[u] = down_add(totals[u], mine, swap(mine), down_weight, row)

    token_rows = []
    for dt in range(chips):
        if dt == 0:
            token_rows += [tokens, neighbour_tokens]
            continue
        else:
            full = jnp.zeros((rows, model), BF16)
            for g in range(chips):
                features = lax.rem(chip + g, chips) * (2 * feat)
                full = lax.dynamic_update_slice_in_dim(full, gathered[dt, g], features, 1)
        token_rows += [full, swap(full)]
    inputs = jnp.concatenate(token_rows, axis=0)
    count = inputs.shape[0]

    blocks, share, size = right_factor.shape
    ratio = tensor_count // fsdp_count
    turn = []
    for a in range(fsdp_count):
        for b in range(tensor_count):
            turn.append((a * tensor_count + b, (b // ratio) * tensor_count + a * ratio + b % ratio))
    back = [(b, a) for a, b in turn]
    right_rows = gather_z(lax.ppermute(right_factor, ("fsdp", "tensor"), turn)[None])
    right_rows = right_rows.reshape(fsdp_count, ratio, blocks, share, size)
    right_rows = right_rows.transpose(0, 2, 1, 3, 4).reshape(
        fsdp_count * blocks, ratio * share, size
    )
    left_rows = jnp.moveaxis(gather_z(jnp.moveaxis(left_factor, 1, 0)), 0, 1)

    block_input = inputs.reshape(count, fsdp_count * blocks, size)
    mixed = jnp.einsum(
        "nim,ijm->nij", block_input, right_rows, preferred_element_type=F32
    ).astype(BF16)
    student = jnp.einsum("nij,jki->njk", mixed, left_rows, preferred_element_type=F32)
    target = jnp.concatenate([totals[u] for u in range(chips)], axis=0)
    scale = 1.0 / math.sqrt(count)
    out_grad = (student * (1.0 / tensor_count) - target.reshape(student.shape)) * scale
    out_grad = out_grad.astype(BF16)
    grad_left = jnp.einsum("njk,nij->kji", out_grad, mixed, preferred_element_type=F32)
    mixed_grad = jnp.einsum(
        "njk,jki->nij", out_grad, left_rows, preferred_element_type=F32
    ).astype(BF16)
    grad_right = jnp.einsum(
        "nij,nim->ijm", mixed_grad, block_input, preferred_element_type=F32
    )
    grad_left = scatter_z(
        grad_left.reshape((tensor_count, -1) + grad_left.shape[1:])
    )
    grad_left = jnp.moveaxis(grad_left, 0, 1)
    grad_right = grad_right.reshape(fsdp_count, blocks, ratio, share, size)
    grad_right = grad_right.transpose(0, 2, 1, 3, 4).reshape(
        tensor_count, blocks, share, size
    )
    grad_right = lax.ppermute(scatter_z(grad_right), ("fsdp", "tensor"), back)
    return grad_right, grad_left


def cut_kernel(idx_ref, in_ref, out_ref):
    out_ref[...] = in_ref[...]


def cut_tokens(tokens, rows, row, column, cost=SMALL):
    block = (rows, tokens.shape[1] // 2)
    return pl.pallas_call(
        cut_kernel,
        grid_spec=pltpu.PrefetchScalarGridSpec(
            num_scalar_prefetch=1,
            grid=(1,),
            in_specs=[pl.BlockSpec(block, lambda n, s: (s[0], s[1]))],
            out_specs=pl.BlockSpec(block, lambda n, s: (0, 0)),
        ),
        out_shape=jax.ShapeDtypeStruct(block, BF16),
        cost_estimate=cost,
        name="cut_tokens",
    )(jnp.stack([row, column]).astype(jnp.int32), tokens)


def products_kernel(sets, idx_ref, *refs):
    pieces, (gate_ref, up_ref, mine_ref, other_ref) = refs[: 4 * sets], refs[4 * sets :]
    lhs = jnp.concatenate([piece[...] for piece in pieces], axis=0)
    rows = mine_ref.shape[2]
    for slot, weight_ref in enumerate((gate_ref, up_ref)):
        product = jnp.dot(lhs, weight_ref[...], preferred_element_type=F32).astype(BF16)
        for u in range(sets):
            mine_ref[u, slot] = product[2 * u * rows : (2 * u + 1) * rows]
            other_ref[u, slot] = product[(2 * u + 1) * rows : (2 * u + 2) * rows]


def products(pieces, scalars, gate, up, first, width):
    feat = gate.shape[0]
    sets = len(pieces) // 4
    half = pieces[0][0].shape[0] // 2
    start = first // BLK

    def piece_spec(row, column):
        return pl.BlockSpec((half, feat), lambda n, s: (s[row], s[column]))

    weight_spec = pl.BlockSpec(
        (feat, BLK), lambda n, s: (0, s[4] + start + n)
    )
    out_spec = pl.BlockSpec((sets, 2, 2 * half, BLK), lambda n, s: (0, 0, 0, n))
    shape = jax.ShapeDtypeStruct((sets, 2, 2 * half, width), BF16)
    return pl.pallas_call(
        functools.partial(products_kernel, sets),
        grid_spec=pltpu.PrefetchScalarGridSpec(
            num_scalar_prefetch=1,
            grid=(width // BLK,),
            in_specs=[piece_spec(row, column) for _, row, column in pieces]
            + [weight_spec, weight_spec],
            out_specs=[out_spec, out_spec],
        ),
        out_shape=[shape, shape],
        compiler_params=pltpu.CompilerParams(vmem_limit_bytes=50 * 2**20),
        cost_estimate=LARGE if sets > 1 else SMALL,
        name="gate_up_products",
    )(scalars, *[piece for piece, _, _ in pieces], gate, up)


def fill_rows(lhs, pieces):
    rows = pieces[0].shape[0]
    for place, which in enumerate((1, 3, 0, 2)):
        lhs[place * rows : (place + 1) * rows, :] = pieces[which][...]


def whole_spec(array):
    return pl.BlockSpec(array.shape, lambda n, s: (0,) * array.ndim)


def target_kernel(sign, idx_ref, mine_ref, near_ref, weight_ref, *refs):
    terms, out_ref = refs[:-1], refs[-1]
    lhs = jnp.concatenate([mine_ref[...], near_ref[...]], axis=0)
    product = jnp.dot(lhs, weight_ref[...], preferred_element_type=F32)
    out_ref[...] = sum((ref[...] for ref in terms), sign * product)


def target_part(sign, terms, mine, near, weight, chip):
    rows, width = mine.shape
    outs = weight.shape[1]
    block = pl.BlockSpec((2 * rows, BLK), lambda n, s: (0, n))
    return pl.pallas_call(
        functools.partial(target_kernel, sign),
        grid_spec=pltpu.PrefetchScalarGridSpec(
            num_scalar_prefetch=1,
            grid=(outs // BLK,),
            in_specs=[whole_spec(mine), whole_spec(near)]
            + [pl.BlockSpec((width, BLK), lambda n, s: (s[0], n))]
            + [block] * len(terms),
            out_specs=block,
        ),
        out_shape=jax.ShapeDtypeStruct((2 * rows, outs), F32),
        compiler_params=pltpu.CompilerParams(vmem_limit_bytes=50 * 2**20),
        cost_estimate=SMALL,
        name="target_part",
    )(jnp.reshape(chip, (1,)).astype(jnp.int32), mine, near, weight, *terms)


TN = (((0,), (0,)), ((), ()))
NT = (((1,), (1,)), ((), ()))
WIDE = 8


def natural(step, chip, per_chip):
    return lax.rem(chip + step // per_chip, 2) * per_chip + lax.rem(step, per_chip)


def spread_kernel(idx_ref, rows_ref, out_ref, scratch):
    groups = out_ref.shape[0]
    parts, _, size = rows_ref.shape
    blocks = size // 2
    share = blocks // parts
    fold = BLK // blocks
    begin = rows_ref.shape[1] - groups * fold // 2 * share
    scratch[...] = jnp.zeros_like(scratch)
    low = lax.broadcasted_iota(jnp.int32, (blocks, size), 1) < blocks
    for g in range(groups):
        for pair in range(fold // 2):
            row = begin + (g * (fold // 2) + pair) * share
            picked = [
                rows_ref[idx_ref[3] ^ owner, row : row + share, :] for owner in range(parts)
            ]
            turned = jnp.concatenate(picked + picked, axis=0).astype(F32).T
            for a in range(2):
                value = turned[a * blocks : (a + 1) * blocks]
                value = jnp.where(low if a == 0 else ~low, value, 0.0)
                lanes = slice(pair * size, (pair + 1) * size)
                for c in range(blocks // WIDE):
                    row = (c * fold + 2 * pair + a) * WIDE
                    scratch[row : row + WIDE, lanes] = value[c * WIDE : (c + 1) * WIDE]
        out_ref[g] = scratch[...].astype(BF16)


def spread_left(scalars, rows, groups):
    return pl.pallas_call(
        spread_kernel,
        grid_spec=pltpu.PrefetchScalarGridSpec(
            num_scalar_prefetch=1,
            grid=(1,),
            in_specs=[whole_spec(rows)],
            out_specs=pl.BlockSpec((groups, BLK, BLK), lambda n, s: (0, 0, 0)),
            scratch_shapes=[pltpu.VMEM((BLK, BLK), F32)],
        ),
        out_shape=jax.ShapeDtypeStruct((groups, BLK, BLK), BF16),
        cost_estimate=SMALL,
        name="spread_left",
    )(scalars, rows)


def student_kernel(steps, late, tensor_count, idx_ref, *refs):
    tokens, refs = refs[: 8 if late else 4], refs[8 if late else 4 :]
    rights, left_ref, targets = refs[:2], refs[2], refs[3:-3]
    mixed_ref, student_ref, spread = refs[-3:]
    step = pl.program_id(0)
    pair = natural(step, idx_ref[2], steps // 2)
    groups = left_ref.shape[0]
    size = spread.shape[2]
    pairs = spread.shape[1] // WIDE
    share = BLK // groups

    @pl.when(step == 0)
    def _():
        spread[...] = jnp.zeros_like(spread)

    def mix(pieces):
        for half, right_ref in enumerate(rights):
            for t in range(WIDE):
                value = right_ref[0, t * pairs : (t + 1) * pairs, :].astype(F32)
                spread[t, pl.ds(t, pairs, stride=WIDE), :] = value
            factor = jnp.concatenate([spread[t] for t in range(WIDE)], axis=1).astype(BF16)
            lanes = slice(half * WIDE * size, (half + 1) * WIDE * size)
            rows = jnp.concatenate([piece[:, lanes] for piece in pieces], axis=0)
            part = lax.dot_general(factor, rows, NT, preferred_element_type=F32).astype(BF16)
            start = pl.multiple_of((2 * pair + half) * share, share)
            for g in range(groups):
                mixed_ref[g, pl.ds(start, share), :] = part[g * share : (g + 1) * share]

    if late:
        pl.when(step < steps // 2)(lambda: mix(tokens[:4]))
        pl.when(step >= steps // 2)(lambda: mix(tokens[4:]))
    else:
        mix(tokens)

    @pl.when(step == steps - 1)
    def _():
        for g in range(groups):
            span = slice(g * BLK, (g + 1) * BLK)
            student = lax.dot_general(
                mixed_ref[g], left_ref[g], TN, preferred_element_type=F32
            )
            student = student * (1.0 / tensor_count)
            student_ref[:, span] = sum((-ref[:, span] for ref in targets), student)


def token_specs(half, width, steps, begin, own):
    def chunk(n, s):
        step = jnp.maximum(n - begin, 0)
        return natural(step, s[2], steps // 2)

    def near(n, s):
        return jnp.clip(n - begin, 0, steps // 2 - 1)

    def far(n, s):
        return jnp.clip(n - begin - steps // 2, 0, steps // 2 - 1)

    def specs(place):
        return [
            pl.BlockSpec((half, width), lambda n, s, p=p: (s[p % 2], place(n, s)))
            for p in range(4)
        ]

    if own:
        return specs(chunk)
    whole = pl.BlockSpec((half, width), lambda n, s: (0, far(n, s)))
    return specs(near) + [whole] * 4


def student_part(tokens, late, scalars, factors, left_diag, targets, pairs, tensor_count):
    parts, _, size = factors.shape
    half = tokens[0].shape[0] // 2
    groups = left_diag.shape[0]
    blocks = groups * BLK // pairs
    steps = blocks // (2 * WIDE)

    def right_spec(half):
        return pl.BlockSpec(
            (1, WIDE * pairs, size),
            lambda n, s: (s[3] ^ natural(n, s[2], steps // 2), half, 0),
        )

    return pl.pallas_call(
        functools.partial(student_kernel, steps, late, tensor_count),
        grid_spec=pltpu.PrefetchScalarGridSpec(
            num_scalar_prefetch=1,
            grid=(steps,),
            in_specs=token_specs(half, 2 * WIDE * size, steps, 0, not late)
            + [right_spec(0), right_spec(1), whole_spec(left_diag)]
            + [whole_spec(target) for target in targets],
            out_specs=[
                pl.BlockSpec((groups, BLK, 4 * half), lambda n, s: (0, 0, 0)),
                pl.BlockSpec((4 * half, groups * BLK), lambda n, s: (0, 0)),
            ],
            scratch_shapes=[pltpu.VMEM((WIDE, pairs * WIDE, size), F32)],
        ),
        out_shape=[
            jax.ShapeDtypeStruct((groups, BLK, 4 * half), BF16),
            jax.ShapeDtypeStruct((4 * half, groups * BLK), F32),
        ],
        compiler_params=pltpu.CompilerParams(vmem_limit_bytes=50 * 2**20),
        cost_estimate=LARGE,
        name="student_part",
    )(scalars, *tokens, factors, factors, left_diag, *targets)


def grads_kernel(groups, steps, scale, idx_ref, *refs):
    hidden, refs = refs[:4], refs[4:]
    weight_ref, rest0, rest1, mixed0, mixed1, left_ref = refs[:6]
    own, near, far = refs[6:10], refs[10:14], refs[14:18]
    out_ref, lhs, back, wide = refs[18:]
    step = pl.program_id(0)
    z = idx_ref[3]
    parts, size = out_ref.shape[0], out_ref.shape[2]
    chunks = 2 * steps
    blocks = chunks * WIDE
    per_part = blocks // parts
    share = BLK // chunks
    pairs = groups * share // WIDE
    fold = BLK // blocks

    def place(owner):
        bits = z ^ owner
        return lax.rem(bits, 2) * 2 + bits // 2

    pl.when(step == 0)(lambda: fill_rows(lhs, hidden))

    @pl.when(step < groups)
    def _():
        target = jnp.dot(lhs[...], weight_ref[...], preferred_element_type=F32)
        rest = jnp.concatenate([rest0[...], rest1[...]], axis=0)
        out_grad = ((rest - target) * scale).astype(BF16)
        mixed = jnp.concatenate([mixed0[0], mixed1[0]], axis=1)
        left = jnp.dot(mixed, out_grad, preferred_element_type=F32)
        value = lax.dot_general(
            left_ref[0], out_grad, NT, preferred_element_type=F32
        ).astype(BF16)
        row = pl.multiple_of(step * share, share)
        for c in range(chunks):
            back[c, pl.ds(row, share), :] = value[c * share : (c + 1) * share]
        low = lax.broadcasted_iota(jnp.int32, (blocks, size), 1) < blocks
        rows = blocks // parts
        for pair in range(fold // 2):
            lanes = slice(pair * size, (pair + 1) * size)
            picked = []
            for a in (2 * pair, 2 * pair + 1):
                for c in range(chunks):
                    begin = (c * fold + a) * WIDE
                    picked.append(left[begin : begin + WIDE, lanes])
            turned = jnp.concatenate(picked, axis=0).T
            both = jnp.where(low, turned[:blocks], turned[blocks:]).astype(BF16)
            begin = per_part * pairs + (step * (fold // 2) + pair) * rows
            begin = pl.multiple_of(begin, rows)
            for owner in range(parts):
                out_ref[place(owner), pl.ds(begin, rows), :] = both[
                    owner * rows : (owner + 1) * rows
                ]

    def right(later):
        pair = natural(step - groups, idx_ref[2], steps // 2)
        for half in range(2):
            chunk = 2 * pair + half
            lanes = slice(half * WIDE * size, (half + 1) * WIDE * size)
            rows = jnp.concatenate([piece[:, lanes] for piece in own + later], axis=0)
            value = jnp.dot(back[chunk], rows, preferred_element_type=F32)
            for t in range(WIDE):
                wide[t] = value[:, t * size : (t + 1) * size]
            for t in range(WIDE):
                block = chunk * WIDE + t
                begin = pl.multiple_of(lax.rem(block, per_part) * pairs, pairs)
                out_ref[place(block // per_part), pl.ds(begin, pairs), :] = wide[
                    t, pl.ds(t, pairs, stride=WIDE), :
                ].astype(BF16)

    pl.when((step >= groups) & (step < groups + steps // 2))(lambda: right(near))
    pl.when(step >= groups + steps // 2)(lambda: right(far))


def factor_grads(
    hidden, weight, rest, mixed, left_diag, own, late, scalars, parts, size, scale
):
    groups, count = left_diag.shape[0], 2 * rest[0].shape[0]
    width = hidden[0].shape[1]
    half = own[0].shape[0] // 2
    steps = own[0].shape[1] // (2 * WIDE * size)
    blocks = 2 * steps * WIDE
    pairs = groups * BLK // blocks

    def group(n):
        return jnp.minimum(n, groups - 1)

    column = pl.BlockSpec((count // 2, BLK), lambda n, s: (0, group(n)))
    slab = pl.BlockSpec((1, BLK, count // 2), lambda n, s: (group(n), 0, 0))
    out_rows = (pairs * blocks + pairs * blocks * blocks // size) // parts
    return pl.pallas_call(
        functools.partial(grads_kernel, groups, steps, scale),
        grid_spec=pltpu.PrefetchScalarGridSpec(
            num_scalar_prefetch=1,
            grid=(groups + steps,),
            in_specs=[whole_spec(piece) for piece in hidden]
            + [pl.BlockSpec((width, BLK), lambda n, s: (1 - s[2], group(n)))]
            + [column, column, slab, slab]
            + [
                pl.BlockSpec(
                    (1, BLK, BLK), lambda n, s: (group(n), 0, 0)
                )
            ]
            + token_specs(half, 2 * WIDE * size, steps, groups, True)
            + token_specs(half, 2 * WIDE * size, steps, groups, False),
            out_specs=pl.BlockSpec((parts, out_rows, size), lambda n, s: (0, 0, 0)),
            scratch_shapes=[
                pltpu.VMEM((count, width), BF16),
                pltpu.VMEM((2 * steps, groups * BLK // (2 * steps), count), BF16),
                pltpu.VMEM((WIDE, pairs * WIDE, size), F32),
            ],
        ),
        out_shape=jax.ShapeDtypeStruct((parts, out_rows, size), BF16),
        compiler_params=pltpu.CompilerParams(vmem_limit_bytes=50 * 2**20),
        cost_estimate=SMALL,
        name="factor_grads",
    )(scalars, *hidden, weight, *rest, *mixed, left_diag, *own, *late)


def tiled_body(tokens, gate_weight, up_weight, down_weight, right_factor, left_factor):
    fsdp_count = lax.axis_size("fsdp")
    tensor_count = lax.axis_size("tensor")
    rows, model = tokens.shape
    part = gate_weight.shape[1] // 2
    me, z = lax.axis_index("fsdp"), lax.axis_index("tensor")
    chip, core, odd = lax.div(me, 2), lax.rem(me, 2), lax.rem(z, 2)
    both_axes = ("fsdp", "tensor")

    def swap(value):
        return lax.ppermute(value, "fsdp", [(i, i ^ 1) for i in range(fsdp_count)])

    def across(value):
        return lax.ppermute(value, "fsdp", [(i, i ^ 2) for i in range(fsdp_count)])

    def along(value, bit):
        return lax.ppermute(value, "tensor", [(i, i ^ bit) for i in range(tensor_count)])

    def turn(value, bit):
        perm = []
        for f in range(fsdp_count):
            for t in range(tensor_count):
                perm.append((f * tensor_count + t, (t ^ bit) * tensor_count + f))
        return lax.ppermute(value, both_axes, perm)

    def after(value, *others):
        return lax.optimization_barrier((value,) + others)[0]

    def add(*terms):
        return sum(term.astype(F32) for term in terms)

    near_tokens = swap(tokens)
    first = cut_tokens(tokens, rows, jnp.int32(0), 1 - chip)
    arrived = across(first)
    turned = turn(after(right_factor, first), 0)
    base = jnp.stack([odd, 1 - odd])
    mine_block = lax.div(part, BLK) * chip
    other_block = lax.div(part, BLK) * (1 - chip)

    def scalars(block):
        return jnp.concatenate([base, jnp.stack([me, core, block])]).astype(jnp.int32)

    own_pieces = [(t, row, 2) for t in (tokens, near_tokens) for row in (0, 1)]
    mine, other = products(
        own_pieces, after(scalars(other_block), turned), gate_weight, up_weight, 0, part
    )

    pairs, blocks = left_factor.shape[0], left_factor.shape[2]
    left_rows = left_factor.reshape(pairs // 2, 2, -1, blocks).transpose(0, 2, 1, 3)
    factors = jnp.concatenate(
        [turned.reshape(-1, LANES), left_rows.reshape(-1, LANES)], axis=0
    )[None]
    more = along(after(factors, mine), 1)
    rest = cut_tokens(after(tokens, mine), rows // 2, odd, chip, LARGE)
    sums = add(mine[0], swap(other[0])).astype(BF16)
    arrived = after(arrived, more, rest, sums)
    got_early = across(sums)
    late_first = across(after(rest, sums))
    factors = jnp.concatenate([factors, more], axis=0)
    more = along(after(factors, arrived), 2)

    order = jnp.concatenate([base, jnp.stack([chip, z])]).astype(jnp.int32)
    own = [tokens, tokens, near_tokens, near_tokens]
    near_arrived = swap(arrived)
    late_pieces = [(t, row, 3) for t in (arrived, near_arrived) for row in (0, 1)]
    late_order = after(scalars(other_block), sums)
    mine, other = products(late_pieces, late_order, gate_weight, up_weight, 0, part)
    near = swap(other[0])
    mine_order = after(scalars(mine_block), mine)
    kept, other = products(
        own_pieces + late_pieces, mine_order, gate_weight, up_weight, 0, part
    )
    sums = add(mine[0], after(near, kept)).astype(BF16)
    got = across(sums)
    near_kept = swap(after(other, got_early, late_first, more, sums))

    factors = jnp.concatenate([factors, after(more, kept)], axis=0)
    def activate(u, term):
        total = add(kept[u], near_kept[u], term)
        return (jax.nn.silu(total[0]) * total[1]).astype(BF16)

    hidden1 = activate(1, got_early)
    got1 = across(hidden1)
    near1 = swap(hidden1)
    left_diag = spread_left(order, after(factors, hidden1), pairs * blocks // BLK)
    late_partner = along(after(late_first, hidden1), 1)
    mixed0, rest0 = student_part(
        [after(tokens, hidden1, sums)] + own[1:],
        False,
        order,
        factors,
        left_diag,
        [],
        pairs,
        tensor_count,
    )
    target1 = target_part(1.0, [], hidden1, after(near1, mixed0), down_weight, chip)
    hidden0 = activate(0, after(got, target1))
    got0 = across(hidden0)
    near0 = swap(hidden0)
    late_partner = after(late_partner, mixed0)
    late = [arrived, arrived, near_arrived, near_arrived]
    late += [late_first, late_partner, swap(late_first), swap(late_partner)]
    mixed1, rest1 = student_part(
        [after(arrived, hidden0)] + late[1:],
        True,
        order,
        factors,
        left_diag,
        [target1],
        pairs,
        tensor_count,
    )
    near0 = after(near0, mixed1)
    rest0 = target_part(-1.0, [rest0], hidden0, near0, down_weight, chip)
    got1, got0 = after(got1, mixed1), after(got0, rest0)
    hidden = [got0, got1, swap(got0), swap(got1)]

    grads = factor_grads(
        hidden,
        down_weight,
        (rest0, rest1),
        (mixed0, mixed1),
        left_diag,
        own,
        late,
        order,
        tensor_count,
        right_factor.shape[2],
        1.0 / math.sqrt(rows * fsdp_count),
    )
    summed = add(grads[:2], along(grads[2:], 1)).astype(BF16)
    right_shape = right_factor.shape
    cut = right_shape[0] * right_shape[1]
    grad_right = add(turn(summed[0, :cut], 0), turn(summed[1, :cut], 2))
    grad_left = add(summed[0, cut:], along(summed[1, cut:], 2))
    grad_left = grad_left.reshape(pairs // 2, -1, 2, blocks).transpose(0, 2, 1, 3)
    return grad_right.reshape(right_shape), grad_left.reshape(left_factor.shape)


def body(*args):
    tokens, gate_weight, _, _, right_factor, left_factor = args
    counts = (lax.axis_size("fsdp"), lax.axis_size("tensor"))
    feat, hid = gate_weight.shape
    per_owner, share, size = right_factor.shape
    blocks = left_factor.shape[2]
    fits = hid % (2 * BLK) == 0
    fits = fits and counts == (4, 4) and tokens.shape[0] == 128
    fits = fits and hid >= 4 * BLK and feat % BLK == 0
    fits = fits and size == 128 and 2 * blocks == size and per_owner % WIDE == 0
    fits = fits and left_factor.shape[0] == share and share % 16 == 0
    return (tiled_body if fits else general_body)(*args)


def solution(mesh):
    return jax.shard_map(
        body,
        mesh=mesh,
        in_specs=(
            P(("groups", "fsdp"), None),
            P("fsdp", "tensor"),
            P("fsdp", "tensor"),
            P("tensor", "fsdp"),
            P("fsdp", "tensor", None),
            P("fsdp", "tensor", None),
        ),
        out_specs=(P(("groups", "fsdp"), "tensor", None), P(("groups", "fsdp"), "tensor", None)),
        check_vma=False,
    )
```

```python
import functools
import math

import jax
import jax.numpy as jnp
from jax import lax
from jax.experimental import pallas as pl
from jax.experimental.pallas import tpu as pltpu
from jax.sharding import PartitionSpec as P

BLK = 256
LANES = 128
SMALL = pl.CostEstimate(flops=1, bytes_accessed=1, transcendentals=0)
LARGE = pl.CostEstimate(flops=10**10, bytes_accessed=10**7, transcendentals=0)
F32 = jnp.float32
BF16 = jnp.bfloat16


def gate_up_kernel(idx_ref, top_ref, bottom_ref, gate_ref, up_ref, mine_ref, other_ref):
    rows = top_ref.shape[0]
    lhs = jnp.concatenate([top_ref[...], bottom_ref[...]], axis=0)
    for slot, weight_ref in enumerate((gate_ref, up_ref)):
        product = jnp.dot(lhs, weight_ref[...], preferred_element_type=F32).astype(BF16)
        mine_ref[slot] = product[:rows]
        other_ref[slot] = product[rows:]


def gate_up(top, top_block, bottom, gate, up, column, first, width):
    rows, feat = bottom.shape
    if width % BLK or gate.shape[1] % BLK or rows % 16 or feat % 128:
        lhs = jnp.concatenate(
            [lax.dynamic_slice_in_dim(top, top_block * feat, feat, 1), bottom], axis=0
        )
        both = [
            jnp.dot(
                lhs,
                lax.dynamic_slice_in_dim(w, column + first, width, 1),
                preferred_element_type=F32,
            ).astype(BF16)
            for w in (gate, up)
        ]
        both = jnp.stack(both)
        return both[:, :rows], both[:, rows:]
    scalars = jnp.stack([top_block, lax.div(column, BLK) + first // BLK]).astype(jnp.int32)
    weight_spec = pl.BlockSpec((feat, BLK), lambda n, s: (0, s[1] + n))
    out_spec = pl.BlockSpec((2, rows, BLK), lambda n, s: (0, 0, n))
    shape = jax.ShapeDtypeStruct((2, rows, width), BF16)
    return pl.pallas_call(
        gate_up_kernel,
        grid_spec=pltpu.PrefetchScalarGridSpec(
            num_scalar_prefetch=1,
            grid=(width // BLK,),
            in_specs=[
                pl.BlockSpec((rows, feat), lambda n, s: (0, s[0])),
                pl.BlockSpec((rows, feat), lambda n, s: (0, 0)),
                weight_spec,
                weight_spec,
            ],
            out_specs=[out_spec, out_spec],
        ),
        out_shape=[shape, shape],
        compiler_params=pltpu.CompilerParams(vmem_limit_bytes=40 * 2**20),
        cost_estimate=pl.CostEstimate(
            flops=2 * 2 * rows * feat * 2 * width,
            bytes_accessed=2 * feat * 2 * width + 2 * 2 * rows * (feat + 2 * width),
            transcendentals=0,
        ),
        name="gate_up",
    )(scalars, top, bottom, gate, up)


def down_kernel(idx_ref, mine_ref, other_ref, weight_ref, *refs):
    out_ref = refs[-1]
    lhs = jnp.concatenate([mine_ref[...], other_ref[...]], axis=0)
    product = jnp.dot(lhs, weight_ref[...], preferred_element_type=F32)

    @pl.when(pl.program_id(0) == 0)
    def _():
        out_ref[...] = refs[0][...] + product if len(refs) > 1 else product

    @pl.when(pl.program_id(0) > 0)
    def _():
        out_ref[...] += product


def down_add(total, mine, other, weight, row):
    rows, width = mine.shape
    outs = weight.shape[1]
    if width % BLK or weight.shape[0] % BLK or rows % 16 or outs % 128:
        lhs = jnp.concatenate([mine, other], axis=0)
        part = lax.dynamic_slice_in_dim(weight, row, width, 0)
        product = jnp.dot(lhs, part, preferred_element_type=F32)
        return product if total is None else total + product
    scalars = jnp.reshape(lax.div(row, BLK), (1,)).astype(jnp.int32)
    hidden_spec = pl.BlockSpec((rows, BLK), lambda k, s: (0, k))
    whole = pl.BlockSpec((2 * rows, outs), lambda k, s: (0, 0))
    totals = [] if total is None else [total]
    return pl.pallas_call(
        down_kernel,
        grid_spec=pltpu.PrefetchScalarGridSpec(
            num_scalar_prefetch=1,
            grid=(width // BLK,),
            in_specs=[
                hidden_spec,
                hidden_spec,
                pl.BlockSpec((BLK, outs), lambda k, s: (s[0] + k, 0)),
            ]
            + [whole] * len(totals),
            out_specs=whole,
        ),
        out_shape=jax.ShapeDtypeStruct((2 * rows, outs), F32),
        compiler_params=pltpu.CompilerParams(vmem_limit_bytes=40 * 2**20),
        cost_estimate=pl.CostEstimate(
            flops=2 * 2 * rows * width * outs,
            bytes_accessed=2 * width * outs + 2 * 2 * rows * width + 16 * rows * outs,
            transcendentals=0,
        ),
        name="down_add",
    )(scalars, mine, other, weight, *totals)


def general_body(tokens, gate_weight, up_weight, down_weight, right_factor, left_factor):
    fsdp_count = lax.axis_size("fsdp")
    tensor_count = lax.axis_size("tensor")
    chips = fsdp_count // 2
    rows, model = tokens.shape
    feat, hid = gate_weight.shape
    part = hid // chips
    me = lax.axis_index("fsdp")
    chip, core = lax.div(me, 2), lax.rem(me, 2)
    z = lax.axis_index("tensor")

    def swap(value):
        return lax.ppermute(value, "fsdp", [(i, i ^ 1) for i in range(fsdp_count)])

    def shift(value, hops):
        perm = [(i, (i + 2 * hops) % fsdp_count) for i in range(fsdp_count)]
        return lax.ppermute(value, "fsdp", perm)

    def gather_z(value):
        if tensor_count > 4:
            return lax.all_gather(value, "tensor", axis=0, tiled=True)
        size = value.shape[0]
        whole = jnp.zeros((size * tensor_count,) + value.shape[1:], value.dtype)
        whole = lax.dynamic_update_slice_in_dim(whole, value, z * size, 0)
        for step in range(1, tensor_count):
            perm = [(i, (i + step) % tensor_count) for i in range(tensor_count)]
            got = lax.ppermute(value, "tensor", perm)
            source = lax.rem(z - step + tensor_count, tensor_count)
            whole = lax.dynamic_update_slice_in_dim(whole, got, source * size, 0)
        return whole

    def scatter_z(value):
        if tensor_count > 4:
            return lax.psum_scatter(value, "tensor", scatter_dimension=0, tiled=False)
        total = lax.dynamic_index_in_dim(value, z, 0, keepdims=False)
        for step in range(1, tensor_count):
            target_z = lax.rem(z + step, tensor_count)
            piece = lax.dynamic_index_in_dim(value, target_z, 0, keepdims=False)
            perm = [(i, (i + step) % tensor_count) for i in range(tensor_count)]
            total += lax.ppermute(piece.astype(BF16), "tensor", perm).astype(F32)
        return total

    def columns(value, start, width):
        return lax.dynamic_slice_in_dim(value, start, width, 1)

    def after(value, *others):
        return lax.optimization_barrier((value,) + others)[0]

    def pair_z(value):
        perm = [(i, i ^ 1) for i in range(tensor_count)]
        got = lax.ppermute(value, "tensor", perm)
        odd = lax.rem(z, 2) == 1
        return jnp.concatenate(
            [jnp.where(odd, got, value), jnp.where(odd, value, got)], axis=0
        )

    if part % BLK == 0 and part // BLK > 1:
        head = (part // BLK + 1) // 2 * BLK
        chunks = [(0, head), (head, part - head)]
    else:
        chunks = [(0, part)]

    half = rows // 2
    own_half = lax.dynamic_slice_in_dim(tokens, lax.rem(z, 2) * half, half, 0)

    def send_tokens(value, dt, g):
        features = lax.rem(chip - dt + g + chips, chips) * (2 * feat)
        return shift(columns(value, features, 2 * feat), -dt)

    def partial(pair, dp, first, width):
        column = lax.rem(chip + dp, chips) * part
        top, block, bottom = pair
        mine, other = gate_up(top, block, bottom, gate_weight, up_weight, column, first, width)
        return mine, swap(other)

    def send_partials(pair, got, dt):
        sums = []
        for dp in range(1, chips):
            pieces = [partial(pair, dp, *chunk) for chunk in chunks]
            for n, (mine, from_core) in enumerate(pieces):
                both = (mine.astype(F32) + from_core.astype(F32)).astype(BF16)
                got[dt, dp, n] = shift(both, dp)
                sums.append(both)
        return sums

    got, kept, gathered = {}, {}, {}
    local = swap(columns(tokens, (me ^ 1) * feat, feat))
    arrived = {dt: send_tokens(own_half, dt, 0) for dt in range(1, chips)}
    sums = send_partials((tokens, me, local), got, 0)
    if sums:
        local = after(local, *sums)
    kept[0] = partial((tokens, me, local), 0, 0, part)
    late_tokens = after(tokens, kept[0][0])
    neighbour_tokens = swap(late_tokens)
    late_half = after(own_half, *sums) if sums else own_half

    for dt in range(1, chips):
        gathered[dt, 0] = pair_z(after(arrived[dt], *sums))
        whole = gathered[dt, 0]
        top = columns(whole, core * feat, feat)
        bottom = swap(columns(whole, (1 - core) * feat, feat))
        pair = (top, jnp.int32(0), bottom)
        sums = send_partials(pair, got, dt)
        pair = (top, jnp.int32(0), after(bottom, *sums))
        kept[dt] = partial(pair, 0, 0, part)
        for g in range(1, chips):
            gathered[dt, g] = pair_z(after(send_tokens(late_half, dt, g), kept[dt][0]))

    def activate(e, first, width, n):
        terms = [lax.slice_in_dim(term, first, first + width, axis=2) for term in kept[e]]
        terms += [got[(e + dp) % chips, dp, n] for dp in range(1, chips)]
        total = sum(term.astype(F32) for term in terms)
        return (jax.nn.silu(total[0]) * total[1]).astype(BF16)

    totals = {u: None for u in range(chips)}
    for e in list(range(1, chips)) + [0]:
        values = [activate(e, *chunk, n) for n, chunk in enumerate(chunks)]
        spans = list(chunks)
        if e:
            values, spans = [jnp.concatenate(values, axis=1)], [(0, part)]
        sent = [[value] + [shift(value, d) for d in range(1, chips)] for value in values]
        for (first, width), copies in zip(spans, sent):
            for d, mine in enumerate(copies):
                u = (e - d + chips) % chips
                row = lax.rem(chip - d + chips, chips) * part + first
                totals[u] = down_add(totals[u], mine, swap(mine), down_weight, row)

    token_rows = []
    for dt in range(chips):
        if dt == 0:
            token_rows += [tokens, neighbour_tokens]
            continue
        else:
            full = jnp.zeros((rows, model), BF16)
            for g in range(chips):
                features = lax.rem(chip + g, chips) * (2 * feat)
                full = lax.dynamic_update_slice_in_dim(full, gathered[dt, g], features, 1)
        token_rows += [full, swap(full)]
    inputs = jnp.concatenate(token_rows, axis=0)
    count = inputs.shape[0]

    blocks, share, size = right_factor.shape
    ratio = tensor_count // fsdp_count
    turn = []
    for a in range(fsdp_count):
        for b in range(tensor_count):
            turn.append((a * tensor_count + b, (b // ratio) * tensor_count + a * ratio + b % ratio))
    back = [(b, a) for a, b in turn]
    right_rows = gather_z(lax.ppermute(right_factor, ("fsdp", "tensor"), turn)[None])
    right_rows = right_rows.reshape(fsdp_count, ratio, blocks, share, size)
    right_rows = right_rows.transpose(0, 2, 1, 3, 4).reshape(
        fsdp_count * blocks, ratio * share, size
    )
    left_rows = jnp.moveaxis(gather_z(jnp.moveaxis(left_factor, 1, 0)), 0, 1)

    block_input = inputs.reshape(count, fsdp_count * blocks, size)
    mixed = jnp.einsum(
        "nim,ijm->nij", block_input, right_rows, preferred_element_type=F32
    ).astype(BF16)
    student = jnp.einsum("nij,jki->njk", mixed, left_rows, preferred_element_type=F32)
    target = jnp.concatenate([totals[u] for u in range(chips)], axis=0)
    scale = 1.0 / math.sqrt(count)
    out_grad = (student * (1.0 / tensor_count) - target.reshape(student.shape)) * scale
    out_grad = out_grad.astype(BF16)
    grad_left = jnp.einsum("njk,nij->kji", out_grad, mixed, preferred_element_type=F32)
    mixed_grad = jnp.einsum(
        "njk,jki->nij", out_grad, left_rows, preferred_element_type=F32
    ).astype(BF16)
    grad_right = jnp.einsum(
        "nij,nim->ijm", mixed_grad, block_input, preferred_element_type=F32
    )
    grad_left = scatter_z(
        grad_left.reshape((tensor_count, -1) + grad_left.shape[1:])
    )
    grad_left = jnp.moveaxis(grad_left, 0, 1)
    grad_right = grad_right.reshape(fsdp_count, blocks, ratio, share, size)
    grad_right = grad_right.transpose(0, 2, 1, 3, 4).reshape(
        tensor_count, blocks, share, size
    )
    grad_right = lax.ppermute(scatter_z(grad_right), ("fsdp", "tensor"), back)
    return grad_right, grad_left


def cut_kernel(idx_ref, in_ref, out_ref):
    out_ref[...] = in_ref[...]


def cut_tokens(tokens, rows, row, column, cost=SMALL):
    block = (rows, tokens.shape[1] // 2)
    return pl.pallas_call(
        cut_kernel,
        grid_spec=pltpu.PrefetchScalarGridSpec(
            num_scalar_prefetch=1,
            grid=(1,),
            in_specs=[pl.BlockSpec(block, lambda n, s: (s[0], s[1]))],
            out_specs=pl.BlockSpec(block, lambda n, s: (0, 0)),
        ),
        out_shape=jax.ShapeDtypeStruct(block, BF16),
        cost_estimate=cost,
        name="cut_tokens",
    )(jnp.stack([row, column]).astype(jnp.int32), tokens)


def products_kernel(sets, idx_ref, *refs):
    pieces, (gate_ref, up_ref, mine_ref, other_ref) = refs[: 4 * sets], refs[4 * sets :]
    lhs = jnp.concatenate([piece[...] for piece in pieces], axis=0)
    rows = mine_ref.shape[2]
    for slot, weight_ref in enumerate((gate_ref, up_ref)):
        product = jnp.dot(lhs, weight_ref[...], preferred_element_type=F32).astype(BF16)
        for u in range(sets):
            mine_ref[u, slot] = product[2 * u * rows : (2 * u + 1) * rows]
            other_ref[u, slot] = product[(2 * u + 1) * rows : (2 * u + 2) * rows]


def products(pieces, scalars, gate, up, first, width):
    feat = gate.shape[0]
    sets = len(pieces) // 4
    half = pieces[0][0].shape[0] // 2
    start = first // BLK

    def piece_spec(row, column):
        return pl.BlockSpec((half, feat), lambda n, s: (s[row], s[column]))

    weight_spec = pl.BlockSpec(
        (feat, BLK), lambda n, s: (0, s[4] + start + n)
    )
    out_spec = pl.BlockSpec((sets, 2, 2 * half, BLK), lambda n, s: (0, 0, 0, n))
    shape = jax.ShapeDtypeStruct((sets, 2, 2 * half, width), BF16)
    return pl.pallas_call(
        functools.partial(products_kernel, sets),
        grid_spec=pltpu.PrefetchScalarGridSpec(
            num_scalar_prefetch=1,
            grid=(width // BLK,),
            in_specs=[piece_spec(row, column) for _, row, column in pieces]
            + [weight_spec, weight_spec],
            out_specs=[out_spec, out_spec],
        ),
        out_shape=[shape, shape],
        compiler_params=pltpu.CompilerParams(vmem_limit_bytes=40 * 2**20),
        cost_estimate=LARGE if sets > 1 else SMALL,
        name="gate_up_products",
    )(scalars, *[piece for piece, _, _ in pieces], gate, up)


def fill_rows(lhs, pieces):
    rows = pieces[0].shape[0]
    for place, which in enumerate((1, 3, 0, 2)):
        lhs[place * rows : (place + 1) * rows, :] = pieces[which][...]


def whole_spec(array):
    return pl.BlockSpec(array.shape, lambda n, s: (0,) * array.ndim)


def target_kernel(sign, idx_ref, mine_ref, near_ref, weight_ref, *refs):
    terms, out_ref = refs[:-1], refs[-1]
    lhs = jnp.concatenate([mine_ref[...], near_ref[...]], axis=0)
    product = jnp.dot(lhs, weight_ref[...], preferred_element_type=F32)
    out_ref[...] = sum((ref[...] for ref in terms), sign * product)


def target_part(sign, terms, mine, near, weight, chip):
    rows, width = mine.shape
    outs = weight.shape[1]
    block = pl.BlockSpec((2 * rows, BLK), lambda n, s: (0, n))
    return pl.pallas_call(
        functools.partial(target_kernel, sign),
        grid_spec=pltpu.PrefetchScalarGridSpec(
            num_scalar_prefetch=1,
            grid=(outs // BLK,),
            in_specs=[whole_spec(mine), whole_spec(near)]
            + [pl.BlockSpec((width, BLK), lambda n, s: (s[0], n))]
            + [block] * len(terms),
            out_specs=block,
        ),
        out_shape=jax.ShapeDtypeStruct((2 * rows, outs), F32),
        compiler_params=pltpu.CompilerParams(vmem_limit_bytes=40 * 2**20),
        cost_estimate=SMALL,
        name="target_part",
    )(jnp.reshape(chip, (1,)).astype(jnp.int32), mine, near, weight, *terms)


TN = (((0,), (0,)), ((), ()))
NT = (((1,), (1,)), ((), ()))
WIDE = 8


def natural(step, chip, per_chip):
    return lax.rem(chip + step // per_chip, 2) * per_chip + lax.rem(step, per_chip)


def spread_kernel(idx_ref, rows_ref, out_ref, scratch):
    groups = out_ref.shape[0]
    parts, _, size = rows_ref.shape
    blocks = size // 2
    share = blocks // parts
    fold = BLK // blocks
    begin = rows_ref.shape[1] - groups * fold // 2 * share
    scratch[...] = jnp.zeros_like(scratch)
    low = lax.broadcasted_iota(jnp.int32, (blocks, size), 1) < blocks
    for g in range(groups):
        for pair in range(fold // 2):
            row = begin + (g * (fold // 2) + pair) * share
            picked = [
                rows_ref[idx_ref[3] ^ owner, row : row + share, :] for owner in range(parts)
            ]
            turned = jnp.concatenate(picked + picked, axis=0).astype(F32).T
            for a in range(2):
                value = turned[a * blocks : (a + 1) * blocks]
                value = jnp.where(low if a == 0 else ~low, value, 0.0)
                lanes = slice(pair * size, (pair + 1) * size)
                for c in range(blocks // WIDE):
                    row = (c * fold + 2 * pair + a) * WIDE
                    scratch[row : row + WIDE, lanes] = value[c * WIDE : (c + 1) * WIDE]
        out_ref[g] = scratch[...].astype(BF16)


def spread_left(scalars, rows, groups):
    return pl.pallas_call(
        spread_kernel,
        grid_spec=pltpu.PrefetchScalarGridSpec(
            num_scalar_prefetch=1,
            grid=(1,),
            in_specs=[whole_spec(rows)],
            out_specs=pl.BlockSpec((groups, BLK, BLK), lambda n, s: (0, 0, 0)),
            scratch_shapes=[pltpu.VMEM((BLK, BLK), F32)],
        ),
        out_shape=jax.ShapeDtypeStruct((groups, BLK, BLK), BF16),
        cost_estimate=SMALL,
        name="spread_left",
    )(scalars, rows)


def student_kernel(steps, late, tensor_count, idx_ref, *refs):
    tokens, refs = refs[: 8 if late else 4], refs[8 if late else 4 :]
    rights, left_ref, targets = refs[:2], refs[2], refs[3:-3]
    mixed_ref, student_ref, spread = refs[-3:]
    step = pl.program_id(0)
    pair = natural(step, idx_ref[2], steps // 2)
    groups = left_ref.shape[0]
    size = spread.shape[2]
    pairs = spread.shape[1] // WIDE
    share = BLK // groups

    @pl.when(step == 0)
    def _():
        spread[...] = jnp.zeros_like(spread)

    def mix(pieces):
        for half, right_ref in enumerate(rights):
            for t in range(WIDE):
                value = right_ref[0, t * pairs : (t + 1) * pairs, :].astype(F32)
                spread[t, pl.ds(t, pairs, stride=WIDE), :] = value
            factor = jnp.concatenate([spread[t] for t in range(WIDE)], axis=1).astype(BF16)
            lanes = slice(half * WIDE * size, (half + 1) * WIDE * size)
            rows = jnp.concatenate([piece[:, lanes] for piece in pieces], axis=0)
            part = lax.dot_general(factor, rows, NT, preferred_element_type=F32).astype(BF16)
            start = pl.multiple_of((2 * pair + half) * share, share)
            for g in range(groups):
                mixed_ref[g, pl.ds(start, share), :] = part[g * share : (g + 1) * share]

    if late:
        pl.when(step < steps // 2)(lambda: mix(tokens[:4]))
        pl.when(step >= steps // 2)(lambda: mix(tokens[4:]))
    else:
        mix(tokens)

    @pl.when(step == steps - 1)
    def _():
        for g in range(groups):
            span = slice(g * BLK, (g + 1) * BLK)
            student = lax.dot_general(
                mixed_ref[g], left_ref[g], TN, preferred_element_type=F32
            )
            student = student * (1.0 / tensor_count)
            student_ref[:, span] = sum((-ref[:, span] for ref in targets), student)


def token_specs(half, width, steps, begin, own):
    def chunk(n, s):
        step = jnp.maximum(n - begin, 0)
        return natural(step, s[2], steps // 2)

    def near(n, s):
        return jnp.clip(n - begin, 0, steps // 2 - 1)

    def far(n, s):
        return jnp.clip(n - begin - steps // 2, 0, steps // 2 - 1)

    def specs(place):
        return [
            pl.BlockSpec((half, width), lambda n, s, p=p: (s[p % 2], place(n, s)))
            for p in range(4)
        ]

    if own:
        return specs(chunk)
    whole = pl.BlockSpec((half, width), lambda n, s: (0, far(n, s)))
    return specs(near) + [whole] * 4


def student_part(tokens, late, scalars, factors, left_diag, targets, pairs, tensor_count):
    parts, _, size = factors.shape
    half = tokens[0].shape[0] // 2
    groups = left_diag.shape[0]
    blocks = groups * BLK // pairs
    steps = blocks // (2 * WIDE)

    def right_spec(half):
        return pl.BlockSpec(
            (1, WIDE * pairs, size),
            lambda n, s: (s[3] ^ natural(n, s[2], steps // 2), half, 0),
        )

    return pl.pallas_call(
        functools.partial(student_kernel, steps, late, tensor_count),
        grid_spec=pltpu.PrefetchScalarGridSpec(
            num_scalar_prefetch=1,
            grid=(steps,),
            in_specs=token_specs(half, 2 * WIDE * size, steps, 0, not late)
            + [right_spec(0), right_spec(1), whole_spec(left_diag)]
            + [whole_spec(target) for target in targets],
            out_specs=[
                pl.BlockSpec((groups, BLK, 4 * half), lambda n, s: (0, 0, 0)),
                pl.BlockSpec((4 * half, groups * BLK), lambda n, s: (0, 0)),
            ],
            scratch_shapes=[pltpu.VMEM((WIDE, pairs * WIDE, size), F32)],
        ),
        out_shape=[
            jax.ShapeDtypeStruct((groups, BLK, 4 * half), BF16),
            jax.ShapeDtypeStruct((4 * half, groups * BLK), F32),
        ],
        compiler_params=pltpu.CompilerParams(vmem_limit_bytes=40 * 2**20),
        cost_estimate=LARGE,
        name="student_part",
    )(scalars, *tokens, factors, factors, left_diag, *targets)


def grads_kernel(groups, steps, scale, idx_ref, *refs):
    hidden, refs = refs[:4], refs[4:]
    weight_ref, rest0, rest1, mixed0, mixed1, left_ref = refs[:6]
    own, near, far = refs[6:10], refs[10:14], refs[14:18]
    out_ref, lhs, back, wide = refs[18:]
    step = pl.program_id(0)
    z = idx_ref[3]
    parts, size = out_ref.shape[0], out_ref.shape[2]
    chunks = 2 * steps
    blocks = chunks * WIDE
    per_part = blocks // parts
    share = BLK // chunks
    pairs = groups * share // WIDE
    fold = BLK // blocks

    def place(owner):
        bits = z ^ owner
        return lax.rem(bits, 2) * 2 + bits // 2

    pl.when(step == 0)(lambda: fill_rows(lhs, hidden))

    @pl.when(step < groups)
    def _():
        target = jnp.dot(lhs[...], weight_ref[...], preferred_element_type=F32)
        rest = jnp.concatenate([rest0[...], rest1[...]], axis=0)
        out_grad = ((rest - target) * scale).astype(BF16)
        mixed = jnp.concatenate([mixed0[0], mixed1[0]], axis=1)
        left = jnp.dot(mixed, out_grad, preferred_element_type=F32)
        value = lax.dot_general(
            left_ref[0], out_grad, NT, preferred_element_type=F32
        ).astype(BF16)
        row = pl.multiple_of(step * share, share)
        for c in range(chunks):
            back[c, pl.ds(row, share), :] = value[c * share : (c + 1) * share]
        low = lax.broadcasted_iota(jnp.int32, (blocks, size), 1) < blocks
        rows = blocks // parts
        for pair in range(fold // 2):
            lanes = slice(pair * size, (pair + 1) * size)
            picked = []
            for a in (2 * pair, 2 * pair + 1):
                for c in range(chunks):
                    begin = (c * fold + a) * WIDE
                    picked.append(left[begin : begin + WIDE, lanes])
            turned = jnp.concatenate(picked, axis=0).T
            both = jnp.where(low, turned[:blocks], turned[blocks:]).astype(BF16)
            begin = per_part * pairs + (step * (fold // 2) + pair) * rows
            begin = pl.multiple_of(begin, rows)
            for owner in range(parts):
                out_ref[place(owner), pl.ds(begin, rows), :] = both[
                    owner * rows : (owner + 1) * rows
                ]

    def right(later):
        pair = natural(step - groups, idx_ref[2], steps // 2)
        for half in range(2):
            chunk = 2 * pair + half
            lanes = slice(half * WIDE * size, (half + 1) * WIDE * size)
            rows = jnp.concatenate([piece[:, lanes] for piece in own + later], axis=0)
            value = jnp.dot(back[chunk], rows, preferred_element_type=F32)
            for t in range(WIDE):
                wide[t] = value[:, t * size : (t + 1) * size]
            for t in range(WIDE):
                block = chunk * WIDE + t
                begin = pl.multiple_of(lax.rem(block, per_part) * pairs, pairs)
                out_ref[place(block // per_part), pl.ds(begin, pairs), :] = wide[
                    t, pl.ds(t, pairs, stride=WIDE), :
                ].astype(BF16)

    pl.when((step >= groups) & (step < groups + steps // 2))(lambda: right(near))
    pl.when(step >= groups + steps // 2)(lambda: right(far))


def factor_grads(
    hidden, weight, rest, mixed, left_diag, own, late, scalars, parts, size, scale
):
    groups, count = left_diag.shape[0], 2 * rest[0].shape[0]
    width = hidden[0].shape[1]
    half = own[0].shape[0] // 2
    steps = own[0].shape[1] // (2 * WIDE * size)
    blocks = 2 * steps * WIDE
    pairs = groups * BLK // blocks

    def group(n):
        return jnp.minimum(n, groups - 1)

    column = pl.BlockSpec((count // 2, BLK), lambda n, s: (0, group(n)))
    slab = pl.BlockSpec((1, BLK, count // 2), lambda n, s: (group(n), 0, 0))
    out_rows = (pairs * blocks + pairs * blocks * blocks // size) // parts
    return pl.pallas_call(
        functools.partial(grads_kernel, groups, steps, scale),
        grid_spec=pltpu.PrefetchScalarGridSpec(
            num_scalar_prefetch=1,
            grid=(groups + steps,),
            in_specs=[whole_spec(piece) for piece in hidden]
            + [pl.BlockSpec((width, BLK), lambda n, s: (1 - s[2], group(n)))]
            + [column, column, slab, slab]
            + [
                pl.BlockSpec(
                    (1, BLK, BLK), lambda n, s: (group(n), 0, 0)
                )
            ]
            + token_specs(half, 2 * WIDE * size, steps, groups, True)
            + token_specs(half, 2 * WIDE * size, steps, groups, False),
            out_specs=pl.BlockSpec((parts, out_rows, size), lambda n, s: (0, 0, 0)),
            scratch_shapes=[
                pltpu.VMEM((count, width), BF16),
                pltpu.VMEM((2 * steps, groups * BLK // (2 * steps), count), BF16),
                pltpu.VMEM((WIDE, pairs * WIDE, size), F32),
            ],
        ),
        out_shape=jax.ShapeDtypeStruct((parts, out_rows, size), BF16),
        compiler_params=pltpu.CompilerParams(vmem_limit_bytes=40 * 2**20),
        cost_estimate=SMALL,
        name="factor_grads",
    )(scalars, *hidden, weight, *rest, *mixed, left_diag, *own, *late)


def tiled_body(tokens, gate_weight, up_weight, down_weight, right_factor, left_factor):
    fsdp_count = lax.axis_size("fsdp")
    tensor_count = lax.axis_size("tensor")
    rows, model = tokens.shape
    part = gate_weight.shape[1] // 2
    me, z = lax.axis_index("fsdp"), lax.axis_index("tensor")
    chip, core, odd = lax.div(me, 2), lax.rem(me, 2), lax.rem(z, 2)
    both_axes = ("fsdp", "tensor")

    def swap(value):
        return lax.ppermute(value, "fsdp", [(i, i ^ 1) for i in range(fsdp_count)])

    def across(value):
        return lax.ppermute(value, "fsdp", [(i, i ^ 2) for i in range(fsdp_count)])

    def along(value, bit):
        return lax.ppermute(value, "tensor", [(i, i ^ bit) for i in range(tensor_count)])

    def turn(value, bit):
        perm = []
        for f in range(fsdp_count):
            for t in range(tensor_count):
                perm.append((f * tensor_count + t, (t ^ bit) * tensor_count + f))
        return lax.ppermute(value, both_axes, perm)

    def after(value, *others):
        return lax.optimization_barrier((value,) + others)[0]

    def add(*terms):
        return sum(term.astype(F32) for term in terms)

    near_tokens = swap(tokens)
    first = cut_tokens(tokens, rows, jnp.int32(0), 1 - chip)
    arrived = across(first)
    base = jnp.stack([odd, 1 - odd])
    mine_block = lax.div(part, BLK) * chip
    other_block = lax.div(part, BLK) * (1 - chip)

    def scalars(block):
        return jnp.concatenate([base, jnp.stack([me, core, block])]).astype(jnp.int32)

    own_pieces = [(t, row, 2) for t in (tokens, near_tokens) for row in (0, 1)]
    mine, other = products(
        own_pieces, after(scalars(other_block), first), gate_weight, up_weight, 0, part
    )

    pairs, blocks = left_factor.shape[0], left_factor.shape[2]
    left_rows = left_factor.reshape(pairs // 2, 2, -1, blocks).transpose(0, 2, 1, 3)
    turned = turn(after(right_factor, mine), 0)
    rest = cut_tokens(after(tokens, mine), rows // 2, odd, chip, LARGE)
    factors = jnp.concatenate(
        [after(turned, rest).reshape(-1, LANES), left_rows.reshape(-1, LANES)], axis=0
    )[None]
    more = along(factors, 1)
    sums = add(mine[0], swap(other[0])).astype(BF16)
    arrived = after(arrived, more, rest, sums)
    got_early = across(sums)
    late_first = across(after(rest, sums))
    factors = jnp.concatenate([factors, more], axis=0)
    more = along(after(factors, arrived), 2)

    order = jnp.concatenate([base, jnp.stack([chip, z])]).astype(jnp.int32)
    own = [tokens, tokens, near_tokens, near_tokens]
    near_arrived = swap(arrived)
    late_pieces = [(t, row, 3) for t in (arrived, near_arrived) for row in (0, 1)]
    late_order = after(scalars(other_block), sums)
    mine, other = products(late_pieces, late_order, gate_weight, up_weight, 0, part)
    near = swap(other[0])
    mine_order = after(scalars(mine_block), mine)
    kept, other = products(
        own_pieces + late_pieces, mine_order, gate_weight, up_weight, 0, part
    )
    sums = add(mine[0], after(near, kept)).astype(BF16)
    got = across(sums)
    near_kept = swap(after(other, got_early, late_first, more, sums))

    factors = jnp.concatenate([factors, after(more, kept)], axis=0)
    def activate(u, term):
        total = add(kept[u], near_kept[u], term)
        return (jax.nn.silu(total[0]) * total[1]).astype(BF16)

    hidden1 = activate(1, got_early)
    got1 = across(hidden1)
    near1 = swap(hidden1)
    left_diag = spread_left(order, after(factors, hidden1), pairs * blocks // BLK)
    late_partner = along(after(late_first, hidden1), 1)
    mixed0, rest0 = student_part(
        [after(tokens, hidden1, sums)] + own[1:],
        False,
        order,
        factors,
        left_diag,
        [],
        pairs,
        tensor_count,
    )
    target1 = target_part(1.0, [], hidden1, after(near1, mixed0), down_weight, chip)
    hidden0 = activate(0, after(got, target1))
    got0 = across(hidden0)
    near0 = swap(hidden0)
    late_partner = after(late_partner, mixed0)
    late = [arrived, arrived, near_arrived, near_arrived]
    late += [late_first, late_partner, swap(late_first), swap(late_partner)]
    mixed1, rest1 = student_part(
        [after(arrived, hidden0)] + late[1:],
        True,
        order,
        factors,
        left_diag,
        [target1],
        pairs,
        tensor_count,
    )
    near0 = after(near0, mixed1)
    rest0 = target_part(-1.0, [rest0], hidden0, near0, down_weight, chip)
    got1, got0 = after(got1, mixed1), after(got0, rest0)
    hidden = [got0, got1, swap(got0), swap(got1)]

    grads = factor_grads(
        hidden,
        down_weight,
        (rest0, rest1),
        (mixed0, mixed1),
        left_diag,
        own,
        late,
        order,
        tensor_count,
        right_factor.shape[2],
        1.0 / math.sqrt(rows * fsdp_count),
    )
    summed = add(grads[:2], along(grads[2:], 1)).astype(BF16)
    right_shape = right_factor.shape
    cut = right_shape[0] * right_shape[1]
    grad_right = add(turn(summed[0, :cut], 0), turn(summed[1, :cut], 2))
    grad_left = add(summed[0, cut:], along(summed[1, cut:], 2))
    grad_left = grad_left.reshape(pairs // 2, -1, 2, blocks).transpose(0, 2, 1, 3)
    return grad_right.reshape(right_shape), grad_left.reshape(left_factor.shape)


def body(*args):
    tokens, gate_weight, _, _, right_factor, left_factor = args
    counts = (lax.axis_size("fsdp"), lax.axis_size("tensor"))
    feat, hid = gate_weight.shape
    per_owner, share, size = right_factor.shape
    blocks = left_factor.shape[2]
    fits = hid % (2 * BLK) == 0
    fits = fits and counts == (4, 4) and tokens.shape[0] == 128
    fits = fits and hid >= 4 * BLK and feat % BLK == 0
    fits = fits and size == 128 and 2 * blocks == size and per_owner % WIDE == 0
    fits = fits and left_factor.shape[0] == share and share % 16 == 0
    return (tiled_body if fits else general_body)(*args)


def solution(mesh):
    return jax.shard_map(
        body,
        mesh=mesh,
        in_specs=(
            P(("groups", "fsdp"), None),
            P("fsdp", "tensor"),
            P("fsdp", "tensor"),
            P("tensor", "fsdp"),
            P("fsdp", "tensor", None),
            P("fsdp", "tensor", None),
        ),
        out_specs=(P(("groups", "fsdp"), "tensor", None), P(("groups", "fsdp"), "tensor", None)),
        check_vma=False,
    )
```

```python
import functools
import math

import jax
import jax.numpy as jnp
from jax import lax
from jax.experimental import pallas as pl
from jax.experimental.pallas import tpu as pltpu
from jax.sharding import PartitionSpec as P

BLK = 256
LANES = 128
SMALL = pl.CostEstimate(flops=1, bytes_accessed=1, transcendentals=0)
LARGE = pl.CostEstimate(flops=10**10, bytes_accessed=10**7, transcendentals=0)
F32 = jnp.float32
BF16 = jnp.bfloat16


def gate_up_kernel(idx_ref, top_ref, bottom_ref, gate_ref, up_ref, mine_ref, other_ref):
    rows = top_ref.shape[0]
    lhs = jnp.concatenate([top_ref[...], bottom_ref[...]], axis=0)
    for slot, weight_ref in enumerate((gate_ref, up_ref)):
        product = jnp.dot(lhs, weight_ref[...], preferred_element_type=F32).astype(BF16)
        mine_ref[slot] = product[:rows]
        other_ref[slot] = product[rows:]


def gate_up(top, top_block, bottom, gate, up, column, first, width):
    rows, feat = bottom.shape
    if width % BLK or gate.shape[1] % BLK or rows % 16 or feat % 128:
        lhs = jnp.concatenate(
            [lax.dynamic_slice_in_dim(top, top_block * feat, feat, 1), bottom], axis=0
        )
        both = [
            jnp.dot(
                lhs,
                lax.dynamic_slice_in_dim(w, column + first, width, 1),
                preferred_element_type=F32,
            ).astype(BF16)
            for w in (gate, up)
        ]
        both = jnp.stack(both)
        return both[:, :rows], both[:, rows:]
    scalars = jnp.stack([top_block, lax.div(column, BLK) + first // BLK]).astype(jnp.int32)
    weight_spec = pl.BlockSpec((feat, BLK), lambda n, s: (0, s[1] + n))
    out_spec = pl.BlockSpec((2, rows, BLK), lambda n, s: (0, 0, n))
    shape = jax.ShapeDtypeStruct((2, rows, width), BF16)
    return pl.pallas_call(
        gate_up_kernel,
        grid_spec=pltpu.PrefetchScalarGridSpec(
            num_scalar_prefetch=1,
            grid=(width // BLK,),
            in_specs=[
                pl.BlockSpec((rows, feat), lambda n, s: (0, s[0])),
                pl.BlockSpec((rows, feat), lambda n, s: (0, 0)),
                weight_spec,
                weight_spec,
            ],
            out_specs=[out_spec, out_spec],
        ),
        out_shape=[shape, shape],
        compiler_params=pltpu.CompilerParams(vmem_limit_bytes=40 * 2**20),
        cost_estimate=pl.CostEstimate(
            flops=2 * 2 * rows * feat * 2 * width,
            bytes_accessed=2 * feat * 2 * width + 2 * 2 * rows * (feat + 2 * width),
            transcendentals=0,
        ),
        name="gate_up",
    )(scalars, top, bottom, gate, up)


def down_kernel(idx_ref, mine_ref, other_ref, weight_ref, *refs):
    out_ref = refs[-1]
    lhs = jnp.concatenate([mine_ref[...], other_ref[...]], axis=0)
    product = jnp.dot(lhs, weight_ref[...], preferred_element_type=F32)

    @pl.when(pl.program_id(0) == 0)
    def _():
        out_ref[...] = refs[0][...] + product if len(refs) > 1 else product

    @pl.when(pl.program_id(0) > 0)
    def _():
        out_ref[...] += product


def down_add(total, mine, other, weight, row):
    rows, width = mine.shape
    outs = weight.shape[1]
    if width % BLK or weight.shape[0] % BLK or rows % 16 or outs % 128:
        lhs = jnp.concatenate([mine, other], axis=0)
        part = lax.dynamic_slice_in_dim(weight, row, width, 0)
        product = jnp.dot(lhs, part, preferred_element_type=F32)
        return product if total is None else total + product
    scalars = jnp.reshape(lax.div(row, BLK), (1,)).astype(jnp.int32)
    hidden_spec = pl.BlockSpec((rows, BLK), lambda k, s: (0, k))
    whole = pl.BlockSpec((2 * rows, outs), lambda k, s: (0, 0))
    totals = [] if total is None else [total]
    return pl.pallas_call(
        down_kernel,
        grid_spec=pltpu.PrefetchScalarGridSpec(
            num_scalar_prefetch=1,
            grid=(width // BLK,),
            in_specs=[
                hidden_spec,
                hidden_spec,
                pl.BlockSpec((BLK, outs), lambda k, s: (s[0] + k, 0)),
            ]
            + [whole] * len(totals),
            out_specs=whole,
        ),
        out_shape=jax.ShapeDtypeStruct((2 * rows, outs), F32),
        compiler_params=pltpu.CompilerParams(vmem_limit_bytes=40 * 2**20),
        cost_estimate=pl.CostEstimate(
            flops=2 * 2 * rows * width * outs,
            bytes_accessed=2 * width * outs + 2 * 2 * rows * width + 16 * rows * outs,
            transcendentals=0,
        ),
        name="down_add",
    )(scalars, mine, other, weight, *totals)


def general_body(tokens, gate_weight, up_weight, down_weight, right_factor, left_factor):
    fsdp_count = lax.axis_size("fsdp")
    tensor_count = lax.axis_size("tensor")
    chips = fsdp_count // 2
    rows, model = tokens.shape
    feat, hid = gate_weight.shape
    part = hid // chips
    me = lax.axis_index("fsdp")
    chip, core = lax.div(me, 2), lax.rem(me, 2)
    z = lax.axis_index("tensor")

    def swap(value):
        return lax.ppermute(value, "fsdp", [(i, i ^ 1) for i in range(fsdp_count)])

    def shift(value, hops):
        perm = [(i, (i + 2 * hops) % fsdp_count) for i in range(fsdp_count)]
        return lax.ppermute(value, "fsdp", perm)

    def gather_z(value):
        if tensor_count > 4:
            return lax.all_gather(value, "tensor", axis=0, tiled=True)
        size = value.shape[0]
        whole = jnp.zeros((size * tensor_count,) + value.shape[1:], value.dtype)
        whole = lax.dynamic_update_slice_in_dim(whole, value, z * size, 0)
        for step in range(1, tensor_count):
            perm = [(i, (i + step) % tensor_count) for i in range(tensor_count)]
            got = lax.ppermute(value, "tensor", perm)
            source = lax.rem(z - step + tensor_count, tensor_count)
            whole = lax.dynamic_update_slice_in_dim(whole, got, source * size, 0)
        return whole

    def scatter_z(value):
        if tensor_count > 4:
            return lax.psum_scatter(value, "tensor", scatter_dimension=0, tiled=False)
        total = lax.dynamic_index_in_dim(value, z, 0, keepdims=False)
        for step in range(1, tensor_count):
            target_z = lax.rem(z + step, tensor_count)
            piece = lax.dynamic_index_in_dim(value, target_z, 0, keepdims=False)
            perm = [(i, (i + step) % tensor_count) for i in range(tensor_count)]
            total += lax.ppermute(piece.astype(BF16), "tensor", perm).astype(F32)
        return total

    def columns(value, start, width):
        return lax.dynamic_slice_in_dim(value, start, width, 1)

    def after(value, *others):
        return lax.optimization_barrier((value,) + others)[0]

    def pair_z(value):
        perm = [(i, i ^ 1) for i in range(tensor_count)]
        got = lax.ppermute(value, "tensor", perm)
        odd = lax.rem(z, 2) == 1
        return jnp.concatenate(
            [jnp.where(odd, got, value), jnp.where(odd, value, got)], axis=0
        )

    if part % BLK == 0 and part // BLK > 1:
        head = (part // BLK + 1) // 2 * BLK
        chunks = [(0, head), (head, part - head)]
    else:
        chunks = [(0, part)]

    half = rows // 2
    own_half = lax.dynamic_slice_in_dim(tokens, lax.rem(z, 2) * half, half, 0)

    def send_tokens(value, dt, g):
        features = lax.rem(chip - dt + g + chips, chips) * (2 * feat)
        return shift(columns(value, features, 2 * feat), -dt)

    def partial(pair, dp, first, width):
        column = lax.rem(chip + dp, chips) * part
        top, block, bottom = pair
        mine, other = gate_up(top, block, bottom, gate_weight, up_weight, column, first, width)
        return mine, swap(other)

    def send_partials(pair, got, dt):
        sums = []
        for dp in range(1, chips):
            pieces = [partial(pair, dp, *chunk) for chunk in chunks]
            for n, (mine, from_core) in enumerate(pieces):
                both = (mine.astype(F32) + from_core.astype(F32)).astype(BF16)
                got[dt, dp, n] = shift(both, dp)
                sums.append(both)
        return sums

    got, kept, gathered = {}, {}, {}
    local = swap(columns(tokens, (me ^ 1) * feat, feat))
    arrived = {dt: send_tokens(own_half, dt, 0) for dt in range(1, chips)}
    sums = send_partials((tokens, me, local), got, 0)
    if sums:
        local = after(local, *sums)
    kept[0] = partial((tokens, me, local), 0, 0, part)
    late_tokens = after(tokens, kept[0][0])
    neighbour_tokens = swap(late_tokens)
    late_half = after(own_half, *sums) if sums else own_half

    for dt in range(1, chips):
        gathered[dt, 0] = pair_z(after(arrived[dt], *sums))
        whole = gathered[dt, 0]
        top = columns(whole, core * feat, feat)
        bottom = swap(columns(whole, (1 - core) * feat, feat))
        pair = (top, jnp.int32(0), bottom)
        sums = send_partials(pair, got, dt)
        pair = (top, jnp.int32(0), after(bottom, *sums))
        kept[dt] = partial(pair, 0, 0, part)
        for g in range(1, chips):
            gathered[dt, g] = pair_z(after(send_tokens(late_half, dt, g), kept[dt][0]))

    def activate(e, first, width, n):
        terms = [lax.slice_in_dim(term, first, first + width, axis=2) for term in kept[e]]
        terms += [got[(e + dp) % chips, dp, n] for dp in range(1, chips)]
        total = sum(term.astype(F32) for term in terms)
        return (jax.nn.silu(total[0]) * total[1]).astype(BF16)

    totals = {u: None for u in range(chips)}
    for e in list(range(1, chips)) + [0]:
        values = [activate(e, *chunk, n) for n, chunk in enumerate(chunks)]
        spans = list(chunks)
        if e:
            values, spans = [jnp.concatenate(values, axis=1)], [(0, part)]
        sent = [[value] + [shift(value, d) for d in range(1, chips)] for value in values]
        for (first, width), copies in zip(spans, sent):
            for d, mine in enumerate(copies):
                u = (e - d + chips) % chips
                row = lax.rem(chip - d + chips, chips) * part + first
                totals[u] = down_add(totals[u], mine, swap(mine), down_weight, row)

    token_rows = []
    for dt in range(chips):
        if dt == 0:
            token_rows += [tokens, neighbour_tokens]
            continue
        else:
            full = jnp.zeros((rows, model), BF16)
            for g in range(chips):
                features = lax.rem(chip + g, chips) * (2 * feat)
                full = lax.dynamic_update_slice_in_dim(full, gathered[dt, g], features, 1)
        token_rows += [full, swap(full)]
    inputs = jnp.concatenate(token_rows, axis=0)
    count = inputs.shape[0]

    blocks, share, size = right_factor.shape
    ratio = tensor_count // fsdp_count
    turn = []
    for a in range(fsdp_count):
        for b in range(tensor_count):
            turn.append((a * tensor_count + b, (b // ratio) * tensor_count + a * ratio + b % ratio))
    back = [(b, a) for a, b in turn]
    right_rows = gather_z(lax.ppermute(right_factor, ("fsdp", "tensor"), turn)[None])
    right_rows = right_rows.reshape(fsdp_count, ratio, blocks, share, size)
    right_rows = right_rows.transpose(0, 2, 1, 3, 4).reshape(
        fsdp_count * blocks, ratio * share, size
    )
    left_rows = jnp.moveaxis(gather_z(jnp.moveaxis(left_factor, 1, 0)), 0, 1)

    block_input = inputs.reshape(count, fsdp_count * blocks, size)
    mixed = jnp.einsum(
        "nim,ijm->nij", block_input, right_rows, preferred_element_type=F32
    ).astype(BF16)
    student = jnp.einsum("nij,jki->njk", mixed, left_rows, preferred_element_type=F32)
    target = jnp.concatenate([totals[u] for u in range(chips)], axis=0)
    scale = 1.0 / math.sqrt(count)
    out_grad = (student * (1.0 / tensor_count) - target.reshape(student.shape)) * scale
    out_grad = out_grad.astype(BF16)
    grad_left = jnp.einsum("njk,nij->kji", out_grad, mixed, preferred_element_type=F32)
    mixed_grad = jnp.einsum(
        "njk,jki->nij", out_grad, left_rows, preferred_element_type=F32
    ).astype(BF16)
    grad_right = jnp.einsum(
        "nij,nim->ijm", mixed_grad, block_input, preferred_element_type=F32
    )
    grad_left = scatter_z(
        grad_left.reshape((tensor_count, -1) + grad_left.shape[1:])
    )
    grad_left = jnp.moveaxis(grad_left, 0, 1)
    grad_right = grad_right.reshape(fsdp_count, blocks, ratio, share, size)
    grad_right = grad_right.transpose(0, 2, 1, 3, 4).reshape(
        tensor_count, blocks, share, size
    )
    grad_right = lax.ppermute(scatter_z(grad_right), ("fsdp", "tensor"), back)
    return grad_right, grad_left


def cut_kernel(count, idx_ref, *refs):
    for in_ref, out_ref in zip(refs[:count], refs[count:]):
        out_ref[...] = in_ref[...]


def cut_tokens(tokens, places, cost=SMALL):
    block = (tokens.shape[0] // 2, tokens.shape[1] // 2)
    shape = jax.ShapeDtypeStruct(block, BF16)
    count = len(places)
    flat = [index for place in places for index in place]
    return pl.pallas_call(
        functools.partial(cut_kernel, count),
        grid_spec=pltpu.PrefetchScalarGridSpec(
            num_scalar_prefetch=1,
            grid=(1,),
            in_specs=[
                pl.BlockSpec(block, lambda n, s, k=k: (s[2 * k], s[2 * k + 1]))
                for k in range(count)
            ],
            out_specs=[pl.BlockSpec(block, lambda n, s: (0, 0))] * count,
        ),
        out_shape=[shape] * count,
        cost_estimate=cost,
        name="cut_tokens",
    )(jnp.stack(flat).astype(jnp.int32), *[tokens] * count)


def products_kernel(sets, idx_ref, *refs):
    pieces, (gate_ref, up_ref, mine_ref, other_ref) = refs[: 4 * sets], refs[4 * sets :]
    lhs = jnp.concatenate([piece[...] for piece in pieces], axis=0)
    rows = mine_ref.shape[2]
    for slot, weight_ref in enumerate((gate_ref, up_ref)):
        product = jnp.dot(lhs, weight_ref[...], preferred_element_type=F32).astype(BF16)
        for u in range(sets):
            mine_ref[u, slot] = product[2 * u * rows : (2 * u + 1) * rows]
            other_ref[u, slot] = product[(2 * u + 1) * rows : (2 * u + 2) * rows]


def products(pieces, scalars, gate, up, first, width):
    feat = gate.shape[0]
    sets = len(pieces) // 4
    half = pieces[0][0].shape[0] // (1 if pieces[0][1] is None else 2)
    start = first // BLK

    def piece_spec(row, column):
        if row is None:
            return pl.BlockSpec((half, feat), lambda n, s: (0, s[column]))
        return pl.BlockSpec((half, feat), lambda n, s: (s[row], s[column]))

    weight_spec = pl.BlockSpec(
        (feat, BLK), lambda n, s: (0, s[4] + start + n)
    )
    out_spec = pl.BlockSpec((sets, 2, 2 * half, BLK), lambda n, s: (0, 0, 0, n))
    shape = jax.ShapeDtypeStruct((sets, 2, 2 * half, width), BF16)
    return pl.pallas_call(
        functools.partial(products_kernel, sets),
        grid_spec=pltpu.PrefetchScalarGridSpec(
            num_scalar_prefetch=1,
            grid=(width // BLK,),
            in_specs=[piece_spec(row, column) for _, row, column in pieces]
            + [weight_spec, weight_spec],
            out_specs=[out_spec, out_spec],
        ),
        out_shape=[shape, shape],
        compiler_params=pltpu.CompilerParams(vmem_limit_bytes=40 * 2**20),
        cost_estimate=LARGE if sets > 1 else SMALL,
        name="gate_up_products",
    )(scalars, *[piece for piece, _, _ in pieces], gate, up)


def fill_rows(lhs, pieces):
    rows = pieces[0].shape[0]
    for place, which in enumerate((1, 3, 0, 2)):
        lhs[place * rows : (place + 1) * rows, :] = pieces[which][...]


def whole_spec(array):
    return pl.BlockSpec(array.shape, lambda n, s: (0,) * array.ndim)


def target_kernel(sign, idx_ref, mine_ref, near_ref, weight_ref, *refs):
    terms, out_ref = refs[:-1], refs[-1]
    lhs = jnp.concatenate([mine_ref[...], near_ref[...]], axis=0)
    product = jnp.dot(lhs, weight_ref[...], preferred_element_type=F32)
    out_ref[...] = sum((ref[...] for ref in terms), sign * product)


def target_part(sign, terms, mine, near, weight, chip):
    rows, width = mine.shape
    outs = weight.shape[1]
    block = pl.BlockSpec((2 * rows, BLK), lambda n, s: (0, n))
    return pl.pallas_call(
        functools.partial(target_kernel, sign),
        grid_spec=pltpu.PrefetchScalarGridSpec(
            num_scalar_prefetch=1,
            grid=(outs // BLK,),
            in_specs=[whole_spec(mine), whole_spec(near)]
            + [pl.BlockSpec((width, BLK), lambda n, s: (s[0], n))]
            + [block] * len(terms),
            out_specs=block,
        ),
        out_shape=jax.ShapeDtypeStruct((2 * rows, outs), F32),
        compiler_params=pltpu.CompilerParams(vmem_limit_bytes=40 * 2**20),
        cost_estimate=SMALL,
        name="target_part",
    )(jnp.reshape(chip, (1,)).astype(jnp.int32), mine, near, weight, *terms)


TN = (((0,), (0,)), ((), ()))
NT = (((1,), (1,)), ((), ()))
WIDE = 8


def natural(step, chip, per_chip):
    return lax.rem(chip + step // per_chip, 2) * per_chip + lax.rem(step, per_chip)


def spread_kernel(idx_ref, rows_ref, out_ref, scratch):
    groups = out_ref.shape[0]
    parts, _, size = rows_ref.shape
    blocks = size // 2
    share = blocks // parts
    fold = BLK // blocks
    begin = rows_ref.shape[1] - groups * fold // 2 * share
    scratch[...] = jnp.zeros_like(scratch)
    low = lax.broadcasted_iota(jnp.int32, (blocks, size), 1) < blocks
    for g in range(groups):
        for pair in range(fold // 2):
            row = begin + (g * (fold // 2) + pair) * share
            picked = [
                rows_ref[idx_ref[3] ^ owner, row : row + share, :] for owner in range(parts)
            ]
            turned = jnp.concatenate(picked + picked, axis=0).astype(F32).T
            for a in range(2):
                value = turned[a * blocks : (a + 1) * blocks]
                value = jnp.where(low if a == 0 else ~low, value, 0.0)
                lanes = slice(pair * size, (pair + 1) * size)
                for c in range(blocks // WIDE):
                    row = (c * fold + 2 * pair + a) * WIDE
                    scratch[row : row + WIDE, lanes] = value[c * WIDE : (c + 1) * WIDE]
        out_ref[g] = scratch[...].astype(BF16)


def spread_left(scalars, rows, groups):
    return pl.pallas_call(
        spread_kernel,
        grid_spec=pltpu.PrefetchScalarGridSpec(
            num_scalar_prefetch=1,
            grid=(1,),
            in_specs=[whole_spec(rows)],
            out_specs=pl.BlockSpec((groups, BLK, BLK), lambda n, s: (0, 0, 0)),
            scratch_shapes=[pltpu.VMEM((BLK, BLK), F32)],
        ),
        out_shape=jax.ShapeDtypeStruct((groups, BLK, BLK), BF16),
        cost_estimate=SMALL,
        name="spread_left",
    )(scalars, rows)


def student_kernel(steps, late, tensor_count, idx_ref, *refs):
    tokens, refs = refs[: 8 if late else 4], refs[8 if late else 4 :]
    rights, left_ref, targets = refs[:2], refs[2], refs[3:-3]
    mixed_ref, student_ref, spread = refs[-3:]
    step = pl.program_id(0)
    pair = natural(step, idx_ref[2], steps // 2)
    groups = left_ref.shape[0]
    size = spread.shape[2]
    pairs = spread.shape[1] // WIDE
    share = BLK // groups

    @pl.when(step == 0)
    def _():
        spread[...] = jnp.zeros_like(spread)

    def mix(pieces):
        for half, right_ref in enumerate(rights):
            for t in range(WIDE):
                value = right_ref[0, t * pairs : (t + 1) * pairs, :].astype(F32)
                spread[t, pl.ds(t, pairs, stride=WIDE), :] = value
            factor = jnp.concatenate([spread[t] for t in range(WIDE)], axis=1).astype(BF16)
            lanes = slice(half * WIDE * size, (half + 1) * WIDE * size)
            rows = jnp.concatenate([piece[:, lanes] for piece in pieces], axis=0)
            part = lax.dot_general(factor, rows, NT, preferred_element_type=F32).astype(BF16)
            start = pl.multiple_of((2 * pair + half) * share, share)
            for g in range(groups):
                mixed_ref[g, pl.ds(start, share), :] = part[g * share : (g + 1) * share]

    if late:
        pl.when(step < steps // 2)(lambda: mix(tokens[:4]))
        pl.when(step >= steps // 2)(lambda: mix(tokens[4:]))
    else:
        mix(tokens)

    @pl.when(step == steps - 1)
    def _():
        for g in range(groups):
            span = slice(g * BLK, (g + 1) * BLK)
            student = lax.dot_general(
                mixed_ref[g], left_ref[g], TN, preferred_element_type=F32
            )
            student = student * (1.0 / tensor_count)
            student_ref[:, span] = sum((-ref[:, span] for ref in targets), student)


def token_specs(half, width, chunk, late):
    if not late:
        return [
            pl.BlockSpec((half, width), lambda n, s, p=p: (s[p % 2], chunk(n, s)))
            for p in range(4)
        ]
    inner = pl.BlockSpec((half, width), lambda n, s: (0, lax.rem(chunk(n, s), 2)))
    return [inner] * 8


def student_part(tokens, late, scalars, factors, left_diag, targets, pairs, tensor_count):
    parts, _, size = factors.shape
    half = tokens[0].shape[0] // (1 if late else 2)
    groups = left_diag.shape[0]
    blocks = groups * BLK // pairs
    steps = blocks // (2 * WIDE)

    def chunk(n, s):
        return natural(n, s[2], steps // 2)

    def right_spec(half):
        return pl.BlockSpec(
            (1, WIDE * pairs, size),
            lambda n, s: (s[3] ^ chunk(n, s), half, 0),
        )

    return pl.pallas_call(
        functools.partial(student_kernel, steps, late, tensor_count),
        grid_spec=pltpu.PrefetchScalarGridSpec(
            num_scalar_prefetch=1,
            grid=(steps,),
            in_specs=token_specs(half, 2 * WIDE * size, chunk, late)
            + [right_spec(0), right_spec(1), whole_spec(left_diag)]
            + [whole_spec(target) for target in targets],
            out_specs=[
                pl.BlockSpec((groups, BLK, 4 * half), lambda n, s: (0, 0, 0)),
                pl.BlockSpec((4 * half, groups * BLK), lambda n, s: (0, 0)),
            ],
            scratch_shapes=[pltpu.VMEM((WIDE, pairs * WIDE, size), F32)],
        ),
        out_shape=[
            jax.ShapeDtypeStruct((groups, BLK, 4 * half), BF16),
            jax.ShapeDtypeStruct((4 * half, groups * BLK), F32),
        ],
        compiler_params=pltpu.CompilerParams(vmem_limit_bytes=40 * 2**20),
        cost_estimate=LARGE,
        name="student_part",
    )(scalars, *tokens, factors, factors, left_diag, *targets)


def place(z, owner):
    bits = z ^ owner
    return lax.rem(bits, 2) * 2 + bits // 2


def left_kernel(chunks, scale, idx_ref, *refs):
    hidden, refs = refs[:4], refs[4:]
    weight_ref, rest0, rest1, mixed0, mixed1, left_ref, out_ref, back_ref, lhs = refs
    step = pl.program_id(0)
    parts, size = out_ref.shape[0], out_ref.shape[2]
    blocks = chunks * WIDE
    share = BLK // chunks
    fold = BLK // blocks
    pl.when(step == 0)(lambda: fill_rows(lhs, hidden))
    target = jnp.dot(lhs[...], weight_ref[...], preferred_element_type=F32)
    rest = jnp.concatenate([rest0[...], rest1[...]], axis=0)
    out_grad = ((rest - target) * scale).astype(BF16)
    mixed = jnp.concatenate([mixed0[0], mixed1[0]], axis=1)
    left = jnp.dot(mixed, out_grad, preferred_element_type=F32)
    value = lax.dot_general(left_ref[0], out_grad, NT, preferred_element_type=F32)
    value = value.astype(BF16)
    for c in range(chunks):
        back_ref[c] = value[c * share : (c + 1) * share]
    low = lax.broadcasted_iota(jnp.int32, (blocks, size), 1) < blocks
    rows = blocks // parts
    for pair in range(fold // 2):
        lanes = slice(pair * size, (pair + 1) * size)
        picked = []
        for a in (2 * pair, 2 * pair + 1):
            for c in range(chunks):
                begin = (c * fold + a) * WIDE
                picked.append(left[begin : begin + WIDE, lanes])
        turned = jnp.concatenate(picked, axis=0).T
        both = jnp.where(low, turned[:blocks], turned[blocks:]).astype(BF16)
        begin = pl.multiple_of((step * (fold // 2) + pair) * rows, rows)
        for owner in range(parts):
            out_ref[place(idx_ref[3], owner), pl.ds(begin, rows), :] = both[
                owner * rows : (owner + 1) * rows
            ]


def left_grads(hidden, weight, rest, mixed, left_diag, scalars, parts, pairs, size, scale):
    groups, count = left_diag.shape[0], 2 * rest[0].shape[0]
    width = hidden[0].shape[1]
    blocks = groups * BLK // pairs
    chunks = blocks // WIDE
    share = BLK // chunks
    column = pl.BlockSpec((count // 2, BLK), lambda n, s: (0, n))
    slab = pl.BlockSpec((1, BLK, count // 2), lambda n, s: (n, 0, 0))
    out_rows = pairs * blocks * blocks // size // parts
    return pl.pallas_call(
        functools.partial(left_kernel, chunks, scale),
        grid_spec=pltpu.PrefetchScalarGridSpec(
            num_scalar_prefetch=1,
            grid=(groups,),
            in_specs=[whole_spec(piece) for piece in hidden]
            + [pl.BlockSpec((width, BLK), lambda n, s: (1 - s[2], n))]
            + [column, column, slab, slab]
            + [pl.BlockSpec((1, BLK, BLK), lambda n, s: (n, 0, 0))],
            out_specs=[
                pl.BlockSpec((parts, out_rows, size), lambda n, s: (0, 0, 0)),
                pl.BlockSpec((chunks, share, count), lambda n, s: (0, n, 0)),
            ],
            scratch_shapes=[pltpu.VMEM((count, width), BF16)],
        ),
        out_shape=[
            jax.ShapeDtypeStruct((parts, out_rows, size), BF16),
            jax.ShapeDtypeStruct((chunks, groups * share, count), BF16),
        ],
        compiler_params=pltpu.CompilerParams(vmem_limit_bytes=40 * 2**20),
        cost_estimate=SMALL,
        name="left_grads",
    )(scalars, *hidden, weight, *rest, *mixed, left_diag)


def right_kernel(pairs, bit, idx_ref, *refs):
    own, near, far, (back_ref, out_ref, wide) = refs[:4], refs[4:8], refs[8:12], refs[12:]
    size = out_ref.shape[2]
    owner = idx_ref[3] ^ (2 * pl.program_id(0) + bit)

    def right(later):
        for half in range(2):
            lanes = slice(half * WIDE * size, (half + 1) * WIDE * size)
            rows = jnp.concatenate([piece[:, lanes] for piece in own + later], axis=0)
            value = jnp.dot(back_ref[half], rows, preferred_element_type=F32)
            for t in range(WIDE):
                wide[t] = value[:, t * size : (t + 1) * size]
            for t in range(WIDE):
                begin = (half * WIDE + t) * pairs
                out_ref[0, begin : begin + pairs, :] = wide[
                    t, pl.ds(t, pairs, stride=WIDE), :
                ].astype(BF16)

    pl.when(owner // 2 == idx_ref[2])(lambda: right(near))
    pl.when(owner // 2 != idx_ref[2])(lambda: right(far))


def right_grads(back, own, late, scalars, pairs, bit, size, cost):
    half = late[0].shape[0]
    rows, count = back.shape[1:]

    def owner(n, s):
        return s[3] ^ (2 * n + bit)

    return pl.pallas_call(
        functools.partial(right_kernel, pairs, bit),
        grid_spec=pltpu.PrefetchScalarGridSpec(
            num_scalar_prefetch=1,
            grid=(2,),
            in_specs=token_specs(half, 2 * WIDE * size, owner, False)
            + token_specs(half, 2 * WIDE * size, owner, True)
            + [pl.BlockSpec((2, rows, count), lambda n, s: (owner(n, s), 0, 0))],
            out_specs=pl.BlockSpec((1, 2 * WIDE * pairs, size), lambda n, s: (n, 0, 0)),
            scratch_shapes=[pltpu.VMEM((WIDE, pairs * WIDE, size), F32)],
        ),
        out_shape=jax.ShapeDtypeStruct((2, 2 * WIDE * pairs, size), BF16),
        compiler_params=pltpu.CompilerParams(vmem_limit_bytes=40 * 2**20),
        cost_estimate=cost,
        name="right_grads",
    )(scalars, *own, *late, back)


def tiled_body(tokens, gate_weight, up_weight, down_weight, right_factor, left_factor):
    fsdp_count = lax.axis_size("fsdp")
    tensor_count = lax.axis_size("tensor")
    rows, model = tokens.shape
    part = gate_weight.shape[1] // 2
    me, z = lax.axis_index("fsdp"), lax.axis_index("tensor")
    chip, core, odd = lax.div(me, 2), lax.rem(me, 2), lax.rem(z, 2)
    both_axes = ("fsdp", "tensor")

    def swap(value):
        return lax.ppermute(value, "fsdp", [(i, i ^ 1) for i in range(fsdp_count)])

    def across(value):
        return lax.ppermute(value, "fsdp", [(i, i ^ 2) for i in range(fsdp_count)])

    def along(value, bit):
        return lax.ppermute(value, "tensor", [(i, i ^ bit) for i in range(tensor_count)])

    def turn(value, bit):
        perm = []
        for f in range(fsdp_count):
            for t in range(tensor_count):
                perm.append((f * tensor_count + t, (t ^ bit) * tensor_count + f))
        return lax.ppermute(value, both_axes, perm)

    def after(value, *others):
        return lax.optimization_barrier((value,) + others)[0]

    def add(*terms):
        return sum(term.astype(F32) for term in terms)

    near_tokens = swap(tokens)
    first = cut_tokens(tokens, [(odd, 1 - chip), (1 - odd, 1 - chip)])
    arrived = [across(value) for value in first]
    base = jnp.stack([odd, 1 - odd])
    mine_block = lax.div(part, BLK) * chip
    other_block = lax.div(part, BLK) * (1 - chip)

    def scalars(block):
        return jnp.concatenate([base, jnp.stack([me, core, block])]).astype(jnp.int32)

    own_pieces = [(t, row, 2) for t in (tokens, near_tokens) for row in (0, 1)]
    mine, other = products(
        own_pieces, after(scalars(other_block), *first), gate_weight, up_weight, 0, part
    )

    pairs, blocks = left_factor.shape[0], left_factor.shape[2]
    left_rows = left_factor.reshape(pairs // 2, 2, -1, blocks).transpose(0, 2, 1, 3)
    turned = turn(after(right_factor, mine), 0)
    (rest,) = cut_tokens(after(tokens, mine), [(odd, chip)], LARGE)
    factors = jnp.concatenate(
        [after(turned, rest).reshape(-1, LANES), left_rows.reshape(-1, LANES)], axis=0
    )[None]
    more = along(factors, 1)
    sums = add(mine[0], swap(other[0])).astype(BF16)
    arrived = [after(arrived[0], rest), after(arrived[1], more, rest, sums)]
    got_early = across(sums)
    late_first = across(after(rest, sums))
    factors = jnp.concatenate([factors, more], axis=0)
    more = along(after(factors, arrived[1]), 2)

    order = jnp.concatenate([base, jnp.stack([chip, z])]).astype(jnp.int32)
    own = [tokens, tokens, near_tokens, near_tokens]
    near_arrived = [swap(value) for value in arrived]
    late = arrived + near_arrived
    late_pieces = [(t, None, 3) for t in late]
    late_order = after(scalars(other_block), sums)
    mine, other = products(late_pieces, late_order, gate_weight, up_weight, 0, part)
    near = swap(other[0])
    mine_order = after(scalars(mine_block), mine)
    kept, other = products(
        own_pieces + late_pieces, mine_order, gate_weight, up_weight, 0, part
    )
    sums = add(mine[0], after(near, kept)).astype(BF16)
    got = across(sums)
    near_kept = swap(after(other, got_early, late_first, more, sums))

    factors = jnp.concatenate([factors, after(more, kept)], axis=0)
    def activate(u, term):
        total = add(kept[u], near_kept[u], term)
        return (jax.nn.silu(total[0]) * total[1]).astype(BF16)

    hidden1 = activate(1, got_early)
    got1 = across(hidden1)
    near1 = swap(hidden1)
    left_diag = spread_left(order, after(factors, hidden1), pairs * blocks // BLK)
    late_partner = along(after(late_first, hidden1), 1)
    target1 = target_part(1.0, [], hidden1, near1, down_weight, chip)
    mixed0, rest0 = student_part(
        [after(tokens, target1)] + own[1:],
        False,
        order,
        factors,
        left_diag,
        [],
        pairs,
        tensor_count,
    )
    hidden0 = activate(0, after(got, mixed0))
    got0 = across(hidden0)
    near0 = swap(hidden0)
    late_partner = after(late_partner, mixed0)
    late += [late_first, late_partner, swap(late_first), swap(late_partner)]
    mixed1, rest1 = student_part(
        [after(late[0], hidden0)] + late[1:],
        True,
        order,
        factors,
        left_diag,
        [target1],
        pairs,
        tensor_count,
    )
    near0 = after(near0, mixed1)
    rest0 = target_part(-1.0, [rest0], hidden0, near0, down_weight, chip)
    got1, got0 = after(got1, mixed1), after(got0, rest0)
    hidden = [got0, got1, swap(got0), swap(got1)]

    size = right_factor.shape[2]
    left, back = left_grads(
        hidden,
        down_weight,
        (rest0, rest1),
        (mixed0, mixed1),
        left_diag,
        order,
        tensor_count,
        pairs,
        size,
        1.0 / math.sqrt(rows * fsdp_count),
    )
    got_left = along(left[2:], 1)
    sent = right_grads(back, own, late, order, pairs, 1, size, SMALL)
    left = add(left[:2], after(got_left, sent)).astype(BF16)
    got_left = along(left[1], 2)
    got_right = along(sent, 1)
    kept_back = after(back, sent, left)
    right = right_grads(kept_back, own, late, order, pairs, 0, size, LARGE)
    right = add(right, got_right).astype(BF16)
    grad_right = add(turn(right[0], 0), turn(right[1], 2))
    grad_left = add(left[0], got_left)
    grad_left = grad_left.reshape(pairs // 2, -1, 2, blocks).transpose(0, 2, 1, 3)
    return grad_right.reshape(right_factor.shape), grad_left.reshape(left_factor.shape)


def body(*args):
    tokens, gate_weight, _, _, right_factor, left_factor = args
    counts = (lax.axis_size("fsdp"), lax.axis_size("tensor"))
    feat, hid = gate_weight.shape
    per_owner, share, size = right_factor.shape
    blocks = left_factor.shape[2]
    fits = hid % (2 * BLK) == 0
    fits = fits and counts == (4, 4) and tokens.shape[0] == 128
    fits = fits and hid >= 4 * BLK and feat % BLK == 0
    fits = fits and size == 128 and 2 * blocks == size and per_owner % WIDE == 0
    fits = fits and left_factor.shape[0] == share and share % 16 == 0
    return (tiled_body if fits else general_body)(*args)


def solution(mesh):
    return jax.shard_map(
        body,
        mesh=mesh,
        in_specs=(
            P(("groups", "fsdp"), None),
            P("fsdp", "tensor"),
            P("fsdp", "tensor"),
            P("tensor", "fsdp"),
            P("fsdp", "tensor", None),
            P("fsdp", "tensor", None),
        ),
        out_specs=(P(("groups", "fsdp"), "tensor", None), P(("groups", "fsdp"), "tensor", None)),
        check_vma=False,
    )
```

```python
import functools
import math

import jax
import jax.numpy as jnp
from jax import lax
from jax.experimental import pallas as pl
from jax.experimental.pallas import tpu as pltpu
from jax.sharding import PartitionSpec as P

BLK = 256
LANES = 128
SMALL = pl.CostEstimate(flops=1, bytes_accessed=1, transcendentals=0)
LARGE = pl.CostEstimate(flops=10**10, bytes_accessed=10**7, transcendentals=0)
F32 = jnp.float32
BF16 = jnp.bfloat16


def gate_up_kernel(idx_ref, top_ref, bottom_ref, gate_ref, up_ref, mine_ref, other_ref):
    rows = top_ref.shape[0]
    lhs = jnp.concatenate([top_ref[...], bottom_ref[...]], axis=0)
    for slot, weight_ref in enumerate((gate_ref, up_ref)):
        product = jnp.dot(lhs, weight_ref[...], preferred_element_type=F32).astype(BF16)
        mine_ref[slot] = product[:rows]
        other_ref[slot] = product[rows:]


def gate_up(top, top_block, bottom, gate, up, column, first, width):
    rows, feat = bottom.shape
    if width % BLK or gate.shape[1] % BLK or rows % 16 or feat % 128:
        lhs = jnp.concatenate(
            [lax.dynamic_slice_in_dim(top, top_block * feat, feat, 1), bottom], axis=0
        )
        both = [
            jnp.dot(
                lhs,
                lax.dynamic_slice_in_dim(w, column + first, width, 1),
                preferred_element_type=F32,
            ).astype(BF16)
            for w in (gate, up)
        ]
        both = jnp.stack(both)
        return both[:, :rows], both[:, rows:]
    scalars = jnp.stack([top_block, lax.div(column, BLK) + first // BLK]).astype(jnp.int32)
    weight_spec = pl.BlockSpec((feat, BLK), lambda n, s: (0, s[1] + n))
    out_spec = pl.BlockSpec((2, rows, BLK), lambda n, s: (0, 0, n))
    shape = jax.ShapeDtypeStruct((2, rows, width), BF16)
    return pl.pallas_call(
        gate_up_kernel,
        grid_spec=pltpu.PrefetchScalarGridSpec(
            num_scalar_prefetch=1,
            grid=(width // BLK,),
            in_specs=[
                pl.BlockSpec((rows, feat), lambda n, s: (0, s[0])),
                pl.BlockSpec((rows, feat), lambda n, s: (0, 0)),
                weight_spec,
                weight_spec,
            ],
            out_specs=[out_spec, out_spec],
        ),
        out_shape=[shape, shape],
        compiler_params=pltpu.CompilerParams(vmem_limit_bytes=40 * 2**20),
        cost_estimate=pl.CostEstimate(
            flops=2 * 2 * rows * feat * 2 * width,
            bytes_accessed=2 * feat * 2 * width + 2 * 2 * rows * (feat + 2 * width),
            transcendentals=0,
        ),
        name="gate_up",
    )(scalars, top, bottom, gate, up)


def down_kernel(idx_ref, mine_ref, other_ref, weight_ref, *refs):
    out_ref = refs[-1]
    lhs = jnp.concatenate([mine_ref[...], other_ref[...]], axis=0)
    product = jnp.dot(lhs, weight_ref[...], preferred_element_type=F32)

    @pl.when(pl.program_id(0) == 0)
    def _():
        out_ref[...] = refs[0][...] + product if len(refs) > 1 else product

    @pl.when(pl.program_id(0) > 0)
    def _():
        out_ref[...] += product


def down_add(total, mine, other, weight, row):
    rows, width = mine.shape
    outs = weight.shape[1]
    if width % BLK or weight.shape[0] % BLK or rows % 16 or outs % 128:
        lhs = jnp.concatenate([mine, other], axis=0)
        part = lax.dynamic_slice_in_dim(weight, row, width, 0)
        product = jnp.dot(lhs, part, preferred_element_type=F32)
        return product if total is None else total + product
    scalars = jnp.reshape(lax.div(row, BLK), (1,)).astype(jnp.int32)
    hidden_spec = pl.BlockSpec((rows, BLK), lambda k, s: (0, k))
    whole = pl.BlockSpec((2 * rows, outs), lambda k, s: (0, 0))
    totals = [] if total is None else [total]
    return pl.pallas_call(
        down_kernel,
        grid_spec=pltpu.PrefetchScalarGridSpec(
            num_scalar_prefetch=1,
            grid=(width // BLK,),
            in_specs=[
                hidden_spec,
                hidden_spec,
                pl.BlockSpec((BLK, outs), lambda k, s: (s[0] + k, 0)),
            ]
            + [whole] * len(totals),
            out_specs=whole,
        ),
        out_shape=jax.ShapeDtypeStruct((2 * rows, outs), F32),
        compiler_params=pltpu.CompilerParams(vmem_limit_bytes=40 * 2**20),
        cost_estimate=pl.CostEstimate(
            flops=2 * 2 * rows * width * outs,
            bytes_accessed=2 * width * outs + 2 * 2 * rows * width + 16 * rows * outs,
            transcendentals=0,
        ),
        name="down_add",
    )(scalars, mine, other, weight, *totals)


def general_body(tokens, gate_weight, up_weight, down_weight, right_factor, left_factor):
    fsdp_count = lax.axis_size("fsdp")
    tensor_count = lax.axis_size("tensor")
    chips = fsdp_count // 2
    rows, model = tokens.shape
    feat, hid = gate_weight.shape
    part = hid // chips
    me = lax.axis_index("fsdp")
    chip, core = lax.div(me, 2), lax.rem(me, 2)
    z = lax.axis_index("tensor")

    def swap(value):
        return lax.ppermute(value, "fsdp", [(i, i ^ 1) for i in range(fsdp_count)])

    def shift(value, hops):
        perm = [(i, (i + 2 * hops) % fsdp_count) for i in range(fsdp_count)]
        return lax.ppermute(value, "fsdp", perm)

    def gather_z(value):
        if tensor_count > 4:
            return lax.all_gather(value, "tensor", axis=0, tiled=True)
        size = value.shape[0]
        whole = jnp.zeros((size * tensor_count,) + value.shape[1:], value.dtype)
        whole = lax.dynamic_update_slice_in_dim(whole, value, z * size, 0)
        for step in range(1, tensor_count):
            perm = [(i, (i + step) % tensor_count) for i in range(tensor_count)]
            got = lax.ppermute(value, "tensor", perm)
            source = lax.rem(z - step + tensor_count, tensor_count)
            whole = lax.dynamic_update_slice_in_dim(whole, got, source * size, 0)
        return whole

    def scatter_z(value):
        if tensor_count > 4:
            return lax.psum_scatter(value, "tensor", scatter_dimension=0, tiled=False)
        total = lax.dynamic_index_in_dim(value, z, 0, keepdims=False)
        for step in range(1, tensor_count):
            target_z = lax.rem(z + step, tensor_count)
            piece = lax.dynamic_index_in_dim(value, target_z, 0, keepdims=False)
            perm = [(i, (i + step) % tensor_count) for i in range(tensor_count)]
            total += lax.ppermute(piece.astype(BF16), "tensor", perm).astype(F32)
        return total

    def columns(value, start, width):
        return lax.dynamic_slice_in_dim(value, start, width, 1)

    def after(value, *others):
        return lax.optimization_barrier((value,) + others)[0]

    def pair_z(value):
        perm = [(i, i ^ 1) for i in range(tensor_count)]
        got = lax.ppermute(value, "tensor", perm)
        odd = lax.rem(z, 2) == 1
        return jnp.concatenate(
            [jnp.where(odd, got, value), jnp.where(odd, value, got)], axis=0
        )

    if part % BLK == 0 and part // BLK > 1:
        head = (part // BLK + 1) // 2 * BLK
        chunks = [(0, head), (head, part - head)]
    else:
        chunks = [(0, part)]

    half = rows // 2
    own_half = lax.dynamic_slice_in_dim(tokens, lax.rem(z, 2) * half, half, 0)

    def send_tokens(value, dt, g):
        features = lax.rem(chip - dt + g + chips, chips) * (2 * feat)
        return shift(columns(value, features, 2 * feat), -dt)

    def partial(pair, dp, first, width):
        column = lax.rem(chip + dp, chips) * part
        top, block, bottom = pair
        mine, other = gate_up(top, block, bottom, gate_weight, up_weight, column, first, width)
        return mine, swap(other)

    def send_partials(pair, got, dt):
        sums = []
        for dp in range(1, chips):
            pieces = [partial(pair, dp, *chunk) for chunk in chunks]
            for n, (mine, from_core) in enumerate(pieces):
                both = (mine.astype(F32) + from_core.astype(F32)).astype(BF16)
                got[dt, dp, n] = shift(both, dp)
                sums.append(both)
        return sums

    got, kept, gathered = {}, {}, {}
    local = swap(columns(tokens, (me ^ 1) * feat, feat))
    arrived = {dt: send_tokens(own_half, dt, 0) for dt in range(1, chips)}
    sums = send_partials((tokens, me, local), got, 0)
    if sums:
        local = after(local, *sums)
    kept[0] = partial((tokens, me, local), 0, 0, part)
    late_tokens = after(tokens, kept[0][0])
    neighbour_tokens = swap(late_tokens)
    late_half = after(own_half, *sums) if sums else own_half

    for dt in range(1, chips):
        gathered[dt, 0] = pair_z(after(arrived[dt], *sums))
        whole = gathered[dt, 0]
        top = columns(whole, core * feat, feat)
        bottom = swap(columns(whole, (1 - core) * feat, feat))
        pair = (top, jnp.int32(0), bottom)
        sums = send_partials(pair, got, dt)
        pair = (top, jnp.int32(0), after(bottom, *sums))
        kept[dt] = partial(pair, 0, 0, part)
        for g in range(1, chips):
            gathered[dt, g] = pair_z(after(send_tokens(late_half, dt, g), kept[dt][0]))

    def activate(e, first, width, n):
        terms = [lax.slice_in_dim(term, first, first + width, axis=2) for term in kept[e]]
        terms += [got[(e + dp) % chips, dp, n] for dp in range(1, chips)]
        total = sum(term.astype(F32) for term in terms)
        return (jax.nn.silu(total[0]) * total[1]).astype(BF16)

    totals = {u: None for u in range(chips)}
    for e in list(range(1, chips)) + [0]:
        values = [activate(e, *chunk, n) for n, chunk in enumerate(chunks)]
        spans = list(chunks)
        if e:
            values, spans = [jnp.concatenate(values, axis=1)], [(0, part)]
        sent = [[value] + [shift(value, d) for d in range(1, chips)] for value in values]
        for (first, width), copies in zip(spans, sent):
            for d, mine in enumerate(copies):
                u = (e - d + chips) % chips
                row = lax.rem(chip - d + chips, chips) * part + first
                totals[u] = down_add(totals[u], mine, swap(mine), down_weight, row)

    token_rows = []
    for dt in range(chips):
        if dt == 0:
            token_rows += [tokens, neighbour_tokens]
            continue
        else:
            full = jnp.zeros((rows, model), BF16)
            for g in range(chips):
                features = lax.rem(chip + g, chips) * (2 * feat)
                full = lax.dynamic_update_slice_in_dim(full, gathered[dt, g], features, 1)
        token_rows += [full, swap(full)]
    inputs = jnp.concatenate(token_rows, axis=0)
    count = inputs.shape[0]

    blocks, share, size = right_factor.shape
    ratio = tensor_count // fsdp_count
    turn = []
    for a in range(fsdp_count):
        for b in range(tensor_count):
            turn.append((a * tensor_count + b, (b // ratio) * tensor_count + a * ratio + b % ratio))
    back = [(b, a) for a, b in turn]
    right_rows = gather_z(lax.ppermute(right_factor, ("fsdp", "tensor"), turn)[None])
    right_rows = right_rows.reshape(fsdp_count, ratio, blocks, share, size)
    right_rows = right_rows.transpose(0, 2, 1, 3, 4).reshape(
        fsdp_count * blocks, ratio * share, size
    )
    left_rows = jnp.moveaxis(gather_z(jnp.moveaxis(left_factor, 1, 0)), 0, 1)

    block_input = inputs.reshape(count, fsdp_count * blocks, size)
    mixed = jnp.einsum(
        "nim,ijm->nij", block_input, right_rows, preferred_element_type=F32
    ).astype(BF16)
    student = jnp.einsum("nij,jki->njk", mixed, left_rows, preferred_element_type=F32)
    target = jnp.concatenate([totals[u] for u in range(chips)], axis=0)
    scale = 1.0 / math.sqrt(count)
    out_grad = (student * (1.0 / tensor_count) - target.reshape(student.shape)) * scale
    out_grad = out_grad.astype(BF16)
    grad_left = jnp.einsum("njk,nij->kji", out_grad, mixed, preferred_element_type=F32)
    mixed_grad = jnp.einsum(
        "njk,jki->nij", out_grad, left_rows, preferred_element_type=F32
    ).astype(BF16)
    grad_right = jnp.einsum(
        "nij,nim->ijm", mixed_grad, block_input, preferred_element_type=F32
    )
    grad_left = scatter_z(
        grad_left.reshape((tensor_count, -1) + grad_left.shape[1:])
    )
    grad_left = jnp.moveaxis(grad_left, 0, 1)
    grad_right = grad_right.reshape(fsdp_count, blocks, ratio, share, size)
    grad_right = grad_right.transpose(0, 2, 1, 3, 4).reshape(
        tensor_count, blocks, share, size
    )
    grad_right = lax.ppermute(scatter_z(grad_right), ("fsdp", "tensor"), back)
    return grad_right, grad_left


def cut_kernel(idx_ref, in_ref, out_ref):
    out_ref[...] = in_ref[...]


def cut_tokens(tokens, rows, row, column, cost=SMALL):
    width = tokens.shape[1] // 2
    steps = 4
    return pl.pallas_call(
        cut_kernel,
        grid_spec=pltpu.PrefetchScalarGridSpec(
            num_scalar_prefetch=1,
            grid=(steps,),
            in_specs=[pl.BlockSpec((rows, width // steps), lambda n, s: (s[0], s[1] * steps + n))],
            out_specs=pl.BlockSpec((rows, width // steps), lambda n, s: (0, n)),
        ),
        out_shape=jax.ShapeDtypeStruct((rows, width), BF16),
        cost_estimate=cost,
        name="cut_tokens",
    )(jnp.stack([row, column]).astype(jnp.int32), tokens)


def join_kernel(mine_ref, more_ref, out_ref):
    count = mine_ref.shape[0]
    out_ref[:count] = mine_ref[...]
    out_ref[count:] = more_ref[...]


def join(mine, more):
    shape = (2 * mine.shape[0],) + mine.shape[1:]
    return pl.pallas_call(
        join_kernel,
        out_shape=jax.ShapeDtypeStruct(shape, mine.dtype),
        cost_estimate=LARGE,
        name="join",
    )(mine, more)


def products_kernel(sets, idx_ref, *refs):
    pieces, (gate_ref, up_ref, mine_ref, other_ref) = refs[: 4 * sets], refs[4 * sets :]
    lhs = jnp.concatenate([piece[...] for piece in pieces], axis=0)
    rows = mine_ref.shape[2]
    for slot, weight_ref in enumerate((gate_ref, up_ref)):
        product = jnp.dot(lhs, weight_ref[...], preferred_element_type=F32).astype(BF16)
        for u in range(sets):
            mine_ref[u, slot] = product[2 * u * rows : (2 * u + 1) * rows]
            other_ref[u, slot] = product[(2 * u + 1) * rows : (2 * u + 2) * rows]


def products(pieces, scalars, gate, up, first, width):
    feat = gate.shape[0]
    sets = len(pieces) // 4
    half = pieces[0][0].shape[0] // (1 if pieces[0][1] is None else 2)
    start = first // BLK

    def piece_spec(row, column):
        if row is None:
            return pl.BlockSpec((half, feat), lambda n, s: (0, s[column]))
        return pl.BlockSpec((half, feat), lambda n, s: (s[row], s[column]))

    weight_spec = pl.BlockSpec(
        (feat, BLK), lambda n, s: (0, s[4] + start + n)
    )
    out_spec = pl.BlockSpec((sets, 2, 2 * half, BLK), lambda n, s: (0, 0, 0, n))
    shape = jax.ShapeDtypeStruct((sets, 2, 2 * half, width), BF16)
    return pl.pallas_call(
        functools.partial(products_kernel, sets),
        grid_spec=pltpu.PrefetchScalarGridSpec(
            num_scalar_prefetch=1,
            grid=(width // BLK,),
            in_specs=[piece_spec(row, column) for _, row, column in pieces]
            + [weight_spec, weight_spec],
            out_specs=[out_spec, out_spec],
        ),
        out_shape=[shape, shape],
        compiler_params=pltpu.CompilerParams(vmem_limit_bytes=40 * 2**20),
        cost_estimate=LARGE if sets > 1 else SMALL,
        name="gate_up_products",
    )(scalars, *[piece for piece, _, _ in pieces], gate, up)


def fill_rows(lhs, pieces):
    rows = pieces[0].shape[0]
    for place, which in enumerate((1, 3, 0, 2)):
        lhs[place * rows : (place + 1) * rows, :] = pieces[which][...]


def whole_spec(array):
    return pl.BlockSpec(array.shape, lambda n, s: (0,) * len(array.shape))


def target_kernel(sign, idx_ref, mine_ref, near_ref, weight_ref, *refs):
    terms, out_ref = refs[:-1], refs[-1]
    lhs = jnp.concatenate([mine_ref[...], near_ref[...]], axis=0)
    product = jnp.dot(lhs, weight_ref[...], preferred_element_type=F32)
    out_ref[...] = sum((ref[...] for ref in terms), sign * product)


def target_part(sign, terms, mine, near, weight, chip):
    rows, width = mine.shape
    outs = weight.shape[1]
    wide = 2 * BLK if outs % (2 * BLK) == 0 else BLK
    block = pl.BlockSpec((2 * rows, wide), lambda n, s: (0, n))
    return pl.pallas_call(
        functools.partial(target_kernel, sign),
        grid_spec=pltpu.PrefetchScalarGridSpec(
            num_scalar_prefetch=1,
            grid=(outs // wide,),
            in_specs=[whole_spec(mine), whole_spec(near)]
            + [pl.BlockSpec((width, wide), lambda n, s: (s[0], n))]
            + [block] * len(terms),
            out_specs=block,
        ),
        out_shape=jax.ShapeDtypeStruct((2 * rows, outs), F32),
        compiler_params=pltpu.CompilerParams(vmem_limit_bytes=40 * 2**20),
        cost_estimate=SMALL,
        name="target_part",
    )(jnp.reshape(chip, (1,)).astype(jnp.int32), mine, near, weight, *terms)


TN = (((0,), (0,)), ((), ()))
NT = (((1,), (1,)), ((), ()))
WIDE = 8


def natural(step, chip, per_chip):
    return lax.rem(chip + step // per_chip, 2) * per_chip + lax.rem(step, per_chip)


def spread_left(z, rows_ref, out_ref, scratch):
    groups = out_ref.shape[0]
    parts, _, size = rows_ref.shape
    blocks = size // 2
    share = blocks // parts
    fold = BLK // blocks
    begin = rows_ref.shape[1] - groups * fold // 2 * share
    scratch[...] = jnp.zeros_like(scratch)
    low = lax.broadcasted_iota(jnp.int32, (blocks, size), 1) < blocks
    for g in range(groups):
        for pair in range(fold // 2):
            row = begin + (g * (fold // 2) + pair) * share
            picked = [
                rows_ref[z ^ owner, row : row + share, :] for owner in range(parts)
            ]
            turned = jnp.concatenate(picked + picked, axis=0).astype(F32).T
            for a in range(2):
                value = turned[a * blocks : (a + 1) * blocks]
                value = jnp.where(low if a == 0 else ~low, value, 0.0)
                lanes = slice(pair * size, (pair + 1) * size)
                for c in range(blocks // WIDE):
                    row = (c * fold + 2 * pair + a) * WIDE
                    scratch[row : row + WIDE, lanes] = value[c * WIDE : (c + 1) * WIDE]
        out_ref[g] = scratch[...].astype(BF16)


def student_kernel(steps, late, tensor_count, idx_ref, *refs):
    tokens, refs = refs[: 8 if late else 4], refs[8 if late else 4 :]
    rights, left_ref, refs = refs[:2], refs[2], refs[3:]
    step = pl.program_id(0)
    if late:
        target_ref, mixed_ref, student_ref, spread = refs
    else:
        mixed_ref, student_ref, diag_ref, spread, scratch = refs
        rows_ref, left_ref = left_ref, diag_ref
        pl.when(step == 0)(lambda: spread_left(idx_ref[3], rows_ref, diag_ref, scratch))
    pair = natural(step, idx_ref[2], steps // 2)
    groups = left_ref.shape[0]
    size = spread.shape[2]
    pairs = spread.shape[1] // WIDE
    share = BLK // groups

    @pl.when(step == 0)
    def _():
        spread[...] = jnp.zeros_like(spread)

    def mix(pieces):
        for half, right_ref in enumerate(rights):
            for t in range(WIDE):
                value = right_ref[0, t * pairs : (t + 1) * pairs, :].astype(F32)
                spread[t, pl.ds(t, pairs, stride=WIDE), :] = value
            factor = jnp.concatenate([spread[t] for t in range(WIDE)], axis=1).astype(BF16)
            lanes = slice(half * WIDE * size, (half + 1) * WIDE * size)
            rows = jnp.concatenate([piece[:, lanes] for piece in pieces], axis=0)
            part = lax.dot_general(factor, rows, NT, preferred_element_type=F32).astype(BF16)
            start = pl.multiple_of((2 * pair + half) * share, share)
            for g in range(groups):
                mixed_ref[g, pl.ds(start, share), :] = part[g * share : (g + 1) * share]

    if late:
        pl.when(step < steps // 2)(lambda: mix(tokens[:4]))
        pl.when(step >= steps // 2)(lambda: mix(tokens[4:]))
    else:
        mix(tokens)

    @pl.when(step == steps - 1)
    def _():
        for g in range(groups):
            span = slice(g * BLK, (g + 1) * BLK)
            student = lax.dot_general(
                mixed_ref[g], left_ref[g], TN, preferred_element_type=F32
            )
            student = student * (1.0 / tensor_count)
            student_ref[:, span] = student - target_ref[:, span] if late else student


def token_specs(half, width, chunk, late):
    def specs(place):
        return [
            pl.BlockSpec((half, width), lambda n, s, p=p: (s[p % 2], place(n, s)))
            for p in range(4)
        ]

    if not late:
        return specs(chunk)

    def inner(n, s):
        return lax.rem(chunk(n, s), 2)

    return specs(inner) + [pl.BlockSpec((half, width), lambda n, s: (0, inner(n, s)))] * 4


def student_part(tokens, scalars, factors, pairs, tensor_count, late=()):
    size = factors.shape[2]
    half = tokens[0].shape[0] // 2
    blocks = size // 2
    groups = pairs * blocks // BLK
    steps = blocks // (2 * WIDE)

    def chunk(n, s):
        return natural(n, s[2], steps // 2)

    def right_spec(half):
        return pl.BlockSpec(
            (1, WIDE * pairs, size), lambda n, s: (s[3] ^ chunk(n, s), half, 0)
        )

    diag = (groups, BLK, BLK)
    shapes = [
        jax.ShapeDtypeStruct((groups, BLK, 4 * half), BF16),
        jax.ShapeDtypeStruct((4 * half, groups * BLK), F32),
    ]
    scratch = [pltpu.VMEM((WIDE, pairs * WIDE, size), F32)]
    extra = list(late)
    if not late:
        shapes.append(jax.ShapeDtypeStruct(diag, BF16))
        scratch.append(pltpu.VMEM((BLK, BLK), F32))
        extra = [factors]
    return pl.pallas_call(
        functools.partial(student_kernel, steps, bool(late), tensor_count),
        grid_spec=pltpu.PrefetchScalarGridSpec(
            num_scalar_prefetch=1,
            grid=(steps,),
            in_specs=token_specs(half, 2 * WIDE * size, chunk, bool(late))
            + [right_spec(0), right_spec(1)]
            + [whole_spec(array) for array in extra],
            out_specs=[whole_spec(shape) for shape in shapes],
            scratch_shapes=scratch,
        ),
        out_shape=shapes,
        compiler_params=pltpu.CompilerParams(vmem_limit_bytes=40 * 2**20),
        cost_estimate=LARGE,
        name="student_part",
    )(scalars, *tokens, factors, factors, *extra)


def place(z, owner):
    bits = z ^ owner
    return lax.rem(bits, 2) * 2 + bits // 2


def left_kernel(chunks, scale, idx_ref, *refs):
    hidden, refs = refs[:4], refs[4:]
    weight_ref, rest0, rest1, mixed0, mixed1, left_ref, out_ref, back_ref, lhs = refs
    step = pl.program_id(0)
    parts, size = out_ref.shape[0], out_ref.shape[2]
    blocks = chunks * WIDE
    share = BLK // chunks
    fold = BLK // blocks
    pl.when(step == 0)(lambda: fill_rows(lhs, hidden))
    target = jnp.dot(lhs[...], weight_ref[...], preferred_element_type=F32)
    rest = jnp.concatenate([rest0[...], rest1[...]], axis=0)
    out_grad = ((rest - target) * scale).astype(BF16)
    mixed = jnp.concatenate([mixed0[0], mixed1[0]], axis=1)
    left = jnp.dot(mixed, out_grad, preferred_element_type=F32)
    value = lax.dot_general(left_ref[0], out_grad, NT, preferred_element_type=F32)
    value = value.astype(BF16)
    for c in range(chunks):
        back_ref[c] = value[c * share : (c + 1) * share]
    low = lax.broadcasted_iota(jnp.int32, (blocks, size), 1) < blocks
    rows = blocks // parts
    for pair in range(fold // 2):
        lanes = slice(pair * size, (pair + 1) * size)
        picked = []
        for a in (2 * pair, 2 * pair + 1):
            for c in range(chunks):
                begin = (c * fold + a) * WIDE
                picked.append(left[begin : begin + WIDE, lanes])
        turned = jnp.concatenate(picked, axis=0).T
        both = jnp.where(low, turned[:blocks], turned[blocks:]).astype(BF16)
        begin = pl.multiple_of((step * (fold // 2) + pair) * rows, rows)
        for owner in range(parts):
            out_ref[place(idx_ref[3], owner), pl.ds(begin, rows), :] = both[
                owner * rows : (owner + 1) * rows
            ]


def left_grads(hidden, weight, rest, mixed, left_diag, scalars, parts, pairs, size, scale):
    groups, count = left_diag.shape[0], 2 * rest[0].shape[0]
    width = hidden[0].shape[1]
    blocks = groups * BLK // pairs
    chunks = blocks // WIDE
    share = BLK // chunks
    column = pl.BlockSpec((count // 2, BLK), lambda n, s: (0, n))
    slab = pl.BlockSpec((1, BLK, count // 2), lambda n, s: (n, 0, 0))
    out_rows = pairs * blocks * blocks // size // parts
    return pl.pallas_call(
        functools.partial(left_kernel, chunks, scale),
        grid_spec=pltpu.PrefetchScalarGridSpec(
            num_scalar_prefetch=1,
            grid=(groups,),
            in_specs=[whole_spec(piece) for piece in hidden]
            + [pl.BlockSpec((width, BLK), lambda n, s: (1 - s[2], n))]
            + [column, column, slab, slab]
            + [pl.BlockSpec((1, BLK, BLK), lambda n, s: (n, 0, 0))],
            out_specs=[
                pl.BlockSpec((parts, out_rows, size), lambda n, s: (0, 0, 0)),
                pl.BlockSpec((chunks, share, count), lambda n, s: (0, n, 0)),
            ],
            scratch_shapes=[pltpu.VMEM((count, width), BF16)],
        ),
        out_shape=[
            jax.ShapeDtypeStruct((parts, out_rows, size), BF16),
            jax.ShapeDtypeStruct((chunks, groups * share, count), BF16),
        ],
        compiler_params=pltpu.CompilerParams(vmem_limit_bytes=40 * 2**20),
        cost_estimate=SMALL,
        name="left_grads",
    )(scalars, *hidden, weight, *rest, *mixed, left_diag)


def right_kernel(pairs, bit, idx_ref, *refs):
    own, near, far, (back_ref, out_ref, wide) = refs[:4], refs[4:8], refs[8:12], refs[12:]
    size = out_ref.shape[2]
    owner = idx_ref[3] ^ (2 * pl.program_id(0) + bit)

    def right(later):
        for half in range(2):
            lanes = slice(half * WIDE * size, (half + 1) * WIDE * size)
            rows = jnp.concatenate([piece[:, lanes] for piece in own + later], axis=0)
            value = jnp.dot(back_ref[half], rows, preferred_element_type=F32)
            for t in range(WIDE):
                wide[t] = value[:, t * size : (t + 1) * size]
            for t in range(WIDE):
                begin = (half * WIDE + t) * pairs
                out_ref[0, begin : begin + pairs, :] = wide[
                    t, pl.ds(t, pairs, stride=WIDE), :
                ].astype(BF16)

    pl.when(owner // 2 == idx_ref[2])(lambda: right(near))
    pl.when(owner // 2 != idx_ref[2])(lambda: right(far))


def right_grads(back, own, late, scalars, pairs, bit, size, cost):
    half = late[0].shape[0] // 2
    rows, count = back.shape[1:]

    def owner(n, s):
        return s[3] ^ (2 * n + bit)

    return pl.pallas_call(
        functools.partial(right_kernel, pairs, bit),
        grid_spec=pltpu.PrefetchScalarGridSpec(
            num_scalar_prefetch=1,
            grid=(2,),
            in_specs=token_specs(half, 2 * WIDE * size, owner, False)
            + token_specs(half, 2 * WIDE * size, owner, True)
            + [pl.BlockSpec((2, rows, count), lambda n, s: (owner(n, s), 0, 0))],
            out_specs=pl.BlockSpec((1, 2 * WIDE * pairs, size), lambda n, s: (n, 0, 0)),
            scratch_shapes=[pltpu.VMEM((WIDE, pairs * WIDE, size), F32)],
        ),
        out_shape=jax.ShapeDtypeStruct((2, 2 * WIDE * pairs, size), BF16),
        compiler_params=pltpu.CompilerParams(vmem_limit_bytes=40 * 2**20),
        cost_estimate=cost,
        name="right_grads",
    )(scalars, *own, *late, back)


def tiled_body(tokens, gate_weight, up_weight, down_weight, right_factor, left_factor):
    fsdp_count = lax.axis_size("fsdp")
    tensor_count = lax.axis_size("tensor")
    rows, model = tokens.shape
    part = gate_weight.shape[1] // 2
    me, z = lax.axis_index("fsdp"), lax.axis_index("tensor")
    chip, core, odd = lax.div(me, 2), lax.rem(me, 2), lax.rem(z, 2)
    both_axes = ("fsdp", "tensor")

    def swap(value):
        return lax.ppermute(value, "fsdp", [(i, i ^ 1) for i in range(fsdp_count)])

    def across(value):
        return lax.ppermute(value, "fsdp", [(i, i ^ 2) for i in range(fsdp_count)])

    def along(value, bit):
        return lax.ppermute(value, "tensor", [(i, i ^ bit) for i in range(tensor_count)])

    def turn(value, bit):
        perm = []
        for f in range(fsdp_count):
            for t in range(tensor_count):
                perm.append((f * tensor_count + t, (t ^ bit) * tensor_count + f))
        return lax.ppermute(value, both_axes, perm)

    def after(value, *others):
        return lax.optimization_barrier((value,) + others)[0]

    def add(*terms):
        return sum(term.astype(F32) for term in terms)

    near_tokens = swap(tokens)
    first = cut_tokens(tokens, rows, jnp.int32(0), 1 - chip)
    arrived = across(first)
    base = jnp.stack([odd, 1 - odd])
    mine_block = lax.div(part, BLK) * chip
    other_block = lax.div(part, BLK) * (1 - chip)

    def scalars(block):
        return jnp.concatenate([base, jnp.stack([me, core, block])]).astype(jnp.int32)

    own_pieces = [(t, row, 2) for t in (tokens, near_tokens) for row in (0, 1)]
    mine, other = products(
        own_pieces, after(scalars(other_block), first), gate_weight, up_weight, 0, part
    )

    pairs, blocks = left_factor.shape[0], left_factor.shape[2]
    left_rows = left_factor.reshape(pairs // 2, 2, -1, blocks).transpose(0, 2, 1, 3)
    turned = turn(after(right_factor, mine), 0)
    rest = cut_tokens(after(tokens, mine), rows // 2, odd, chip, LARGE)
    factors = jnp.concatenate(
        [after(turned, rest).reshape(-1, LANES), left_rows.reshape(-1, LANES)], axis=0
    )[None]
    more = along(factors, 1)
    sums = add(mine[0], swap(other[0])).astype(BF16)
    arrived = after(arrived, more, rest, sums)
    got_early = across(sums)
    late_first = across(after(rest, sums))
    factors = join(after(factors, arrived), more)
    more = along(factors, 2)

    order = jnp.concatenate([base, jnp.stack([chip, z])]).astype(jnp.int32)
    own = [tokens, tokens, near_tokens, near_tokens]
    near_arrived = swap(arrived)
    late = [arrived, arrived, near_arrived, near_arrived]
    late_pieces = [(t, row, 3) for t in (arrived, near_arrived) for row in (0, 1)]
    late_order = after(scalars(other_block), factors)
    mine, other = products(late_pieces, late_order, gate_weight, up_weight, 0, part)
    near = swap(other[0])
    mine_order = after(scalars(mine_block), mine)
    kept, other = products(
        own_pieces + late_pieces, mine_order, gate_weight, up_weight, 0, part
    )
    sums = add(mine[0], after(near, kept)).astype(BF16)
    got = across(sums)
    near_kept = swap(after(other, got_early, late_first, more, sums))

    factors = jnp.concatenate([factors, after(more, kept)], axis=0)
    def activate(u, term):
        total = add(kept[u], near_kept[u], term)
        return (jax.nn.silu(total[0]) * total[1]).astype(BF16)

    hidden1 = activate(1, got_early)
    got1 = across(hidden1)
    near1 = swap(hidden1)
    late_partner = along(after(late_first, hidden1), 1)
    mixed0, rest0, left_diag = student_part(
        [after(tokens, hidden1, sums)] + own[1:], order, factors, pairs, tensor_count
    )
    target1 = target_part(1.0, [], hidden1, after(near1, mixed0), down_weight, chip)
    hidden0 = activate(0, after(got, target1))
    got0 = across(hidden0)
    near0 = swap(hidden0)
    late_partner = after(late_partner, mixed0)
    late += [late_first, late_partner, swap(late_first), swap(late_partner)]
    mixed1, rest1 = student_part(
        [after(late[0], hidden0)] + late[1:],
        order,
        factors,
        pairs,
        tensor_count,
        (left_diag, target1),
    )
    near0 = after(near0, mixed1)
    rest0 = target_part(-1.0, [rest0], hidden0, near0, down_weight, chip)
    got1, got0 = after(got1, mixed1), after(got0, rest0)
    hidden = [got0, got1, swap(got0), swap(got1)]

    size = right_factor.shape[2]
    left, back = left_grads(
        hidden,
        down_weight,
        (rest0, rest1),
        (mixed0, mixed1),
        left_diag,
        order,
        tensor_count,
        pairs,
        size,
        1.0 / math.sqrt(rows * fsdp_count),
    )
    got_left = along(left[2:], 1)
    sent = right_grads(back, own, late, order, pairs, 1, size, SMALL)
    left = add(left[:2], after(got_left, sent)).astype(BF16)
    got_left = along(left[1], 2)
    got_right = along(sent, 1)
    kept_back = after(back, sent, left)
    right = right_grads(kept_back, own, late, order, pairs, 0, size, LARGE)
    right = add(right, got_right).astype(BF16)
    grad_right = add(turn(right[0], 0), turn(right[1], 2))
    grad_left = add(left[0], got_left)
    grad_left = grad_left.reshape(pairs // 2, -1, 2, blocks).transpose(0, 2, 1, 3)
    return grad_right.reshape(right_factor.shape), grad_left.reshape(left_factor.shape)


def body(*args):
    tokens, gate_weight, _, _, right_factor, left_factor = args
    counts = (lax.axis_size("fsdp"), lax.axis_size("tensor"))
    feat, hid = gate_weight.shape
    per_owner, share, size = right_factor.shape
    blocks = left_factor.shape[2]
    fits = hid % (2 * BLK) == 0
    fits = fits and counts == (4, 4) and tokens.shape[0] == 128
    fits = fits and hid >= 4 * BLK and feat % BLK == 0
    fits = fits and size == 128 and 2 * blocks == size and per_owner % WIDE == 0
    fits = fits and left_factor.shape[0] == share and share % 16 == 0
    return (tiled_body if fits else general_body)(*args)


def solution(mesh):
    return jax.shard_map(
        body,
        mesh=mesh,
        in_specs=(
            P(("groups", "fsdp"), None),
            P("fsdp", "tensor"),
            P("fsdp", "tensor"),
            P("tensor", "fsdp"),
            P("fsdp", "tensor", None),
            P("fsdp", "tensor", None),
        ),
        out_specs=(P(("groups", "fsdp"), "tensor", None), P(("groups", "fsdp"), "tensor", None)),
        check_vma=False,
    )
```

```python
import functools
import math

import jax
import jax.numpy as jnp
from jax import lax
from jax.experimental import pallas as pl
from jax.experimental.pallas import tpu as pltpu
from jax.sharding import PartitionSpec as P

BLK = 256
LANES = 128
SMALL = pl.CostEstimate(flops=1, bytes_accessed=1, transcendentals=0)
LARGE = pl.CostEstimate(flops=10**10, bytes_accessed=10**7, transcendentals=0)
F32 = jnp.float32
BF16 = jnp.bfloat16


def gate_up_kernel(idx_ref, top_ref, bottom_ref, gate_ref, up_ref, mine_ref, other_ref):
    rows = top_ref.shape[0]
    lhs = jnp.concatenate([top_ref[...], bottom_ref[...]], axis=0)
    for slot, weight_ref in enumerate((gate_ref, up_ref)):
        product = jnp.dot(lhs, weight_ref[...], preferred_element_type=F32).astype(BF16)
        mine_ref[slot] = product[:rows]
        other_ref[slot] = product[rows:]


def gate_up(top, top_block, bottom, gate, up, column, first, width):
    rows, feat = bottom.shape
    if width % BLK or gate.shape[1] % BLK or rows % 16 or feat % 128:
        lhs = jnp.concatenate(
            [lax.dynamic_slice_in_dim(top, top_block * feat, feat, 1), bottom], axis=0
        )
        both = [
            jnp.dot(
                lhs,
                lax.dynamic_slice_in_dim(w, column + first, width, 1),
                preferred_element_type=F32,
            ).astype(BF16)
            for w in (gate, up)
        ]
        both = jnp.stack(both)
        return both[:, :rows], both[:, rows:]
    scalars = jnp.stack([top_block, lax.div(column, BLK) + first // BLK]).astype(jnp.int32)
    weight_spec = pl.BlockSpec((feat, BLK), lambda n, s: (0, s[1] + n))
    out_spec = pl.BlockSpec((2, rows, BLK), lambda n, s: (0, 0, n))
    shape = jax.ShapeDtypeStruct((2, rows, width), BF16)
    return pl.pallas_call(
        gate_up_kernel,
        grid_spec=pltpu.PrefetchScalarGridSpec(
            num_scalar_prefetch=1,
            grid=(width // BLK,),
            in_specs=[
                pl.BlockSpec((rows, feat), lambda n, s: (0, s[0])),
                pl.BlockSpec((rows, feat), lambda n, s: (0, 0)),
                weight_spec,
                weight_spec,
            ],
            out_specs=[out_spec, out_spec],
        ),
        out_shape=[shape, shape],
        compiler_params=pltpu.CompilerParams(vmem_limit_bytes=40 * 2**20),
        cost_estimate=pl.CostEstimate(
            flops=2 * 2 * rows * feat * 2 * width,
            bytes_accessed=2 * feat * 2 * width + 2 * 2 * rows * (feat + 2 * width),
            transcendentals=0,
        ),
        name="gate_up",
    )(scalars, top, bottom, gate, up)


def down_kernel(idx_ref, mine_ref, other_ref, weight_ref, *refs):
    out_ref = refs[-1]
    lhs = jnp.concatenate([mine_ref[...], other_ref[...]], axis=0)
    product = jnp.dot(lhs, weight_ref[...], preferred_element_type=F32)

    @pl.when(pl.program_id(0) == 0)
    def _():
        out_ref[...] = refs[0][...] + product if len(refs) > 1 else product

    @pl.when(pl.program_id(0) > 0)
    def _():
        out_ref[...] += product


def down_add(total, mine, other, weight, row):
    rows, width = mine.shape
    outs = weight.shape[1]
    if width % BLK or weight.shape[0] % BLK or rows % 16 or outs % 128:
        lhs = jnp.concatenate([mine, other], axis=0)
        part = lax.dynamic_slice_in_dim(weight, row, width, 0)
        product = jnp.dot(lhs, part, preferred_element_type=F32)
        return product if total is None else total + product
    scalars = jnp.reshape(lax.div(row, BLK), (1,)).astype(jnp.int32)
    hidden_spec = pl.BlockSpec((rows, BLK), lambda k, s: (0, k))
    whole = pl.BlockSpec((2 * rows, outs), lambda k, s: (0, 0))
    totals = [] if total is None else [total]
    return pl.pallas_call(
        down_kernel,
        grid_spec=pltpu.PrefetchScalarGridSpec(
            num_scalar_prefetch=1,
            grid=(width // BLK,),
            in_specs=[
                hidden_spec,
                hidden_spec,
                pl.BlockSpec((BLK, outs), lambda k, s: (s[0] + k, 0)),
            ]
            + [whole] * len(totals),
            out_specs=whole,
        ),
        out_shape=jax.ShapeDtypeStruct((2 * rows, outs), F32),
        compiler_params=pltpu.CompilerParams(vmem_limit_bytes=40 * 2**20),
        cost_estimate=pl.CostEstimate(
            flops=2 * 2 * rows * width * outs,
            bytes_accessed=2 * width * outs + 2 * 2 * rows * width + 16 * rows * outs,
            transcendentals=0,
        ),
        name="down_add",
    )(scalars, mine, other, weight, *totals)


def general_body(tokens, gate_weight, up_weight, down_weight, right_factor, left_factor):
    fsdp_count = lax.axis_size("fsdp")
    tensor_count = lax.axis_size("tensor")
    chips = fsdp_count // 2
    rows, model = tokens.shape
    feat, hid = gate_weight.shape
    part = hid // chips
    me = lax.axis_index("fsdp")
    chip, core = lax.div(me, 2), lax.rem(me, 2)
    z = lax.axis_index("tensor")

    def swap(value):
        return lax.ppermute(value, "fsdp", [(i, i ^ 1) for i in range(fsdp_count)])

    def shift(value, hops):
        perm = [(i, (i + 2 * hops) % fsdp_count) for i in range(fsdp_count)]
        return lax.ppermute(value, "fsdp", perm)

    def gather_z(value):
        if tensor_count > 4:
            return lax.all_gather(value, "tensor", axis=0, tiled=True)
        size = value.shape[0]
        whole = jnp.zeros((size * tensor_count,) + value.shape[1:], value.dtype)
        whole = lax.dynamic_update_slice_in_dim(whole, value, z * size, 0)
        for step in range(1, tensor_count):
            perm = [(i, (i + step) % tensor_count) for i in range(tensor_count)]
            got = lax.ppermute(value, "tensor", perm)
            source = lax.rem(z - step + tensor_count, tensor_count)
            whole = lax.dynamic_update_slice_in_dim(whole, got, source * size, 0)
        return whole

    def scatter_z(value):
        if tensor_count > 4:
            return lax.psum_scatter(value, "tensor", scatter_dimension=0, tiled=False)
        total = lax.dynamic_index_in_dim(value, z, 0, keepdims=False)
        for step in range(1, tensor_count):
            target_z = lax.rem(z + step, tensor_count)
            piece = lax.dynamic_index_in_dim(value, target_z, 0, keepdims=False)
            perm = [(i, (i + step) % tensor_count) for i in range(tensor_count)]
            total += lax.ppermute(piece.astype(BF16), "tensor", perm).astype(F32)
        return total

    def columns(value, start, width):
        return lax.dynamic_slice_in_dim(value, start, width, 1)

    def after(value, *others):
        return lax.optimization_barrier((value,) + others)[0]

    def pair_z(value):
        perm = [(i, i ^ 1) for i in range(tensor_count)]
        got = lax.ppermute(value, "tensor", perm)
        odd = lax.rem(z, 2) == 1
        return jnp.concatenate(
            [jnp.where(odd, got, value), jnp.where(odd, value, got)], axis=0
        )

    if part % BLK == 0 and part // BLK > 1:
        head = (part // BLK + 1) // 2 * BLK
        chunks = [(0, head), (head, part - head)]
    else:
        chunks = [(0, part)]

    half = rows // 2
    own_half = lax.dynamic_slice_in_dim(tokens, lax.rem(z, 2) * half, half, 0)

    def send_tokens(value, dt, g):
        features = lax.rem(chip - dt + g + chips, chips) * (2 * feat)
        return shift(columns(value, features, 2 * feat), -dt)

    def partial(pair, dp, first, width):
        column = lax.rem(chip + dp, chips) * part
        top, block, bottom = pair
        mine, other = gate_up(top, block, bottom, gate_weight, up_weight, column, first, width)
        return mine, swap(other)

    def send_partials(pair, got, dt):
        sums = []
        for dp in range(1, chips):
            pieces = [partial(pair, dp, *chunk) for chunk in chunks]
            for n, (mine, from_core) in enumerate(pieces):
                both = (mine.astype(F32) + from_core.astype(F32)).astype(BF16)
                got[dt, dp, n] = shift(both, dp)
                sums.append(both)
        return sums

    got, kept, gathered = {}, {}, {}
    local = swap(columns(tokens, (me ^ 1) * feat, feat))
    arrived = {dt: send_tokens(own_half, dt, 0) for dt in range(1, chips)}
    sums = send_partials((tokens, me, local), got, 0)
    if sums:
        local = after(local, *sums)
    kept[0] = partial((tokens, me, local), 0, 0, part)
    late_tokens = after(tokens, kept[0][0])
    neighbour_tokens = swap(late_tokens)
    late_half = after(own_half, *sums) if sums else own_half

    for dt in range(1, chips):
        gathered[dt, 0] = pair_z(after(arrived[dt], *sums))
        whole = gathered[dt, 0]
        top = columns(whole, core * feat, feat)
        bottom = swap(columns(whole, (1 - core) * feat, feat))
        pair = (top, jnp.int32(0), bottom)
        sums = send_partials(pair, got, dt)
        pair = (top, jnp.int32(0), after(bottom, *sums))
        kept[dt] = partial(pair, 0, 0, part)
        for g in range(1, chips):
            gathered[dt, g] = pair_z(after(send_tokens(late_half, dt, g), kept[dt][0]))

    def activate(e, first, width, n):
        terms = [lax.slice_in_dim(term, first, first + width, axis=2) for term in kept[e]]
        terms += [got[(e + dp) % chips, dp, n] for dp in range(1, chips)]
        total = sum(term.astype(F32) for term in terms)
        return (jax.nn.silu(total[0]) * total[1]).astype(BF16)

    totals = {u: None for u in range(chips)}
    for e in list(range(1, chips)) + [0]:
        values = [activate(e, *chunk, n) for n, chunk in enumerate(chunks)]
        spans = list(chunks)
        if e:
            values, spans = [jnp.concatenate(values, axis=1)], [(0, part)]
        sent = [[value] + [shift(value, d) for d in range(1, chips)] for value in values]
        for (first, width), copies in zip(spans, sent):
            for d, mine in enumerate(copies):
                u = (e - d + chips) % chips
                row = lax.rem(chip - d + chips, chips) * part + first
                totals[u] = down_add(totals[u], mine, swap(mine), down_weight, row)

    token_rows = []
    for dt in range(chips):
        if dt == 0:
            token_rows += [tokens, neighbour_tokens]
            continue
        else:
            full = jnp.zeros((rows, model), BF16)
            for g in range(chips):
                features = lax.rem(chip + g, chips) * (2 * feat)
                full = lax.dynamic_update_slice_in_dim(full, gathered[dt, g], features, 1)
        token_rows += [full, swap(full)]
    inputs = jnp.concatenate(token_rows, axis=0)
    count = inputs.shape[0]

    blocks, share, size = right_factor.shape
    ratio = tensor_count // fsdp_count
    turn = []
    for a in range(fsdp_count):
        for b in range(tensor_count):
            turn.append((a * tensor_count + b, (b // ratio) * tensor_count + a * ratio + b % ratio))
    back = [(b, a) for a, b in turn]
    right_rows = gather_z(lax.ppermute(right_factor, ("fsdp", "tensor"), turn)[None])
    right_rows = right_rows.reshape(fsdp_count, ratio, blocks, share, size)
    right_rows = right_rows.transpose(0, 2, 1, 3, 4).reshape(
        fsdp_count * blocks, ratio * share, size
    )
    left_rows = jnp.moveaxis(gather_z(jnp.moveaxis(left_factor, 1, 0)), 0, 1)

    block_input = inputs.reshape(count, fsdp_count * blocks, size)
    mixed = jnp.einsum(
        "nim,ijm->nij", block_input, right_rows, preferred_element_type=F32
    ).astype(BF16)
    student = jnp.einsum("nij,jki->njk", mixed, left_rows, preferred_element_type=F32)
    target = jnp.concatenate([totals[u] for u in range(chips)], axis=0)
    scale = 1.0 / math.sqrt(count)
    out_grad = (student * (1.0 / tensor_count) - target.reshape(student.shape)) * scale
    out_grad = out_grad.astype(BF16)
    grad_left = jnp.einsum("njk,nij->kji", out_grad, mixed, preferred_element_type=F32)
    mixed_grad = jnp.einsum(
        "njk,jki->nij", out_grad, left_rows, preferred_element_type=F32
    ).astype(BF16)
    grad_right = jnp.einsum(
        "nij,nim->ijm", mixed_grad, block_input, preferred_element_type=F32
    )
    grad_left = scatter_z(
        grad_left.reshape((tensor_count, -1) + grad_left.shape[1:])
    )
    grad_left = jnp.moveaxis(grad_left, 0, 1)
    grad_right = grad_right.reshape(fsdp_count, blocks, ratio, share, size)
    grad_right = grad_right.transpose(0, 2, 1, 3, 4).reshape(
        tensor_count, blocks, share, size
    )
    grad_right = lax.ppermute(scatter_z(grad_right), ("fsdp", "tensor"), back)
    return grad_right, grad_left


def cut_kernel(idx_ref, in_ref, out_ref):
    out_ref[...] = in_ref[...]


def cut_tokens(tokens, rows, row, column, cost=SMALL):
    width = tokens.shape[1] // 2
    steps = 4
    return pl.pallas_call(
        cut_kernel,
        grid_spec=pltpu.PrefetchScalarGridSpec(
            num_scalar_prefetch=1,
            grid=(steps,),
            in_specs=[pl.BlockSpec((rows, width // steps), lambda n, s: (s[0], s[1] * steps + n))],
            out_specs=pl.BlockSpec((rows, width // steps), lambda n, s: (0, n)),
        ),
        out_shape=jax.ShapeDtypeStruct((rows, width), BF16),
        cost_estimate=cost,
        name="cut_tokens",
    )(jnp.stack([row, column]).astype(jnp.int32), tokens)


def pack_kernel(left_ref, out_ref):
    share = left_ref.shape[1]
    for pair in range(left_ref.shape[0] // 2):
        both = [left_ref[2 * pair].astype(F32), left_ref[2 * pair + 1].astype(F32)]
        both = jnp.concatenate(both, axis=1)
        out_ref[pair * share : (pair + 1) * share, :] = both.astype(BF16)


def pack_left(left):
    pairs, share, blocks = left.shape
    return pl.pallas_call(
        pack_kernel,
        out_shape=jax.ShapeDtypeStruct((pairs // 2 * share, 2 * blocks), BF16),
        cost_estimate=LARGE,
        name="pack_left",
    )(left)


def products_kernel(sets, idx_ref, *refs):
    pieces, (gate_ref, up_ref, mine_ref, other_ref) = refs[: 4 * sets], refs[4 * sets :]
    lhs = jnp.concatenate([piece[...] for piece in pieces], axis=0)
    rows = mine_ref.shape[2]
    for slot, weight_ref in enumerate((gate_ref, up_ref)):
        product = jnp.dot(lhs, weight_ref[...], preferred_element_type=F32).astype(BF16)
        for u in range(sets):
            mine_ref[u, slot] = product[2 * u * rows : (2 * u + 1) * rows]
            other_ref[u, slot] = product[(2 * u + 1) * rows : (2 * u + 2) * rows]


def products(pieces, scalars, gate, up, first, width):
    feat = gate.shape[0]
    sets = len(pieces) // 4
    half = pieces[0][0].shape[0] // (1 if pieces[0][1] is None else 2)
    start = first // BLK

    def piece_spec(row, column):
        if row is None:
            return pl.BlockSpec((half, feat), lambda n, s: (0, s[column]))
        return pl.BlockSpec((half, feat), lambda n, s: (s[row], s[column]))

    weight_spec = pl.BlockSpec(
        (feat, BLK), lambda n, s: (0, s[4] + start + n)
    )
    out_spec = pl.BlockSpec((sets, 2, 2 * half, BLK), lambda n, s: (0, 0, 0, n))
    shape = jax.ShapeDtypeStruct((sets, 2, 2 * half, width), BF16)
    return pl.pallas_call(
        functools.partial(products_kernel, sets),
        grid_spec=pltpu.PrefetchScalarGridSpec(
            num_scalar_prefetch=1,
            grid=(width // BLK,),
            in_specs=[piece_spec(row, column) for _, row, column in pieces]
            + [weight_spec, weight_spec],
            out_specs=[out_spec, out_spec],
        ),
        out_shape=[shape, shape],
        compiler_params=pltpu.CompilerParams(vmem_limit_bytes=40 * 2**20),
        cost_estimate=LARGE if sets > 1 else SMALL,
        name="gate_up_products",
    )(scalars, *[piece for piece, _, _ in pieces], gate, up)


def fill_rows(lhs, pieces):
    rows = pieces[0].shape[0]
    for place, which in enumerate((1, 3, 0, 2)):
        lhs[place * rows : (place + 1) * rows, :] = pieces[which][...]


def whole_spec(array):
    return pl.BlockSpec(array.shape, lambda n, s: (0,) * len(array.shape))


def target_kernel(sign, idx_ref, mine_ref, near_ref, weight_ref, *refs):
    terms, out_ref = refs[:-1], refs[-1]
    lhs = jnp.concatenate([mine_ref[...], near_ref[...]], axis=0)
    product = jnp.dot(lhs, weight_ref[...], preferred_element_type=F32)
    out_ref[...] = sum((ref[...] for ref in terms), sign * product)


def target_part(sign, terms, mine, near, weight, chip):
    rows, width = mine.shape
    outs = weight.shape[1]
    wide = 2 * BLK if outs % (2 * BLK) == 0 else BLK
    block = pl.BlockSpec((2 * rows, wide), lambda n, s: (0, n))
    return pl.pallas_call(
        functools.partial(target_kernel, sign),
        grid_spec=pltpu.PrefetchScalarGridSpec(
            num_scalar_prefetch=1,
            grid=(outs // wide,),
            in_specs=[whole_spec(mine), whole_spec(near)]
            + [pl.BlockSpec((width, wide), lambda n, s: (s[0], n))]
            + [block] * len(terms),
            out_specs=block,
        ),
        out_shape=jax.ShapeDtypeStruct((2 * rows, outs), F32),
        compiler_params=pltpu.CompilerParams(vmem_limit_bytes=40 * 2**20),
        cost_estimate=SMALL,
        name="target_part",
    )(jnp.reshape(chip, (1,)).astype(jnp.int32), mine, near, weight, *terms)


TN = (((0,), (0,)), ((), ()))
NT = (((1,), (1,)), ((), ()))
WIDE = 8


def natural(step, chip, per_chip):
    return lax.rem(chip + step // per_chip, 2) * per_chip + lax.rem(step, per_chip)


def spread_left(z, rows_ref, out_ref, scratch):
    groups = out_ref.shape[0]
    parts, _, size = rows_ref.shape
    blocks = size // 2
    share = blocks // parts
    fold = BLK // blocks
    begin = rows_ref.shape[1] - groups * fold // 2 * share
    scratch[...] = jnp.zeros_like(scratch)
    low = lax.broadcasted_iota(jnp.int32, (blocks, size), 1) < blocks
    for g in range(groups):
        for pair in range(fold // 2):
            row = begin + (g * (fold // 2) + pair) * share
            picked = [
                rows_ref[z ^ owner, row : row + share, :] for owner in range(parts)
            ]
            turned = jnp.concatenate(picked + picked, axis=0).astype(F32).T
            for a in range(2):
                value = turned[a * blocks : (a + 1) * blocks]
                value = jnp.where(low if a == 0 else ~low, value, 0.0)
                lanes = slice(pair * size, (pair + 1) * size)
                for c in range(blocks // WIDE):
                    row = (c * fold + 2 * pair + a) * WIDE
                    scratch[row : row + WIDE, lanes] = value[c * WIDE : (c + 1) * WIDE]
        out_ref[g] = scratch[...].astype(BF16)


def student_kernel(steps, late, tensor_count, idx_ref, *refs):
    tokens, refs = refs[: 8 if late else 4], refs[8 if late else 4 :]
    rights, left_ref, refs = refs[:2], refs[2], refs[3:]
    step = pl.program_id(0)
    if late:
        target_ref, mixed_ref, student_ref, spread = refs
    else:
        mixed_ref, student_ref, diag_ref, spread, scratch = refs
        rows_ref, left_ref = left_ref, diag_ref
        pl.when(step == 0)(lambda: spread_left(idx_ref[3], rows_ref, diag_ref, scratch))
    pair = natural(step, idx_ref[2], steps // 2)
    groups = left_ref.shape[0]
    size = spread.shape[2]
    pairs = spread.shape[1] // WIDE
    share = BLK // groups

    @pl.when(step == 0)
    def _():
        spread[...] = jnp.zeros_like(spread)

    def mix(pieces):
        for half, right_ref in enumerate(rights):
            for t in range(WIDE):
                value = right_ref[0, t * pairs : (t + 1) * pairs, :].astype(F32)
                spread[t, pl.ds(t, pairs, stride=WIDE), :] = value
            factor = jnp.concatenate([spread[t] for t in range(WIDE)], axis=1).astype(BF16)
            lanes = slice(half * WIDE * size, (half + 1) * WIDE * size)
            rows = jnp.concatenate([piece[:, lanes] for piece in pieces], axis=0)
            part = lax.dot_general(factor, rows, NT, preferred_element_type=F32).astype(BF16)
            start = pl.multiple_of((2 * pair + half) * share, share)
            for g in range(groups):
                mixed_ref[g, pl.ds(start, share), :] = part[g * share : (g + 1) * share]

    if late:
        pl.when(step < steps // 2)(lambda: mix(tokens[:4]))
        pl.when(step >= steps // 2)(lambda: mix(tokens[4:]))
    else:
        mix(tokens)

    @pl.when(step == steps - 1)
    def _():
        for g in range(groups):
            span = slice(g * BLK, (g + 1) * BLK)
            student = lax.dot_general(
                mixed_ref[g], left_ref[g], TN, preferred_element_type=F32
            )
            student = student * (1.0 / tensor_count)
            student_ref[:, span] = student - target_ref[:, span] if late else student


def token_specs(half, width, chunk, late):
    def specs(place):
        return [
            pl.BlockSpec((half, width), lambda n, s, p=p: (s[p % 2], place(n, s)))
            for p in range(4)
        ]

    if not late:
        return specs(chunk)

    def inner(n, s):
        return lax.rem(chunk(n, s), 2)

    return specs(inner) + [pl.BlockSpec((half, width), lambda n, s: (0, inner(n, s)))] * 4


def student_part(tokens, scalars, factors, pairs, tensor_count, late=()):
    size = factors.shape[2]
    half = tokens[0].shape[0] // 2
    blocks = size // 2
    groups = pairs * blocks // BLK
    steps = blocks // (2 * WIDE)

    def chunk(n, s):
        return natural(n, s[2], steps // 2)

    def right_spec(half):
        return pl.BlockSpec(
            (1, WIDE * pairs, size), lambda n, s: (s[3] ^ chunk(n, s), half, 0)
        )

    diag = (groups, BLK, BLK)
    shapes = [
        jax.ShapeDtypeStruct((groups, BLK, 4 * half), BF16),
        jax.ShapeDtypeStruct((4 * half, groups * BLK), F32),
    ]
    scratch = [pltpu.VMEM((WIDE, pairs * WIDE, size), F32)]
    extra = list(late)
    if not late:
        shapes.append(jax.ShapeDtypeStruct(diag, BF16))
        scratch.append(pltpu.VMEM((BLK, BLK), F32))
        extra = [factors]
    return pl.pallas_call(
        functools.partial(student_kernel, steps, bool(late), tensor_count),
        grid_spec=pltpu.PrefetchScalarGridSpec(
            num_scalar_prefetch=1,
            grid=(steps,),
            in_specs=token_specs(half, 2 * WIDE * size, chunk, bool(late))
            + [right_spec(0), right_spec(1)]
            + [whole_spec(array) for array in extra],
            out_specs=[whole_spec(shape) for shape in shapes],
            scratch_shapes=scratch,
        ),
        out_shape=shapes,
        compiler_params=pltpu.CompilerParams(vmem_limit_bytes=40 * 2**20),
        cost_estimate=LARGE,
        name="student_part",
    )(scalars, *tokens, factors, factors, *extra)


def place(z, owner):
    bits = z ^ owner
    return lax.rem(bits, 2) * 2 + bits // 2


def left_kernel(chunks, scale, idx_ref, *refs):
    hidden, refs = refs[:4], refs[4:]
    weight_ref, rest0, rest1, mixed0, mixed1, left_ref, out_ref, back_ref, lhs = refs
    step = pl.program_id(0)
    parts, size = out_ref.shape[0], out_ref.shape[2]
    blocks = chunks * WIDE
    share = BLK // chunks
    fold = BLK // blocks
    pl.when(step == 0)(lambda: fill_rows(lhs, hidden))
    target = jnp.dot(lhs[...], weight_ref[...], preferred_element_type=F32)
    rest = jnp.concatenate([rest0[...], rest1[...]], axis=0)
    out_grad = ((rest - target) * scale).astype(BF16)
    mixed = jnp.concatenate([mixed0[0], mixed1[0]], axis=1)
    left = jnp.dot(mixed, out_grad, preferred_element_type=F32)
    value = lax.dot_general(left_ref[0], out_grad, NT, preferred_element_type=F32)
    value = value.astype(BF16)
    for c in range(chunks):
        back_ref[c] = value[c * share : (c + 1) * share]
    low = lax.broadcasted_iota(jnp.int32, (blocks, size), 1) < blocks
    rows = blocks // parts
    for pair in range(fold // 2):
        lanes = slice(pair * size, (pair + 1) * size)
        picked = []
        for a in (2 * pair, 2 * pair + 1):
            for c in range(chunks):
                begin = (c * fold + a) * WIDE
                picked.append(left[begin : begin + WIDE, lanes])
        turned = jnp.concatenate(picked, axis=0).T
        both = jnp.where(low, turned[:blocks], turned[blocks:]).astype(BF16)
        begin = pl.multiple_of((step * (fold // 2) + pair) * rows, rows)
        for owner in range(parts):
            out_ref[place(idx_ref[3], owner), pl.ds(begin, rows), :] = both[
                owner * rows : (owner + 1) * rows
            ]


def left_grads(hidden, weight, rest, mixed, left_diag, scalars, parts, pairs, size, scale):
    groups, count = left_diag.shape[0], 2 * rest[0].shape[0]
    width = hidden[0].shape[1]
    blocks = groups * BLK // pairs
    chunks = blocks // WIDE
    share = BLK // chunks
    column = pl.BlockSpec((count // 2, BLK), lambda n, s: (0, n))
    slab = pl.BlockSpec((1, BLK, count // 2), lambda n, s: (n, 0, 0))
    out_rows = pairs * blocks * blocks // size // parts
    return pl.pallas_call(
        functools.partial(left_kernel, chunks, scale),
        grid_spec=pltpu.PrefetchScalarGridSpec(
            num_scalar_prefetch=1,
            grid=(groups,),
            in_specs=[whole_spec(piece) for piece in hidden]
            + [pl.BlockSpec((width, BLK), lambda n, s: (1 - s[2], n))]
            + [column, column, slab, slab]
            + [pl.BlockSpec((1, BLK, BLK), lambda n, s: (n, 0, 0))],
            out_specs=[
                pl.BlockSpec((parts, out_rows, size), lambda n, s: (0, 0, 0)),
                pl.BlockSpec((chunks, share, count), lambda n, s: (0, n, 0)),
            ],
            scratch_shapes=[pltpu.VMEM((count, width), BF16)],
        ),
        out_shape=[
            jax.ShapeDtypeStruct((parts, out_rows, size), BF16),
            jax.ShapeDtypeStruct((chunks, groups * share, count), BF16),
        ],
        compiler_params=pltpu.CompilerParams(vmem_limit_bytes=40 * 2**20),
        cost_estimate=SMALL,
        name="left_grads",
    )(scalars, *hidden, weight, *rest, *mixed, left_diag)


def right_kernel(pairs, bit, idx_ref, *refs):
    own, near, far, (back_ref, out_ref, wide) = refs[:4], refs[4:8], refs[8:12], refs[12:]
    size = out_ref.shape[2]
    owner = idx_ref[3] ^ (2 * pl.program_id(0) + bit)

    def right(later):
        for half in range(2):
            lanes = slice(half * WIDE * size, (half + 1) * WIDE * size)
            rows = jnp.concatenate([piece[:, lanes] for piece in own + later], axis=0)
            value = jnp.dot(back_ref[half], rows, preferred_element_type=F32)
            for t in range(WIDE):
                wide[t] = value[:, t * size : (t + 1) * size]
            for t in range(WIDE):
                begin = (half * WIDE + t) * pairs
                out_ref[0, begin : begin + pairs, :] = wide[
                    t, pl.ds(t, pairs, stride=WIDE), :
                ].astype(BF16)

    pl.when(owner // 2 == idx_ref[2])(lambda: right(near))
    pl.when(owner // 2 != idx_ref[2])(lambda: right(far))


def right_grads(back, own, late, scalars, pairs, bit, size, cost):
    half = late[0].shape[0] // 2
    rows, count = back.shape[1:]

    def owner(n, s):
        return s[3] ^ (2 * n + bit)

    return pl.pallas_call(
        functools.partial(right_kernel, pairs, bit),
        grid_spec=pltpu.PrefetchScalarGridSpec(
            num_scalar_prefetch=1,
            grid=(2,),
            in_specs=token_specs(half, 2 * WIDE * size, owner, False)
            + token_specs(half, 2 * WIDE * size, owner, True)
            + [pl.BlockSpec((2, rows, count), lambda n, s: (owner(n, s), 0, 0))],
            out_specs=pl.BlockSpec((1, 2 * WIDE * pairs, size), lambda n, s: (n, 0, 0)),
            scratch_shapes=[pltpu.VMEM((WIDE, pairs * WIDE, size), F32)],
        ),
        out_shape=jax.ShapeDtypeStruct((2, 2 * WIDE * pairs, size), BF16),
        compiler_params=pltpu.CompilerParams(vmem_limit_bytes=40 * 2**20),
        cost_estimate=cost,
        name="right_grads",
    )(scalars, *own, *late, back)


def tiled_body(tokens, gate_weight, up_weight, down_weight, right_factor, left_factor):
    fsdp_count = lax.axis_size("fsdp")
    tensor_count = lax.axis_size("tensor")
    rows, model = tokens.shape
    part = gate_weight.shape[1] // 2
    me, z = lax.axis_index("fsdp"), lax.axis_index("tensor")
    chip, core, odd = lax.div(me, 2), lax.rem(me, 2), lax.rem(z, 2)
    both_axes = ("fsdp", "tensor")

    def swap(value):
        return lax.ppermute(value, "fsdp", [(i, i ^ 1) for i in range(fsdp_count)])

    def across(value):
        return lax.ppermute(value, "fsdp", [(i, i ^ 2) for i in range(fsdp_count)])

    def along(value, bit):
        return lax.ppermute(value, "tensor", [(i, i ^ bit) for i in range(tensor_count)])

    def turn(value, bit):
        perm = []
        for f in range(fsdp_count):
            for t in range(tensor_count):
                perm.append((f * tensor_count + t, (t ^ bit) * tensor_count + f))
        return lax.ppermute(value, both_axes, perm)

    def after(value, *others):
        return lax.optimization_barrier((value,) + others)[0]

    def add(*terms):
        return sum(term.astype(F32) for term in terms)

    near_tokens = swap(tokens)
    first = cut_tokens(tokens, rows, jnp.int32(0), 1 - chip)
    arrived = across(first)
    base = jnp.stack([odd, 1 - odd])
    mine_block = lax.div(part, BLK) * chip
    other_block = lax.div(part, BLK) * (1 - chip)

    def scalars(block):
        return jnp.concatenate([base, jnp.stack([me, core, block])]).astype(jnp.int32)

    own_pieces = [(t, row, 2) for t in (tokens, near_tokens) for row in (0, 1)]
    mine, other = products(
        own_pieces, after(scalars(other_block), first), gate_weight, up_weight, 0, part
    )

    pairs, blocks = left_factor.shape[0], left_factor.shape[2]
    turned = turn(after(right_factor, mine), 0)
    left_rows = pack_left(after(left_factor, mine))
    factors = jnp.concatenate(
        [after(turned, left_rows).reshape(-1, LANES), left_rows], axis=0
    )[None]
    more = along(factors, 1)
    sums = add(mine[0], swap(other[0])).astype(BF16)
    rest = cut_tokens(after(tokens, left_rows), rows // 2, odd, chip)
    arrived = after(arrived, more, sums, rest)
    got_early = across(sums)
    late_first = across(after(rest, sums))
    factors = jnp.concatenate([factors, more], axis=0)

    order = jnp.concatenate([base, jnp.stack([chip, z])]).astype(jnp.int32)
    own = [tokens, tokens, near_tokens, near_tokens]
    near_arrived = swap(arrived)
    late = [arrived, arrived, near_arrived, near_arrived]
    late_pieces = [(t, row, 3) for t in (arrived, near_arrived) for row in (0, 1)]
    late_order = after(scalars(other_block), rest)
    mine, other = products(late_pieces, late_order, gate_weight, up_weight, 0, part)
    near = swap(other[0])
    mine_order = after(scalars(mine_block), mine)
    kept, other = products(
        own_pieces + late_pieces, mine_order, gate_weight, up_weight, 0, part
    )
    sums = add(mine[0], after(near, kept)).astype(BF16)
    got = across(sums)
    near_kept = swap(after(other, got_early, late_first, sums))
    factors = after(factors, kept)
    more = along(factors, 2)

    def activate(u, term):
        total = add(kept[u], near_kept[u], term)
        return (jax.nn.silu(total[0]) * total[1]).astype(BF16)

    hidden1 = activate(1, got_early)
    got1 = across(hidden1)
    near1 = swap(hidden1)
    late_partner = along(after(late_first, hidden1), 1)
    factors = jnp.concatenate([factors, after(more, hidden1)], axis=0)
    mixed0, rest0, left_diag = student_part(
        [after(tokens, hidden1, sums)] + own[1:], order, factors, pairs, tensor_count
    )
    target1 = target_part(1.0, [], hidden1, after(near1, mixed0), down_weight, chip)
    hidden0 = activate(0, after(got, target1))
    got0 = across(hidden0)
    near0 = swap(hidden0)
    late_partner = after(late_partner, mixed0)
    late += [late_first, late_partner, swap(late_first), swap(late_partner)]
    mixed1, rest1 = student_part(
        [after(late[0], hidden0)] + late[1:],
        order,
        factors,
        pairs,
        tensor_count,
        (left_diag, target1),
    )
    near0 = after(near0, mixed1)
    rest0 = target_part(-1.0, [rest0], hidden0, near0, down_weight, chip)
    got1, got0 = after(got1, mixed1), after(got0, rest0)
    hidden = [got0, got1, swap(got0), swap(got1)]

    size = right_factor.shape[2]
    left, back = left_grads(
        hidden,
        down_weight,
        (rest0, rest1),
        (mixed0, mixed1),
        left_diag,
        order,
        tensor_count,
        pairs,
        size,
        1.0 / math.sqrt(rows * fsdp_count),
    )
    got_left = along(left[2:], 1)
    sent = right_grads(back, own, late, order, pairs, 1, size, SMALL)
    left = add(left[:2], after(got_left, sent)).astype(BF16)
    got_left = along(left[1], 2)
    got_right = along(sent, 1)
    kept_back = after(back, sent, left)
    right = right_grads(kept_back, own, late, order, pairs, 0, size, LARGE)
    right = add(right, got_right).astype(BF16)
    grad_right = add(turn(right[0], 0), turn(right[1], 2))
    grad_left = add(left[0], got_left)
    grad_left = grad_left.reshape(pairs // 2, -1, 2, blocks).transpose(0, 2, 1, 3)
    return grad_right.reshape(right_factor.shape), grad_left.reshape(left_factor.shape)


def body(*args):
    tokens, gate_weight, _, _, right_factor, left_factor = args
    counts = (lax.axis_size("fsdp"), lax.axis_size("tensor"))
    feat, hid = gate_weight.shape
    per_owner, share, size = right_factor.shape
    blocks = left_factor.shape[2]
    fits = hid % (2 * BLK) == 0
    fits = fits and counts == (4, 4) and tokens.shape[0] == 128
    fits = fits and hid >= 4 * BLK and feat % BLK == 0
    fits = fits and size == 128 and 2 * blocks == size and per_owner % WIDE == 0
    fits = fits and left_factor.shape[0] == share and share % 16 == 0
    return (tiled_body if fits else general_body)(*args)


def solution(mesh):
    return jax.shard_map(
        body,
        mesh=mesh,
        in_specs=(
            P(("groups", "fsdp"), None),
            P("fsdp", "tensor"),
            P("fsdp", "tensor"),
            P("tensor", "fsdp"),
            P("fsdp", "tensor", None),
            P("fsdp", "tensor", None),
        ),
        out_specs=(P(("groups", "fsdp"), "tensor", None), P(("groups", "fsdp"), "tensor", None)),
        check_vma=False,
    )
```

```python
import functools
import math

import jax
import jax.numpy as jnp
from jax import lax
from jax.experimental import pallas as pl
from jax.experimental.pallas import tpu as pltpu
from jax.sharding import PartitionSpec as P

BLK = 256
LANES = 128
SMALL = pl.CostEstimate(flops=1, bytes_accessed=1, transcendentals=0)
LARGE = pl.CostEstimate(flops=10**10, bytes_accessed=10**7, transcendentals=0)
F32 = jnp.float32
BF16 = jnp.bfloat16


def gate_up_kernel(idx_ref, top_ref, bottom_ref, gate_ref, up_ref, mine_ref, other_ref):
    rows = top_ref.shape[0]
    lhs = jnp.concatenate([top_ref[...], bottom_ref[...]], axis=0)
    for slot, weight_ref in enumerate((gate_ref, up_ref)):
        product = jnp.dot(lhs, weight_ref[...], preferred_element_type=F32).astype(BF16)
        mine_ref[slot] = product[:rows]
        other_ref[slot] = product[rows:]


def gate_up(top, top_block, bottom, gate, up, column, first, width):
    rows, feat = bottom.shape
    if width % BLK or gate.shape[1] % BLK or rows % 16 or feat % 128:
        lhs = jnp.concatenate(
            [lax.dynamic_slice_in_dim(top, top_block * feat, feat, 1), bottom], axis=0
        )
        both = [
            jnp.dot(
                lhs,
                lax.dynamic_slice_in_dim(w, column + first, width, 1),
                preferred_element_type=F32,
            ).astype(BF16)
            for w in (gate, up)
        ]
        both = jnp.stack(both)
        return both[:, :rows], both[:, rows:]
    scalars = jnp.stack([top_block, lax.div(column, BLK) + first // BLK]).astype(jnp.int32)
    weight_spec = pl.BlockSpec((feat, BLK), lambda n, s: (0, s[1] + n))
    out_spec = pl.BlockSpec((2, rows, BLK), lambda n, s: (0, 0, n))
    shape = jax.ShapeDtypeStruct((2, rows, width), BF16)
    return pl.pallas_call(
        gate_up_kernel,
        grid_spec=pltpu.PrefetchScalarGridSpec(
            num_scalar_prefetch=1,
            grid=(width // BLK,),
            in_specs=[
                pl.BlockSpec((rows, feat), lambda n, s: (0, s[0])),
                pl.BlockSpec((rows, feat), lambda n, s: (0, 0)),
                weight_spec,
                weight_spec,
            ],
            out_specs=[out_spec, out_spec],
        ),
        out_shape=[shape, shape],
        compiler_params=pltpu.CompilerParams(vmem_limit_bytes=40 * 2**20),
        cost_estimate=pl.CostEstimate(
            flops=2 * 2 * rows * feat * 2 * width,
            bytes_accessed=2 * feat * 2 * width + 2 * 2 * rows * (feat + 2 * width),
            transcendentals=0,
        ),
        name="gate_up",
    )(scalars, top, bottom, gate, up)


def down_kernel(idx_ref, mine_ref, other_ref, weight_ref, *refs):
    out_ref = refs[-1]
    lhs = jnp.concatenate([mine_ref[...], other_ref[...]], axis=0)
    product = jnp.dot(lhs, weight_ref[...], preferred_element_type=F32)

    @pl.when(pl.program_id(0) == 0)
    def _():
        out_ref[...] = refs[0][...] + product if len(refs) > 1 else product

    @pl.when(pl.program_id(0) > 0)
    def _():
        out_ref[...] += product


def down_add(total, mine, other, weight, row):
    rows, width = mine.shape
    outs = weight.shape[1]
    if width % BLK or weight.shape[0] % BLK or rows % 16 or outs % 128:
        lhs = jnp.concatenate([mine, other], axis=0)
        part = lax.dynamic_slice_in_dim(weight, row, width, 0)
        product = jnp.dot(lhs, part, preferred_element_type=F32)
        return product if total is None else total + product
    scalars = jnp.reshape(lax.div(row, BLK), (1,)).astype(jnp.int32)
    hidden_spec = pl.BlockSpec((rows, BLK), lambda k, s: (0, k))
    whole = pl.BlockSpec((2 * rows, outs), lambda k, s: (0, 0))
    totals = [] if total is None else [total]
    return pl.pallas_call(
        down_kernel,
        grid_spec=pltpu.PrefetchScalarGridSpec(
            num_scalar_prefetch=1,
            grid=(width // BLK,),
            in_specs=[
                hidden_spec,
                hidden_spec,
                pl.BlockSpec((BLK, outs), lambda k, s: (s[0] + k, 0)),
            ]
            + [whole] * len(totals),
            out_specs=whole,
        ),
        out_shape=jax.ShapeDtypeStruct((2 * rows, outs), F32),
        compiler_params=pltpu.CompilerParams(vmem_limit_bytes=40 * 2**20),
        cost_estimate=pl.CostEstimate(
            flops=2 * 2 * rows * width * outs,
            bytes_accessed=2 * width * outs + 2 * 2 * rows * width + 16 * rows * outs,
            transcendentals=0,
        ),
        name="down_add",
    )(scalars, mine, other, weight, *totals)


def general_body(tokens, gate_weight, up_weight, down_weight, right_factor, left_factor):
    fsdp_count = lax.axis_size("fsdp")
    tensor_count = lax.axis_size("tensor")
    chips = fsdp_count // 2
    rows, model = tokens.shape
    feat, hid = gate_weight.shape
    part = hid // chips
    me = lax.axis_index("fsdp")
    chip, core = lax.div(me, 2), lax.rem(me, 2)
    z = lax.axis_index("tensor")

    def swap(value):
        return lax.ppermute(value, "fsdp", [(i, i ^ 1) for i in range(fsdp_count)])

    def shift(value, hops):
        perm = [(i, (i + 2 * hops) % fsdp_count) for i in range(fsdp_count)]
        return lax.ppermute(value, "fsdp", perm)

    def gather_z(value):
        if tensor_count > 4:
            return lax.all_gather(value, "tensor", axis=0, tiled=True)
        size = value.shape[0]
        whole = jnp.zeros((size * tensor_count,) + value.shape[1:], value.dtype)
        whole = lax.dynamic_update_slice_in_dim(whole, value, z * size, 0)
        for step in range(1, tensor_count):
            perm = [(i, (i + step) % tensor_count) for i in range(tensor_count)]
            got = lax.ppermute(value, "tensor", perm)
            source = lax.rem(z - step + tensor_count, tensor_count)
            whole = lax.dynamic_update_slice_in_dim(whole, got, source * size, 0)
        return whole

    def scatter_z(value):
        if tensor_count > 4:
            return lax.psum_scatter(value, "tensor", scatter_dimension=0, tiled=False)
        total = lax.dynamic_index_in_dim(value, z, 0, keepdims=False)
        for step in range(1, tensor_count):
            target_z = lax.rem(z + step, tensor_count)
            piece = lax.dynamic_index_in_dim(value, target_z, 0, keepdims=False)
            perm = [(i, (i + step) % tensor_count) for i in range(tensor_count)]
            total += lax.ppermute(piece.astype(BF16), "tensor", perm).astype(F32)
        return total

    def columns(value, start, width):
        return lax.dynamic_slice_in_dim(value, start, width, 1)

    def after(value, *others):
        return lax.optimization_barrier((value,) + others)[0]

    def pair_z(value):
        perm = [(i, i ^ 1) for i in range(tensor_count)]
        got = lax.ppermute(value, "tensor", perm)
        odd = lax.rem(z, 2) == 1
        return jnp.concatenate(
            [jnp.where(odd, got, value), jnp.where(odd, value, got)], axis=0
        )

    if part % BLK == 0 and part // BLK > 1:
        head = (part // BLK + 1) // 2 * BLK
        chunks = [(0, head), (head, part - head)]
    else:
        chunks = [(0, part)]

    half = rows // 2
    own_half = lax.dynamic_slice_in_dim(tokens, lax.rem(z, 2) * half, half, 0)

    def send_tokens(value, dt, g):
        features = lax.rem(chip - dt + g + chips, chips) * (2 * feat)
        return shift(columns(value, features, 2 * feat), -dt)

    def partial(pair, dp, first, width):
        column = lax.rem(chip + dp, chips) * part
        top, block, bottom = pair
        mine, other = gate_up(top, block, bottom, gate_weight, up_weight, column, first, width)
        return mine, swap(other)

    def send_partials(pair, got, dt):
        sums = []
        for dp in range(1, chips):
            pieces = [partial(pair, dp, *chunk) for chunk in chunks]
            for n, (mine, from_core) in enumerate(pieces):
                both = (mine.astype(F32) + from_core.astype(F32)).astype(BF16)
                got[dt, dp, n] = shift(both, dp)
                sums.append(both)
        return sums

    got, kept, gathered = {}, {}, {}
    local = swap(columns(tokens, (me ^ 1) * feat, feat))
    arrived = {dt: send_tokens(own_half, dt, 0) for dt in range(1, chips)}
    sums = send_partials((tokens, me, local), got, 0)
    if sums:
        local = after(local, *sums)
    kept[0] = partial((tokens, me, local), 0, 0, part)
    late_tokens = after(tokens, kept[0][0])
    neighbour_tokens = swap(late_tokens)
    late_half = after(own_half, *sums) if sums else own_half

    for dt in range(1, chips):
        gathered[dt, 0] = pair_z(after(arrived[dt], *sums))
        whole = gathered[dt, 0]
        top = columns(whole, core * feat, feat)
        bottom = swap(columns(whole, (1 - core) * feat, feat))
        pair = (top, jnp.int32(0), bottom)
        sums = send_partials(pair, got, dt)
        pair = (top, jnp.int32(0), after(bottom, *sums))
        kept[dt] = partial(pair, 0, 0, part)
        for g in range(1, chips):
            gathered[dt, g] = pair_z(after(send_tokens(late_half, dt, g), kept[dt][0]))

    def activate(e, first, width, n):
        terms = [lax.slice_in_dim(term, first, first + width, axis=2) for term in kept[e]]
        terms += [got[(e + dp) % chips, dp, n] for dp in range(1, chips)]
        total = sum(term.astype(F32) for term in terms)
        return (jax.nn.silu(total[0]) * total[1]).astype(BF16)

    totals = {u: None for u in range(chips)}
    for e in list(range(1, chips)) + [0]:
        values = [activate(e, *chunk, n) for n, chunk in enumerate(chunks)]
        spans = list(chunks)
        if e:
            values, spans = [jnp.concatenate(values, axis=1)], [(0, part)]
        sent = [[value] + [shift(value, d) for d in range(1, chips)] for value in values]
        for (first, width), copies in zip(spans, sent):
            for d, mine in enumerate(copies):
                u = (e - d + chips) % chips
                row = lax.rem(chip - d + chips, chips) * part + first
                totals[u] = down_add(totals[u], mine, swap(mine), down_weight, row)

    token_rows = []
    for dt in range(chips):
        if dt == 0:
            token_rows += [tokens, neighbour_tokens]
            continue
        else:
            full = jnp.zeros((rows, model), BF16)
            for g in range(chips):
                features = lax.rem(chip + g, chips) * (2 * feat)
                full = lax.dynamic_update_slice_in_dim(full, gathered[dt, g], features, 1)
        token_rows += [full, swap(full)]
    inputs = jnp.concatenate(token_rows, axis=0)
    count = inputs.shape[0]

    blocks, share, size = right_factor.shape
    ratio = tensor_count // fsdp_count
    turn = []
    for a in range(fsdp_count):
        for b in range(tensor_count):
            turn.append((a * tensor_count + b, (b // ratio) * tensor_count + a * ratio + b % ratio))
    back = [(b, a) for a, b in turn]
    right_rows = gather_z(lax.ppermute(right_factor, ("fsdp", "tensor"), turn)[None])
    right_rows = right_rows.reshape(fsdp_count, ratio, blocks, share, size)
    right_rows = right_rows.transpose(0, 2, 1, 3, 4).reshape(
        fsdp_count * blocks, ratio * share, size
    )
    left_rows = jnp.moveaxis(gather_z(jnp.moveaxis(left_factor, 1, 0)), 0, 1)

    block_input = inputs.reshape(count, fsdp_count * blocks, size)
    mixed = jnp.einsum(
        "nim,ijm->nij", block_input, right_rows, preferred_element_type=F32
    ).astype(BF16)
    student = jnp.einsum("nij,jki->njk", mixed, left_rows, preferred_element_type=F32)
    target = jnp.concatenate([totals[u] for u in range(chips)], axis=0)
    scale = 1.0 / math.sqrt(count)
    out_grad = (student * (1.0 / tensor_count) - target.reshape(student.shape)) * scale
    out_grad = out_grad.astype(BF16)
    grad_left = jnp.einsum("njk,nij->kji", out_grad, mixed, preferred_element_type=F32)
    mixed_grad = jnp.einsum(
        "njk,jki->nij", out_grad, left_rows, preferred_element_type=F32
    ).astype(BF16)
    grad_right = jnp.einsum(
        "nij,nim->ijm", mixed_grad, block_input, preferred_element_type=F32
    )
    grad_left = scatter_z(
        grad_left.reshape((tensor_count, -1) + grad_left.shape[1:])
    )
    grad_left = jnp.moveaxis(grad_left, 0, 1)
    grad_right = grad_right.reshape(fsdp_count, blocks, ratio, share, size)
    grad_right = grad_right.transpose(0, 2, 1, 3, 4).reshape(
        tensor_count, blocks, share, size
    )
    grad_right = lax.ppermute(scatter_z(grad_right), ("fsdp", "tensor"), back)
    return grad_right, grad_left


def cut_kernel(idx_ref, in_ref, out_ref):
    out_ref[...] = in_ref[...]


def cut_tokens(tokens, rows, row, column, cost=SMALL):
    width = tokens.shape[1] // 2
    steps = 4
    return pl.pallas_call(
        cut_kernel,
        grid_spec=pltpu.PrefetchScalarGridSpec(
            num_scalar_prefetch=1,
            grid=(steps,),
            in_specs=[pl.BlockSpec((rows, width // steps), lambda n, s: (s[0], s[1] * steps + n))],
            out_specs=pl.BlockSpec((rows, width // steps), lambda n, s: (0, n)),
        ),
        out_shape=jax.ShapeDtypeStruct((rows, width), BF16),
        cost_estimate=cost,
        name="cut_tokens",
    )(jnp.stack([row, column]).astype(jnp.int32), tokens)


def pack_kernel(left_ref, out_ref):
    share = left_ref.shape[1]
    for pair in range(left_ref.shape[0] // 2):
        both = [left_ref[2 * pair].astype(F32), left_ref[2 * pair + 1].astype(F32)]
        both = jnp.concatenate(both, axis=1)
        out_ref[pair * share : (pair + 1) * share, :] = both.astype(BF16)


def pack_left(left):
    pairs, share, blocks = left.shape
    return pl.pallas_call(
        pack_kernel,
        out_shape=jax.ShapeDtypeStruct((pairs // 2 * share, 2 * blocks), BF16),
        cost_estimate=LARGE,
        name="pack_left",
    )(left)


def products_kernel(sets, idx_ref, *refs):
    pieces, (gate_ref, up_ref, mine_ref, other_ref) = refs[: 4 * sets], refs[4 * sets :]
    lhs = jnp.concatenate([piece[...] for piece in pieces], axis=0)
    rows = mine_ref.shape[2]
    for slot, weight_ref in enumerate((gate_ref, up_ref)):
        product = jnp.dot(lhs, weight_ref[...], preferred_element_type=F32).astype(BF16)
        for u in range(sets):
            mine_ref[u, slot] = product[2 * u * rows : (2 * u + 1) * rows]
            other_ref[u, slot] = product[(2 * u + 1) * rows : (2 * u + 2) * rows]


def products(pieces, scalars, gate, up, first, width):
    feat = gate.shape[0]
    sets = len(pieces) // 4
    half = pieces[0][0].shape[0] // (1 if pieces[0][1] is None else 2)
    start = first // BLK

    def piece_spec(row, column):
        if row is None:
            return pl.BlockSpec((half, feat), lambda n, s: (0, s[column]))
        return pl.BlockSpec((half, feat), lambda n, s: (s[row], s[column]))

    weight_spec = pl.BlockSpec(
        (feat, BLK), lambda n, s: (0, s[4] + start + n)
    )
    out_spec = pl.BlockSpec((sets, 2, 2 * half, BLK), lambda n, s: (0, 0, 0, n))
    shape = jax.ShapeDtypeStruct((sets, 2, 2 * half, width), BF16)
    return pl.pallas_call(
        functools.partial(products_kernel, sets),
        grid_spec=pltpu.PrefetchScalarGridSpec(
            num_scalar_prefetch=1,
            grid=(width // BLK,),
            in_specs=[piece_spec(row, column) for _, row, column in pieces]
            + [weight_spec, weight_spec],
            out_specs=[out_spec, out_spec],
        ),
        out_shape=[shape, shape],
        compiler_params=pltpu.CompilerParams(vmem_limit_bytes=40 * 2**20),
        cost_estimate=LARGE if sets > 1 else SMALL,
        name="gate_up_products",
    )(scalars, *[piece for piece, _, _ in pieces], gate, up)


def fill_rows(lhs, pieces):
    rows = pieces[0].shape[0]
    for place, which in enumerate((1, 3, 0, 2)):
        lhs[place * rows : (place + 1) * rows, :] = pieces[which][...]


def whole_spec(array):
    return pl.BlockSpec(array.shape, lambda n, s: (0,) * len(array.shape))


def target_kernel(sign, idx_ref, mine_ref, near_ref, weight_ref, *refs):
    terms, out_ref = refs[:-1], refs[-1]
    lhs = jnp.concatenate([mine_ref[...], near_ref[...]], axis=0)
    product = jnp.dot(lhs, weight_ref[...], preferred_element_type=F32)
    out_ref[...] = sum((ref[...] for ref in terms), sign * product)


def target_part(sign, terms, mine, near, weight, chip):
    rows, width = mine.shape
    outs = weight.shape[1]
    wide = 2 * BLK if outs % (2 * BLK) == 0 else BLK
    block = pl.BlockSpec((2 * rows, wide), lambda n, s: (0, n))
    return pl.pallas_call(
        functools.partial(target_kernel, sign),
        grid_spec=pltpu.PrefetchScalarGridSpec(
            num_scalar_prefetch=1,
            grid=(outs // wide,),
            in_specs=[whole_spec(mine), whole_spec(near)]
            + [pl.BlockSpec((width, wide), lambda n, s: (s[0], n))]
            + [block] * len(terms),
            out_specs=block,
        ),
        out_shape=jax.ShapeDtypeStruct((2 * rows, outs), F32),
        compiler_params=pltpu.CompilerParams(vmem_limit_bytes=40 * 2**20),
        cost_estimate=SMALL,
        name="target_part",
    )(jnp.reshape(chip, (1,)).astype(jnp.int32), mine, near, weight, *terms)


TN = (((0,), (0,)), ((), ()))
NT = (((1,), (1,)), ((), ()))
WIDE = 8


def natural(step, chip, per_chip):
    return lax.rem(chip + step // per_chip, 2) * per_chip + lax.rem(step, per_chip)


def spread_left(z, rows_ref, out_ref, scratch):
    groups = out_ref.shape[0]
    parts, _, size = rows_ref.shape
    blocks = size // 2
    share = blocks // parts
    fold = BLK // blocks
    begin = rows_ref.shape[1] - groups * fold // 2 * share
    scratch[...] = jnp.zeros_like(scratch)
    low = lax.broadcasted_iota(jnp.int32, (blocks, size), 1) < blocks
    for g in range(groups):
        for pair in range(fold // 2):
            row = begin + (g * (fold // 2) + pair) * share
            picked = [
                rows_ref[z ^ owner, row : row + share, :] for owner in range(parts)
            ]
            turned = jnp.concatenate(picked + picked, axis=0).astype(F32).T
            for a in range(2):
                value = turned[a * blocks : (a + 1) * blocks]
                value = jnp.where(low if a == 0 else ~low, value, 0.0)
                lanes = slice(pair * size, (pair + 1) * size)
                for c in range(blocks // WIDE):
                    row = (c * fold + 2 * pair + a) * WIDE
                    scratch[row : row + WIDE, lanes] = value[c * WIDE : (c + 1) * WIDE]
        out_ref[g] = scratch[...].astype(BF16)


def student_kernel(steps, late, tensor_count, idx_ref, *refs):
    tokens, refs = refs[: 8 if late else 4], refs[8 if late else 4 :]
    rights, left_ref, refs = refs[:2], refs[2], refs[3:]
    step = pl.program_id(0)
    if late:
        target_ref, mixed_ref, student_ref, spread = refs
    else:
        mixed_ref, student_ref, diag_ref, spread, scratch = refs
        rows_ref, left_ref = left_ref, diag_ref
        pl.when(step == 0)(lambda: spread_left(idx_ref[3], rows_ref, diag_ref, scratch))
    pair = natural(step, idx_ref[2], steps // 2)
    groups = left_ref.shape[0]
    size = spread.shape[2]
    pairs = spread.shape[1] // WIDE
    share = BLK // groups

    @pl.when(step == 0)
    def _():
        spread[...] = jnp.zeros_like(spread)

    def mix(pieces):
        for half, right_ref in enumerate(rights):
            for t in range(WIDE):
                value = right_ref[0, t * pairs : (t + 1) * pairs, :].astype(F32)
                spread[t, pl.ds(t, pairs, stride=WIDE), :] = value
            factor = jnp.concatenate([spread[t] for t in range(WIDE)], axis=1).astype(BF16)
            lanes = slice(half * WIDE * size, (half + 1) * WIDE * size)
            rows = jnp.concatenate([piece[:, lanes] for piece in pieces], axis=0)
            part = lax.dot_general(factor, rows, NT, preferred_element_type=F32).astype(BF16)
            start = pl.multiple_of((2 * pair + half) * share, share)
            for g in range(groups):
                mixed_ref[g, pl.ds(start, share), :] = part[g * share : (g + 1) * share]

    if late:
        pl.when(step < steps // 2)(lambda: mix(tokens[:4]))
        pl.when(step >= steps // 2)(lambda: mix(tokens[4:]))
    else:
        mix(tokens)

    @pl.when(step == steps - 1)
    def _():
        for g in range(groups):
            span = slice(g * BLK, (g + 1) * BLK)
            student = lax.dot_general(
                mixed_ref[g], left_ref[g], TN, preferred_element_type=F32
            )
            student = student * (1.0 / tensor_count)
            student_ref[:, span] = student - target_ref[:, span] if late else student


def token_specs(half, width, chunk, late):
    def specs(place):
        return [
            pl.BlockSpec((half, width), lambda n, s, p=p: (s[p % 2], place(n, s)))
            for p in range(4)
        ]

    if not late:
        return specs(chunk)

    def inner(n, s):
        return lax.rem(chunk(n, s), 2)

    return specs(inner) + [pl.BlockSpec((half, width), lambda n, s: (0, inner(n, s)))] * 4


def student_part(tokens, scalars, factors, pairs, tensor_count, late=()):
    size = factors.shape[2]
    half = tokens[0].shape[0] // 2
    blocks = size // 2
    groups = pairs * blocks // BLK
    steps = blocks // (2 * WIDE)

    def chunk(n, s):
        return natural(n, s[2], steps // 2)

    def right_spec(half):
        return pl.BlockSpec(
            (1, WIDE * pairs, size), lambda n, s: (s[3] ^ chunk(n, s), half, 0)
        )

    diag = (groups, BLK, BLK)
    shapes = [
        jax.ShapeDtypeStruct((groups, BLK, 4 * half), BF16),
        jax.ShapeDtypeStruct((4 * half, groups * BLK), F32),
    ]
    scratch = [pltpu.VMEM((WIDE, pairs * WIDE, size), F32)]
    extra = list(late)
    if not late:
        shapes.append(jax.ShapeDtypeStruct(diag, BF16))
        scratch.append(pltpu.VMEM((BLK, BLK), F32))
        extra = [factors]
    return pl.pallas_call(
        functools.partial(student_kernel, steps, bool(late), tensor_count),
        grid_spec=pltpu.PrefetchScalarGridSpec(
            num_scalar_prefetch=1,
            grid=(steps,),
            in_specs=token_specs(half, 2 * WIDE * size, chunk, bool(late))
            + [right_spec(0), right_spec(1)]
            + [whole_spec(array) for array in extra],
            out_specs=[whole_spec(shape) for shape in shapes],
            scratch_shapes=scratch,
        ),
        out_shape=shapes,
        compiler_params=pltpu.CompilerParams(vmem_limit_bytes=40 * 2**20),
        cost_estimate=LARGE,
        name="student_part",
    )(scalars, *tokens, factors, factors, *extra)


def place(z, owner):
    bits = z ^ owner
    return lax.rem(bits, 2) * 2 + bits // 2


def left_kernel(chunks, scale, idx_ref, *refs):
    hidden, refs = refs[:4], refs[4:]
    weight_ref, rest0, rest1, mixed0, mixed1, left_ref, out_ref, back_ref, lhs = refs
    step = pl.program_id(0)
    parts, size = out_ref.shape[0], out_ref.shape[2]
    blocks = chunks * WIDE
    share = BLK // chunks
    fold = BLK // blocks
    pl.when(step == 0)(lambda: fill_rows(lhs, hidden))
    target = jnp.dot(lhs[...], weight_ref[...], preferred_element_type=F32)
    rest = jnp.concatenate([rest0[...], rest1[...]], axis=0)
    out_grad = ((rest - target) * scale).astype(BF16)
    mixed = jnp.concatenate([mixed0[0], mixed1[0]], axis=1)
    left = jnp.dot(mixed, out_grad, preferred_element_type=F32)
    value = lax.dot_general(left_ref[0], out_grad, NT, preferred_element_type=F32)
    value = value.astype(BF16)
    for c in range(chunks):
        back_ref[c] = value[c * share : (c + 1) * share]
    low = lax.broadcasted_iota(jnp.int32, (blocks, size), 1) < blocks
    rows = blocks // parts
    for pair in range(fold // 2):
        lanes = slice(pair * size, (pair + 1) * size)
        picked = []
        for a in (2 * pair, 2 * pair + 1):
            for c in range(chunks):
                begin = (c * fold + a) * WIDE
                picked.append(left[begin : begin + WIDE, lanes])
        turned = jnp.concatenate(picked, axis=0).T
        both = jnp.where(low, turned[:blocks], turned[blocks:]).astype(BF16)
        begin = pl.multiple_of((step * (fold // 2) + pair) * rows, rows)
        for owner in range(parts):
            out_ref[place(idx_ref[3], owner), pl.ds(begin, rows), :] = both[
                owner * rows : (owner + 1) * rows
            ]


def left_grads(hidden, weight, rest, mixed, left_diag, scalars, parts, pairs, size, scale):
    groups, count = left_diag.shape[0], 2 * rest[0].shape[0]
    width = hidden[0].shape[1]
    blocks = groups * BLK // pairs
    chunks = blocks // WIDE
    share = BLK // chunks
    column = pl.BlockSpec((count // 2, BLK), lambda n, s: (0, n))
    slab = pl.BlockSpec((1, BLK, count // 2), lambda n, s: (n, 0, 0))
    out_rows = pairs * blocks * blocks // size // parts
    return pl.pallas_call(
        functools.partial(left_kernel, chunks, scale),
        grid_spec=pltpu.PrefetchScalarGridSpec(
            num_scalar_prefetch=1,
            grid=(groups,),
            in_specs=[whole_spec(piece) for piece in hidden]
            + [pl.BlockSpec((width, BLK), lambda n, s: (1 - s[2], n))]
            + [column, column, slab, slab]
            + [pl.BlockSpec((1, BLK, BLK), lambda n, s: (n, 0, 0))],
            out_specs=[
                pl.BlockSpec((parts, out_rows, size), lambda n, s: (0, 0, 0)),
                pl.BlockSpec((chunks, share, count), lambda n, s: (0, n, 0)),
            ],
            scratch_shapes=[pltpu.VMEM((count, width), BF16)],
        ),
        out_shape=[
            jax.ShapeDtypeStruct((parts, out_rows, size), BF16),
            jax.ShapeDtypeStruct((chunks, groups * share, count), BF16),
        ],
        compiler_params=pltpu.CompilerParams(vmem_limit_bytes=40 * 2**20),
        cost_estimate=SMALL,
        name="left_grads",
    )(scalars, *hidden, weight, *rest, *mixed, left_diag)


def right_kernel(pairs, bit, idx_ref, *refs):
    own, near, far, (back_ref, out_ref, wide) = refs[:4], refs[4:8], refs[8:12], refs[12:]
    size = out_ref.shape[2]
    owner = idx_ref[3] ^ (2 * pl.program_id(0) + bit)

    def right(later):
        for half in range(2):
            lanes = slice(half * WIDE * size, (half + 1) * WIDE * size)
            rows = jnp.concatenate([piece[:, lanes] for piece in own + later], axis=0)
            value = jnp.dot(back_ref[half], rows, preferred_element_type=F32)
            for t in range(WIDE):
                wide[t] = value[:, t * size : (t + 1) * size]
            for t in range(WIDE):
                begin = (half * WIDE + t) * pairs
                out_ref[0, begin : begin + pairs, :] = wide[
                    t, pl.ds(t, pairs, stride=WIDE), :
                ].astype(BF16)

    pl.when(owner // 2 == idx_ref[2])(lambda: right(near))
    pl.when(owner // 2 != idx_ref[2])(lambda: right(far))


def right_grads(back, own, late, scalars, pairs, bit, size, cost):
    half = late[0].shape[0] // 2
    rows, count = back.shape[1:]

    def owner(n, s):
        return s[3] ^ (2 * n + bit)

    return pl.pallas_call(
        functools.partial(right_kernel, pairs, bit),
        grid_spec=pltpu.PrefetchScalarGridSpec(
            num_scalar_prefetch=1,
            grid=(2,),
            in_specs=token_specs(half, 2 * WIDE * size, owner, False)
            + token_specs(half, 2 * WIDE * size, owner, True)
            + [pl.BlockSpec((2, rows, count), lambda n, s: (owner(n, s), 0, 0))],
            out_specs=pl.BlockSpec((1, 2 * WIDE * pairs, size), lambda n, s: (n, 0, 0)),
            scratch_shapes=[pltpu.VMEM((WIDE, pairs * WIDE, size), F32)],
        ),
        out_shape=jax.ShapeDtypeStruct((2, 2 * WIDE * pairs, size), BF16),
        compiler_params=pltpu.CompilerParams(vmem_limit_bytes=40 * 2**20),
        cost_estimate=cost,
        name="right_grads",
    )(scalars, *own, *late, back)


def tiled_body(tokens, gate_weight, up_weight, down_weight, right_factor, left_factor):
    fsdp_count = lax.axis_size("fsdp")
    tensor_count = lax.axis_size("tensor")
    rows, model = tokens.shape
    part = gate_weight.shape[1] // 2
    me, z = lax.axis_index("fsdp"), lax.axis_index("tensor")
    chip, core, odd = lax.div(me, 2), lax.rem(me, 2), lax.rem(z, 2)
    both_axes = ("fsdp", "tensor")

    def swap(value):
        return lax.ppermute(value, "fsdp", [(i, i ^ 1) for i in range(fsdp_count)])

    def across(value):
        return lax.ppermute(value, "fsdp", [(i, i ^ 2) for i in range(fsdp_count)])

    def along(value, bit):
        return lax.ppermute(value, "tensor", [(i, i ^ bit) for i in range(tensor_count)])

    def turn(value, bit):
        perm = []
        for f in range(fsdp_count):
            for t in range(tensor_count):
                perm.append((f * tensor_count + t, (t ^ bit) * tensor_count + f))
        return lax.ppermute(value, both_axes, perm)

    def after(value, *others):
        return lax.optimization_barrier((value,) + others)[0]

    def add(*terms):
        return sum(term.astype(F32) for term in terms)

    near_tokens = swap(tokens)
    first = cut_tokens(tokens, rows, jnp.int32(0), 1 - chip)
    arrived = across(first)
    base = jnp.stack([odd, 1 - odd])
    mine_block = lax.div(part, BLK) * chip
    other_block = lax.div(part, BLK) * (1 - chip)

    def scalars(block):
        return jnp.concatenate([base, jnp.stack([me, core, block])]).astype(jnp.int32)

    own_pieces = [(t, row, 2) for t in (tokens, near_tokens) for row in (0, 1)]
    mine, other = products(
        own_pieces, after(scalars(other_block), first), gate_weight, up_weight, 0, part
    )

    pairs, blocks = left_factor.shape[0], left_factor.shape[2]
    turned = turn(after(right_factor, mine), 0)
    left_rows = pack_left(after(left_factor, mine))
    factors = jnp.concatenate(
        [after(turned, left_rows).reshape(-1, LANES), left_rows], axis=0
    )[None]
    more = along(factors, 1)
    sums = add(mine[0], swap(other[0])).astype(BF16)
    rest = cut_tokens(after(tokens, left_rows), rows // 2, odd, chip)
    arrived = after(arrived, more, sums, rest)
    got_early = across(sums)
    late_first = across(after(rest, sums))
    factors = jnp.concatenate([factors, more], axis=0)

    order = jnp.concatenate([base, jnp.stack([chip, z])]).astype(jnp.int32)
    own = [tokens, tokens, near_tokens, near_tokens]
    near_arrived = swap(arrived)
    late = [arrived, arrived, near_arrived, near_arrived]
    late_pieces = [(t, row, 3) for t in (arrived, near_arrived) for row in (0, 1)]
    late_order = after(scalars(other_block), rest)
    mine, other = products(late_pieces, late_order, gate_weight, up_weight, 0, part)
    near = swap(after(other[0], late_first))
    mine_order = after(scalars(mine_block), mine)
    kept, other = products(
        own_pieces + late_pieces, mine_order, gate_weight, up_weight, 0, part
    )
    sums = add(mine[0], after(near, kept)).astype(BF16)
    got = across(sums)
    near_kept = swap(after(other, got_early, sums))
    factors = after(factors, kept)
    more = along(factors, 2)

    def activate(u, term):
        total = add(kept[u], near_kept[u], term)
        return (jax.nn.silu(total[0]) * total[1]).astype(BF16)

    hidden1 = activate(1, got_early)
    near1 = swap(hidden1)
    late_partner = along(after(late_first, kept), 1)
    factors = jnp.concatenate([factors, after(more, hidden1)], axis=0)
    mixed0, rest0, left_diag = student_part(
        [after(tokens, hidden1, sums)] + own[1:], order, factors, pairs, tensor_count
    )
    got1 = across(after(hidden1, mixed0))
    target1 = target_part(1.0, [], hidden1, after(near1, mixed0), down_weight, chip)
    hidden0 = activate(0, after(got, target1))
    got0 = across(hidden0)
    near0 = swap(hidden0)
    late_partner = after(late_partner, mixed0)
    late += [late_first, late_partner, swap(late_first), swap(late_partner)]
    mixed1, rest1 = student_part(
        [after(late[0], hidden0)] + late[1:],
        order,
        factors,
        pairs,
        tensor_count,
        (left_diag, target1),
    )
    near0 = after(near0, mixed1)
    rest0 = target_part(-1.0, [rest0], hidden0, near0, down_weight, chip)
    got1, got0 = after(got1, mixed1), after(got0, rest0)
    hidden = [got0, got1, swap(got0), swap(got1)]

    size = right_factor.shape[2]
    left, back = left_grads(
        hidden,
        down_weight,
        (rest0, rest1),
        (mixed0, mixed1),
        left_diag,
        order,
        tensor_count,
        pairs,
        size,
        1.0 / math.sqrt(rows * fsdp_count),
    )
    got_left = along(left[2:], 1)
    sent = right_grads(back, own, late, order, pairs, 1, size, SMALL)
    left = add(left[:2], after(got_left, sent)).astype(BF16)
    got_left = along(left[1], 2)
    got_right = along(sent, 1)
    kept_back = after(back, sent, left)
    right = right_grads(kept_back, own, late, order, pairs, 0, size, LARGE)
    right = add(right, got_right).astype(BF16)
    grad_right = add(turn(right[0], 0), turn(right[1], 2))
    grad_left = add(left[0], got_left)
    grad_left = grad_left.reshape(pairs // 2, -1, 2, blocks).transpose(0, 2, 1, 3)
    return grad_right.reshape(right_factor.shape), grad_left.reshape(left_factor.shape)


def body(*args):
    tokens, gate_weight, _, _, right_factor, left_factor = args
    counts = (lax.axis_size("fsdp"), lax.axis_size("tensor"))
    feat, hid = gate_weight.shape
    per_owner, share, size = right_factor.shape
    blocks = left_factor.shape[2]
    fits = hid % (2 * BLK) == 0
    fits = fits and counts == (4, 4) and tokens.shape[0] == 128
    fits = fits and hid >= 4 * BLK and feat % BLK == 0
    fits = fits and size == 128 and 2 * blocks == size and per_owner % WIDE == 0
    fits = fits and left_factor.shape[0] == share and share % 16 == 0
    return (tiled_body if fits else general_body)(*args)


def solution(mesh):
    return jax.shard_map(
        body,
        mesh=mesh,
        in_specs=(
            P(("groups", "fsdp"), None),
            P("fsdp", "tensor"),
            P("fsdp", "tensor"),
            P("tensor", "fsdp"),
            P("fsdp", "tensor", None),
            P("fsdp", "tensor", None),
        ),
        out_specs=(P(("groups", "fsdp"), "tensor", None), P(("groups", "fsdp"), "tensor", None)),
        check_vma=False,
    )
```

```python
import functools
import math

import jax
import jax.numpy as jnp
from jax import lax
from jax.experimental import pallas as pl
from jax.experimental.pallas import tpu as pltpu
from jax.sharding import PartitionSpec as P

BLK = 256
LANES = 128
SMALL = pl.CostEstimate(flops=1, bytes_accessed=1, transcendentals=0)
LARGE = pl.CostEstimate(flops=10**10, bytes_accessed=10**7, transcendentals=0)
F32 = jnp.float32
BF16 = jnp.bfloat16


def gate_up_kernel(idx_ref, top_ref, bottom_ref, gate_ref, up_ref, mine_ref, other_ref):
    rows = top_ref.shape[0]
    lhs = jnp.concatenate([top_ref[...], bottom_ref[...]], axis=0)
    for slot, weight_ref in enumerate((gate_ref, up_ref)):
        product = jnp.dot(lhs, weight_ref[...], preferred_element_type=F32).astype(BF16)
        mine_ref[slot] = product[:rows]
        other_ref[slot] = product[rows:]


def gate_up(top, top_block, bottom, gate, up, column, first, width):
    rows, feat = bottom.shape
    if width % BLK or gate.shape[1] % BLK or rows % 16 or feat % 128:
        lhs = jnp.concatenate(
            [lax.dynamic_slice_in_dim(top, top_block * feat, feat, 1), bottom], axis=0
        )
        both = [
            jnp.dot(
                lhs,
                lax.dynamic_slice_in_dim(w, column + first, width, 1),
                preferred_element_type=F32,
            ).astype(BF16)
            for w in (gate, up)
        ]
        both = jnp.stack(both)
        return both[:, :rows], both[:, rows:]
    scalars = jnp.stack([top_block, lax.div(column, BLK) + first // BLK]).astype(jnp.int32)
    weight_spec = pl.BlockSpec((feat, BLK), lambda n, s: (0, s[1] + n))
    out_spec = pl.BlockSpec((2, rows, BLK), lambda n, s: (0, 0, n))
    shape = jax.ShapeDtypeStruct((2, rows, width), BF16)
    return pl.pallas_call(
        gate_up_kernel,
        grid_spec=pltpu.PrefetchScalarGridSpec(
            num_scalar_prefetch=1,
            grid=(width // BLK,),
            in_specs=[
                pl.BlockSpec((rows, feat), lambda n, s: (0, s[0])),
                pl.BlockSpec((rows, feat), lambda n, s: (0, 0)),
                weight_spec,
                weight_spec,
            ],
            out_specs=[out_spec, out_spec],
        ),
        out_shape=[shape, shape],
        compiler_params=pltpu.CompilerParams(vmem_limit_bytes=40 * 2**20),
        cost_estimate=pl.CostEstimate(
            flops=2 * 2 * rows * feat * 2 * width,
            bytes_accessed=2 * feat * 2 * width + 2 * 2 * rows * (feat + 2 * width),
            transcendentals=0,
        ),
        name="gate_up",
    )(scalars, top, bottom, gate, up)


def down_kernel(idx_ref, mine_ref, other_ref, weight_ref, *refs):
    out_ref = refs[-1]
    lhs = jnp.concatenate([mine_ref[...], other_ref[...]], axis=0)
    product = jnp.dot(lhs, weight_ref[...], preferred_element_type=F32)

    @pl.when(pl.program_id(0) == 0)
    def _():
        out_ref[...] = refs[0][...] + product if len(refs) > 1 else product

    @pl.when(pl.program_id(0) > 0)
    def _():
        out_ref[...] += product


def down_add(total, mine, other, weight, row):
    rows, width = mine.shape
    outs = weight.shape[1]
    if width % BLK or weight.shape[0] % BLK or rows % 16 or outs % 128:
        lhs = jnp.concatenate([mine, other], axis=0)
        part = lax.dynamic_slice_in_dim(weight, row, width, 0)
        product = jnp.dot(lhs, part, preferred_element_type=F32)
        return product if total is None else total + product
    scalars = jnp.reshape(lax.div(row, BLK), (1,)).astype(jnp.int32)
    hidden_spec = pl.BlockSpec((rows, BLK), lambda k, s: (0, k))
    whole = pl.BlockSpec((2 * rows, outs), lambda k, s: (0, 0))
    totals = [] if total is None else [total]
    return pl.pallas_call(
        down_kernel,
        grid_spec=pltpu.PrefetchScalarGridSpec(
            num_scalar_prefetch=1,
            grid=(width // BLK,),
            in_specs=[
                hidden_spec,
                hidden_spec,
                pl.BlockSpec((BLK, outs), lambda k, s: (s[0] + k, 0)),
            ]
            + [whole] * len(totals),
            out_specs=whole,
        ),
        out_shape=jax.ShapeDtypeStruct((2 * rows, outs), F32),
        compiler_params=pltpu.CompilerParams(vmem_limit_bytes=40 * 2**20),
        cost_estimate=pl.CostEstimate(
            flops=2 * 2 * rows * width * outs,
            bytes_accessed=2 * width * outs + 2 * 2 * rows * width + 16 * rows * outs,
            transcendentals=0,
        ),
        name="down_add",
    )(scalars, mine, other, weight, *totals)


def general_body(tokens, gate_weight, up_weight, down_weight, right_factor, left_factor):
    fsdp_count = lax.axis_size("fsdp")
    tensor_count = lax.axis_size("tensor")
    chips = fsdp_count // 2
    rows, model = tokens.shape
    feat, hid = gate_weight.shape
    part = hid // chips
    me = lax.axis_index("fsdp")
    chip, core = lax.div(me, 2), lax.rem(me, 2)
    z = lax.axis_index("tensor")

    def swap(value):
        return lax.ppermute(value, "fsdp", [(i, i ^ 1) for i in range(fsdp_count)])

    def shift(value, hops):
        perm = [(i, (i + 2 * hops) % fsdp_count) for i in range(fsdp_count)]
        return lax.ppermute(value, "fsdp", perm)

    def gather_z(value):
        if tensor_count > 4:
            return lax.all_gather(value, "tensor", axis=0, tiled=True)
        size = value.shape[0]
        whole = jnp.zeros((size * tensor_count,) + value.shape[1:], value.dtype)
        whole = lax.dynamic_update_slice_in_dim(whole, value, z * size, 0)
        for step in range(1, tensor_count):
            perm = [(i, (i + step) % tensor_count) for i in range(tensor_count)]
            got = lax.ppermute(value, "tensor", perm)
            source = lax.rem(z - step + tensor_count, tensor_count)
            whole = lax.dynamic_update_slice_in_dim(whole, got, source * size, 0)
        return whole

    def scatter_z(value):
        if tensor_count > 4:
            return lax.psum_scatter(value, "tensor", scatter_dimension=0, tiled=False)
        total = lax.dynamic_index_in_dim(value, z, 0, keepdims=False)
        for step in range(1, tensor_count):
            target_z = lax.rem(z + step, tensor_count)
            piece = lax.dynamic_index_in_dim(value, target_z, 0, keepdims=False)
            perm = [(i, (i + step) % tensor_count) for i in range(tensor_count)]
            total += lax.ppermute(piece.astype(BF16), "tensor", perm).astype(F32)
        return total

    def columns(value, start, width):
        return lax.dynamic_slice_in_dim(value, start, width, 1)

    def after(value, *others):
        return lax.optimization_barrier((value,) + others)[0]

    def pair_z(value):
        perm = [(i, i ^ 1) for i in range(tensor_count)]
        got = lax.ppermute(value, "tensor", perm)
        odd = lax.rem(z, 2) == 1
        return jnp.concatenate(
            [jnp.where(odd, got, value), jnp.where(odd, value, got)], axis=0
        )

    if part % BLK == 0 and part // BLK > 1:
        head = (part // BLK + 1) // 2 * BLK
        chunks = [(0, head), (head, part - head)]
    else:
        chunks = [(0, part)]

    half = rows // 2
    own_half = lax.dynamic_slice_in_dim(tokens, lax.rem(z, 2) * half, half, 0)

    def send_tokens(value, dt, g):
        features = lax.rem(chip - dt + g + chips, chips) * (2 * feat)
        return shift(columns(value, features, 2 * feat), -dt)

    def partial(pair, dp, first, width):
        column = lax.rem(chip + dp, chips) * part
        top, block, bottom = pair
        mine, other = gate_up(top, block, bottom, gate_weight, up_weight, column, first, width)
        return mine, swap(other)

    def send_partials(pair, got, dt):
        sums = []
        for dp in range(1, chips):
            pieces = [partial(pair, dp, *chunk) for chunk in chunks]
            for n, (mine, from_core) in enumerate(pieces):
                both = (mine.astype(F32) + from_core.astype(F32)).astype(BF16)
                got[dt, dp, n] = shift(both, dp)
                sums.append(both)
        return sums

    got, kept, gathered = {}, {}, {}
    local = swap(columns(tokens, (me ^ 1) * feat, feat))
    arrived = {dt: send_tokens(own_half, dt, 0) for dt in range(1, chips)}
    sums = send_partials((tokens, me, local), got, 0)
    if sums:
        local = after(local, *sums)
    kept[0] = partial((tokens, me, local), 0, 0, part)
    late_tokens = after(tokens, kept[0][0])
    neighbour_tokens = swap(late_tokens)
    late_half = after(own_half, *sums) if sums else own_half

    for dt in range(1, chips):
        gathered[dt, 0] = pair_z(after(arrived[dt], *sums))
        whole = gathered[dt, 0]
        top = columns(whole, core * feat, feat)
        bottom = swap(columns(whole, (1 - core) * feat, feat))
        pair = (top, jnp.int32(0), bottom)
        sums = send_partials(pair, got, dt)
        pair = (top, jnp.int32(0), after(bottom, *sums))
        kept[dt] = partial(pair, 0, 0, part)
        for g in range(1, chips):
            gathered[dt, g] = pair_z(after(send_tokens(late_half, dt, g), kept[dt][0]))

    def activate(e, first, width, n):
        terms = [lax.slice_in_dim(term, first, first + width, axis=2) for term in kept[e]]
        terms += [got[(e + dp) % chips, dp, n] for dp in range(1, chips)]
        total = sum(term.astype(F32) for term in terms)
        return (jax.nn.silu(total[0]) * total[1]).astype(BF16)

    totals = {u: None for u in range(chips)}
    for e in list(range(1, chips)) + [0]:
        values = [activate(e, *chunk, n) for n, chunk in enumerate(chunks)]
        spans = list(chunks)
        if e:
            values, spans = [jnp.concatenate(values, axis=1)], [(0, part)]
        sent = [[value] + [shift(value, d) for d in range(1, chips)] for value in values]
        for (first, width), copies in zip(spans, sent):
            for d, mine in enumerate(copies):
                u = (e - d + chips) % chips
                row = lax.rem(chip - d + chips, chips) * part + first
                totals[u] = down_add(totals[u], mine, swap(mine), down_weight, row)

    token_rows = []
    for dt in range(chips):
        if dt == 0:
            token_rows += [tokens, neighbour_tokens]
            continue
        else:
            full = jnp.zeros((rows, model), BF16)
            for g in range(chips):
                features = lax.rem(chip + g, chips) * (2 * feat)
                full = lax.dynamic_update_slice_in_dim(full, gathered[dt, g], features, 1)
        token_rows += [full, swap(full)]
    inputs = jnp.concatenate(token_rows, axis=0)
    count = inputs.shape[0]

    blocks, share, size = right_factor.shape
    ratio = tensor_count // fsdp_count
    turn = []
    for a in range(fsdp_count):
        for b in range(tensor_count):
            turn.append((a * tensor_count + b, (b // ratio) * tensor_count + a * ratio + b % ratio))
    back = [(b, a) for a, b in turn]
    right_rows = gather_z(lax.ppermute(right_factor, ("fsdp", "tensor"), turn)[None])
    right_rows = right_rows.reshape(fsdp_count, ratio, blocks, share, size)
    right_rows = right_rows.transpose(0, 2, 1, 3, 4).reshape(
        fsdp_count * blocks, ratio * share, size
    )
    left_rows = jnp.moveaxis(gather_z(jnp.moveaxis(left_factor, 1, 0)), 0, 1)

    block_input = inputs.reshape(count, fsdp_count * blocks, size)
    mixed = jnp.einsum(
        "nim,ijm->nij", block_input, right_rows, preferred_element_type=F32
    ).astype(BF16)
    student = jnp.einsum("nij,jki->njk", mixed, left_rows, preferred_element_type=F32)
    target = jnp.concatenate([totals[u] for u in range(chips)], axis=0)
    scale = 1.0 / math.sqrt(count)
    out_grad = (student * (1.0 / tensor_count) - target.reshape(student.shape)) * scale
    out_grad = out_grad.astype(BF16)
    grad_left = jnp.einsum("njk,nij->kji", out_grad, mixed, preferred_element_type=F32)
    mixed_grad = jnp.einsum(
        "njk,jki->nij", out_grad, left_rows, preferred_element_type=F32
    ).astype(BF16)
    grad_right = jnp.einsum(
        "nij,nim->ijm", mixed_grad, block_input, preferred_element_type=F32
    )
    grad_left = scatter_z(
        grad_left.reshape((tensor_count, -1) + grad_left.shape[1:])
    )
    grad_left = jnp.moveaxis(grad_left, 0, 1)
    grad_right = grad_right.reshape(fsdp_count, blocks, ratio, share, size)
    grad_right = grad_right.transpose(0, 2, 1, 3, 4).reshape(
        tensor_count, blocks, share, size
    )
    grad_right = lax.ppermute(scatter_z(grad_right), ("fsdp", "tensor"), back)
    return grad_right, grad_left


def cut_kernel(idx_ref, in_ref, out_ref):
    out_ref[...] = in_ref[...]


def cut_tokens(tokens, rows, row, column, cost=SMALL):
    width = tokens.shape[1] // 2
    steps = 4
    return pl.pallas_call(
        cut_kernel,
        grid_spec=pltpu.PrefetchScalarGridSpec(
            num_scalar_prefetch=1,
            grid=(steps,),
            in_specs=[pl.BlockSpec((rows, width // steps), lambda n, s: (s[0], s[1] * steps + n))],
            out_specs=pl.BlockSpec((rows, width // steps), lambda n, s: (0, n)),
        ),
        out_shape=jax.ShapeDtypeStruct((rows, width), BF16),
        cost_estimate=cost,
        name="cut_tokens",
    )(jnp.stack([row, column]).astype(jnp.int32), tokens)


def pack_kernel(left_ref, out_ref):
    share = left_ref.shape[1]
    for pair in range(left_ref.shape[0] // 2):
        both = [left_ref[2 * pair].astype(F32), left_ref[2 * pair + 1].astype(F32)]
        both = jnp.concatenate(both, axis=1)
        out_ref[pair * share : (pair + 1) * share, :] = both.astype(BF16)


def pack_left(left):
    pairs, share, blocks = left.shape
    return pl.pallas_call(
        pack_kernel,
        out_shape=jax.ShapeDtypeStruct((pairs // 2 * share, 2 * blocks), BF16),
        cost_estimate=LARGE,
        name="pack_left",
    )(left)


def products_kernel(sets, idx_ref, *refs):
    pieces, (gate_ref, up_ref, mine_ref, other_ref) = refs[: 4 * sets], refs[4 * sets :]
    lhs = jnp.concatenate([piece[...] for piece in pieces], axis=0)
    rows = mine_ref.shape[2]
    for slot, weight_ref in enumerate((gate_ref, up_ref)):
        product = jnp.dot(lhs, weight_ref[...], preferred_element_type=F32).astype(BF16)
        for u in range(sets):
            mine_ref[u, slot] = product[2 * u * rows : (2 * u + 1) * rows]
            other_ref[u, slot] = product[(2 * u + 1) * rows : (2 * u + 2) * rows]


def products(pieces, scalars, gate, up, first, width):
    feat = gate.shape[0]
    sets = len(pieces) // 4
    half = pieces[0][0].shape[0] // (1 if pieces[0][1] is None else 2)
    start = first // BLK

    def piece_spec(row, column):
        if row is None:
            return pl.BlockSpec((half, feat), lambda n, s: (0, s[column]))
        return pl.BlockSpec((half, feat), lambda n, s: (s[row], s[column]))

    weight_spec = pl.BlockSpec(
        (feat, BLK), lambda n, s: (0, s[4] + start + n)
    )
    out_spec = pl.BlockSpec((sets, 2, 2 * half, BLK), lambda n, s: (0, 0, 0, n))
    shape = jax.ShapeDtypeStruct((sets, 2, 2 * half, width), BF16)
    return pl.pallas_call(
        functools.partial(products_kernel, sets),
        grid_spec=pltpu.PrefetchScalarGridSpec(
            num_scalar_prefetch=1,
            grid=(width // BLK,),
            in_specs=[piece_spec(row, column) for _, row, column in pieces]
            + [weight_spec, weight_spec],
            out_specs=[out_spec, out_spec],
        ),
        out_shape=[shape, shape],
        compiler_params=pltpu.CompilerParams(vmem_limit_bytes=40 * 2**20),
        cost_estimate=LARGE if sets > 1 else SMALL,
        name="gate_up_products",
    )(scalars, *[piece for piece, _, _ in pieces], gate, up)


def fill_rows(lhs, pieces):
    rows = pieces[0].shape[0]
    for place, which in enumerate((1, 3, 0, 2)):
        lhs[place * rows : (place + 1) * rows, :] = pieces[which][...]


def whole_spec(array):
    return pl.BlockSpec(array.shape, lambda n, s: (0,) * len(array.shape))


def target_kernel(sign, idx_ref, mine_ref, near_ref, weight_ref, *refs):
    terms, out_ref = refs[:-1], refs[-1]
    lhs = jnp.concatenate([mine_ref[...], near_ref[...]], axis=0)
    product = jnp.dot(lhs, weight_ref[...], preferred_element_type=F32)
    out_ref[...] = sum((ref[...] for ref in terms), sign * product)


def target_part(sign, terms, mine, near, weight, chip):
    rows, width = mine.shape
    outs = weight.shape[1]
    wide = 2 * BLK if outs % (2 * BLK) == 0 else BLK
    block = pl.BlockSpec((2 * rows, wide), lambda n, s: (0, n))
    return pl.pallas_call(
        functools.partial(target_kernel, sign),
        grid_spec=pltpu.PrefetchScalarGridSpec(
            num_scalar_prefetch=1,
            grid=(outs // wide,),
            in_specs=[whole_spec(mine), whole_spec(near)]
            + [pl.BlockSpec((width, wide), lambda n, s: (s[0], n))]
            + [block] * len(terms),
            out_specs=block,
        ),
        out_shape=jax.ShapeDtypeStruct((2 * rows, outs), F32),
        compiler_params=pltpu.CompilerParams(vmem_limit_bytes=40 * 2**20),
        cost_estimate=SMALL,
        name="target_part",
    )(jnp.reshape(chip, (1,)).astype(jnp.int32), mine, near, weight, *terms)


TN = (((0,), (0,)), ((), ()))
NT = (((1,), (1,)), ((), ()))
WIDE = 8


def natural(step, chip, per_chip):
    return lax.rem(chip + step // per_chip, 2) * per_chip + lax.rem(step, per_chip)


def spread_left(z, rows_ref, out_ref, scratch):
    groups = out_ref.shape[0]
    parts, _, size = rows_ref.shape
    blocks = size // 2
    share = blocks // parts
    fold = BLK // blocks
    begin = rows_ref.shape[1] - groups * fold // 2 * share
    scratch[...] = jnp.zeros_like(scratch)
    low = lax.broadcasted_iota(jnp.int32, (blocks, size), 1) < blocks
    for g in range(groups):
        for pair in range(fold // 2):
            row = begin + (g * (fold // 2) + pair) * share
            picked = [
                rows_ref[place(z, owner), row : row + share, :] for owner in range(parts)
            ]
            turned = jnp.concatenate(picked + picked, axis=0).astype(F32).T
            for a in range(2):
                value = turned[a * blocks : (a + 1) * blocks]
                value = jnp.where(low if a == 0 else ~low, value, 0.0)
                lanes = slice(pair * size, (pair + 1) * size)
                for c in range(blocks // WIDE):
                    row = (c * fold + 2 * pair + a) * WIDE
                    scratch[row : row + WIDE, lanes] = value[c * WIDE : (c + 1) * WIDE]
        out_ref[g] = scratch[...].astype(BF16)


def student_kernel(steps, late, tensor_count, idx_ref, *refs):
    tokens, refs = refs[: 8 if late else 4], refs[8 if late else 4 :]
    rights, left_ref, refs = refs[:2], refs[2], refs[3:]
    step = pl.program_id(0)
    if late:
        target_ref, mixed_ref, student_ref, spread = refs
    else:
        mixed_ref, student_ref, diag_ref, spread, scratch = refs
        rows_ref, left_ref = left_ref, diag_ref
        pl.when(step == 0)(lambda: spread_left(idx_ref[3], rows_ref, diag_ref, scratch))
    pair = natural(step, idx_ref[2], steps // 2)
    groups = left_ref.shape[0]
    size = spread.shape[2]
    pairs = spread.shape[1] // WIDE
    share = BLK // groups

    @pl.when(step == 0)
    def _():
        spread[...] = jnp.zeros_like(spread)

    def mix(pieces):
        for half, right_ref in enumerate(rights):
            for t in range(WIDE):
                value = right_ref[0, t * pairs : (t + 1) * pairs, :].astype(F32)
                spread[t, pl.ds(t, pairs, stride=WIDE), :] = value
            factor = jnp.concatenate([spread[t] for t in range(WIDE)], axis=1).astype(BF16)
            lanes = slice(half * WIDE * size, (half + 1) * WIDE * size)
            rows = jnp.concatenate([piece[:, lanes] for piece in pieces], axis=0)
            part = lax.dot_general(factor, rows, NT, preferred_element_type=F32).astype(BF16)
            start = pl.multiple_of((2 * pair + half) * share, share)
            for g in range(groups):
                mixed_ref[g, pl.ds(start, share), :] = part[g * share : (g + 1) * share]

    if late:
        pl.when(step < steps // 2)(lambda: mix(tokens[:4]))
        pl.when(step >= steps // 2)(lambda: mix(tokens[4:]))
    else:
        mix(tokens)

    @pl.when(step == steps - 1)
    def _():
        for g in range(groups):
            span = slice(g * BLK, (g + 1) * BLK)
            student = lax.dot_general(
                mixed_ref[g], left_ref[g], TN, preferred_element_type=F32
            )
            student = student * (1.0 / tensor_count)
            student_ref[:, span] = student - target_ref[:, span] if late else student


def token_specs(half, width, chunk, late):
    if not late:
        return [
            pl.BlockSpec((half, width), lambda n, s, p=p: (s[p % 2], chunk(n, s)))
            for p in range(4)
        ]
    inner = pl.BlockSpec((half, width), lambda n, s: (0, lax.rem(chunk(n, s), 2)))
    return [inner] * 8


def student_part(tokens, scalars, factors, pairs, tensor_count, late=()):
    size = factors.shape[2]
    half = tokens[0].shape[0] // (1 if late else 2)
    blocks = size // 2
    groups = pairs * blocks // BLK
    steps = blocks // (2 * WIDE)

    def chunk(n, s):
        return natural(n, s[2], steps // 2)

    def right_spec(half):
        return pl.BlockSpec(
            (1, WIDE * pairs, size), lambda n, s: (place(s[3], chunk(n, s)), half, 0)
        )

    diag = (groups, BLK, BLK)
    shapes = [
        jax.ShapeDtypeStruct((groups, BLK, 4 * half), BF16),
        jax.ShapeDtypeStruct((4 * half, groups * BLK), F32),
    ]
    scratch = [pltpu.VMEM((WIDE, pairs * WIDE, size), F32)]
    extra = list(late)
    if not late:
        shapes.append(jax.ShapeDtypeStruct(diag, BF16))
        scratch.append(pltpu.VMEM((BLK, BLK), F32))
        extra = [factors]
    return pl.pallas_call(
        functools.partial(student_kernel, steps, bool(late), tensor_count),
        grid_spec=pltpu.PrefetchScalarGridSpec(
            num_scalar_prefetch=1,
            grid=(steps,),
            in_specs=token_specs(half, 2 * WIDE * size, chunk, bool(late))
            + [right_spec(0), right_spec(1)]
            + [whole_spec(array) for array in extra],
            out_specs=[whole_spec(shape) for shape in shapes],
            scratch_shapes=scratch,
        ),
        out_shape=shapes,
        compiler_params=pltpu.CompilerParams(vmem_limit_bytes=40 * 2**20),
        cost_estimate=LARGE,
        name="student_part",
    )(scalars, *tokens, factors, factors, *extra)


def place(z, owner):
    bits = z ^ owner
    return lax.rem(bits, 2) * 2 + bits // 2


def left_kernel(chunks, scale, idx_ref, *refs):
    hidden, refs = refs[:4], refs[4:]
    weight_ref, rest0, rest1, mixed0, mixed1, left_ref, out_ref, back_ref, lhs = refs
    step = pl.program_id(0)
    parts, size = out_ref.shape[0], out_ref.shape[2]
    blocks = chunks * WIDE
    share = BLK // chunks
    fold = BLK // blocks
    pl.when(step == 0)(lambda: fill_rows(lhs, hidden))
    target = jnp.dot(lhs[...], weight_ref[...], preferred_element_type=F32)
    rest = jnp.concatenate([rest0[...], rest1[...]], axis=0)
    out_grad = ((rest - target) * scale).astype(BF16)
    mixed = jnp.concatenate([mixed0[0], mixed1[0]], axis=1)
    left = jnp.dot(mixed, out_grad, preferred_element_type=F32)
    value = lax.dot_general(left_ref[0], out_grad, NT, preferred_element_type=F32)
    value = value.astype(BF16)
    for c in range(chunks):
        back_ref[c] = value[c * share : (c + 1) * share]
    low = lax.broadcasted_iota(jnp.int32, (blocks, size), 1) < blocks
    rows = blocks // parts
    for pair in range(fold // 2):
        lanes = slice(pair * size, (pair + 1) * size)
        picked = []
        for a in (2 * pair, 2 * pair + 1):
            for c in range(chunks):
                begin = (c * fold + a) * WIDE
                picked.append(left[begin : begin + WIDE, lanes])
        turned = jnp.concatenate(picked, axis=0).T
        both = jnp.where(low, turned[:blocks], turned[blocks:]).astype(BF16)
        begin = pl.multiple_of((step * (fold // 2) + pair) * rows, rows)
        for owner in range(parts):
            out_ref[place(idx_ref[3], owner), pl.ds(begin, rows), :] = both[
                owner * rows : (owner + 1) * rows
            ]


def left_grads(hidden, weight, rest, mixed, left_diag, scalars, parts, pairs, size, scale):
    groups, count = left_diag.shape[0], 2 * rest[0].shape[0]
    width = hidden[0].shape[1]
    blocks = groups * BLK // pairs
    chunks = blocks // WIDE
    share = BLK // chunks
    column = pl.BlockSpec((count // 2, BLK), lambda n, s: (0, n))
    slab = pl.BlockSpec((1, BLK, count // 2), lambda n, s: (n, 0, 0))
    out_rows = pairs * blocks * blocks // size // parts
    return pl.pallas_call(
        functools.partial(left_kernel, chunks, scale),
        grid_spec=pltpu.PrefetchScalarGridSpec(
            num_scalar_prefetch=1,
            grid=(groups,),
            in_specs=[whole_spec(piece) for piece in hidden]
            + [pl.BlockSpec((width, BLK), lambda n, s: (1 - s[2], n))]
            + [column, column, slab, slab]
            + [pl.BlockSpec((1, BLK, BLK), lambda n, s: (n, 0, 0))],
            out_specs=[
                pl.BlockSpec((parts, out_rows, size), lambda n, s: (0, 0, 0)),
                pl.BlockSpec((chunks, share, count), lambda n, s: (0, n, 0)),
            ],
            scratch_shapes=[pltpu.VMEM((count, width), BF16)],
        ),
        out_shape=[
            jax.ShapeDtypeStruct((parts, out_rows, size), BF16),
            jax.ShapeDtypeStruct((chunks, groups * share, count), BF16),
        ],
        compiler_params=pltpu.CompilerParams(vmem_limit_bytes=40 * 2**20),
        cost_estimate=SMALL,
        name="left_grads",
    )(scalars, *hidden, weight, *rest, *mixed, left_diag)


def right_kernel(pairs, bit, idx_ref, *refs):
    own, near, far, (back_ref, out_ref, wide) = refs[:4], refs[4:8], refs[8:12], refs[12:]
    size = out_ref.shape[2]
    owner = idx_ref[3] ^ (2 * pl.program_id(0) + bit)

    def right(later):
        for half in range(2):
            lanes = slice(half * WIDE * size, (half + 1) * WIDE * size)
            rows = jnp.concatenate([piece[:, lanes] for piece in own + later], axis=0)
            value = jnp.dot(back_ref[half], rows, preferred_element_type=F32)
            for t in range(WIDE):
                wide[t] = value[:, t * size : (t + 1) * size]
            for t in range(WIDE):
                begin = (half * WIDE + t) * pairs
                out_ref[0, begin : begin + pairs, :] = wide[
                    t, pl.ds(t, pairs, stride=WIDE), :
                ].astype(BF16)

    pl.when(owner // 2 == idx_ref[2])(lambda: right(near))
    pl.when(owner // 2 != idx_ref[2])(lambda: right(far))


def right_grads(back, own, late, scalars, pairs, bit, size, cost):
    half = late[0].shape[0]
    rows, count = back.shape[1:]

    def owner(n, s):
        return s[3] ^ (2 * n + bit)

    return pl.pallas_call(
        functools.partial(right_kernel, pairs, bit),
        grid_spec=pltpu.PrefetchScalarGridSpec(
            num_scalar_prefetch=1,
            grid=(2,),
            in_specs=token_specs(half, 2 * WIDE * size, owner, False)
            + token_specs(half, 2 * WIDE * size, owner, True)
            + [pl.BlockSpec((2, rows, count), lambda n, s: (owner(n, s), 0, 0))],
            out_specs=pl.BlockSpec((1, 2 * WIDE * pairs, size), lambda n, s: (n, 0, 0)),
            scratch_shapes=[pltpu.VMEM((WIDE, pairs * WIDE, size), F32)],
        ),
        out_shape=jax.ShapeDtypeStruct((2, 2 * WIDE * pairs, size), BF16),
        compiler_params=pltpu.CompilerParams(vmem_limit_bytes=40 * 2**20),
        cost_estimate=cost,
        name="right_grads",
    )(scalars, *own, *late, back)


def tiled_body(tokens, gate_weight, up_weight, down_weight, right_factor, left_factor):
    fsdp_count = lax.axis_size("fsdp")
    tensor_count = lax.axis_size("tensor")
    rows, model = tokens.shape
    part = gate_weight.shape[1] // 2
    me, z = lax.axis_index("fsdp"), lax.axis_index("tensor")
    chip, core, odd = lax.div(me, 2), lax.rem(me, 2), lax.rem(z, 2)
    both_axes = ("fsdp", "tensor")

    def swap(value):
        return lax.ppermute(value, "fsdp", [(i, i ^ 1) for i in range(fsdp_count)])

    def across(value):
        return lax.ppermute(value, "fsdp", [(i, i ^ 2) for i in range(fsdp_count)])

    def along(value, bit):
        return lax.ppermute(value, "tensor", [(i, i ^ bit) for i in range(tensor_count)])

    def turn(value, bit):
        perm = []
        for f in range(fsdp_count):
            for t in range(tensor_count):
                perm.append((f * tensor_count + t, (t ^ bit) * tensor_count + f))
        return lax.ppermute(value, both_axes, perm)

    def after(value, *others):
        return lax.optimization_barrier((value,) + others)[0]

    def add(*terms):
        return sum(term.astype(F32) for term in terms)

    near_tokens = swap(tokens)
    first = cut_tokens(tokens, rows // 2, odd, 1 - chip)
    arrived = across(first)
    base = jnp.stack([odd, 1 - odd])
    mine_block = lax.div(part, BLK) * chip
    other_block = lax.div(part, BLK) * (1 - chip)

    def scalars(block):
        return jnp.concatenate([base, jnp.stack([me, core, block])]).astype(jnp.int32)

    own_pieces = [(t, row, 2) for t in (tokens, near_tokens) for row in (0, 1)]
    mine, other = products(
        own_pieces, after(scalars(other_block), first), gate_weight, up_weight, 0, part
    )

    pairs, blocks = left_factor.shape[0], left_factor.shape[2]
    turned = turn(after(right_factor, mine), 0)
    left_rows = pack_left(after(left_factor, mine))
    factors = jnp.concatenate(
        [after(turned, left_rows).reshape(-1, LANES), left_rows], axis=0
    )[None]
    sums = add(mine[0], swap(other[0])).astype(BF16)

    arrived = after(arrived, mine)
    partner = along(arrived, 1)
    near_arrived = swap(arrived)
    late_first = across(cut_tokens(after(tokens, left_rows), rows // 2, odd, chip))
    partner = after(partner, late_first, sums, factors)
    got_early = across(sums)
    more = along(after(factors, partner), 2)
    order = jnp.concatenate([base, jnp.stack([chip, z])]).astype(jnp.int32)
    own = [tokens, tokens, near_tokens, near_tokens]
    late = [arrived, partner, near_arrived, swap(partner)]
    late_pieces = [(t, None, 3) for t in late]
    late_order = after(scalars(other_block), sums)
    mine, other = products(late_pieces, late_order, gate_weight, up_weight, 0, part)
    near = swap(other[0])
    mine_order = after(scalars(mine_block), mine)
    kept, other = products(
        own_pieces + late_pieces, mine_order, gate_weight, up_weight, 0, part
    )
    sums = add(mine[0], after(near, kept)).astype(BF16)
    got = across(sums)
    near_kept = swap(after(other, got_early, sums, more))
    factors = jnp.concatenate([factors, after(more, kept)], axis=0)
    more = along(factors, 1)

    def activate(u, term):
        total = add(kept[u], near_kept[u], term)
        return (jax.nn.silu(total[0]) * total[1]).astype(BF16)

    hidden1 = activate(1, got_early)
    near1 = swap(hidden1)
    factors = jnp.concatenate([factors, after(more, hidden1)], axis=0)
    mixed0, rest0, left_diag = student_part(
        [after(tokens, hidden1, sums)] + own[1:], order, factors, pairs, tensor_count
    )
    got1 = across(after(hidden1, mixed0))
    late_partner = along(after(late_first, mixed0), 1)
    target1 = target_part(1.0, [], hidden1, after(near1, mixed0), down_weight, chip)
    hidden0 = activate(0, after(got, target1))
    got0 = across(hidden0)
    near0 = swap(hidden0)
    late += [late_first, late_partner, swap(late_first), swap(late_partner)]
    mixed1, rest1 = student_part(
        [after(late[0], hidden0)] + late[1:],
        order,
        factors,
        pairs,
        tensor_count,
        (left_diag, target1),
    )
    near0 = after(near0, mixed1)
    rest0 = target_part(-1.0, [rest0], hidden0, near0, down_weight, chip)
    got1, got0 = after(got1, mixed1), after(got0, rest0)
    hidden = [got0, got1, swap(got0), swap(got1)]

    size = right_factor.shape[2]
    left, back = left_grads(
        hidden,
        down_weight,
        (rest0, rest1),
        (mixed0, mixed1),
        left_diag,
        order,
        tensor_count,
        pairs,
        size,
        1.0 / math.sqrt(rows * fsdp_count),
    )
    got_left = along(left[2:], 1)
    sent = right_grads(back, own, late, order, pairs, 1, size, SMALL)
    left = add(left[:2], after(got_left, sent)).astype(BF16)
    got_left = along(left[1], 2)
    got_right = along(sent, 1)
    kept_back = after(back, sent, left)
    right = right_grads(kept_back, own, late, order, pairs, 0, size, LARGE)
    right = add(right, got_right).astype(BF16)
    grad_right = add(turn(right[0], 0), turn(right[1], 2))
    grad_left = add(left[0], got_left)
    grad_left = grad_left.reshape(pairs // 2, -1, 2, blocks).transpose(0, 2, 1, 3)
    return grad_right.reshape(right_factor.shape), grad_left.reshape(left_factor.shape)


def body(*args):
    tokens, gate_weight, _, _, right_factor, left_factor = args
    counts = (lax.axis_size("fsdp"), lax.axis_size("tensor"))
    feat, hid = gate_weight.shape
    per_owner, share, size = right_factor.shape
    blocks = left_factor.shape[2]
    fits = hid % (2 * BLK) == 0
    fits = fits and counts == (4, 4) and tokens.shape[0] == 128
    fits = fits and hid >= 4 * BLK and feat % BLK == 0
    fits = fits and size == 128 and 2 * blocks == size and per_owner % WIDE == 0
    fits = fits and left_factor.shape[0] == share and share % 16 == 0
    return (tiled_body if fits else general_body)(*args)


def solution(mesh):
    return jax.shard_map(
        body,
        mesh=mesh,
        in_specs=(
            P(("groups", "fsdp"), None),
            P("fsdp", "tensor"),
            P("fsdp", "tensor"),
            P("tensor", "fsdp"),
            P("fsdp", "tensor", None),
            P("fsdp", "tensor", None),
        ),
        out_specs=(P(("groups", "fsdp"), "tensor", None), P(("groups", "fsdp"), "tensor", None)),
        check_vma=False,
    )
```

```python
import functools
import math

import jax
import jax.numpy as jnp
from jax import lax
from jax.experimental import pallas as pl
from jax.experimental.pallas import tpu as pltpu
from jax.sharding import PartitionSpec as P

BLK = 256
LANES = 128
SMALL = pl.CostEstimate(flops=1, bytes_accessed=1, transcendentals=0)
LARGE = pl.CostEstimate(flops=10**10, bytes_accessed=10**7, transcendentals=0)
F32 = jnp.float32
BF16 = jnp.bfloat16


def gate_up_kernel(idx_ref, top_ref, bottom_ref, gate_ref, up_ref, mine_ref, other_ref):
    rows = top_ref.shape[0]
    lhs = jnp.concatenate([top_ref[...], bottom_ref[...]], axis=0)
    for slot, weight_ref in enumerate((gate_ref, up_ref)):
        product = jnp.dot(lhs, weight_ref[...], preferred_element_type=F32).astype(BF16)
        mine_ref[slot] = product[:rows]
        other_ref[slot] = product[rows:]


def gate_up(top, top_block, bottom, gate, up, column, first, width):
    rows, feat = bottom.shape
    if width % BLK or gate.shape[1] % BLK or rows % 16 or feat % 128:
        lhs = jnp.concatenate(
            [lax.dynamic_slice_in_dim(top, top_block * feat, feat, 1), bottom], axis=0
        )
        both = [
            jnp.dot(
                lhs,
                lax.dynamic_slice_in_dim(w, column + first, width, 1),
                preferred_element_type=F32,
            ).astype(BF16)
            for w in (gate, up)
        ]
        both = jnp.stack(both)
        return both[:, :rows], both[:, rows:]
    scalars = jnp.stack([top_block, lax.div(column, BLK) + first // BLK]).astype(jnp.int32)
    weight_spec = pl.BlockSpec((feat, BLK), lambda n, s: (0, s[1] + n))
    out_spec = pl.BlockSpec((2, rows, BLK), lambda n, s: (0, 0, n))
    shape = jax.ShapeDtypeStruct((2, rows, width), BF16)
    return pl.pallas_call(
        gate_up_kernel,
        grid_spec=pltpu.PrefetchScalarGridSpec(
            num_scalar_prefetch=1,
            grid=(width // BLK,),
            in_specs=[
                pl.BlockSpec((rows, feat), lambda n, s: (0, s[0])),
                pl.BlockSpec((rows, feat), lambda n, s: (0, 0)),
                weight_spec,
                weight_spec,
            ],
            out_specs=[out_spec, out_spec],
        ),
        out_shape=[shape, shape],
        compiler_params=pltpu.CompilerParams(vmem_limit_bytes=40 * 2**20),
        cost_estimate=pl.CostEstimate(
            flops=2 * 2 * rows * feat * 2 * width,
            bytes_accessed=2 * feat * 2 * width + 2 * 2 * rows * (feat + 2 * width),
            transcendentals=0,
        ),
        name="gate_up",
    )(scalars, top, bottom, gate, up)


def down_kernel(idx_ref, mine_ref, other_ref, weight_ref, *refs):
    out_ref = refs[-1]
    lhs = jnp.concatenate([mine_ref[...], other_ref[...]], axis=0)
    product = jnp.dot(lhs, weight_ref[...], preferred_element_type=F32)

    @pl.when(pl.program_id(0) == 0)
    def _():
        out_ref[...] = refs[0][...] + product if len(refs) > 1 else product

    @pl.when(pl.program_id(0) > 0)
    def _():
        out_ref[...] += product


def down_add(total, mine, other, weight, row):
    rows, width = mine.shape
    outs = weight.shape[1]
    if width % BLK or weight.shape[0] % BLK or rows % 16 or outs % 128:
        lhs = jnp.concatenate([mine, other], axis=0)
        part = lax.dynamic_slice_in_dim(weight, row, width, 0)
        product = jnp.dot(lhs, part, preferred_element_type=F32)
        return product if total is None else total + product
    scalars = jnp.reshape(lax.div(row, BLK), (1,)).astype(jnp.int32)
    hidden_spec = pl.BlockSpec((rows, BLK), lambda k, s: (0, k))
    whole = pl.BlockSpec((2 * rows, outs), lambda k, s: (0, 0))
    totals = [] if total is None else [total]
    return pl.pallas_call(
        down_kernel,
        grid_spec=pltpu.PrefetchScalarGridSpec(
            num_scalar_prefetch=1,
            grid=(width // BLK,),
            in_specs=[
                hidden_spec,
                hidden_spec,
                pl.BlockSpec((BLK, outs), lambda k, s: (s[0] + k, 0)),
            ]
            + [whole] * len(totals),
            out_specs=whole,
        ),
        out_shape=jax.ShapeDtypeStruct((2 * rows, outs), F32),
        compiler_params=pltpu.CompilerParams(vmem_limit_bytes=40 * 2**20),
        cost_estimate=pl.CostEstimate(
            flops=2 * 2 * rows * width * outs,
            bytes_accessed=2 * width * outs + 2 * 2 * rows * width + 16 * rows * outs,
            transcendentals=0,
        ),
        name="down_add",
    )(scalars, mine, other, weight, *totals)


def general_body(tokens, gate_weight, up_weight, down_weight, right_factor, left_factor):
    fsdp_count = lax.axis_size("fsdp")
    tensor_count = lax.axis_size("tensor")
    chips = fsdp_count // 2
    rows, model = tokens.shape
    feat, hid = gate_weight.shape
    part = hid // chips
    me = lax.axis_index("fsdp")
    chip, core = lax.div(me, 2), lax.rem(me, 2)
    z = lax.axis_index("tensor")

    def swap(value):
        return lax.ppermute(value, "fsdp", [(i, i ^ 1) for i in range(fsdp_count)])

    def shift(value, hops):
        perm = [(i, (i + 2 * hops) % fsdp_count) for i in range(fsdp_count)]
        return lax.ppermute(value, "fsdp", perm)

    def gather_z(value):
        if tensor_count > 4:
            return lax.all_gather(value, "tensor", axis=0, tiled=True)
        size = value.shape[0]
        whole = jnp.zeros((size * tensor_count,) + value.shape[1:], value.dtype)
        whole = lax.dynamic_update_slice_in_dim(whole, value, z * size, 0)
        for step in range(1, tensor_count):
            perm = [(i, (i + step) % tensor_count) for i in range(tensor_count)]
            got = lax.ppermute(value, "tensor", perm)
            source = lax.rem(z - step + tensor_count, tensor_count)
            whole = lax.dynamic_update_slice_in_dim(whole, got, source * size, 0)
        return whole

    def scatter_z(value):
        if tensor_count > 4:
            return lax.psum_scatter(value, "tensor", scatter_dimension=0, tiled=False)
        total = lax.dynamic_index_in_dim(value, z, 0, keepdims=False)
        for step in range(1, tensor_count):
            target_z = lax.rem(z + step, tensor_count)
            piece = lax.dynamic_index_in_dim(value, target_z, 0, keepdims=False)
            perm = [(i, (i + step) % tensor_count) for i in range(tensor_count)]
            total += lax.ppermute(piece.astype(BF16), "tensor", perm).astype(F32)
        return total

    def columns(value, start, width):
        return lax.dynamic_slice_in_dim(value, start, width, 1)

    def after(value, *others):
        return lax.optimization_barrier((value,) + others)[0]

    def pair_z(value):
        perm = [(i, i ^ 1) for i in range(tensor_count)]
        got = lax.ppermute(value, "tensor", perm)
        odd = lax.rem(z, 2) == 1
        return jnp.concatenate(
            [jnp.where(odd, got, value), jnp.where(odd, value, got)], axis=0
        )

    if part % BLK == 0 and part // BLK > 1:
        head = (part // BLK + 1) // 2 * BLK
        chunks = [(0, head), (head, part - head)]
    else:
        chunks = [(0, part)]

    half = rows // 2
    own_half = lax.dynamic_slice_in_dim(tokens, lax.rem(z, 2) * half, half, 0)

    def send_tokens(value, dt, g):
        features = lax.rem(chip - dt + g + chips, chips) * (2 * feat)
        return shift(columns(value, features, 2 * feat), -dt)

    def partial(pair, dp, first, width):
        column = lax.rem(chip + dp, chips) * part
        top, block, bottom = pair
        mine, other = gate_up(top, block, bottom, gate_weight, up_weight, column, first, width)
        return mine, swap(other)

    def send_partials(pair, got, dt):
        sums = []
        for dp in range(1, chips):
            pieces = [partial(pair, dp, *chunk) for chunk in chunks]
            for n, (mine, from_core) in enumerate(pieces):
                both = (mine.astype(F32) + from_core.astype(F32)).astype(BF16)
                got[dt, dp, n] = shift(both, dp)
                sums.append(both)
        return sums

    got, kept, gathered = {}, {}, {}
    local = swap(columns(tokens, (me ^ 1) * feat, feat))
    arrived = {dt: send_tokens(own_half, dt, 0) for dt in range(1, chips)}
    sums = send_partials((tokens, me, local), got, 0)
    if sums:
        local = after(local, *sums)
    kept[0] = partial((tokens, me, local), 0, 0, part)
    late_tokens = after(tokens, kept[0][0])
    neighbour_tokens = swap(late_tokens)
    late_half = after(own_half, *sums) if sums else own_half

    for dt in range(1, chips):
        gathered[dt, 0] = pair_z(after(arrived[dt], *sums))
        whole = gathered[dt, 0]
        top = columns(whole, core * feat, feat)
        bottom = swap(columns(whole, (1 - core) * feat, feat))
        pair = (top, jnp.int32(0), bottom)
        sums = send_partials(pair, got, dt)
        pair = (top, jnp.int32(0), after(bottom, *sums))
        kept[dt] = partial(pair, 0, 0, part)
        for g in range(1, chips):
            gathered[dt, g] = pair_z(after(send_tokens(late_half, dt, g), kept[dt][0]))

    def activate(e, first, width, n):
        terms = [lax.slice_in_dim(term, first, first + width, axis=2) for term in kept[e]]
        terms += [got[(e + dp) % chips, dp, n] for dp in range(1, chips)]
        total = sum(term.astype(F32) for term in terms)
        return (jax.nn.silu(total[0]) * total[1]).astype(BF16)

    totals = {u: None for u in range(chips)}
    for e in list(range(1, chips)) + [0]:
        values = [activate(e, *chunk, n) for n, chunk in enumerate(chunks)]
        spans = list(chunks)
        if e:
            values, spans = [jnp.concatenate(values, axis=1)], [(0, part)]
        sent = [[value] + [shift(value, d) for d in range(1, chips)] for value in values]
        for (first, width), copies in zip(spans, sent):
            for d, mine in enumerate(copies):
                u = (e - d + chips) % chips
                row = lax.rem(chip - d + chips, chips) * part + first
                totals[u] = down_add(totals[u], mine, swap(mine), down_weight, row)

    token_rows = []
    for dt in range(chips):
        if dt == 0:
            token_rows += [tokens, neighbour_tokens]
            continue
        else:
            full = jnp.zeros((rows, model), BF16)
            for g in range(chips):
                features = lax.rem(chip + g, chips) * (2 * feat)
                full = lax.dynamic_update_slice_in_dim(full, gathered[dt, g], features, 1)
        token_rows += [full, swap(full)]
    inputs = jnp.concatenate(token_rows, axis=0)
    count = inputs.shape[0]

    blocks, share, size = right_factor.shape
    ratio = tensor_count // fsdp_count
    turn = []
    for a in range(fsdp_count):
        for b in range(tensor_count):
            turn.append((a * tensor_count + b, (b // ratio) * tensor_count + a * ratio + b % ratio))
    back = [(b, a) for a, b in turn]
    right_rows = gather_z(lax.ppermute(right_factor, ("fsdp", "tensor"), turn)[None])
    right_rows = right_rows.reshape(fsdp_count, ratio, blocks, share, size)
    right_rows = right_rows.transpose(0, 2, 1, 3, 4).reshape(
        fsdp_count * blocks, ratio * share, size
    )
    left_rows = jnp.moveaxis(gather_z(jnp.moveaxis(left_factor, 1, 0)), 0, 1)

    block_input = inputs.reshape(count, fsdp_count * blocks, size)
    mixed = jnp.einsum(
        "nim,ijm->nij", block_input, right_rows, preferred_element_type=F32
    ).astype(BF16)
    student = jnp.einsum("nij,jki->njk", mixed, left_rows, preferred_element_type=F32)
    target = jnp.concatenate([totals[u] for u in range(chips)], axis=0)
    scale = 1.0 / math.sqrt(count)
    out_grad = (student * (1.0 / tensor_count) - target.reshape(student.shape)) * scale
    out_grad = out_grad.astype(BF16)
    grad_left = jnp.einsum("njk,nij->kji", out_grad, mixed, preferred_element_type=F32)
    mixed_grad = jnp.einsum(
        "njk,jki->nij", out_grad, left_rows, preferred_element_type=F32
    ).astype(BF16)
    grad_right = jnp.einsum(
        "nij,nim->ijm", mixed_grad, block_input, preferred_element_type=F32
    )
    grad_left = scatter_z(
        grad_left.reshape((tensor_count, -1) + grad_left.shape[1:])
    )
    grad_left = jnp.moveaxis(grad_left, 0, 1)
    grad_right = grad_right.reshape(fsdp_count, blocks, ratio, share, size)
    grad_right = grad_right.transpose(0, 2, 1, 3, 4).reshape(
        tensor_count, blocks, share, size
    )
    grad_right = lax.ppermute(scatter_z(grad_right), ("fsdp", "tensor"), back)
    return grad_right, grad_left


def cut_kernel(count, idx_ref, *refs):
    for in_ref, out_ref in zip(refs[:count], refs[count:]):
        out_ref[...] = in_ref[...]


def cut_tokens(tokens, row, columns):
    block = (tokens.shape[0] // 2, tokens.shape[1] // 2)
    count = len(columns)
    return pl.pallas_call(
        functools.partial(cut_kernel, count),
        grid_spec=pltpu.PrefetchScalarGridSpec(
            num_scalar_prefetch=1,
            grid=(1,),
            in_specs=[
                pl.BlockSpec(block, lambda n, s, k=k: (s[0], s[1 + k])) for k in range(count)
            ],
            out_specs=[pl.BlockSpec(block, lambda n, s: (0, 0))] * count,
        ),
        out_shape=[jax.ShapeDtypeStruct(block, BF16)] * count,
        cost_estimate=SMALL,
        name="cut_tokens",
    )(jnp.stack([row, *columns]).astype(jnp.int32), *[tokens] * count)


def pack_kernel(left_ref, out_ref):
    share = left_ref.shape[1]
    for pair in range(left_ref.shape[0] // 2):
        both = [left_ref[2 * pair].astype(F32), left_ref[2 * pair + 1].astype(F32)]
        both = jnp.concatenate(both, axis=1)
        out_ref[pair * share : (pair + 1) * share, :] = both.astype(BF16)


def pack_left(left):
    pairs, share, blocks = left.shape
    return pl.pallas_call(
        pack_kernel,
        out_shape=jax.ShapeDtypeStruct((pairs // 2 * share, 2 * blocks), BF16),
        cost_estimate=LARGE,
        name="pack_left",
    )(left)


def products_kernel(sets, idx_ref, *refs):
    pieces, (gate_ref, up_ref, mine_ref, other_ref) = refs[: 4 * sets], refs[4 * sets :]
    lhs = jnp.concatenate([piece[...] for piece in pieces], axis=0)
    rows = mine_ref.shape[2]
    for slot, weight_ref in enumerate((gate_ref, up_ref)):
        product = jnp.dot(lhs, weight_ref[...], preferred_element_type=F32).astype(BF16)
        for u in range(sets):
            mine_ref[u, slot] = product[2 * u * rows : (2 * u + 1) * rows]
            other_ref[u, slot] = product[(2 * u + 1) * rows : (2 * u + 2) * rows]


def products(pieces, scalars, gate, up, first, width):
    feat = gate.shape[0]
    sets = len(pieces) // 4
    half = pieces[0][0].shape[0] // (1 if pieces[0][1] is None else 2)
    start = first // BLK

    def piece_spec(row, column):
        if row is None:
            return pl.BlockSpec((half, feat), lambda n, s: (0, s[column]))
        return pl.BlockSpec((half, feat), lambda n, s: (s[row], s[column]))

    weight_spec = pl.BlockSpec(
        (feat, BLK), lambda n, s: (0, s[4] + start + n)
    )
    out_spec = pl.BlockSpec((sets, 2, 2 * half, BLK), lambda n, s: (0, 0, 0, n))
    shape = jax.ShapeDtypeStruct((sets, 2, 2 * half, width), BF16)
    return pl.pallas_call(
        functools.partial(products_kernel, sets),
        grid_spec=pltpu.PrefetchScalarGridSpec(
            num_scalar_prefetch=1,
            grid=(width // BLK,),
            in_specs=[piece_spec(row, column) for _, row, column in pieces]
            + [weight_spec, weight_spec],
            out_specs=[out_spec, out_spec],
        ),
        out_shape=[shape, shape],
        compiler_params=pltpu.CompilerParams(vmem_limit_bytes=40 * 2**20),
        cost_estimate=LARGE if sets > 1 else SMALL,
        name="gate_up_products",
    )(scalars, *[piece for piece, _, _ in pieces], gate, up)


def fill_rows(lhs, pieces):
    rows = pieces[0].shape[0]
    for place, which in enumerate((1, 3, 0, 2)):
        lhs[place * rows : (place + 1) * rows, :] = pieces[which][...]


def whole_spec(array):
    return pl.BlockSpec(array.shape, lambda n, s: (0,) * len(array.shape))


def target_kernel(sign, idx_ref, mine_ref, near_ref, weight_ref, *refs):
    terms, out_ref = refs[:-1], refs[-1]
    lhs = jnp.concatenate([mine_ref[...], near_ref[...]], axis=0)
    product = jnp.dot(lhs, weight_ref[...], preferred_element_type=F32)
    out_ref[...] = sum((ref[...] for ref in terms), sign * product)


def target_part(sign, terms, mine, near, weight, chip):
    rows, width = mine.shape
    outs = weight.shape[1]
    wide = 2 * BLK if outs % (2 * BLK) == 0 else BLK
    block = pl.BlockSpec((2 * rows, wide), lambda n, s: (0, n))
    return pl.pallas_call(
        functools.partial(target_kernel, sign),
        grid_spec=pltpu.PrefetchScalarGridSpec(
            num_scalar_prefetch=1,
            grid=(outs // wide,),
            in_specs=[whole_spec(mine), whole_spec(near)]
            + [pl.BlockSpec((width, wide), lambda n, s: (s[0], n))]
            + [block] * len(terms),
            out_specs=block,
        ),
        out_shape=jax.ShapeDtypeStruct((2 * rows, outs), F32),
        compiler_params=pltpu.CompilerParams(vmem_limit_bytes=40 * 2**20),
        cost_estimate=SMALL,
        name="target_part",
    )(jnp.reshape(chip, (1,)).astype(jnp.int32), mine, near, weight, *terms)


TN = (((0,), (0,)), ((), ()))
NT = (((1,), (1,)), ((), ()))
WIDE = 8


def natural(step, chip, per_chip):
    return lax.rem(chip + step // per_chip, 2) * per_chip + lax.rem(step, per_chip)


def spread_left(z, rows_ref, out_ref, scratch):
    groups = out_ref.shape[0]
    parts, _, size = rows_ref.shape
    blocks = size // 2
    share = blocks // parts
    fold = BLK // blocks
    begin = rows_ref.shape[1] - groups * fold // 2 * share
    scratch[...] = jnp.zeros_like(scratch)
    low = lax.broadcasted_iota(jnp.int32, (blocks, size), 1) < blocks
    for g in range(groups):
        for pair in range(fold // 2):
            row = begin + (g * (fold // 2) + pair) * share
            picked = [
                rows_ref[place(z, owner), row : row + share, :] for owner in range(parts)
            ]
            turned = jnp.concatenate(picked + picked, axis=0).astype(F32).T
            for a in range(2):
                value = turned[a * blocks : (a + 1) * blocks]
                value = jnp.where(low if a == 0 else ~low, value, 0.0)
                lanes = slice(pair * size, (pair + 1) * size)
                for c in range(blocks // WIDE):
                    row = (c * fold + 2 * pair + a) * WIDE
                    scratch[row : row + WIDE, lanes] = value[c * WIDE : (c + 1) * WIDE]
        out_ref[g] = scratch[...].astype(BF16)


def student_kernel(steps, late, tensor_count, idx_ref, *refs):
    tokens, refs = refs[: 8 if late else 4], refs[8 if late else 4 :]
    rights, left_ref, refs = refs[:2], refs[2], refs[3:]
    step = pl.program_id(0)
    if late:
        target_ref, mixed_ref, student_ref, spread = refs
    else:
        mixed_ref, student_ref, diag_ref, spread, scratch = refs
        rows_ref, left_ref = left_ref, diag_ref
        pl.when(step == 0)(lambda: spread_left(idx_ref[3], rows_ref, diag_ref, scratch))
    pair = natural(step, idx_ref[2], steps // 2)
    groups = left_ref.shape[0]
    size = spread.shape[2]
    pairs = spread.shape[1] // WIDE
    share = BLK // groups

    @pl.when(step == 0)
    def _():
        spread[...] = jnp.zeros_like(spread)

    def mix(pieces):
        for half, right_ref in enumerate(rights):
            for t in range(WIDE):
                value = right_ref[0, t * pairs : (t + 1) * pairs, :].astype(F32)
                spread[t, pl.ds(t, pairs, stride=WIDE), :] = value
            factor = jnp.concatenate([spread[t] for t in range(WIDE)], axis=1).astype(BF16)
            lanes = slice(half * WIDE * size, (half + 1) * WIDE * size)
            rows = jnp.concatenate([piece[:, lanes] for piece in pieces], axis=0)
            part = lax.dot_general(factor, rows, NT, preferred_element_type=F32).astype(BF16)
            start = pl.multiple_of((2 * pair + half) * share, share)
            for g in range(groups):
                mixed_ref[g, pl.ds(start, share), :] = part[g * share : (g + 1) * share]

    if late:
        pl.when(step < steps // 2)(lambda: mix(tokens[:4]))
        pl.when(step >= steps // 2)(lambda: mix(tokens[4:]))
    else:
        mix(tokens)

    @pl.when(step == steps - 1)
    def _():
        for g in range(groups):
            span = slice(g * BLK, (g + 1) * BLK)
            student = lax.dot_general(
                mixed_ref[g], left_ref[g], TN, preferred_element_type=F32
            )
            student = student * (1.0 / tensor_count)
            student_ref[:, span] = student - target_ref[:, span] if late else student


def token_specs(half, width, chunk, late):
    if not late:
        return [
            pl.BlockSpec((half, width), lambda n, s, p=p: (s[p % 2], chunk(n, s)))
            for p in range(4)
        ]
    inner = pl.BlockSpec((half, width), lambda n, s: (0, lax.rem(chunk(n, s), 2)))
    return [inner] * 8


def student_part(tokens, scalars, factors, pairs, tensor_count, late=()):
    size = factors.shape[2]
    half = tokens[0].shape[0] // (1 if late else 2)
    blocks = size // 2
    groups = pairs * blocks // BLK
    steps = blocks // (2 * WIDE)

    def chunk(n, s):
        return natural(n, s[2], steps // 2)

    def right_spec(half):
        return pl.BlockSpec(
            (1, WIDE * pairs, size), lambda n, s: (place(s[3], chunk(n, s)), half, 0)
        )

    diag = (groups, BLK, BLK)
    shapes = [
        jax.ShapeDtypeStruct((groups, BLK, 4 * half), BF16),
        jax.ShapeDtypeStruct((4 * half, groups * BLK), F32),
    ]
    scratch = [pltpu.VMEM((WIDE, pairs * WIDE, size), F32)]
    extra = list(late)
    if not late:
        shapes.append(jax.ShapeDtypeStruct(diag, BF16))
        scratch.append(pltpu.VMEM((BLK, BLK), F32))
        extra = [factors]
    return pl.pallas_call(
        functools.partial(student_kernel, steps, bool(late), tensor_count),
        grid_spec=pltpu.PrefetchScalarGridSpec(
            num_scalar_prefetch=1,
            grid=(steps,),
            in_specs=token_specs(half, 2 * WIDE * size, chunk, bool(late))
            + [right_spec(0), right_spec(1)]
            + [whole_spec(array) for array in extra],
            out_specs=[whole_spec(shape) for shape in shapes],
            scratch_shapes=scratch,
        ),
        out_shape=shapes,
        compiler_params=pltpu.CompilerParams(vmem_limit_bytes=40 * 2**20),
        cost_estimate=LARGE,
        name="student_part",
    )(scalars, *tokens, factors, factors, *extra)


def place(z, owner):
    bits = z ^ owner
    return lax.rem(bits, 2) * 2 + bits // 2


def left_kernel(chunks, scale, idx_ref, *refs):
    hidden, refs = refs[:4], refs[4:]
    weight_ref, rest0, rest1, mixed0, mixed1, left_ref, out_ref, back_ref, lhs = refs
    step = pl.program_id(0)
    parts, size = out_ref.shape[0], out_ref.shape[2]
    blocks = chunks * WIDE
    share = BLK // chunks
    fold = BLK // blocks
    pl.when(step == 0)(lambda: fill_rows(lhs, hidden))
    target = jnp.dot(lhs[...], weight_ref[...], preferred_element_type=F32)
    rest = jnp.concatenate([rest0[...], rest1[...]], axis=0)
    out_grad = ((rest - target) * scale).astype(BF16)
    mixed = jnp.concatenate([mixed0[0], mixed1[0]], axis=1)
    left = jnp.dot(mixed, out_grad, preferred_element_type=F32)
    value = lax.dot_general(left_ref[0], out_grad, NT, preferred_element_type=F32)
    value = value.astype(BF16)
    for c in range(chunks):
        back_ref[c] = value[c * share : (c + 1) * share]
    low = lax.broadcasted_iota(jnp.int32, (blocks, size), 1) < blocks
    rows = blocks // parts
    for pair in range(fold // 2):
        lanes = slice(pair * size, (pair + 1) * size)
        picked = []
        for a in (2 * pair, 2 * pair + 1):
            for c in range(chunks):
                begin = (c * fold + a) * WIDE
                picked.append(left[begin : begin + WIDE, lanes])
        turned = jnp.concatenate(picked, axis=0).T
        both = jnp.where(low, turned[:blocks], turned[blocks:]).astype(BF16)
        begin = pl.multiple_of((step * (fold // 2) + pair) * rows, rows)
        for owner in range(parts):
            out_ref[place(idx_ref[3], owner), pl.ds(begin, rows), :] = both[
                owner * rows : (owner + 1) * rows
            ]


def left_grads(hidden, weight, rest, mixed, left_diag, scalars, parts, pairs, size, scale):
    groups, count = left_diag.shape[0], 2 * rest[0].shape[0]
    width = hidden[0].shape[1]
    blocks = groups * BLK // pairs
    chunks = blocks // WIDE
    share = BLK // chunks
    column = pl.BlockSpec((count // 2, BLK), lambda n, s: (0, n))
    slab = pl.BlockSpec((1, BLK, count // 2), lambda n, s: (n, 0, 0))
    out_rows = pairs * blocks * blocks // size // parts
    return pl.pallas_call(
        functools.partial(left_kernel, chunks, scale),
        grid_spec=pltpu.PrefetchScalarGridSpec(
            num_scalar_prefetch=1,
            grid=(groups,),
            in_specs=[whole_spec(piece) for piece in hidden]
            + [pl.BlockSpec((width, BLK), lambda n, s: (1 - s[2], n))]
            + [column, column, slab, slab]
            + [pl.BlockSpec((1, BLK, BLK), lambda n, s: (n, 0, 0))],
            out_specs=[
                pl.BlockSpec((parts, out_rows, size), lambda n, s: (0, 0, 0)),
                pl.BlockSpec((chunks, share, count), lambda n, s: (0, n, 0)),
            ],
            scratch_shapes=[pltpu.VMEM((count, width), BF16)],
        ),
        out_shape=[
            jax.ShapeDtypeStruct((parts, out_rows, size), BF16),
            jax.ShapeDtypeStruct((chunks, groups * share, count), BF16),
        ],
        compiler_params=pltpu.CompilerParams(vmem_limit_bytes=40 * 2**20),
        cost_estimate=SMALL,
        name="left_grads",
    )(scalars, *hidden, weight, *rest, *mixed, left_diag)


def right_kernel(pairs, bit, idx_ref, *refs):
    own, near, far, (back_ref, out_ref, wide) = refs[:4], refs[4:8], refs[8:12], refs[12:]
    size = out_ref.shape[2]
    owner = idx_ref[3] ^ (2 * pl.program_id(0) + bit)

    def right(later):
        for half in range(2):
            lanes = slice(half * WIDE * size, (half + 1) * WIDE * size)
            rows = jnp.concatenate([piece[:, lanes] for piece in own + later], axis=0)
            value = jnp.dot(back_ref[half], rows, preferred_element_type=F32)
            for t in range(WIDE):
                wide[t] = value[:, t * size : (t + 1) * size]
            for t in range(WIDE):
                begin = (half * WIDE + t) * pairs
                out_ref[0, begin : begin + pairs, :] = wide[
                    t, pl.ds(t, pairs, stride=WIDE), :
                ].astype(BF16)

    pl.when(owner // 2 == idx_ref[2])(lambda: right(near))
    pl.when(owner // 2 != idx_ref[2])(lambda: right(far))


def right_grads(back, own, late, scalars, pairs, bit, size, cost):
    half = late[0].shape[0]
    rows, count = back.shape[1:]

    def owner(n, s):
        return s[3] ^ (2 * n + bit)

    return pl.pallas_call(
        functools.partial(right_kernel, pairs, bit),
        grid_spec=pltpu.PrefetchScalarGridSpec(
            num_scalar_prefetch=1,
            grid=(2,),
            in_specs=token_specs(half, 2 * WIDE * size, owner, False)
            + token_specs(half, 2 * WIDE * size, owner, True)
            + [pl.BlockSpec((2, rows, count), lambda n, s: (owner(n, s), 0, 0))],
            out_specs=pl.BlockSpec((1, 2 * WIDE * pairs, size), lambda n, s: (n, 0, 0)),
            scratch_shapes=[pltpu.VMEM((WIDE, pairs * WIDE, size), F32)],
        ),
        out_shape=jax.ShapeDtypeStruct((2, 2 * WIDE * pairs, size), BF16),
        compiler_params=pltpu.CompilerParams(vmem_limit_bytes=40 * 2**20),
        cost_estimate=cost,
        name="right_grads",
    )(scalars, *own, *late, back)


def tiled_body(tokens, gate_weight, up_weight, down_weight, right_factor, left_factor):
    fsdp_count = lax.axis_size("fsdp")
    tensor_count = lax.axis_size("tensor")
    rows, model = tokens.shape
    part = gate_weight.shape[1] // 2
    me, z = lax.axis_index("fsdp"), lax.axis_index("tensor")
    chip, core, odd = lax.div(me, 2), lax.rem(me, 2), lax.rem(z, 2)
    both_axes = ("fsdp", "tensor")

    def swap(value):
        return lax.ppermute(value, "fsdp", [(i, i ^ 1) for i in range(fsdp_count)])

    def across(value):
        return lax.ppermute(value, "fsdp", [(i, i ^ 2) for i in range(fsdp_count)])

    def along(value, bit):
        return lax.ppermute(value, "tensor", [(i, i ^ bit) for i in range(tensor_count)])

    def turn(value, bit):
        perm = []
        for f in range(fsdp_count):
            for t in range(tensor_count):
                perm.append((f * tensor_count + t, (t ^ bit) * tensor_count + f))
        return lax.ppermute(value, both_axes, perm)

    def after(value, *others):
        return lax.optimization_barrier((value,) + others)[0]

    def add(*terms):
        return sum(term.astype(F32) for term in terms)

    near_tokens = swap(tokens)
    first, rest = cut_tokens(tokens, odd, [1 - chip, chip])
    arrived = across(first)
    base = jnp.stack([odd, 1 - odd])
    mine_block = lax.div(part, BLK) * chip
    other_block = lax.div(part, BLK) * (1 - chip)

    def scalars(block):
        return jnp.concatenate([base, jnp.stack([me, core, block])]).astype(jnp.int32)

    own_pieces = [(t, row, 2) for t in (tokens, near_tokens) for row in (0, 1)]
    mine, other = products(
        own_pieces, after(scalars(other_block), first), gate_weight, up_weight, 0, part
    )

    pairs, blocks = left_factor.shape[0], left_factor.shape[2]
    turned = turn(after(right_factor, mine), 0)
    left_rows = pack_left(after(left_factor, mine))
    factors = jnp.concatenate(
        [after(turned, left_rows).reshape(-1, LANES), left_rows], axis=0
    )[None]
    sums = add(mine[0], swap(other[0])).astype(BF16)

    arrived = after(arrived, mine)
    partner = along(arrived, 1)
    near_arrived = swap(arrived)
    late_first = across(after(rest, mine))
    partner = after(partner, late_first, sums, factors)
    got_early = across(sums)
    more = along(after(factors, partner), 2)
    order = jnp.concatenate([base, jnp.stack([chip, z])]).astype(jnp.int32)
    own = [tokens, tokens, near_tokens, near_tokens]
    late = [arrived, partner, near_arrived, swap(partner)]
    late_pieces = [(t, None, 3) for t in late]
    late_order = after(scalars(other_block), sums)
    mine, other = products(late_pieces, late_order, gate_weight, up_weight, 0, part)
    near = swap(other[0])
    late_partner = along(after(late_first, mine), 1)
    mine_order = after(scalars(mine_block), mine)
    kept, other = products(
        own_pieces + late_pieces, mine_order, gate_weight, up_weight, 0, part
    )
    sums = add(mine[0], after(near, kept)).astype(BF16)
    got = across(sums)
    near_kept = swap(after(other, got_early, sums, more, late_partner))
    factors = jnp.concatenate([factors, after(more, kept)], axis=0)
    more = along(factors, 1)

    def activate(u, term):
        total = add(kept[u], near_kept[u], term)
        return (jax.nn.silu(total[0]) * total[1]).astype(BF16)

    hidden1 = activate(1, got_early)
    near1 = swap(hidden1)
    factors = jnp.concatenate([factors, after(more, hidden1)], axis=0)
    mixed0, rest0, left_diag = student_part(
        [after(tokens, hidden1, sums)] + own[1:], order, factors, pairs, tensor_count
    )
    got1 = across(after(hidden1, mixed0))
    target1 = target_part(1.0, [], hidden1, after(near1, mixed0), down_weight, chip)
    hidden0 = activate(0, after(got, target1))
    got0 = across(hidden0)
    near0 = swap(hidden0)
    late_partner = after(late_partner, mixed0)
    late += [late_first, late_partner, swap(after(late_first, mixed0)), swap(late_partner)]
    mixed1, rest1 = student_part(
        [after(late[0], hidden0)] + late[1:],
        order,
        factors,
        pairs,
        tensor_count,
        (left_diag, target1),
    )
    near0 = after(near0, mixed1)
    rest0 = target_part(-1.0, [rest0], hidden0, near0, down_weight, chip)
    got1, got0 = after(got1, mixed1), after(got0, rest0)
    hidden = [got0, got1, swap(got0), swap(got1)]

    size = right_factor.shape[2]
    left, back = left_grads(
        hidden,
        down_weight,
        (rest0, rest1),
        (mixed0, mixed1),
        left_diag,
        order,
        tensor_count,
        pairs,
        size,
        1.0 / math.sqrt(rows * fsdp_count),
    )
    got_left = along(left[2:], 1)
    sent = right_grads(back, own, late, order, pairs, 1, size, SMALL)
    left = add(left[:2], after(got_left, sent)).astype(BF16)
    got_left = along(left[1], 2)
    got_right = along(sent, 1)
    kept_back = after(back, sent, left)
    right = right_grads(kept_back, own, late, order, pairs, 0, size, LARGE)
    right = add(right, got_right).astype(BF16)
    grad_right = add(turn(right[0], 0), turn(right[1], 2))
    grad_left = add(left[0], got_left)
    grad_left = grad_left.reshape(pairs // 2, -1, 2, blocks).transpose(0, 2, 1, 3)
    return grad_right.reshape(right_factor.shape), grad_left.reshape(left_factor.shape)


def body(*args):
    tokens, gate_weight, _, _, right_factor, left_factor = args
    counts = (lax.axis_size("fsdp"), lax.axis_size("tensor"))
    feat, hid = gate_weight.shape
    per_owner, share, size = right_factor.shape
    blocks = left_factor.shape[2]
    fits = hid % (2 * BLK) == 0
    fits = fits and counts == (4, 4) and tokens.shape[0] == 128
    fits = fits and hid >= 4 * BLK and feat % BLK == 0
    fits = fits and size == 128 and 2 * blocks == size and per_owner % WIDE == 0
    fits = fits and left_factor.shape[0] == share and share % 16 == 0
    return (tiled_body if fits else general_body)(*args)


def solution(mesh):
    return jax.shard_map(
        body,
        mesh=mesh,
        in_specs=(
            P(("groups", "fsdp"), None),
            P("fsdp", "tensor"),
            P("fsdp", "tensor"),
            P("tensor", "fsdp"),
            P("fsdp", "tensor", None),
            P("fsdp", "tensor", None),
        ),
        out_specs=(P(("groups", "fsdp"), "tensor", None), P(("groups", "fsdp"), "tensor", None)),
        check_vma=False,
    )
```

```python
import functools
import math

import jax
import jax.numpy as jnp
from jax import lax
from jax.experimental import pallas as pl
from jax.experimental.pallas import tpu as pltpu
from jax.sharding import PartitionSpec as P

BLK = 256
LANES = 128
SMALL = pl.CostEstimate(flops=1, bytes_accessed=1, transcendentals=0)
LARGE = pl.CostEstimate(flops=10**10, bytes_accessed=10**7, transcendentals=0)
F32 = jnp.float32
BF16 = jnp.bfloat16


def gate_up_kernel(idx_ref, top_ref, bottom_ref, gate_ref, up_ref, mine_ref, other_ref):
    rows = top_ref.shape[0]
    lhs = jnp.concatenate([top_ref[...], bottom_ref[...]], axis=0)
    for slot, weight_ref in enumerate((gate_ref, up_ref)):
        product = jnp.dot(lhs, weight_ref[...], preferred_element_type=F32).astype(BF16)
        mine_ref[slot] = product[:rows]
        other_ref[slot] = product[rows:]


def gate_up(top, top_block, bottom, gate, up, column, first, width):
    rows, feat = bottom.shape
    if width % BLK or gate.shape[1] % BLK or rows % 16 or feat % 128:
        lhs = jnp.concatenate(
            [lax.dynamic_slice_in_dim(top, top_block * feat, feat, 1), bottom], axis=0
        )
        both = [
            jnp.dot(
                lhs,
                lax.dynamic_slice_in_dim(w, column + first, width, 1),
                preferred_element_type=F32,
            ).astype(BF16)
            for w in (gate, up)
        ]
        both = jnp.stack(both)
        return both[:, :rows], both[:, rows:]
    scalars = jnp.stack([top_block, lax.div(column, BLK) + first // BLK]).astype(jnp.int32)
    weight_spec = pl.BlockSpec((feat, BLK), lambda n, s: (0, s[1] + n))
    out_spec = pl.BlockSpec((2, rows, BLK), lambda n, s: (0, 0, n))
    shape = jax.ShapeDtypeStruct((2, rows, width), BF16)
    return pl.pallas_call(
        gate_up_kernel,
        grid_spec=pltpu.PrefetchScalarGridSpec(
            num_scalar_prefetch=1,
            grid=(width // BLK,),
            in_specs=[
                pl.BlockSpec((rows, feat), lambda n, s: (0, s[0])),
                pl.BlockSpec((rows, feat), lambda n, s: (0, 0)),
                weight_spec,
                weight_spec,
            ],
            out_specs=[out_spec, out_spec],
        ),
        out_shape=[shape, shape],
        compiler_params=pltpu.CompilerParams(vmem_limit_bytes=40 * 2**20),
        cost_estimate=pl.CostEstimate(
            flops=2 * 2 * rows * feat * 2 * width,
            bytes_accessed=2 * feat * 2 * width + 2 * 2 * rows * (feat + 2 * width),
            transcendentals=0,
        ),
        name="gate_up",
    )(scalars, top, bottom, gate, up)


def down_kernel(idx_ref, mine_ref, other_ref, weight_ref, *refs):
    out_ref = refs[-1]
    lhs = jnp.concatenate([mine_ref[...], other_ref[...]], axis=0)
    product = jnp.dot(lhs, weight_ref[...], preferred_element_type=F32)

    @pl.when(pl.program_id(0) == 0)
    def _():
        out_ref[...] = refs[0][...] + product if len(refs) > 1 else product

    @pl.when(pl.program_id(0) > 0)
    def _():
        out_ref[...] += product


def down_add(total, mine, other, weight, row):
    rows, width = mine.shape
    outs = weight.shape[1]
    if width % BLK or weight.shape[0] % BLK or rows % 16 or outs % 128:
        lhs = jnp.concatenate([mine, other], axis=0)
        part = lax.dynamic_slice_in_dim(weight, row, width, 0)
        product = jnp.dot(lhs, part, preferred_element_type=F32)
        return product if total is None else total + product
    scalars = jnp.reshape(lax.div(row, BLK), (1,)).astype(jnp.int32)
    hidden_spec = pl.BlockSpec((rows, BLK), lambda k, s: (0, k))
    whole = pl.BlockSpec((2 * rows, outs), lambda k, s: (0, 0))
    totals = [] if total is None else [total]
    return pl.pallas_call(
        down_kernel,
        grid_spec=pltpu.PrefetchScalarGridSpec(
            num_scalar_prefetch=1,
            grid=(width // BLK,),
            in_specs=[
                hidden_spec,
                hidden_spec,
                pl.BlockSpec((BLK, outs), lambda k, s: (s[0] + k, 0)),
            ]
            + [whole] * len(totals),
            out_specs=whole,
        ),
        out_shape=jax.ShapeDtypeStruct((2 * rows, outs), F32),
        compiler_params=pltpu.CompilerParams(vmem_limit_bytes=40 * 2**20),
        cost_estimate=pl.CostEstimate(
            flops=2 * 2 * rows * width * outs,
            bytes_accessed=2 * width * outs + 2 * 2 * rows * width + 16 * rows * outs,
            transcendentals=0,
        ),
        name="down_add",
    )(scalars, mine, other, weight, *totals)


def general_body(tokens, gate_weight, up_weight, down_weight, right_factor, left_factor):
    fsdp_count = lax.axis_size("fsdp")
    tensor_count = lax.axis_size("tensor")
    chips = fsdp_count // 2
    rows, model = tokens.shape
    feat, hid = gate_weight.shape
    part = hid // chips
    me = lax.axis_index("fsdp")
    chip, core = lax.div(me, 2), lax.rem(me, 2)
    z = lax.axis_index("tensor")

    def swap(value):
        return lax.ppermute(value, "fsdp", [(i, i ^ 1) for i in range(fsdp_count)])

    def shift(value, hops):
        perm = [(i, (i + 2 * hops) % fsdp_count) for i in range(fsdp_count)]
        return lax.ppermute(value, "fsdp", perm)

    def gather_z(value):
        if tensor_count > 4:
            return lax.all_gather(value, "tensor", axis=0, tiled=True)
        size = value.shape[0]
        whole = jnp.zeros((size * tensor_count,) + value.shape[1:], value.dtype)
        whole = lax.dynamic_update_slice_in_dim(whole, value, z * size, 0)
        for step in range(1, tensor_count):
            perm = [(i, (i + step) % tensor_count) for i in range(tensor_count)]
            got = lax.ppermute(value, "tensor", perm)
            source = lax.rem(z - step + tensor_count, tensor_count)
            whole = lax.dynamic_update_slice_in_dim(whole, got, source * size, 0)
        return whole

    def scatter_z(value):
        if tensor_count > 4:
            return lax.psum_scatter(value, "tensor", scatter_dimension=0, tiled=False)
        total = lax.dynamic_index_in_dim(value, z, 0, keepdims=False)
        for step in range(1, tensor_count):
            target_z = lax.rem(z + step, tensor_count)
            piece = lax.dynamic_index_in_dim(value, target_z, 0, keepdims=False)
            perm = [(i, (i + step) % tensor_count) for i in range(tensor_count)]
            total += lax.ppermute(piece.astype(BF16), "tensor", perm).astype(F32)
        return total

    def columns(value, start, width):
        return lax.dynamic_slice_in_dim(value, start, width, 1)

    def after(value, *others):
        return lax.optimization_barrier((value,) + others)[0]

    def pair_z(value):
        perm = [(i, i ^ 1) for i in range(tensor_count)]
        got = lax.ppermute(value, "tensor", perm)
        odd = lax.rem(z, 2) == 1
        return jnp.concatenate(
            [jnp.where(odd, got, value), jnp.where(odd, value, got)], axis=0
        )

    if part % BLK == 0 and part // BLK > 1:
        head = (part // BLK + 1) // 2 * BLK
        chunks = [(0, head), (head, part - head)]
    else:
        chunks = [(0, part)]

    half = rows // 2
    own_half = lax.dynamic_slice_in_dim(tokens, lax.rem(z, 2) * half, half, 0)

    def send_tokens(value, dt, g):
        features = lax.rem(chip - dt + g + chips, chips) * (2 * feat)
        return shift(columns(value, features, 2 * feat), -dt)

    def partial(pair, dp, first, width):
        column = lax.rem(chip + dp, chips) * part
        top, block, bottom = pair
        mine, other = gate_up(top, block, bottom, gate_weight, up_weight, column, first, width)
        return mine, swap(other)

    def send_partials(pair, got, dt):
        sums = []
        for dp in range(1, chips):
            pieces = [partial(pair, dp, *chunk) for chunk in chunks]
            for n, (mine, from_core) in enumerate(pieces):
                both = (mine.astype(F32) + from_core.astype(F32)).astype(BF16)
                got[dt, dp, n] = shift(both, dp)
                sums.append(both)
        return sums

    got, kept, gathered = {}, {}, {}
    local = swap(columns(tokens, (me ^ 1) * feat, feat))
    arrived = {dt: send_tokens(own_half, dt, 0) for dt in range(1, chips)}
    sums = send_partials((tokens, me, local), got, 0)
    if sums:
        local = after(local, *sums)
    kept[0] = partial((tokens, me, local), 0, 0, part)
    late_tokens = after(tokens, kept[0][0])
    neighbour_tokens = swap(late_tokens)
    late_half = after(own_half, *sums) if sums else own_half

    for dt in range(1, chips):
        gathered[dt, 0] = pair_z(after(arrived[dt], *sums))
        whole = gathered[dt, 0]
        top = columns(whole, core * feat, feat)
        bottom = swap(columns(whole, (1 - core) * feat, feat))
        pair = (top, jnp.int32(0), bottom)
        sums = send_partials(pair, got, dt)
        pair = (top, jnp.int32(0), after(bottom, *sums))
        kept[dt] = partial(pair, 0, 0, part)
        for g in range(1, chips):
            gathered[dt, g] = pair_z(after(send_tokens(late_half, dt, g), kept[dt][0]))

    def activate(e, first, width, n):
        terms = [lax.slice_in_dim(term, first, first + width, axis=2) for term in kept[e]]
        terms += [got[(e + dp) % chips, dp, n] for dp in range(1, chips)]
        total = sum(term.astype(F32) for term in terms)
        return (jax.nn.silu(total[0]) * total[1]).astype(BF16)

    totals = {u: None for u in range(chips)}
    for e in list(range(1, chips)) + [0]:
        values = [activate(e, *chunk, n) for n, chunk in enumerate(chunks)]
        spans = list(chunks)
        if e:
            values, spans = [jnp.concatenate(values, axis=1)], [(0, part)]
        sent = [[value] + [shift(value, d) for d in range(1, chips)] for value in values]
        for (first, width), copies in zip(spans, sent):
            for d, mine in enumerate(copies):
                u = (e - d + chips) % chips
                row = lax.rem(chip - d + chips, chips) * part + first
                totals[u] = down_add(totals[u], mine, swap(mine), down_weight, row)

    token_rows = []
    for dt in range(chips):
        if dt == 0:
            token_rows += [tokens, neighbour_tokens]
            continue
        else:
            full = jnp.zeros((rows, model), BF16)
            for g in range(chips):
                features = lax.rem(chip + g, chips) * (2 * feat)
                full = lax.dynamic_update_slice_in_dim(full, gathered[dt, g], features, 1)
        token_rows += [full, swap(full)]
    inputs = jnp.concatenate(token_rows, axis=0)
    count = inputs.shape[0]

    blocks, share, size = right_factor.shape
    ratio = tensor_count // fsdp_count
    turn = []
    for a in range(fsdp_count):
        for b in range(tensor_count):
            turn.append((a * tensor_count + b, (b // ratio) * tensor_count + a * ratio + b % ratio))
    back = [(b, a) for a, b in turn]
    right_rows = gather_z(lax.ppermute(right_factor, ("fsdp", "tensor"), turn)[None])
    right_rows = right_rows.reshape(fsdp_count, ratio, blocks, share, size)
    right_rows = right_rows.transpose(0, 2, 1, 3, 4).reshape(
        fsdp_count * blocks, ratio * share, size
    )
    left_rows = jnp.moveaxis(gather_z(jnp.moveaxis(left_factor, 1, 0)), 0, 1)

    block_input = inputs.reshape(count, fsdp_count * blocks, size)
    mixed = jnp.einsum(
        "nim,ijm->nij", block_input, right_rows, preferred_element_type=F32
    ).astype(BF16)
    student = jnp.einsum("nij,jki->njk", mixed, left_rows, preferred_element_type=F32)
    target = jnp.concatenate([totals[u] for u in range(chips)], axis=0)
    scale = 1.0 / math.sqrt(count)
    out_grad = (student * (1.0 / tensor_count) - target.reshape(student.shape)) * scale
    out_grad = out_grad.astype(BF16)
    grad_left = jnp.einsum("njk,nij->kji", out_grad, mixed, preferred_element_type=F32)
    mixed_grad = jnp.einsum(
        "njk,jki->nij", out_grad, left_rows, preferred_element_type=F32
    ).astype(BF16)
    grad_right = jnp.einsum(
        "nij,nim->ijm", mixed_grad, block_input, preferred_element_type=F32
    )
    grad_left = scatter_z(
        grad_left.reshape((tensor_count, -1) + grad_left.shape[1:])
    )
    grad_left = jnp.moveaxis(grad_left, 0, 1)
    grad_right = grad_right.reshape(fsdp_count, blocks, ratio, share, size)
    grad_right = grad_right.transpose(0, 2, 1, 3, 4).reshape(
        tensor_count, blocks, share, size
    )
    grad_right = lax.ppermute(scatter_z(grad_right), ("fsdp", "tensor"), back)
    return grad_right, grad_left


def cut_kernel(count, idx_ref, *refs):
    for in_ref, out_ref in zip(refs[:count], refs[count:]):
        out_ref[...] = in_ref[...]


def cut_tokens(tokens, row, columns):
    block = (tokens.shape[0] // 2, tokens.shape[1] // 2)
    count = len(columns)
    return pl.pallas_call(
        functools.partial(cut_kernel, count),
        grid_spec=pltpu.PrefetchScalarGridSpec(
            num_scalar_prefetch=1,
            grid=(1,),
            in_specs=[
                pl.BlockSpec(block, lambda n, s, k=k: (s[0], s[1 + k])) for k in range(count)
            ],
            out_specs=[pl.BlockSpec(block, lambda n, s: (0, 0))] * count,
        ),
        out_shape=[jax.ShapeDtypeStruct(block, BF16)] * count,
        cost_estimate=SMALL,
        name="cut_tokens",
    )(jnp.stack([row, *columns]).astype(jnp.int32), *[tokens] * count)


def pack_kernel(left_ref, out_ref):
    share = left_ref.shape[1]
    for pair in range(left_ref.shape[0] // 2):
        both = [left_ref[2 * pair].astype(F32), left_ref[2 * pair + 1].astype(F32)]
        both = jnp.concatenate(both, axis=1)
        out_ref[pair * share : (pair + 1) * share, :] = both.astype(BF16)


def pack_left(left):
    pairs, share, blocks = left.shape
    return pl.pallas_call(
        pack_kernel,
        out_shape=jax.ShapeDtypeStruct((pairs // 2 * share, 2 * blocks), BF16),
        cost_estimate=LARGE,
        name="pack_left",
    )(left)


def products_kernel(sets, idx_ref, *refs):
    pieces, (gate_ref, up_ref, mine_ref, other_ref) = refs[: 4 * sets], refs[4 * sets :]
    lhs = jnp.concatenate([piece[...] for piece in pieces], axis=0)
    rows = mine_ref.shape[2]
    for slot, weight_ref in enumerate((gate_ref, up_ref)):
        product = jnp.dot(lhs, weight_ref[...], preferred_element_type=F32).astype(BF16)
        for u in range(sets):
            mine_ref[u, slot] = product[2 * u * rows : (2 * u + 1) * rows]
            other_ref[u, slot] = product[(2 * u + 1) * rows : (2 * u + 2) * rows]


def products(pieces, scalars, gate, up, first, width):
    feat = gate.shape[0]
    sets = len(pieces) // 4
    half = pieces[0][0].shape[0] // (1 if pieces[0][1] is None else 2)
    start = first // BLK

    def piece_spec(row, column):
        if row is None:
            return pl.BlockSpec((half, feat), lambda n, s: (0, s[column]))
        return pl.BlockSpec((half, feat), lambda n, s: (s[row], s[column]))

    weight_spec = pl.BlockSpec(
        (feat, BLK), lambda n, s: (0, s[4] + start + n)
    )
    out_spec = pl.BlockSpec((sets, 2, 2 * half, BLK), lambda n, s: (0, 0, 0, n))
    shape = jax.ShapeDtypeStruct((sets, 2, 2 * half, width), BF16)
    return pl.pallas_call(
        functools.partial(products_kernel, sets),
        grid_spec=pltpu.PrefetchScalarGridSpec(
            num_scalar_prefetch=1,
            grid=(width // BLK,),
            in_specs=[piece_spec(row, column) for _, row, column in pieces]
            + [weight_spec, weight_spec],
            out_specs=[out_spec, out_spec],
        ),
        out_shape=[shape, shape],
        compiler_params=pltpu.CompilerParams(vmem_limit_bytes=40 * 2**20),
        cost_estimate=LARGE if sets > 1 else SMALL,
        name="gate_up_products",
    )(scalars, *[piece for piece, _, _ in pieces], gate, up)


def fill_rows(lhs, pieces):
    rows = pieces[0].shape[0]
    for place, which in enumerate((1, 3, 0, 2)):
        lhs[place * rows : (place + 1) * rows, :] = pieces[which][...]


def whole_spec(array):
    return pl.BlockSpec(array.shape, lambda n, s: (0,) * len(array.shape))


def target_kernel(sign, idx_ref, mine_ref, near_ref, weight_ref, *refs):
    terms, out_ref = refs[:-1], refs[-1]
    lhs = jnp.concatenate([mine_ref[...], near_ref[...]], axis=0)
    product = jnp.dot(lhs, weight_ref[...], preferred_element_type=F32)
    out_ref[...] = sum((ref[...] for ref in terms), sign * product)


def target_part(sign, terms, mine, near, weight, chip):
    rows, width = mine.shape
    outs = weight.shape[1]
    wide = 2 * BLK if outs % (2 * BLK) == 0 else BLK
    block = pl.BlockSpec((2 * rows, wide), lambda n, s: (0, n))
    return pl.pallas_call(
        functools.partial(target_kernel, sign),
        grid_spec=pltpu.PrefetchScalarGridSpec(
            num_scalar_prefetch=1,
            grid=(outs // wide,),
            in_specs=[whole_spec(mine), whole_spec(near)]
            + [pl.BlockSpec((width, wide), lambda n, s: (s[0], n))]
            + [block] * len(terms),
            out_specs=block,
        ),
        out_shape=jax.ShapeDtypeStruct((2 * rows, outs), F32),
        compiler_params=pltpu.CompilerParams(vmem_limit_bytes=40 * 2**20),
        cost_estimate=SMALL,
        name="target_part",
    )(jnp.reshape(chip, (1,)).astype(jnp.int32), mine, near, weight, *terms)


TN = (((0,), (0,)), ((), ()))
NT = (((1,), (1,)), ((), ()))
WIDE = 8


def natural(step, chip, per_chip):
    return lax.rem(chip + step // per_chip, 2) * per_chip + lax.rem(step, per_chip)


def spread_left(z, rows_ref, out_ref, scratch):
    groups = out_ref.shape[0]
    parts, _, size = rows_ref.shape
    blocks = size // 2
    share = blocks // parts
    fold = BLK // blocks
    begin = rows_ref.shape[1] - groups * fold // 2 * share
    scratch[...] = jnp.zeros_like(scratch)
    low = lax.broadcasted_iota(jnp.int32, (blocks, size), 1) < blocks
    for g in range(groups):
        for pair in range(fold // 2):
            row = begin + (g * (fold // 2) + pair) * share
            picked = [
                rows_ref[place(z, owner), row : row + share, :] for owner in range(parts)
            ]
            turned = jnp.concatenate(picked + picked, axis=0).astype(F32).T
            for a in range(2):
                value = turned[a * blocks : (a + 1) * blocks]
                value = jnp.where(low if a == 0 else ~low, value, 0.0)
                lanes = slice(pair * size, (pair + 1) * size)
                for c in range(blocks // WIDE):
                    row = (c * fold + 2 * pair + a) * WIDE
                    scratch[row : row + WIDE, lanes] = value[c * WIDE : (c + 1) * WIDE]
        out_ref[g] = scratch[...].astype(BF16)


def student_kernel(steps, late, tensor_count, idx_ref, *refs):
    tokens, refs = refs[: 8 if late else 4], refs[8 if late else 4 :]
    rights, left_ref, refs = refs[:2], refs[2], refs[3:]
    step = pl.program_id(0)
    if late:
        target_ref, mixed_ref, student_ref, spread = refs
    else:
        mixed_ref, student_ref, diag_ref, spread, scratch = refs
        rows_ref, left_ref = left_ref, diag_ref
        pl.when(step == 0)(lambda: spread_left(idx_ref[3], rows_ref, diag_ref, scratch))
    pair = natural(step, idx_ref[2], steps // 2)
    groups = left_ref.shape[0]
    size = spread.shape[2]
    pairs = spread.shape[1] // WIDE
    share = BLK // groups

    @pl.when(step == 0)
    def _():
        spread[...] = jnp.zeros_like(spread)

    def mix(pieces):
        for half, right_ref in enumerate(rights):
            for t in range(WIDE):
                value = right_ref[0, t * pairs : (t + 1) * pairs, :].astype(F32)
                spread[t, pl.ds(t, pairs, stride=WIDE), :] = value
            factor = jnp.concatenate([spread[t] for t in range(WIDE)], axis=1).astype(BF16)
            lanes = slice(half * WIDE * size, (half + 1) * WIDE * size)
            rows = jnp.concatenate([piece[:, lanes] for piece in pieces], axis=0)
            part = lax.dot_general(factor, rows, NT, preferred_element_type=F32).astype(BF16)
            start = pl.multiple_of((2 * pair + half) * share, share)
            for g in range(groups):
                mixed_ref[g, pl.ds(start, share), :] = part[g * share : (g + 1) * share]

    if late:
        pl.when(step < steps // 2)(lambda: mix(tokens[:4]))
        pl.when(step >= steps // 2)(lambda: mix(tokens[4:]))
    else:
        mix(tokens)

    @pl.when(step == steps - 1)
    def _():
        for g in range(groups):
            span = slice(g * BLK, (g + 1) * BLK)
            student = lax.dot_general(
                mixed_ref[g], left_ref[g], TN, preferred_element_type=F32
            )
            student = student * (1.0 / tensor_count)
            student_ref[:, span] = student - target_ref[:, span] if late else student


def token_specs(half, width, chunk, late):
    if not late:
        return [
            pl.BlockSpec((half, width), lambda n, s, p=p: (s[p % 2], chunk(n, s)))
            for p in range(4)
        ]
    inner = pl.BlockSpec((half, width), lambda n, s: (0, lax.rem(chunk(n, s), 2)))
    return [inner] * 8


def student_part(tokens, scalars, factors, pairs, tensor_count, late=()):
    size = factors.shape[2]
    half = tokens[0].shape[0] // (1 if late else 2)
    blocks = size // 2
    groups = pairs * blocks // BLK
    steps = blocks // (2 * WIDE)

    def chunk(n, s):
        return natural(n, s[2], steps // 2)

    def right_spec(half):
        return pl.BlockSpec(
            (1, WIDE * pairs, size), lambda n, s: (place(s[3], chunk(n, s)), half, 0)
        )

    diag = (groups, BLK, BLK)
    shapes = [
        jax.ShapeDtypeStruct((groups, BLK, 4 * half), BF16),
        jax.ShapeDtypeStruct((4 * half, groups * BLK), F32),
    ]
    scratch = [pltpu.VMEM((WIDE, pairs * WIDE, size), F32)]
    extra = list(late)
    if not late:
        shapes.append(jax.ShapeDtypeStruct(diag, BF16))
        scratch.append(pltpu.VMEM((BLK, BLK), F32))
        extra = [factors]
    return pl.pallas_call(
        functools.partial(student_kernel, steps, bool(late), tensor_count),
        grid_spec=pltpu.PrefetchScalarGridSpec(
            num_scalar_prefetch=1,
            grid=(steps,),
            in_specs=token_specs(half, 2 * WIDE * size, chunk, bool(late))
            + [right_spec(0), right_spec(1)]
            + [whole_spec(array) for array in extra],
            out_specs=[whole_spec(shape) for shape in shapes],
            scratch_shapes=scratch,
        ),
        out_shape=shapes,
        compiler_params=pltpu.CompilerParams(vmem_limit_bytes=40 * 2**20),
        cost_estimate=LARGE,
        name="student_part",
    )(scalars, *tokens, factors, factors, *extra)


def place(z, owner):
    bits = z ^ owner
    return lax.rem(bits, 2) * 2 + bits // 2


def left_kernel(chunks, scale, idx_ref, *refs):
    hidden, refs = refs[:4], refs[4:]
    weight_ref, rest0, rest1, mixed0, mixed1, left_ref, out_ref, back_ref, lhs = refs
    step = pl.program_id(0)
    parts, size = out_ref.shape[0], out_ref.shape[2]
    blocks = chunks * WIDE
    share = BLK // chunks
    fold = BLK // blocks
    pl.when(step == 0)(lambda: fill_rows(lhs, hidden))
    target = jnp.dot(lhs[...], weight_ref[...], preferred_element_type=F32)
    rest = jnp.concatenate([rest0[...], rest1[...]], axis=0)
    out_grad = ((rest - target) * scale).astype(BF16)
    mixed = jnp.concatenate([mixed0[0], mixed1[0]], axis=1)
    left = jnp.dot(mixed, out_grad, preferred_element_type=F32)
    value = lax.dot_general(left_ref[0], out_grad, NT, preferred_element_type=F32)
    value = value.astype(BF16)
    for c in range(chunks):
        back_ref[c] = value[c * share : (c + 1) * share]
    low = lax.broadcasted_iota(jnp.int32, (blocks, size), 1) < blocks
    rows = blocks // parts
    for pair in range(fold // 2):
        lanes = slice(pair * size, (pair + 1) * size)
        picked = []
        for a in (2 * pair, 2 * pair + 1):
            for c in range(chunks):
                begin = (c * fold + a) * WIDE
                picked.append(left[begin : begin + WIDE, lanes])
        turned = jnp.concatenate(picked, axis=0).T
        both = jnp.where(low, turned[:blocks], turned[blocks:]).astype(BF16)
        begin = pl.multiple_of((step * (fold // 2) + pair) * rows, rows)
        for owner in range(parts):
            out_ref[place(idx_ref[3], owner), pl.ds(begin, rows), :] = both[
                owner * rows : (owner + 1) * rows
            ]


def left_grads(hidden, weight, rest, mixed, left_diag, scalars, parts, pairs, size, scale):
    groups, count = left_diag.shape[0], 2 * rest[0].shape[0]
    width = hidden[0].shape[1]
    blocks = groups * BLK // pairs
    chunks = blocks // WIDE
    share = BLK // chunks
    column = pl.BlockSpec((count // 2, BLK), lambda n, s: (0, n))
    slab = pl.BlockSpec((1, BLK, count // 2), lambda n, s: (n, 0, 0))
    out_rows = pairs * blocks * blocks // size // parts
    return pl.pallas_call(
        functools.partial(left_kernel, chunks, scale),
        grid_spec=pltpu.PrefetchScalarGridSpec(
            num_scalar_prefetch=1,
            grid=(groups,),
            in_specs=[whole_spec(piece) for piece in hidden]
            + [pl.BlockSpec((width, BLK), lambda n, s: (1 - s[2], n))]
            + [column, column, slab, slab]
            + [pl.BlockSpec((1, BLK, BLK), lambda n, s: (n, 0, 0))],
            out_specs=[
                pl.BlockSpec((parts, out_rows, size), lambda n, s: (0, 0, 0)),
                pl.BlockSpec((chunks, share, count), lambda n, s: (0, n, 0)),
            ],
            scratch_shapes=[pltpu.VMEM((count, width), BF16)],
        ),
        out_shape=[
            jax.ShapeDtypeStruct((parts, out_rows, size), BF16),
            jax.ShapeDtypeStruct((chunks, groups * share, count), BF16),
        ],
        compiler_params=pltpu.CompilerParams(vmem_limit_bytes=40 * 2**20),
        cost_estimate=SMALL,
        name="left_grads",
    )(scalars, *hidden, weight, *rest, *mixed, left_diag)


def right_kernel(pairs, bit, idx_ref, *refs):
    own, near, far, (back_ref, out_ref, wide) = refs[:4], refs[4:8], refs[8:12], refs[12:]
    size = out_ref.shape[2]
    owner = idx_ref[3] ^ (2 * pl.program_id(0) + bit)

    def right(later):
        for half in range(2):
            lanes = slice(half * WIDE * size, (half + 1) * WIDE * size)
            rows = jnp.concatenate([piece[:, lanes] for piece in own + later], axis=0)
            value = jnp.dot(back_ref[half], rows, preferred_element_type=F32)
            for t in range(WIDE):
                wide[t] = value[:, t * size : (t + 1) * size]
            for t in range(WIDE):
                begin = (half * WIDE + t) * pairs
                out_ref[0, begin : begin + pairs, :] = wide[
                    t, pl.ds(t, pairs, stride=WIDE), :
                ].astype(BF16)

    pl.when(owner // 2 == idx_ref[2])(lambda: right(near))
    pl.when(owner // 2 != idx_ref[2])(lambda: right(far))


def right_grads(back, own, late, scalars, pairs, bit, size, cost):
    half = late[0].shape[0]
    rows, count = back.shape[1:]

    def owner(n, s):
        return s[3] ^ (2 * n + bit)

    return pl.pallas_call(
        functools.partial(right_kernel, pairs, bit),
        grid_spec=pltpu.PrefetchScalarGridSpec(
            num_scalar_prefetch=1,
            grid=(2,),
            in_specs=token_specs(half, 2 * WIDE * size, owner, False)
            + token_specs(half, 2 * WIDE * size, owner, True)
            + [pl.BlockSpec((2, rows, count), lambda n, s: (owner(n, s), 0, 0))],
            out_specs=pl.BlockSpec((1, 2 * WIDE * pairs, size), lambda n, s: (n, 0, 0)),
            scratch_shapes=[pltpu.VMEM((WIDE, pairs * WIDE, size), F32)],
        ),
        out_shape=jax.ShapeDtypeStruct((2, 2 * WIDE * pairs, size), BF16),
        compiler_params=pltpu.CompilerParams(vmem_limit_bytes=40 * 2**20),
        cost_estimate=cost,
        name="right_grads",
    )(scalars, *own, *late, back)


def tiled_body(tokens, gate_weight, up_weight, down_weight, right_factor, left_factor):
    fsdp_count = lax.axis_size("fsdp")
    tensor_count = lax.axis_size("tensor")
    rows, model = tokens.shape
    part = gate_weight.shape[1] // 2
    me, z = lax.axis_index("fsdp"), lax.axis_index("tensor")
    chip, core, odd = lax.div(me, 2), lax.rem(me, 2), lax.rem(z, 2)
    both_axes = ("fsdp", "tensor")

    def swap(value):
        return lax.ppermute(value, "fsdp", [(i, i ^ 1) for i in range(fsdp_count)])

    def across(value):
        return lax.ppermute(value, "fsdp", [(i, i ^ 2) for i in range(fsdp_count)])

    def along(value, bit):
        return lax.ppermute(value, "tensor", [(i, i ^ bit) for i in range(tensor_count)])

    def turn(value, bit):
        perm = []
        for f in range(fsdp_count):
            for t in range(tensor_count):
                perm.append((f * tensor_count + t, (t ^ bit) * tensor_count + f))
        return lax.ppermute(value, both_axes, perm)

    def after(value, *others):
        return lax.optimization_barrier((value,) + others)[0]

    def add(*terms):
        return sum(term.astype(F32) for term in terms)

    near_tokens = swap(tokens)
    first, rest = cut_tokens(tokens, odd, [1 - chip, chip])
    arrived = across(first)
    base = jnp.stack([odd, 1 - odd])
    mine_block = lax.div(part, BLK) * chip
    other_block = lax.div(part, BLK) * (1 - chip)

    def scalars(block):
        return jnp.concatenate([base, jnp.stack([me, core, block])]).astype(jnp.int32)

    own_pieces = [(t, row, 2) for t in (tokens, near_tokens) for row in (0, 1)]
    mine, other = products(
        own_pieces, after(scalars(other_block), first), gate_weight, up_weight, 0, part
    )

    pairs, blocks = left_factor.shape[0], left_factor.shape[2]
    turned = turn(after(right_factor, mine), 0)
    left_rows = pack_left(after(left_factor, mine))
    factors = jnp.concatenate(
        [after(turned, left_rows).reshape(-1, LANES), left_rows], axis=0
    )[None]
    sums = add(mine[0], swap(other[0])).astype(BF16)

    arrived = after(arrived, mine)
    partner = along(arrived, 1)
    near_arrived = swap(arrived)
    late_first = across(after(rest, mine))
    partner = after(partner, sums, factors)
    got_early = across(sums)
    more = along(after(factors, partner), 2)
    order = jnp.concatenate([base, jnp.stack([chip, z])]).astype(jnp.int32)
    own = [tokens, tokens, near_tokens, near_tokens]
    late = [arrived, partner, near_arrived, swap(partner)]
    late_pieces = [(t, None, 3) for t in late]
    late_order = after(scalars(other_block), sums)
    mine, other = products(late_pieces, late_order, gate_weight, up_weight, 0, part)
    near = swap(after(other[0], late_first))
    factors = jnp.concatenate([factors, after(more, mine)], axis=0)
    more = along(factors, 1)
    mine_order = after(scalars(mine_block), mine)
    kept, other = products(
        own_pieces + late_pieces, mine_order, gate_weight, up_weight, 0, part
    )
    sums = add(mine[0], after(near, kept)).astype(BF16)
    got = across(sums)
    near_kept = swap(after(other, got_early, sums, more))
    late_partner = along(after(late_first, kept), 1)

    def activate(u, term):
        total = add(kept[u], near_kept[u], term)
        return (jax.nn.silu(total[0]) * total[1]).astype(BF16)

    hidden1 = activate(1, got_early)
    near1 = swap(hidden1)
    factors = jnp.concatenate([factors, after(more, hidden1)], axis=0)
    mixed0, rest0, left_diag = student_part(
        [after(tokens, hidden1, sums)] + own[1:], order, factors, pairs, tensor_count
    )
    got1 = across(after(hidden1, mixed0))
    target1 = target_part(1.0, [], hidden1, after(near1, mixed0), down_weight, chip)
    hidden0 = activate(0, after(got, target1))
    got0 = across(hidden0)
    near0 = swap(hidden0)
    late_partner = after(late_partner, mixed0)
    late += [late_first, late_partner, swap(after(late_first, mixed0)), swap(late_partner)]
    mixed1, rest1 = student_part(
        [after(late[0], hidden0)] + late[1:],
        order,
        factors,
        pairs,
        tensor_count,
        (left_diag, target1),
    )
    near0 = after(near0, mixed1)
    rest0 = target_part(-1.0, [rest0], hidden0, near0, down_weight, chip)
    got1, got0 = after(got1, mixed1), after(got0, rest0)
    hidden = [got0, got1, swap(got0), swap(got1)]

    size = right_factor.shape[2]
    left, back = left_grads(
        hidden,
        down_weight,
        (rest0, rest1),
        (mixed0, mixed1),
        left_diag,
        order,
        tensor_count,
        pairs,
        size,
        1.0 / math.sqrt(rows * fsdp_count),
    )
    got_left = along(left[2:], 1)
    sent = right_grads(back, own, late, order, pairs, 1, size, SMALL)
    left = add(left[:2], after(got_left, sent)).astype(BF16)
    got_left = along(left[1], 2)
    got_right = along(sent, 1)
    kept_back = after(back, sent, left)
    right = right_grads(kept_back, own, late, order, pairs, 0, size, LARGE)
    right = add(right, got_right).astype(BF16)
    grad_right = add(turn(right[0], 0), turn(right[1], 2))
    grad_left = add(left[0], got_left)
    grad_left = grad_left.reshape(pairs // 2, -1, 2, blocks).transpose(0, 2, 1, 3)
    return grad_right.reshape(right_factor.shape), grad_left.reshape(left_factor.shape)


def body(*args):
    tokens, gate_weight, _, _, right_factor, left_factor = args
    counts = (lax.axis_size("fsdp"), lax.axis_size("tensor"))
    feat, hid = gate_weight.shape
    per_owner, share, size = right_factor.shape
    blocks = left_factor.shape[2]
    fits = hid % (2 * BLK) == 0
    fits = fits and counts == (4, 4) and tokens.shape[0] == 128
    fits = fits and hid >= 4 * BLK and feat % BLK == 0
    fits = fits and size == 128 and 2 * blocks == size and per_owner % WIDE == 0
    fits = fits and left_factor.shape[0] == share and share % 16 == 0
    return (tiled_body if fits else general_body)(*args)


def solution(mesh):
    return jax.shard_map(
        body,
        mesh=mesh,
        in_specs=(
            P(("groups", "fsdp"), None),
            P("fsdp", "tensor"),
            P("fsdp", "tensor"),
            P("tensor", "fsdp"),
            P("fsdp", "tensor", None),
            P("fsdp", "tensor", None),
        ),
        out_specs=(P(("groups", "fsdp"), "tensor", None), P(("groups", "fsdp"), "tensor", None)),
        check_vma=False,
    )
```

```python
import functools
import math

import jax
import jax.numpy as jnp
from jax import lax
from jax.experimental import pallas as pl
from jax.experimental.pallas import tpu as pltpu
from jax.sharding import PartitionSpec as P

BLK = 256
LANES = 128
SMALL = pl.CostEstimate(flops=1, bytes_accessed=1, transcendentals=0)
LARGE = pl.CostEstimate(flops=10**10, bytes_accessed=10**7, transcendentals=0)
F32 = jnp.float32
BF16 = jnp.bfloat16


def gate_up_kernel(idx_ref, top_ref, bottom_ref, gate_ref, up_ref, mine_ref, other_ref):
    rows = top_ref.shape[0]
    lhs = jnp.concatenate([top_ref[...], bottom_ref[...]], axis=0)
    for slot, weight_ref in enumerate((gate_ref, up_ref)):
        product = jnp.dot(lhs, weight_ref[...], preferred_element_type=F32).astype(BF16)
        mine_ref[slot] = product[:rows]
        other_ref[slot] = product[rows:]


def gate_up(top, top_block, bottom, gate, up, column, first, width):
    rows, feat = bottom.shape
    if width % BLK or gate.shape[1] % BLK or rows % 16 or feat % 128:
        lhs = jnp.concatenate(
            [lax.dynamic_slice_in_dim(top, top_block * feat, feat, 1), bottom], axis=0
        )
        both = [
            jnp.dot(
                lhs,
                lax.dynamic_slice_in_dim(w, column + first, width, 1),
                preferred_element_type=F32,
            ).astype(BF16)
            for w in (gate, up)
        ]
        both = jnp.stack(both)
        return both[:, :rows], both[:, rows:]
    scalars = jnp.stack([top_block, lax.div(column, BLK) + first // BLK]).astype(jnp.int32)
    weight_spec = pl.BlockSpec((feat, BLK), lambda n, s: (0, s[1] + n))
    out_spec = pl.BlockSpec((2, rows, BLK), lambda n, s: (0, 0, n))
    shape = jax.ShapeDtypeStruct((2, rows, width), BF16)
    return pl.pallas_call(
        gate_up_kernel,
        grid_spec=pltpu.PrefetchScalarGridSpec(
            num_scalar_prefetch=1,
            grid=(width // BLK,),
            in_specs=[
                pl.BlockSpec((rows, feat), lambda n, s: (0, s[0])),
                pl.BlockSpec((rows, feat), lambda n, s: (0, 0)),
                weight_spec,
                weight_spec,
            ],
            out_specs=[out_spec, out_spec],
        ),
        out_shape=[shape, shape],
        compiler_params=pltpu.CompilerParams(vmem_limit_bytes=40 * 2**20),
        cost_estimate=pl.CostEstimate(
            flops=2 * 2 * rows * feat * 2 * width,
            bytes_accessed=2 * feat * 2 * width + 2 * 2 * rows * (feat + 2 * width),
            transcendentals=0,
        ),
        name="gate_up",
    )(scalars, top, bottom, gate, up)


def down_kernel(idx_ref, mine_ref, other_ref, weight_ref, *refs):
    out_ref = refs[-1]
    lhs = jnp.concatenate([mine_ref[...], other_ref[...]], axis=0)
    product = jnp.dot(lhs, weight_ref[...], preferred_element_type=F32)

    @pl.when(pl.program_id(0) == 0)
    def _():
        out_ref[...] = refs[0][...] + product if len(refs) > 1 else product

    @pl.when(pl.program_id(0) > 0)
    def _():
        out_ref[...] += product


def down_add(total, mine, other, weight, row):
    rows, width = mine.shape
    outs = weight.shape[1]
    if width % BLK or weight.shape[0] % BLK or rows % 16 or outs % 128:
        lhs = jnp.concatenate([mine, other], axis=0)
        part = lax.dynamic_slice_in_dim(weight, row, width, 0)
        product = jnp.dot(lhs, part, preferred_element_type=F32)
        return product if total is None else total + product
    scalars = jnp.reshape(lax.div(row, BLK), (1,)).astype(jnp.int32)
    hidden_spec = pl.BlockSpec((rows, BLK), lambda k, s: (0, k))
    whole = pl.BlockSpec((2 * rows, outs), lambda k, s: (0, 0))
    totals = [] if total is None else [total]
    return pl.pallas_call(
        down_kernel,
        grid_spec=pltpu.PrefetchScalarGridSpec(
            num_scalar_prefetch=1,
            grid=(width // BLK,),
            in_specs=[
                hidden_spec,
                hidden_spec,
                pl.BlockSpec((BLK, outs), lambda k, s: (s[0] + k, 0)),
            ]
            + [whole] * len(totals),
            out_specs=whole,
        ),
        out_shape=jax.ShapeDtypeStruct((2 * rows, outs), F32),
        compiler_params=pltpu.CompilerParams(vmem_limit_bytes=40 * 2**20),
        cost_estimate=pl.CostEstimate(
            flops=2 * 2 * rows * width * outs,
            bytes_accessed=2 * width * outs + 2 * 2 * rows * width + 16 * rows * outs,
            transcendentals=0,
        ),
        name="down_add",
    )(scalars, mine, other, weight, *totals)


def general_body(tokens, gate_weight, up_weight, down_weight, right_factor, left_factor):
    fsdp_count = lax.axis_size("fsdp")
    tensor_count = lax.axis_size("tensor")
    chips = fsdp_count // 2
    rows, model = tokens.shape
    feat, hid = gate_weight.shape
    part = hid // chips
    me = lax.axis_index("fsdp")
    chip, core = lax.div(me, 2), lax.rem(me, 2)
    z = lax.axis_index("tensor")

    def swap(value):
        return lax.ppermute(value, "fsdp", [(i, i ^ 1) for i in range(fsdp_count)])

    def shift(value, hops):
        perm = [(i, (i + 2 * hops) % fsdp_count) for i in range(fsdp_count)]
        return lax.ppermute(value, "fsdp", perm)

    def gather_z(value):
        if tensor_count > 4:
            return lax.all_gather(value, "tensor", axis=0, tiled=True)
        size = value.shape[0]
        whole = jnp.zeros((size * tensor_count,) + value.shape[1:], value.dtype)
        whole = lax.dynamic_update_slice_in_dim(whole, value, z * size, 0)
        for step in range(1, tensor_count):
            perm = [(i, (i + step) % tensor_count) for i in range(tensor_count)]
            got = lax.ppermute(value, "tensor", perm)
            source = lax.rem(z - step + tensor_count, tensor_count)
            whole = lax.dynamic_update_slice_in_dim(whole, got, source * size, 0)
        return whole

    def scatter_z(value):
        if tensor_count > 4:
            return lax.psum_scatter(value, "tensor", scatter_dimension=0, tiled=False)
        total = lax.dynamic_index_in_dim(value, z, 0, keepdims=False)
        for step in range(1, tensor_count):
            target_z = lax.rem(z + step, tensor_count)
            piece = lax.dynamic_index_in_dim(value, target_z, 0, keepdims=False)
            perm = [(i, (i + step) % tensor_count) for i in range(tensor_count)]
            total += lax.ppermute(piece.astype(BF16), "tensor", perm).astype(F32)
        return total

    def columns(value, start, width):
        return lax.dynamic_slice_in_dim(value, start, width, 1)

    def after(value, *others):
        return lax.optimization_barrier((value,) + others)[0]

    def pair_z(value):
        perm = [(i, i ^ 1) for i in range(tensor_count)]
        got = lax.ppermute(value, "tensor", perm)
        odd = lax.rem(z, 2) == 1
        return jnp.concatenate(
            [jnp.where(odd, got, value), jnp.where(odd, value, got)], axis=0
        )

    if part % BLK == 0 and part // BLK > 1:
        head = (part // BLK + 1) // 2 * BLK
        chunks = [(0, head), (head, part - head)]
    else:
        chunks = [(0, part)]

    half = rows // 2
    own_half = lax.dynamic_slice_in_dim(tokens, lax.rem(z, 2) * half, half, 0)

    def send_tokens(value, dt, g):
        features = lax.rem(chip - dt + g + chips, chips) * (2 * feat)
        return shift(columns(value, features, 2 * feat), -dt)

    def partial(pair, dp, first, width):
        column = lax.rem(chip + dp, chips) * part
        top, block, bottom = pair
        mine, other = gate_up(top, block, bottom, gate_weight, up_weight, column, first, width)
        return mine, swap(other)

    def send_partials(pair, got, dt):
        sums = []
        for dp in range(1, chips):
            pieces = [partial(pair, dp, *chunk) for chunk in chunks]
            for n, (mine, from_core) in enumerate(pieces):
                both = (mine.astype(F32) + from_core.astype(F32)).astype(BF16)
                got[dt, dp, n] = shift(both, dp)
                sums.append(both)
        return sums

    got, kept, gathered = {}, {}, {}
    local = swap(columns(tokens, (me ^ 1) * feat, feat))
    arrived = {dt: send_tokens(own_half, dt, 0) for dt in range(1, chips)}
    sums = send_partials((tokens, me, local), got, 0)
    if sums:
        local = after(local, *sums)
    kept[0] = partial((tokens, me, local), 0, 0, part)
    late_tokens = after(tokens, kept[0][0])
    neighbour_tokens = swap(late_tokens)
    late_half = after(own_half, *sums) if sums else own_half

    for dt in range(1, chips):
        gathered[dt, 0] = pair_z(after(arrived[dt], *sums))
        whole = gathered[dt, 0]
        top = columns(whole, core * feat, feat)
        bottom = swap(columns(whole, (1 - core) * feat, feat))
        pair = (top, jnp.int32(0), bottom)
        sums = send_partials(pair, got, dt)
        pair = (top, jnp.int32(0), after(bottom, *sums))
        kept[dt] = partial(pair, 0, 0, part)
        for g in range(1, chips):
            gathered[dt, g] = pair_z(after(send_tokens(late_half, dt, g), kept[dt][0]))

    def activate(e, first, width, n):
        terms = [lax.slice_in_dim(term, first, first + width, axis=2) for term in kept[e]]
        terms += [got[(e + dp) % chips, dp, n] for dp in range(1, chips)]
        total = sum(term.astype(F32) for term in terms)
        return (jax.nn.silu(total[0]) * total[1]).astype(BF16)

    totals = {u: None for u in range(chips)}
    for e in list(range(1, chips)) + [0]:
        values = [activate(e, *chunk, n) for n, chunk in enumerate(chunks)]
        spans = list(chunks)
        if e:
            values, spans = [jnp.concatenate(values, axis=1)], [(0, part)]
        sent = [[value] + [shift(value, d) for d in range(1, chips)] for value in values]
        for (first, width), copies in zip(spans, sent):
            for d, mine in enumerate(copies):
                u = (e - d + chips) % chips
                row = lax.rem(chip - d + chips, chips) * part + first
                totals[u] = down_add(totals[u], mine, swap(mine), down_weight, row)

    token_rows = []
    for dt in range(chips):
        if dt == 0:
            token_rows += [tokens, neighbour_tokens]
            continue
        else:
            full = jnp.zeros((rows, model), BF16)
            for g in range(chips):
                features = lax.rem(chip + g, chips) * (2 * feat)
                full = lax.dynamic_update_slice_in_dim(full, gathered[dt, g], features, 1)
        token_rows += [full, swap(full)]
    inputs = jnp.concatenate(token_rows, axis=0)
    count = inputs.shape[0]

    blocks, share, size = right_factor.shape
    ratio = tensor_count // fsdp_count
    turn = []
    for a in range(fsdp_count):
        for b in range(tensor_count):
            turn.append((a * tensor_count + b, (b // ratio) * tensor_count + a * ratio + b % ratio))
    back = [(b, a) for a, b in turn]
    right_rows = gather_z(lax.ppermute(right_factor, ("fsdp", "tensor"), turn)[None])
    right_rows = right_rows.reshape(fsdp_count, ratio, blocks, share, size)
    right_rows = right_rows.transpose(0, 2, 1, 3, 4).reshape(
        fsdp_count * blocks, ratio * share, size
    )
    left_rows = jnp.moveaxis(gather_z(jnp.moveaxis(left_factor, 1, 0)), 0, 1)

    block_input = inputs.reshape(count, fsdp_count * blocks, size)
    mixed = jnp.einsum(
        "nim,ijm->nij", block_input, right_rows, preferred_element_type=F32
    ).astype(BF16)
    student = jnp.einsum("nij,jki->njk", mixed, left_rows, preferred_element_type=F32)
    target = jnp.concatenate([totals[u] for u in range(chips)], axis=0)
    scale = 1.0 / math.sqrt(count)
    out_grad = (student * (1.0 / tensor_count) - target.reshape(student.shape)) * scale
    out_grad = out_grad.astype(BF16)
    grad_left = jnp.einsum("njk,nij->kji", out_grad, mixed, preferred_element_type=F32)
    mixed_grad = jnp.einsum(
        "njk,jki->nij", out_grad, left_rows, preferred_element_type=F32
    ).astype(BF16)
    grad_right = jnp.einsum(
        "nij,nim->ijm", mixed_grad, block_input, preferred_element_type=F32
    )
    grad_left = scatter_z(
        grad_left.reshape((tensor_count, -1) + grad_left.shape[1:])
    )
    grad_left = jnp.moveaxis(grad_left, 0, 1)
    grad_right = grad_right.reshape(fsdp_count, blocks, ratio, share, size)
    grad_right = grad_right.transpose(0, 2, 1, 3, 4).reshape(
        tensor_count, blocks, share, size
    )
    grad_right = lax.ppermute(scatter_z(grad_right), ("fsdp", "tensor"), back)
    return grad_right, grad_left


def cut_kernel(count, idx_ref, *refs):
    for in_ref, out_ref in zip(refs[:count], refs[count:]):
        out_ref[...] = in_ref[...]


def cut_tokens(tokens, row, columns):
    block = (tokens.shape[0] // 2, tokens.shape[1] // 2)
    count = len(columns)
    return pl.pallas_call(
        functools.partial(cut_kernel, count),
        grid_spec=pltpu.PrefetchScalarGridSpec(
            num_scalar_prefetch=1,
            grid=(1,),
            in_specs=[
                pl.BlockSpec(block, lambda n, s, k=k: (s[0], s[1 + k])) for k in range(count)
            ],
            out_specs=[pl.BlockSpec(block, lambda n, s: (0, 0))] * count,
        ),
        out_shape=[jax.ShapeDtypeStruct(block, BF16)] * count,
        cost_estimate=SMALL,
        name="cut_tokens",
    )(jnp.stack([row, *columns]).astype(jnp.int32), *[tokens] * count)


def pack_kernel(left_ref, out_ref):
    share = left_ref.shape[1]
    for pair in range(left_ref.shape[0] // 2):
        both = [left_ref[2 * pair].astype(F32), left_ref[2 * pair + 1].astype(F32)]
        both = jnp.concatenate(both, axis=1)
        out_ref[pair * share : (pair + 1) * share, :] = both.astype(BF16)


def pack_left(left):
    pairs, share, blocks = left.shape
    return pl.pallas_call(
        pack_kernel,
        out_shape=jax.ShapeDtypeStruct((pairs // 2 * share, 2 * blocks), BF16),
        cost_estimate=LARGE,
        name="pack_left",
    )(left)


def products_kernel(sets, idx_ref, *refs):
    pieces, (gate_ref, up_ref, mine_ref, other_ref) = refs[: 4 * sets], refs[4 * sets :]
    lhs = jnp.concatenate([piece[...] for piece in pieces], axis=0)
    rows = mine_ref.shape[2]
    for slot, weight_ref in enumerate((gate_ref, up_ref)):
        product = jnp.dot(lhs, weight_ref[...], preferred_element_type=F32).astype(BF16)
        for u in range(sets):
            mine_ref[u, slot] = product[2 * u * rows : (2 * u + 1) * rows]
            other_ref[u, slot] = product[(2 * u + 1) * rows : (2 * u + 2) * rows]


def products(pieces, scalars, gate, up, first, width):
    feat = gate.shape[0]
    sets = len(pieces) // 4
    half = pieces[0][0].shape[0] // (1 if pieces[0][1] is None else 2)
    start = first // BLK

    def piece_spec(row, column):
        if row is None:
            return pl.BlockSpec((half, feat), lambda n, s: (0, s[column]))
        return pl.BlockSpec((half, feat), lambda n, s: (s[row], s[column]))

    weight_spec = pl.BlockSpec(
        (feat, BLK), lambda n, s: (0, s[4] + start + n)
    )
    out_spec = pl.BlockSpec((sets, 2, 2 * half, BLK), lambda n, s: (0, 0, 0, n))
    shape = jax.ShapeDtypeStruct((sets, 2, 2 * half, width), BF16)
    return pl.pallas_call(
        functools.partial(products_kernel, sets),
        grid_spec=pltpu.PrefetchScalarGridSpec(
            num_scalar_prefetch=1,
            grid=(width // BLK,),
            in_specs=[piece_spec(row, column) for _, row, column in pieces]
            + [weight_spec, weight_spec],
            out_specs=[out_spec, out_spec],
        ),
        out_shape=[shape, shape],
        compiler_params=pltpu.CompilerParams(vmem_limit_bytes=40 * 2**20),
        cost_estimate=LARGE if sets > 1 else SMALL,
        name="gate_up_products",
    )(scalars, *[piece for piece, _, _ in pieces], gate, up)


def fill_rows(lhs, pieces):
    rows = pieces[0].shape[0]
    for place, which in enumerate((1, 3, 0, 2)):
        lhs[place * rows : (place + 1) * rows, :] = pieces[which][...]


def whole_spec(array):
    return pl.BlockSpec(array.shape, lambda n, s: (0,) * len(array.shape))


def target_kernel(sign, idx_ref, mine_ref, near_ref, weight_ref, *refs):
    terms, out_ref = refs[:-1], refs[-1]
    lhs = jnp.concatenate([mine_ref[...], near_ref[...]], axis=0)
    product = jnp.dot(lhs, weight_ref[...], preferred_element_type=F32)
    out_ref[...] = sum((ref[...] for ref in terms), sign * product)


def target_part(sign, terms, mine, near, weight, chip):
    rows, width = mine.shape
    outs = weight.shape[1]
    wide = 2 * BLK if outs % (2 * BLK) == 0 else BLK
    block = pl.BlockSpec((2 * rows, wide), lambda n, s: (0, n))
    return pl.pallas_call(
        functools.partial(target_kernel, sign),
        grid_spec=pltpu.PrefetchScalarGridSpec(
            num_scalar_prefetch=1,
            grid=(outs // wide,),
            in_specs=[whole_spec(mine), whole_spec(near)]
            + [pl.BlockSpec((width, wide), lambda n, s: (s[0], n))]
            + [block] * len(terms),
            out_specs=block,
        ),
        out_shape=jax.ShapeDtypeStruct((2 * rows, outs), F32),
        compiler_params=pltpu.CompilerParams(vmem_limit_bytes=40 * 2**20),
        cost_estimate=SMALL,
        name="target_part",
    )(jnp.reshape(chip, (1,)).astype(jnp.int32), mine, near, weight, *terms)


TN = (((0,), (0,)), ((), ()))
NT = (((1,), (1,)), ((), ()))
WIDE = 8


def natural(step, chip, per_chip):
    return lax.rem(chip + step // per_chip, 2) * per_chip + lax.rem(step, per_chip)


def spread_left(z, rows_ref, out_ref, scratch):
    groups = out_ref.shape[0]
    parts, _, size = rows_ref.shape
    blocks = size // 2
    share = blocks // parts
    fold = BLK // blocks
    begin = rows_ref.shape[1] - groups * fold // 2 * share
    scratch[...] = jnp.zeros_like(scratch)
    low = lax.broadcasted_iota(jnp.int32, (blocks, size), 1) < blocks
    for g in range(groups):
        for pair in range(fold // 2):
            row = begin + (g * (fold // 2) + pair) * share
            picked = [
                rows_ref[place(z, owner), row : row + share, :] for owner in range(parts)
            ]
            turned = jnp.concatenate(picked + picked, axis=0).astype(F32).T
            for a in range(2):
                value = turned[a * blocks : (a + 1) * blocks]
                value = jnp.where(low if a == 0 else ~low, value, 0.0)
                lanes = slice(pair * size, (pair + 1) * size)
                for c in range(blocks // WIDE):
                    row = (c * fold + 2 * pair + a) * WIDE
                    scratch[row : row + WIDE, lanes] = value[c * WIDE : (c + 1) * WIDE]
        out_ref[g] = scratch[...].astype(BF16)


def student_kernel(steps, late, tensor_count, idx_ref, *refs):
    tokens, refs = refs[: 8 if late else 4], refs[8 if late else 4 :]
    rights, left_ref, refs = refs[:2], refs[2], refs[3:]
    step = pl.program_id(0)
    if late:
        target_ref, mixed_ref, student_ref, spread = refs
    else:
        mixed_ref, student_ref, diag_ref, spread, scratch = refs
        rows_ref, left_ref = left_ref, diag_ref
        pl.when(step == 0)(lambda: spread_left(idx_ref[3], rows_ref, diag_ref, scratch))
    pair = natural(step, idx_ref[2], steps // 2)
    groups = left_ref.shape[0]
    size = spread.shape[2]
    pairs = spread.shape[1] // WIDE
    share = BLK // groups

    @pl.when(step == 0)
    def _():
        spread[...] = jnp.zeros_like(spread)

    def mix(pieces):
        for half, right_ref in enumerate(rights):
            for t in range(WIDE):
                value = right_ref[0, t * pairs : (t + 1) * pairs, :].astype(F32)
                spread[t, pl.ds(t, pairs, stride=WIDE), :] = value
            factor = jnp.concatenate([spread[t] for t in range(WIDE)], axis=1).astype(BF16)
            lanes = slice(half * WIDE * size, (half + 1) * WIDE * size)
            rows = jnp.concatenate([piece[:, lanes] for piece in pieces], axis=0)
            part = lax.dot_general(factor, rows, NT, preferred_element_type=F32).astype(BF16)
            start = pl.multiple_of((2 * pair + half) * share, share)
            for g in range(groups):
                mixed_ref[g, pl.ds(start, share), :] = part[g * share : (g + 1) * share]

    if late:
        pl.when(step < steps // 2)(lambda: mix(tokens[:4]))
        pl.when(step >= steps // 2)(lambda: mix(tokens[4:]))
    else:
        mix(tokens)

    @pl.when(step == steps - 1)
    def _():
        for g in range(groups):
            span = slice(g * BLK, (g + 1) * BLK)
            student = lax.dot_general(
                mixed_ref[g], left_ref[g], TN, preferred_element_type=F32
            )
            student = student * (1.0 / tensor_count)
            student_ref[:, span] = student - target_ref[:, span] if late else student


def token_specs(half, width, chunk, late):
    if not late:
        return [
            pl.BlockSpec((half, width), lambda n, s, p=p: (s[p % 2], chunk(n, s)))
            for p in range(4)
        ]
    inner = pl.BlockSpec((half, width), lambda n, s: (0, lax.rem(chunk(n, s), 2)))
    return [inner] * 8


def student_part(tokens, scalars, factors, pairs, tensor_count, late=()):
    size = factors.shape[2]
    half = tokens[0].shape[0] // (1 if late else 2)
    blocks = size // 2
    groups = pairs * blocks // BLK
    steps = blocks // (2 * WIDE)

    def chunk(n, s):
        return natural(n, s[2], steps // 2)

    def right_spec(half):
        return pl.BlockSpec(
            (1, WIDE * pairs, size), lambda n, s: (place(s[3], chunk(n, s)), half, 0)
        )

    diag = (groups, BLK, BLK)
    shapes = [
        jax.ShapeDtypeStruct((groups, BLK, 4 * half), BF16),
        jax.ShapeDtypeStruct((4 * half, groups * BLK), F32),
    ]
    scratch = [pltpu.VMEM((WIDE, pairs * WIDE, size), F32)]
    extra = list(late)
    if not late:
        shapes.append(jax.ShapeDtypeStruct(diag, BF16))
        scratch.append(pltpu.VMEM((BLK, BLK), F32))
        extra = [factors]
    return pl.pallas_call(
        functools.partial(student_kernel, steps, bool(late), tensor_count),
        grid_spec=pltpu.PrefetchScalarGridSpec(
            num_scalar_prefetch=1,
            grid=(steps,),
            in_specs=token_specs(half, 2 * WIDE * size, chunk, bool(late))
            + [right_spec(0), right_spec(1)]
            + [whole_spec(array) for array in extra],
            out_specs=[whole_spec(shape) for shape in shapes],
            scratch_shapes=scratch,
        ),
        out_shape=shapes,
        compiler_params=pltpu.CompilerParams(vmem_limit_bytes=40 * 2**20),
        cost_estimate=LARGE,
        name="student_part",
    )(scalars, *tokens, factors, factors, *extra)


def place(z, owner):
    bits = z ^ owner
    return lax.rem(bits, 2) * 2 + bits // 2


def left_kernel(chunks, scale, idx_ref, *refs):
    hidden, refs = refs[:4], refs[4:]
    weight_ref, rest0, rest1, mixed0, mixed1, left_ref, out_ref, back_ref, lhs = refs
    step = pl.program_id(0)
    parts, size = out_ref.shape[0], out_ref.shape[2]
    blocks = chunks * WIDE
    share = BLK // chunks
    fold = BLK // blocks
    pl.when(step == 0)(lambda: fill_rows(lhs, hidden))
    target = jnp.dot(lhs[...], weight_ref[...], preferred_element_type=F32)
    rest = jnp.concatenate([rest0[...], rest1[...]], axis=0)
    out_grad = ((rest - target) * scale).astype(BF16)
    mixed = jnp.concatenate([mixed0[0], mixed1[0]], axis=1)
    left = jnp.dot(mixed, out_grad, preferred_element_type=F32)
    value = lax.dot_general(left_ref[0], out_grad, NT, preferred_element_type=F32)
    value = value.astype(BF16)
    for c in range(chunks):
        back_ref[c] = value[c * share : (c + 1) * share]
    low = lax.broadcasted_iota(jnp.int32, (blocks, size), 1) < blocks
    rows = blocks // parts
    for pair in range(fold // 2):
        lanes = slice(pair * size, (pair + 1) * size)
        picked = []
        for a in (2 * pair, 2 * pair + 1):
            for c in range(chunks):
                begin = (c * fold + a) * WIDE
                picked.append(left[begin : begin + WIDE, lanes])
        turned = jnp.concatenate(picked, axis=0).T
        both = jnp.where(low, turned[:blocks], turned[blocks:]).astype(BF16)
        begin = pl.multiple_of((step * (fold // 2) + pair) * rows, rows)
        for owner in range(parts):
            out_ref[place(idx_ref[3], owner), pl.ds(begin, rows), :] = both[
                owner * rows : (owner + 1) * rows
            ]


def left_grads(hidden, weight, rest, mixed, left_diag, scalars, parts, pairs, size, scale):
    groups, count = left_diag.shape[0], 2 * rest[0].shape[0]
    width = hidden[0].shape[1]
    blocks = groups * BLK // pairs
    chunks = blocks // WIDE
    share = BLK // chunks
    column = pl.BlockSpec((count // 2, BLK), lambda n, s: (0, n))
    slab = pl.BlockSpec((1, BLK, count // 2), lambda n, s: (n, 0, 0))
    out_rows = pairs * blocks * blocks // size // parts
    return pl.pallas_call(
        functools.partial(left_kernel, chunks, scale),
        grid_spec=pltpu.PrefetchScalarGridSpec(
            num_scalar_prefetch=1,
            grid=(groups,),
            in_specs=[whole_spec(piece) for piece in hidden]
            + [pl.BlockSpec((width, BLK), lambda n, s: (1 - s[2], n))]
            + [column, column, slab, slab]
            + [pl.BlockSpec((1, BLK, BLK), lambda n, s: (n, 0, 0))],
            out_specs=[
                pl.BlockSpec((parts, out_rows, size), lambda n, s: (0, 0, 0)),
                pl.BlockSpec((chunks, share, count), lambda n, s: (0, n, 0)),
            ],
            scratch_shapes=[pltpu.VMEM((count, width), BF16)],
        ),
        out_shape=[
            jax.ShapeDtypeStruct((parts, out_rows, size), BF16),
            jax.ShapeDtypeStruct((chunks, groups * share, count), BF16),
        ],
        compiler_params=pltpu.CompilerParams(vmem_limit_bytes=40 * 2**20),
        cost_estimate=SMALL,
        name="left_grads",
    )(scalars, *hidden, weight, *rest, *mixed, left_diag)


def right_kernel(pairs, bit, idx_ref, *refs):
    own, near, far, (back_ref, out_ref, wide) = refs[:4], refs[4:8], refs[8:12], refs[12:]
    size = out_ref.shape[2]
    owner = idx_ref[3] ^ (2 * pl.program_id(0) + bit)

    def right(later):
        for half in range(2):
            lanes = slice(half * WIDE * size, (half + 1) * WIDE * size)
            rows = jnp.concatenate([piece[:, lanes] for piece in own + later], axis=0)
            value = jnp.dot(back_ref[half], rows, preferred_element_type=F32)
            for t in range(WIDE):
                wide[t] = value[:, t * size : (t + 1) * size]
            for t in range(WIDE):
                begin = (half * WIDE + t) * pairs
                out_ref[0, begin : begin + pairs, :] = wide[
                    t, pl.ds(t, pairs, stride=WIDE), :
                ].astype(BF16)

    pl.when(owner // 2 == idx_ref[2])(lambda: right(near))
    pl.when(owner // 2 != idx_ref[2])(lambda: right(far))


def right_grads(back, own, late, scalars, pairs, bit, size, cost):
    half = late[0].shape[0]
    rows, count = back.shape[1:]

    def owner(n, s):
        return s[3] ^ (2 * n + bit)

    return pl.pallas_call(
        functools.partial(right_kernel, pairs, bit),
        grid_spec=pltpu.PrefetchScalarGridSpec(
            num_scalar_prefetch=1,
            grid=(2,),
            in_specs=token_specs(half, 2 * WIDE * size, owner, False)
            + token_specs(half, 2 * WIDE * size, owner, True)
            + [pl.BlockSpec((2, rows, count), lambda n, s: (owner(n, s), 0, 0))],
            out_specs=pl.BlockSpec((1, 2 * WIDE * pairs, size), lambda n, s: (n, 0, 0)),
            scratch_shapes=[pltpu.VMEM((WIDE, pairs * WIDE, size), F32)],
        ),
        out_shape=jax.ShapeDtypeStruct((2, 2 * WIDE * pairs, size), BF16),
        compiler_params=pltpu.CompilerParams(vmem_limit_bytes=40 * 2**20),
        cost_estimate=cost,
        name="right_grads",
    )(scalars, *own, *late, back)


def tiled_body(tokens, gate_weight, up_weight, down_weight, right_factor, left_factor):
    fsdp_count = lax.axis_size("fsdp")
    tensor_count = lax.axis_size("tensor")
    rows, model = tokens.shape
    part = gate_weight.shape[1] // 2
    me, z = lax.axis_index("fsdp"), lax.axis_index("tensor")
    chip, core, odd = lax.div(me, 2), lax.rem(me, 2), lax.rem(z, 2)
    both_axes = ("fsdp", "tensor")

    def swap(value):
        return lax.ppermute(value, "fsdp", [(i, i ^ 1) for i in range(fsdp_count)])

    def across(value):
        return lax.ppermute(value, "fsdp", [(i, i ^ 2) for i in range(fsdp_count)])

    def along(value, bit):
        return lax.ppermute(value, "tensor", [(i, i ^ bit) for i in range(tensor_count)])

    def turn(value, bit):
        perm = []
        for f in range(fsdp_count):
            for t in range(tensor_count):
                perm.append((f * tensor_count + t, (t ^ bit) * tensor_count + f))
        return lax.ppermute(value, both_axes, perm)

    def after(value, *others):
        return lax.optimization_barrier((value,) + others)[0]

    def add(*terms):
        return sum(term.astype(F32) for term in terms)

    near_tokens = swap(tokens)
    first, rest = cut_tokens(tokens, odd, [1 - chip, chip])
    arrived = across(first)
    base = jnp.stack([odd, 1 - odd])
    mine_block = lax.div(part, BLK) * chip
    other_block = lax.div(part, BLK) * (1 - chip)

    def scalars(block):
        return jnp.concatenate([base, jnp.stack([me, core, block])]).astype(jnp.int32)

    own_pieces = [(t, row, 2) for t in (tokens, near_tokens) for row in (0, 1)]
    mine, other = products(
        own_pieces, after(scalars(other_block), first), gate_weight, up_weight, 0, part
    )

    pairs, blocks = left_factor.shape[0], left_factor.shape[2]
    turned = turn(after(right_factor, mine), 0)
    left_rows = pack_left(after(left_factor, mine))
    late_first = across(after(rest, mine))
    turned = after(turned, left_rows, late_first)
    factors = jnp.concatenate([turned.reshape(-1, LANES), left_rows], axis=0)[None]
    sums = add(mine[0], swap(other[0])).astype(BF16)

    arrived = after(arrived, mine)
    partner = along(arrived, 1)
    near_arrived = swap(arrived)
    partner = after(partner, factors)
    got_early = across(sums)
    more = along(after(factors, partner), 2)
    order = jnp.concatenate([base, jnp.stack([chip, z])]).astype(jnp.int32)
    own = [tokens, tokens, near_tokens, near_tokens]
    late = [arrived, partner, near_arrived, swap(partner)]
    late_pieces = [(t, None, 3) for t in late]
    late_order = after(scalars(other_block), sums)
    mine, other = products(late_pieces, late_order, gate_weight, up_weight, 0, part)
    near = swap(other[0])
    late_partner = along(after(late_first, mine), 1)
    mine_order = after(scalars(mine_block), mine)
    kept, other = products(
        own_pieces + late_pieces, mine_order, gate_weight, up_weight, 0, part
    )
    sums = add(mine[0], after(near, kept)).astype(BF16)
    got = across(sums)
    near_kept = swap(after(other, got_early, sums, more, late_partner))
    factors = jnp.concatenate([factors, after(more, kept)], axis=0)
    more = along(factors, 1)

    def activate(u, term):
        total = add(kept[u], near_kept[u], term)
        return (jax.nn.silu(total[0]) * total[1]).astype(BF16)

    hidden1 = activate(1, got_early)
    near1 = swap(hidden1)
    factors = jnp.concatenate([factors, after(more, hidden1)], axis=0)
    mixed0, rest0, left_diag = student_part(
        [after(tokens, hidden1, sums)] + own[1:], order, factors, pairs, tensor_count
    )
    got1 = across(after(hidden1, mixed0))
    target1 = target_part(1.0, [], hidden1, after(near1, mixed0), down_weight, chip)
    hidden0 = activate(0, after(got, target1))
    got0 = across(hidden0)
    near0 = swap(hidden0)
    late_partner = after(late_partner, mixed0)
    late += [late_first, late_partner, swap(after(late_first, mixed0)), swap(late_partner)]
    mixed1, rest1 = student_part(
        [after(late[0], hidden0)] + late[1:],
        order,
        factors,
        pairs,
        tensor_count,
        (left_diag, target1),
    )
    near0 = after(near0, mixed1)
    rest0 = target_part(-1.0, [rest0], hidden0, near0, down_weight, chip)
    got1, got0 = after(got1, mixed1), after(got0, rest0)
    hidden = [got0, got1, swap(got0), swap(got1)]

    size = right_factor.shape[2]
    left, back = left_grads(
        hidden,
        down_weight,
        (rest0, rest1),
        (mixed0, mixed1),
        left_diag,
        order,
        tensor_count,
        pairs,
        size,
        1.0 / math.sqrt(rows * fsdp_count),
    )
    got_left = along(left[2:], 1)
    sent = right_grads(back, own, late, order, pairs, 1, size, SMALL)
    left = add(left[:2], after(got_left, sent)).astype(BF16)
    got_left = along(left[1], 2)
    got_right = along(sent, 1)
    kept_back = after(back, sent, left)
    right = right_grads(kept_back, own, late, order, pairs, 0, size, LARGE)
    right = add(right, got_right).astype(BF16)
    grad_right = add(turn(right[0], 0), turn(right[1], 2))
    grad_left = add(left[0], got_left)
    grad_left = grad_left.reshape(pairs // 2, -1, 2, blocks).transpose(0, 2, 1, 3)
    return grad_right.reshape(right_factor.shape), grad_left.reshape(left_factor.shape)


def body(*args):
    tokens, gate_weight, _, _, right_factor, left_factor = args
    counts = (lax.axis_size("fsdp"), lax.axis_size("tensor"))
    feat, hid = gate_weight.shape
    per_owner, share, size = right_factor.shape
    blocks = left_factor.shape[2]
    fits = hid % (2 * BLK) == 0
    fits = fits and counts == (4, 4) and tokens.shape[0] == 128
    fits = fits and hid >= 4 * BLK and feat % BLK == 0
    fits = fits and size == 128 and 2 * blocks == size and per_owner % WIDE == 0
    fits = fits and left_factor.shape[0] == share and share % 16 == 0
    return (tiled_body if fits else general_body)(*args)


def solution(mesh):
    return jax.shard_map(
        body,
        mesh=mesh,
        in_specs=(
            P(("groups", "fsdp"), None),
            P("fsdp", "tensor"),
            P("fsdp", "tensor"),
            P("tensor", "fsdp"),
            P("fsdp", "tensor", None),
            P("fsdp", "tensor", None),
        ),
        out_specs=(P(("groups", "fsdp"), "tensor", None), P(("groups", "fsdp"), "tensor", None)),
        check_vma=False,
    )
```

```python
import functools
import math

import jax
import jax.numpy as jnp
from jax import lax
from jax.experimental import pallas as pl
from jax.experimental.pallas import tpu as pltpu
from jax.sharding import PartitionSpec as P

BLK = 256
LANES = 128
SMALL = pl.CostEstimate(flops=1, bytes_accessed=1, transcendentals=0)
LARGE = pl.CostEstimate(flops=10**10, bytes_accessed=10**7, transcendentals=0)
F32 = jnp.float32
BF16 = jnp.bfloat16


def gate_up_kernel(idx_ref, top_ref, bottom_ref, gate_ref, up_ref, mine_ref, other_ref):
    rows = top_ref.shape[0]
    lhs = jnp.concatenate([top_ref[...], bottom_ref[...]], axis=0)
    for slot, weight_ref in enumerate((gate_ref, up_ref)):
        product = jnp.dot(lhs, weight_ref[...], preferred_element_type=F32).astype(BF16)
        mine_ref[slot] = product[:rows]
        other_ref[slot] = product[rows:]


def gate_up(top, top_block, bottom, gate, up, column, first, width):
    rows, feat = bottom.shape
    if width % BLK or gate.shape[1] % BLK or rows % 16 or feat % 128:
        lhs = jnp.concatenate(
            [lax.dynamic_slice_in_dim(top, top_block * feat, feat, 1), bottom], axis=0
        )
        both = [
            jnp.dot(
                lhs,
                lax.dynamic_slice_in_dim(w, column + first, width, 1),
                preferred_element_type=F32,
            ).astype(BF16)
            for w in (gate, up)
        ]
        both = jnp.stack(both)
        return both[:, :rows], both[:, rows:]
    scalars = jnp.stack([top_block, lax.div(column, BLK) + first // BLK]).astype(jnp.int32)
    weight_spec = pl.BlockSpec((feat, BLK), lambda n, s: (0, s[1] + n))
    out_spec = pl.BlockSpec((2, rows, BLK), lambda n, s: (0, 0, n))
    shape = jax.ShapeDtypeStruct((2, rows, width), BF16)
    return pl.pallas_call(
        gate_up_kernel,
        grid_spec=pltpu.PrefetchScalarGridSpec(
            num_scalar_prefetch=1,
            grid=(width // BLK,),
            in_specs=[
                pl.BlockSpec((rows, feat), lambda n, s: (0, s[0])),
                pl.BlockSpec((rows, feat), lambda n, s: (0, 0)),
                weight_spec,
                weight_spec,
            ],
            out_specs=[out_spec, out_spec],
        ),
        out_shape=[shape, shape],
        compiler_params=pltpu.CompilerParams(vmem_limit_bytes=40 * 2**20),
        cost_estimate=pl.CostEstimate(
            flops=2 * 2 * rows * feat * 2 * width,
            bytes_accessed=2 * feat * 2 * width + 2 * 2 * rows * (feat + 2 * width),
            transcendentals=0,
        ),
        name="gate_up",
    )(scalars, top, bottom, gate, up)


def down_kernel(idx_ref, mine_ref, other_ref, weight_ref, *refs):
    out_ref = refs[-1]
    lhs = jnp.concatenate([mine_ref[...], other_ref[...]], axis=0)
    product = jnp.dot(lhs, weight_ref[...], preferred_element_type=F32)

    @pl.when(pl.program_id(0) == 0)
    def _():
        out_ref[...] = refs[0][...] + product if len(refs) > 1 else product

    @pl.when(pl.program_id(0) > 0)
    def _():
        out_ref[...] += product


def down_add(total, mine, other, weight, row):
    rows, width = mine.shape
    outs = weight.shape[1]
    if width % BLK or weight.shape[0] % BLK or rows % 16 or outs % 128:
        lhs = jnp.concatenate([mine, other], axis=0)
        part = lax.dynamic_slice_in_dim(weight, row, width, 0)
        product = jnp.dot(lhs, part, preferred_element_type=F32)
        return product if total is None else total + product
    scalars = jnp.reshape(lax.div(row, BLK), (1,)).astype(jnp.int32)
    hidden_spec = pl.BlockSpec((rows, BLK), lambda k, s: (0, k))
    whole = pl.BlockSpec((2 * rows, outs), lambda k, s: (0, 0))
    totals = [] if total is None else [total]
    return pl.pallas_call(
        down_kernel,
        grid_spec=pltpu.PrefetchScalarGridSpec(
            num_scalar_prefetch=1,
            grid=(width // BLK,),
            in_specs=[
                hidden_spec,
                hidden_spec,
                pl.BlockSpec((BLK, outs), lambda k, s: (s[0] + k, 0)),
            ]
            + [whole] * len(totals),
            out_specs=whole,
        ),
        out_shape=jax.ShapeDtypeStruct((2 * rows, outs), F32),
        compiler_params=pltpu.CompilerParams(vmem_limit_bytes=40 * 2**20),
        cost_estimate=pl.CostEstimate(
            flops=2 * 2 * rows * width * outs,
            bytes_accessed=2 * width * outs + 2 * 2 * rows * width + 16 * rows * outs,
            transcendentals=0,
        ),
        name="down_add",
    )(scalars, mine, other, weight, *totals)


def general_body(tokens, gate_weight, up_weight, down_weight, right_factor, left_factor):
    fsdp_count = lax.axis_size("fsdp")
    tensor_count = lax.axis_size("tensor")
    chips = fsdp_count // 2
    rows, model = tokens.shape
    feat, hid = gate_weight.shape
    part = hid // chips
    me = lax.axis_index("fsdp")
    chip, core = lax.div(me, 2), lax.rem(me, 2)
    z = lax.axis_index("tensor")

    def swap(value):
        return lax.ppermute(value, "fsdp", [(i, i ^ 1) for i in range(fsdp_count)])

    def shift(value, hops):
        perm = [(i, (i + 2 * hops) % fsdp_count) for i in range(fsdp_count)]
        return lax.ppermute(value, "fsdp", perm)

    def gather_z(value):
        if tensor_count > 4:
            return lax.all_gather(value, "tensor", axis=0, tiled=True)
        size = value.shape[0]
        whole = jnp.zeros((size * tensor_count,) + value.shape[1:], value.dtype)
        whole = lax.dynamic_update_slice_in_dim(whole, value, z * size, 0)
        for step in range(1, tensor_count):
            perm = [(i, (i + step) % tensor_count) for i in range(tensor_count)]
            got = lax.ppermute(value, "tensor", perm)
            source = lax.rem(z - step + tensor_count, tensor_count)
            whole = lax.dynamic_update_slice_in_dim(whole, got, source * size, 0)
        return whole

    def scatter_z(value):
        if tensor_count > 4:
            return lax.psum_scatter(value, "tensor", scatter_dimension=0, tiled=False)
        total = lax.dynamic_index_in_dim(value, z, 0, keepdims=False)
        for step in range(1, tensor_count):
            target_z = lax.rem(z + step, tensor_count)
            piece = lax.dynamic_index_in_dim(value, target_z, 0, keepdims=False)
            perm = [(i, (i + step) % tensor_count) for i in range(tensor_count)]
            total += lax.ppermute(piece.astype(BF16), "tensor", perm).astype(F32)
        return total

    def columns(value, start, width):
        return lax.dynamic_slice_in_dim(value, start, width, 1)

    def after(value, *others):
        return lax.optimization_barrier((value,) + others)[0]

    def pair_z(value):
        perm = [(i, i ^ 1) for i in range(tensor_count)]
        got = lax.ppermute(value, "tensor", perm)
        odd = lax.rem(z, 2) == 1
        return jnp.concatenate(
            [jnp.where(odd, got, value), jnp.where(odd, value, got)], axis=0
        )

    if part % BLK == 0 and part // BLK > 1:
        head = (part // BLK + 1) // 2 * BLK
        chunks = [(0, head), (head, part - head)]
    else:
        chunks = [(0, part)]

    half = rows // 2
    own_half = lax.dynamic_slice_in_dim(tokens, lax.rem(z, 2) * half, half, 0)

    def send_tokens(value, dt, g):
        features = lax.rem(chip - dt + g + chips, chips) * (2 * feat)
        return shift(columns(value, features, 2 * feat), -dt)

    def partial(pair, dp, first, width):
        column = lax.rem(chip + dp, chips) * part
        top, block, bottom = pair
        mine, other = gate_up(top, block, bottom, gate_weight, up_weight, column, first, width)
        return mine, swap(other)

    def send_partials(pair, got, dt):
        sums = []
        for dp in range(1, chips):
            pieces = [partial(pair, dp, *chunk) for chunk in chunks]
            for n, (mine, from_core) in enumerate(pieces):
                both = (mine.astype(F32) + from_core.astype(F32)).astype(BF16)
                got[dt, dp, n] = shift(both, dp)
                sums.append(both)
        return sums

    got, kept, gathered = {}, {}, {}
    local = swap(columns(tokens, (me ^ 1) * feat, feat))
    arrived = {dt: send_tokens(own_half, dt, 0) for dt in range(1, chips)}
    sums = send_partials((tokens, me, local), got, 0)
    if sums:
        local = after(local, *sums)
    kept[0] = partial((tokens, me, local), 0, 0, part)
    late_tokens = after(tokens, kept[0][0])
    neighbour_tokens = swap(late_tokens)
    late_half = after(own_half, *sums) if sums else own_half

    for dt in range(1, chips):
        gathered[dt, 0] = pair_z(after(arrived[dt], *sums))
        whole = gathered[dt, 0]
        top = columns(whole, core * feat, feat)
        bottom = swap(columns(whole, (1 - core) * feat, feat))
        pair = (top, jnp.int32(0), bottom)
        sums = send_partials(pair, got, dt)
        pair = (top, jnp.int32(0), after(bottom, *sums))
        kept[dt] = partial(pair, 0, 0, part)
        for g in range(1, chips):
            gathered[dt, g] = pair_z(after(send_tokens(late_half, dt, g), kept[dt][0]))

    def activate(e, first, width, n):
        terms = [lax.slice_in_dim(term, first, first + width, axis=2) for term in kept[e]]
        terms += [got[(e + dp) % chips, dp, n] for dp in range(1, chips)]
        total = sum(term.astype(F32) for term in terms)
        return (jax.nn.silu(total[0]) * total[1]).astype(BF16)

    totals = {u: None for u in range(chips)}
    for e in list(range(1, chips)) + [0]:
        values = [activate(e, *chunk, n) for n, chunk in enumerate(chunks)]
        spans = list(chunks)
        if e:
            values, spans = [jnp.concatenate(values, axis=1)], [(0, part)]
        sent = [[value] + [shift(value, d) for d in range(1, chips)] for value in values]
        for (first, width), copies in zip(spans, sent):
            for d, mine in enumerate(copies):
                u = (e - d + chips) % chips
                row = lax.rem(chip - d + chips, chips) * part + first
                totals[u] = down_add(totals[u], mine, swap(mine), down_weight, row)

    token_rows = []
    for dt in range(chips):
        if dt == 0:
            token_rows += [tokens, neighbour_tokens]
            continue
        else:
            full = jnp.zeros((rows, model), BF16)
            for g in range(chips):
                features = lax.rem(chip + g, chips) * (2 * feat)
                full = lax.dynamic_update_slice_in_dim(full, gathered[dt, g], features, 1)
        token_rows += [full, swap(full)]
    inputs = jnp.concatenate(token_rows, axis=0)
    count = inputs.shape[0]

    blocks, share, size = right_factor.shape
    ratio = tensor_count // fsdp_count
    turn = []
    for a in range(fsdp_count):
        for b in range(tensor_count):
            turn.append((a * tensor_count + b, (b // ratio) * tensor_count + a * ratio + b % ratio))
    back = [(b, a) for a, b in turn]
    right_rows = gather_z(lax.ppermute(right_factor, ("fsdp", "tensor"), turn)[None])
    right_rows = right_rows.reshape(fsdp_count, ratio, blocks, share, size)
    right_rows = right_rows.transpose(0, 2, 1, 3, 4).reshape(
        fsdp_count * blocks, ratio * share, size
    )
    left_rows = jnp.moveaxis(gather_z(jnp.moveaxis(left_factor, 1, 0)), 0, 1)

    block_input = inputs.reshape(count, fsdp_count * blocks, size)
    mixed = jnp.einsum(
        "nim,ijm->nij", block_input, right_rows, preferred_element_type=F32
    ).astype(BF16)
    student = jnp.einsum("nij,jki->njk", mixed, left_rows, preferred_element_type=F32)
    target = jnp.concatenate([totals[u] for u in range(chips)], axis=0)
    scale = 1.0 / math.sqrt(count)
    out_grad = (student * (1.0 / tensor_count) - target.reshape(student.shape)) * scale
    out_grad = out_grad.astype(BF16)
    grad_left = jnp.einsum("njk,nij->kji", out_grad, mixed, preferred_element_type=F32)
    mixed_grad = jnp.einsum(
        "njk,jki->nij", out_grad, left_rows, preferred_element_type=F32
    ).astype(BF16)
    grad_right = jnp.einsum(
        "nij,nim->ijm", mixed_grad, block_input, preferred_element_type=F32
    )
    grad_left = scatter_z(
        grad_left.reshape((tensor_count, -1) + grad_left.shape[1:])
    )
    grad_left = jnp.moveaxis(grad_left, 0, 1)
    grad_right = grad_right.reshape(fsdp_count, blocks, ratio, share, size)
    grad_right = grad_right.transpose(0, 2, 1, 3, 4).reshape(
        tensor_count, blocks, share, size
    )
    grad_right = lax.ppermute(scatter_z(grad_right), ("fsdp", "tensor"), back)
    return grad_right, grad_left


def cut_kernel(count, idx_ref, *refs):
    for in_ref, out_ref in zip(refs[:count], refs[count:]):
        out_ref[...] = in_ref[...]


def cut_tokens(tokens, row, columns):
    block = (tokens.shape[0] // 2, tokens.shape[1] // 2)
    count = len(columns)
    return pl.pallas_call(
        functools.partial(cut_kernel, count),
        grid_spec=pltpu.PrefetchScalarGridSpec(
            num_scalar_prefetch=1,
            grid=(1,),
            in_specs=[
                pl.BlockSpec(block, lambda n, s, k=k: (s[0], s[1 + k])) for k in range(count)
            ],
            out_specs=[pl.BlockSpec(block, lambda n, s: (0, 0))] * count,
        ),
        out_shape=[jax.ShapeDtypeStruct(block, BF16)] * count,
        cost_estimate=SMALL,
        name="cut_tokens",
    )(jnp.stack([row, *columns]).astype(jnp.int32), *[tokens] * count)


def pack_kernel(left_ref, out_ref):
    share = left_ref.shape[1]
    for pair in range(left_ref.shape[0] // 2):
        both = [left_ref[2 * pair].astype(F32), left_ref[2 * pair + 1].astype(F32)]
        both = jnp.concatenate(both, axis=1)
        out_ref[pair * share : (pair + 1) * share, :] = both.astype(BF16)


def pack_left(left):
    pairs, share, blocks = left.shape
    return pl.pallas_call(
        pack_kernel,
        out_shape=jax.ShapeDtypeStruct((pairs // 2 * share, 2 * blocks), BF16),
        cost_estimate=LARGE,
        name="pack_left",
    )(left)


def products_kernel(sets, idx_ref, *refs):
    pieces, (gate_ref, up_ref, mine_ref, other_ref) = refs[: 4 * sets], refs[4 * sets :]
    lhs = jnp.concatenate([piece[...] for piece in pieces], axis=0)
    rows = mine_ref.shape[2]
    for slot, weight_ref in enumerate((gate_ref, up_ref)):
        product = jnp.dot(lhs, weight_ref[...], preferred_element_type=F32).astype(BF16)
        for u in range(sets):
            mine_ref[u, slot] = product[2 * u * rows : (2 * u + 1) * rows]
            other_ref[u, slot] = product[(2 * u + 1) * rows : (2 * u + 2) * rows]


def products(pieces, scalars, gate, up, first, width):
    feat = gate.shape[0]
    sets = len(pieces) // 4
    half = pieces[0][0].shape[0] // (1 if pieces[0][1] is None else 2)
    start = first // BLK

    def piece_spec(row, column):
        if row is None:
            return pl.BlockSpec((half, feat), lambda n, s: (0, s[column]))
        return pl.BlockSpec((half, feat), lambda n, s: (s[row], s[column]))

    weight_spec = pl.BlockSpec(
        (feat, BLK), lambda n, s: (0, s[4] + start + n)
    )
    out_spec = pl.BlockSpec((sets, 2, 2 * half, BLK), lambda n, s: (0, 0, 0, n))
    shape = jax.ShapeDtypeStruct((sets, 2, 2 * half, width), BF16)
    return pl.pallas_call(
        functools.partial(products_kernel, sets),
        grid_spec=pltpu.PrefetchScalarGridSpec(
            num_scalar_prefetch=1,
            grid=(width // BLK,),
            in_specs=[piece_spec(row, column) for _, row, column in pieces]
            + [weight_spec, weight_spec],
            out_specs=[out_spec, out_spec],
        ),
        out_shape=[shape, shape],
        compiler_params=pltpu.CompilerParams(vmem_limit_bytes=40 * 2**20),
        cost_estimate=LARGE if sets > 1 else SMALL,
        name="gate_up_products",
    )(scalars, *[piece for piece, _, _ in pieces], gate, up)


def fill_rows(lhs, pieces):
    rows = pieces[0].shape[0]
    for place, which in enumerate((1, 3, 0, 2)):
        lhs[place * rows : (place + 1) * rows, :] = pieces[which][...]


def whole_spec(array):
    return pl.BlockSpec(array.shape, lambda n, s: (0,) * len(array.shape))


def target_kernel(sign, idx_ref, mine_ref, near_ref, weight_ref, *refs):
    terms, out_ref = refs[:-1], refs[-1]
    lhs = jnp.concatenate([mine_ref[...], near_ref[...]], axis=0)
    product = jnp.dot(lhs, weight_ref[...], preferred_element_type=F32)
    out_ref[...] = sum((ref[...] for ref in terms), sign * product)


def target_part(sign, terms, mine, near, weight, chip):
    rows, width = mine.shape
    outs = weight.shape[1]
    wide = 2 * BLK if outs % (2 * BLK) == 0 else BLK
    block = pl.BlockSpec((2 * rows, wide), lambda n, s: (0, n))
    return pl.pallas_call(
        functools.partial(target_kernel, sign),
        grid_spec=pltpu.PrefetchScalarGridSpec(
            num_scalar_prefetch=1,
            grid=(outs // wide,),
            in_specs=[whole_spec(mine), whole_spec(near)]
            + [pl.BlockSpec((width, wide), lambda n, s: (s[0], n))]
            + [block] * len(terms),
            out_specs=block,
        ),
        out_shape=jax.ShapeDtypeStruct((2 * rows, outs), F32),
        compiler_params=pltpu.CompilerParams(vmem_limit_bytes=40 * 2**20),
        cost_estimate=SMALL,
        name="target_part",
    )(jnp.reshape(chip, (1,)).astype(jnp.int32), mine, near, weight, *terms)


TN = (((0,), (0,)), ((), ()))
NT = (((1,), (1,)), ((), ()))
WIDE = 8


def natural(step, chip, per_chip):
    return lax.rem(chip + step // per_chip, 2) * per_chip + lax.rem(step, per_chip)


def spread_left(z, rows_ref, out_ref, scratch):
    groups = out_ref.shape[0]
    parts, _, size = rows_ref.shape
    blocks = size // 2
    share = blocks // parts
    fold = BLK // blocks
    begin = rows_ref.shape[1] - groups * fold // 2 * share
    scratch[...] = jnp.zeros_like(scratch)
    low = lax.broadcasted_iota(jnp.int32, (blocks, size), 1) < blocks
    for g in range(groups):
        for pair in range(fold // 2):
            row = begin + (g * (fold // 2) + pair) * share
            picked = [
                rows_ref[place(z, owner), row : row + share, :] for owner in range(parts)
            ]
            turned = jnp.concatenate(picked + picked, axis=0).astype(F32).T
            for a in range(2):
                value = turned[a * blocks : (a + 1) * blocks]
                value = jnp.where(low if a == 0 else ~low, value, 0.0)
                lanes = slice(pair * size, (pair + 1) * size)
                for c in range(blocks // WIDE):
                    row = (c * fold + 2 * pair + a) * WIDE
                    scratch[row : row + WIDE, lanes] = value[c * WIDE : (c + 1) * WIDE]
        out_ref[g] = scratch[...].astype(BF16)


def student_kernel(steps, late, tensor_count, idx_ref, *refs):
    tokens, refs = refs[: 8 if late else 4], refs[8 if late else 4 :]
    rights, left_ref, refs = refs[:2], refs[2], refs[3:]
    step = pl.program_id(0)
    if late:
        target_ref, mixed_ref, student_ref, spread = refs
    else:
        mixed_ref, student_ref, diag_ref, spread, scratch = refs
        rows_ref, left_ref = left_ref, diag_ref
        pl.when(step == 0)(lambda: spread_left(idx_ref[3], rows_ref, diag_ref, scratch))
    pair = natural(step, idx_ref[2], steps // 2)
    groups = left_ref.shape[0]
    size = spread.shape[2]
    pairs = spread.shape[1] // WIDE
    share = BLK // groups

    @pl.when(step == 0)
    def _():
        spread[...] = jnp.zeros_like(spread)

    def mix(pieces):
        for half, right_ref in enumerate(rights):
            for t in range(WIDE):
                value = right_ref[0, t * pairs : (t + 1) * pairs, :].astype(F32)
                spread[t, pl.ds(t, pairs, stride=WIDE), :] = value
            factor = jnp.concatenate([spread[t] for t in range(WIDE)], axis=1).astype(BF16)
            lanes = slice(half * WIDE * size, (half + 1) * WIDE * size)
            rows = jnp.concatenate([piece[:, lanes] for piece in pieces], axis=0)
            part = lax.dot_general(factor, rows, NT, preferred_element_type=F32).astype(BF16)
            start = pl.multiple_of((2 * pair + half) * share, share)
            for g in range(groups):
                mixed_ref[g, pl.ds(start, share), :] = part[g * share : (g + 1) * share]

    if late:
        pl.when(step < steps // 2)(lambda: mix(tokens[:4]))
        pl.when(step >= steps // 2)(lambda: mix(tokens[4:]))
    else:
        mix(tokens)

    @pl.when(step == steps - 1)
    def _():
        for g in range(groups):
            span = slice(g * BLK, (g + 1) * BLK)
            student = lax.dot_general(
                mixed_ref[g], left_ref[g], TN, preferred_element_type=F32
            )
            student = student * (1.0 / tensor_count)
            student_ref[:, span] = student - target_ref[:, span] if late else student


def token_specs(half, width, chunk, late):
    if not late:
        return [
            pl.BlockSpec((half, width), lambda n, s, p=p: (s[p % 2], chunk(n, s)))
            for p in range(4)
        ]
    inner = pl.BlockSpec((half, width), lambda n, s: (0, lax.rem(chunk(n, s), 2)))
    return [inner] * 8


def student_part(tokens, scalars, factors, pairs, tensor_count, late=()):
    size = factors.shape[2]
    half = tokens[0].shape[0] // (1 if late else 2)
    blocks = size // 2
    groups = pairs * blocks // BLK
    steps = blocks // (2 * WIDE)

    def chunk(n, s):
        return natural(n, s[2], steps // 2)

    def right_spec(half):
        return pl.BlockSpec(
            (1, WIDE * pairs, size), lambda n, s: (place(s[3], chunk(n, s)), half, 0)
        )

    diag = (groups, BLK, BLK)
    shapes = [
        jax.ShapeDtypeStruct((groups, BLK, 4 * half), BF16),
        jax.ShapeDtypeStruct((4 * half, groups * BLK), F32),
    ]
    scratch = [pltpu.VMEM((WIDE, pairs * WIDE, size), F32)]
    extra = list(late)
    if not late:
        shapes.append(jax.ShapeDtypeStruct(diag, BF16))
        scratch.append(pltpu.VMEM((BLK, BLK), F32))
        extra = [factors]
    return pl.pallas_call(
        functools.partial(student_kernel, steps, bool(late), tensor_count),
        grid_spec=pltpu.PrefetchScalarGridSpec(
            num_scalar_prefetch=1,
            grid=(steps,),
            in_specs=token_specs(half, 2 * WIDE * size, chunk, bool(late))
            + [right_spec(0), right_spec(1)]
            + [whole_spec(array) for array in extra],
            out_specs=[whole_spec(shape) for shape in shapes],
            scratch_shapes=scratch,
        ),
        out_shape=shapes,
        compiler_params=pltpu.CompilerParams(vmem_limit_bytes=40 * 2**20),
        cost_estimate=LARGE,
        name="student_part",
    )(scalars, *tokens, factors, factors, *extra)


def place(z, owner):
    bits = z ^ owner
    return lax.rem(bits, 2) * 2 + bits // 2


def left_kernel(chunks, scale, idx_ref, *refs):
    hidden, refs = refs[:4], refs[4:]
    weight_ref, rest0, rest1, mixed0, mixed1, left_ref, out_ref, back_ref, lhs = refs
    step = pl.program_id(0)
    parts, size = out_ref.shape[0], out_ref.shape[2]
    blocks = chunks * WIDE
    share = BLK // chunks
    fold = BLK // blocks
    pl.when(step == 0)(lambda: fill_rows(lhs, hidden))
    target = jnp.dot(lhs[...], weight_ref[...], preferred_element_type=F32)
    rest = jnp.concatenate([rest0[...], rest1[...]], axis=0)
    out_grad = ((rest - target) * scale).astype(BF16)
    mixed = jnp.concatenate([mixed0[0], mixed1[0]], axis=1)
    left = jnp.dot(mixed, out_grad, preferred_element_type=F32)
    value = lax.dot_general(left_ref[0], out_grad, NT, preferred_element_type=F32)
    value = value.astype(BF16)
    for c in range(chunks):
        back_ref[c] = value[c * share : (c + 1) * share]
    low = lax.broadcasted_iota(jnp.int32, (blocks, size), 1) < blocks
    rows = blocks // parts
    for pair in range(fold // 2):
        lanes = slice(pair * size, (pair + 1) * size)
        picked = []
        for a in (2 * pair, 2 * pair + 1):
            for c in range(chunks):
                begin = (c * fold + a) * WIDE
                picked.append(left[begin : begin + WIDE, lanes])
        turned = jnp.concatenate(picked, axis=0).T
        both = jnp.where(low, turned[:blocks], turned[blocks:]).astype(BF16)
        begin = pl.multiple_of((step * (fold // 2) + pair) * rows, rows)
        for owner in range(parts):
            out_ref[place(idx_ref[3], owner), pl.ds(begin, rows), :] = both[
                owner * rows : (owner + 1) * rows
            ]


def left_grads(hidden, weight, rest, mixed, left_diag, scalars, parts, pairs, size, scale):
    groups, count = left_diag.shape[0], 2 * rest[0].shape[0]
    width = hidden[0].shape[1]
    blocks = groups * BLK // pairs
    chunks = blocks // WIDE
    share = BLK // chunks
    column = pl.BlockSpec((count // 2, BLK), lambda n, s: (0, n))
    slab = pl.BlockSpec((1, BLK, count // 2), lambda n, s: (n, 0, 0))
    out_rows = pairs * blocks * blocks // size // parts
    return pl.pallas_call(
        functools.partial(left_kernel, chunks, scale),
        grid_spec=pltpu.PrefetchScalarGridSpec(
            num_scalar_prefetch=1,
            grid=(groups,),
            in_specs=[whole_spec(piece) for piece in hidden]
            + [pl.BlockSpec((width, BLK), lambda n, s: (1 - s[2], n))]
            + [column, column, slab, slab]
            + [pl.BlockSpec((1, BLK, BLK), lambda n, s: (n, 0, 0))],
            out_specs=[
                pl.BlockSpec((parts, out_rows, size), lambda n, s: (0, 0, 0)),
                pl.BlockSpec((chunks, share, count), lambda n, s: (0, n, 0)),
            ],
            scratch_shapes=[pltpu.VMEM((count, width), BF16)],
        ),
        out_shape=[
            jax.ShapeDtypeStruct((parts, out_rows, size), BF16),
            jax.ShapeDtypeStruct((chunks, groups * share, count), BF16),
        ],
        compiler_params=pltpu.CompilerParams(vmem_limit_bytes=40 * 2**20),
        cost_estimate=SMALL,
        name="left_grads",
    )(scalars, *hidden, weight, *rest, *mixed, left_diag)


def right_kernel(pairs, bit, idx_ref, *refs):
    own, near, far, (back_ref, out_ref, wide) = refs[:4], refs[4:8], refs[8:12], refs[12:]
    size = out_ref.shape[2]
    owner = idx_ref[3] ^ (2 * pl.program_id(0) + bit)

    def right(later):
        for half in range(2):
            lanes = slice(half * WIDE * size, (half + 1) * WIDE * size)
            rows = jnp.concatenate([piece[:, lanes] for piece in own + later], axis=0)
            value = jnp.dot(back_ref[half], rows, preferred_element_type=F32)
            for t in range(WIDE):
                wide[t] = value[:, t * size : (t + 1) * size]
            for t in range(WIDE):
                begin = (half * WIDE + t) * pairs
                out_ref[0, begin : begin + pairs, :] = wide[
                    t, pl.ds(t, pairs, stride=WIDE), :
                ].astype(BF16)

    pl.when(owner // 2 == idx_ref[2])(lambda: right(near))
    pl.when(owner // 2 != idx_ref[2])(lambda: right(far))


def right_grads(back, own, late, scalars, pairs, bit, size, cost):
    half = late[0].shape[0]
    rows, count = back.shape[1:]

    def owner(n, s):
        return s[3] ^ (2 * n + bit)

    return pl.pallas_call(
        functools.partial(right_kernel, pairs, bit),
        grid_spec=pltpu.PrefetchScalarGridSpec(
            num_scalar_prefetch=1,
            grid=(2,),
            in_specs=token_specs(half, 2 * WIDE * size, owner, False)
            + token_specs(half, 2 * WIDE * size, owner, True)
            + [pl.BlockSpec((2, rows, count), lambda n, s: (owner(n, s), 0, 0))],
            out_specs=pl.BlockSpec((1, 2 * WIDE * pairs, size), lambda n, s: (n, 0, 0)),
            scratch_shapes=[pltpu.VMEM((WIDE, pairs * WIDE, size), F32)],
        ),
        out_shape=jax.ShapeDtypeStruct((2, 2 * WIDE * pairs, size), BF16),
        compiler_params=pltpu.CompilerParams(vmem_limit_bytes=40 * 2**20),
        cost_estimate=cost,
        name="right_grads",
    )(scalars, *own, *late, back)


def tiled_body(tokens, gate_weight, up_weight, down_weight, right_factor, left_factor):
    fsdp_count = lax.axis_size("fsdp")
    tensor_count = lax.axis_size("tensor")
    rows, model = tokens.shape
    part = gate_weight.shape[1] // 2
    me, z = lax.axis_index("fsdp"), lax.axis_index("tensor")
    chip, core, odd = lax.div(me, 2), lax.rem(me, 2), lax.rem(z, 2)
    both_axes = ("fsdp", "tensor")

    def swap(value):
        return lax.ppermute(value, "fsdp", [(i, i ^ 1) for i in range(fsdp_count)])

    def across(value):
        return lax.ppermute(value, "fsdp", [(i, i ^ 2) for i in range(fsdp_count)])

    def along(value, bit):
        return lax.ppermute(value, "tensor", [(i, i ^ bit) for i in range(tensor_count)])

    def turn(value, bit):
        perm = []
        for f in range(fsdp_count):
            for t in range(tensor_count):
                perm.append((f * tensor_count + t, (t ^ bit) * tensor_count + f))
        return lax.ppermute(value, both_axes, perm)

    def after(value, *others):
        return lax.optimization_barrier((value,) + others)[0]

    def add(*terms):
        return sum(term.astype(F32) for term in terms)

    near_tokens = swap(tokens)
    first, rest = cut_tokens(tokens, odd, [1 - chip, chip])
    arrived = across(first)
    base = jnp.stack([odd, 1 - odd])
    mine_block = lax.div(part, BLK) * chip
    other_block = lax.div(part, BLK) * (1 - chip)

    def scalars(block):
        return jnp.concatenate([base, jnp.stack([me, core, block])]).astype(jnp.int32)

    own_pieces = [(t, row, 2) for t in (tokens, near_tokens) for row in (0, 1)]
    mine, other = products(
        own_pieces, after(scalars(other_block), first), gate_weight, up_weight, 0, part
    )

    pairs, blocks = left_factor.shape[0], left_factor.shape[2]
    turned = turn(after(right_factor, mine), 0)
    left_rows = pack_left(after(left_factor, mine))
    late_first = across(after(rest, mine))
    turned = after(turned, left_rows, late_first)
    factors = jnp.concatenate([turned.reshape(-1, LANES), left_rows], axis=0)[None]
    sums = add(mine[0], after(swap(other[0]), left_rows)).astype(BF16)

    arrived = after(arrived, mine)
    partner = along(arrived, 1)
    near_arrived = swap(arrived)
    partner = after(partner, factors)
    got_early = across(sums)
    order = jnp.concatenate([base, jnp.stack([chip, z])]).astype(jnp.int32)
    own = [tokens, tokens, near_tokens, near_tokens]
    late = [arrived, partner, near_arrived, swap(partner)]
    late_pieces = [(t, None, 3) for t in late]
    late_order = after(scalars(other_block), sums)
    mine, other = products(late_pieces, late_order, gate_weight, up_weight, 0, part)
    near = swap(after(other[0], got_early))
    more = along(after(factors, mine), 2)
    late_partner = along(after(late_first, mine), 1)
    sums = add(mine[0], near).astype(BF16)
    got = across(sums)
    mine_order = after(scalars(mine_block), sums)
    kept, other = products(
        own_pieces + late_pieces, mine_order, gate_weight, up_weight, 0, part
    )
    near_kept = swap(after(other, got, more, late_partner))
    factors = jnp.concatenate([factors, after(more, kept)], axis=0)
    more = along(factors, 1)

    def activate(u, term):
        total = add(kept[u], near_kept[u], term)
        return (jax.nn.silu(total[0]) * total[1]).astype(BF16)

    hidden1 = activate(1, got_early)
    got1 = across(hidden1)
    near1 = swap(hidden1)
    hidden0 = activate(0, after(got, hidden1))
    got0 = across(hidden0)
    near0 = swap(hidden0)
    target1 = target_part(1.0, [], hidden1, after(near1, hidden0), down_weight, chip)
    factors = jnp.concatenate([factors, after(more, target1)], axis=0)
    mixed0, rest0, left_diag = student_part(
        [after(tokens, target1)] + own[1:], order, factors, pairs, tensor_count
    )
    late_partner = after(late_partner, target1)
    late += [late_first, late_partner, swap(after(late_first, target1)), swap(late_partner)]
    mixed1, rest1 = student_part(
        [after(late[0], mixed0)] + late[1:],
        order,
        factors,
        pairs,
        tensor_count,
        (left_diag, target1),
    )
    near0 = after(near0, mixed1)
    rest0 = target_part(-1.0, [rest0], hidden0, near0, down_weight, chip)
    got1, got0 = after(got1, mixed1), after(got0, rest0)
    hidden = [got0, got1, swap(got0), swap(got1)]

    size = right_factor.shape[2]
    left, back = left_grads(
        hidden,
        down_weight,
        (rest0, rest1),
        (mixed0, mixed1),
        left_diag,
        order,
        tensor_count,
        pairs,
        size,
        1.0 / math.sqrt(rows * fsdp_count),
    )
    got_left = along(left[2:], 1)
    sent = right_grads(back, own, late, order, pairs, 1, size, SMALL)
    left = add(left[:2], after(got_left, sent)).astype(BF16)
    got_left = along(left[1], 2)
    got_right = along(sent, 1)
    kept_back = after(back, sent, left)
    right = right_grads(kept_back, own, late, order, pairs, 0, size, LARGE)
    right = add(right, got_right).astype(BF16)
    grad_right = add(turn(right[0], 0), turn(right[1], 2))
    grad_left = add(left[0], got_left)
    grad_left = grad_left.reshape(pairs // 2, -1, 2, blocks).transpose(0, 2, 1, 3)
    return grad_right.reshape(right_factor.shape), grad_left.reshape(left_factor.shape)


def body(*args):
    tokens, gate_weight, _, _, right_factor, left_factor = args
    counts = (lax.axis_size("fsdp"), lax.axis_size("tensor"))
    feat, hid = gate_weight.shape
    per_owner, share, size = right_factor.shape
    blocks = left_factor.shape[2]
    fits = hid % (2 * BLK) == 0
    fits = fits and counts == (4, 4) and tokens.shape[0] == 128
    fits = fits and hid >= 4 * BLK and feat % BLK == 0
    fits = fits and size == 128 and 2 * blocks == size and per_owner % WIDE == 0
    fits = fits and left_factor.shape[0] == share and share % 16 == 0
    return (tiled_body if fits else general_body)(*args)


def solution(mesh):
    return jax.shard_map(
        body,
        mesh=mesh,
        in_specs=(
            P(("groups", "fsdp"), None),
            P("fsdp", "tensor"),
            P("fsdp", "tensor"),
            P("tensor", "fsdp"),
            P("fsdp", "tensor", None),
            P("fsdp", "tensor", None),
        ),
        out_specs=(P(("groups", "fsdp"), "tensor", None), P(("groups", "fsdp"), "tensor", None)),
        check_vma=False,
    )
```

```python
import functools
import math

import jax
import jax.numpy as jnp
from jax import lax
from jax.experimental import pallas as pl
from jax.experimental.pallas import tpu as pltpu
from jax.sharding import PartitionSpec as P

BLK = 256
LANES = 128
SMALL = pl.CostEstimate(flops=1, bytes_accessed=1, transcendentals=0)
LARGE = pl.CostEstimate(flops=10**10, bytes_accessed=10**7, transcendentals=0)
F32 = jnp.float32
BF16 = jnp.bfloat16


def gate_up_kernel(idx_ref, top_ref, bottom_ref, gate_ref, up_ref, mine_ref, other_ref):
    rows = top_ref.shape[0]
    lhs = jnp.concatenate([top_ref[...], bottom_ref[...]], axis=0)
    for slot, weight_ref in enumerate((gate_ref, up_ref)):
        product = jnp.dot(lhs, weight_ref[...], preferred_element_type=F32).astype(BF16)
        mine_ref[slot] = product[:rows]
        other_ref[slot] = product[rows:]


def gate_up(top, top_block, bottom, gate, up, column, first, width):
    rows, feat = bottom.shape
    if width % BLK or gate.shape[1] % BLK or rows % 16 or feat % 128:
        lhs = jnp.concatenate(
            [lax.dynamic_slice_in_dim(top, top_block * feat, feat, 1), bottom], axis=0
        )
        both = [
            jnp.dot(
                lhs,
                lax.dynamic_slice_in_dim(w, column + first, width, 1),
                preferred_element_type=F32,
            ).astype(BF16)
            for w in (gate, up)
        ]
        both = jnp.stack(both)
        return both[:, :rows], both[:, rows:]
    scalars = jnp.stack([top_block, lax.div(column, BLK) + first // BLK]).astype(jnp.int32)
    weight_spec = pl.BlockSpec((feat, BLK), lambda n, s: (0, s[1] + n))
    out_spec = pl.BlockSpec((2, rows, BLK), lambda n, s: (0, 0, n))
    shape = jax.ShapeDtypeStruct((2, rows, width), BF16)
    return pl.pallas_call(
        gate_up_kernel,
        grid_spec=pltpu.PrefetchScalarGridSpec(
            num_scalar_prefetch=1,
            grid=(width // BLK,),
            in_specs=[
                pl.BlockSpec((rows, feat), lambda n, s: (0, s[0])),
                pl.BlockSpec((rows, feat), lambda n, s: (0, 0)),
                weight_spec,
                weight_spec,
            ],
            out_specs=[out_spec, out_spec],
        ),
        out_shape=[shape, shape],
        compiler_params=pltpu.CompilerParams(vmem_limit_bytes=40 * 2**20),
        cost_estimate=pl.CostEstimate(
            flops=2 * 2 * rows * feat * 2 * width,
            bytes_accessed=2 * feat * 2 * width + 2 * 2 * rows * (feat + 2 * width),
            transcendentals=0,
        ),
        name="gate_up",
    )(scalars, top, bottom, gate, up)


def down_kernel(idx_ref, mine_ref, other_ref, weight_ref, *refs):
    out_ref = refs[-1]
    lhs = jnp.concatenate([mine_ref[...], other_ref[...]], axis=0)
    product = jnp.dot(lhs, weight_ref[...], preferred_element_type=F32)

    @pl.when(pl.program_id(0) == 0)
    def _():
        out_ref[...] = refs[0][...] + product if len(refs) > 1 else product

    @pl.when(pl.program_id(0) > 0)
    def _():
        out_ref[...] += product


def down_add(total, mine, other, weight, row):
    rows, width = mine.shape
    outs = weight.shape[1]
    if width % BLK or weight.shape[0] % BLK or rows % 16 or outs % 128:
        lhs = jnp.concatenate([mine, other], axis=0)
        part = lax.dynamic_slice_in_dim(weight, row, width, 0)
        product = jnp.dot(lhs, part, preferred_element_type=F32)
        return product if total is None else total + product
    scalars = jnp.reshape(lax.div(row, BLK), (1,)).astype(jnp.int32)
    hidden_spec = pl.BlockSpec((rows, BLK), lambda k, s: (0, k))
    whole = pl.BlockSpec((2 * rows, outs), lambda k, s: (0, 0))
    totals = [] if total is None else [total]
    return pl.pallas_call(
        down_kernel,
        grid_spec=pltpu.PrefetchScalarGridSpec(
            num_scalar_prefetch=1,
            grid=(width // BLK,),
            in_specs=[
                hidden_spec,
                hidden_spec,
                pl.BlockSpec((BLK, outs), lambda k, s: (s[0] + k, 0)),
            ]
            + [whole] * len(totals),
            out_specs=whole,
        ),
        out_shape=jax.ShapeDtypeStruct((2 * rows, outs), F32),
        compiler_params=pltpu.CompilerParams(vmem_limit_bytes=40 * 2**20),
        cost_estimate=pl.CostEstimate(
            flops=2 * 2 * rows * width * outs,
            bytes_accessed=2 * width * outs + 2 * 2 * rows * width + 16 * rows * outs,
            transcendentals=0,
        ),
        name="down_add",
    )(scalars, mine, other, weight, *totals)


def general_body(tokens, gate_weight, up_weight, down_weight, right_factor, left_factor):
    fsdp_count = lax.axis_size("fsdp")
    tensor_count = lax.axis_size("tensor")
    chips = fsdp_count // 2
    rows, model = tokens.shape
    feat, hid = gate_weight.shape
    part = hid // chips
    me = lax.axis_index("fsdp")
    chip, core = lax.div(me, 2), lax.rem(me, 2)
    z = lax.axis_index("tensor")

    def swap(value):
        return lax.ppermute(value, "fsdp", [(i, i ^ 1) for i in range(fsdp_count)])

    def shift(value, hops):
        perm = [(i, (i + 2 * hops) % fsdp_count) for i in range(fsdp_count)]
        return lax.ppermute(value, "fsdp", perm)

    def gather_z(value):
        if tensor_count > 4:
            return lax.all_gather(value, "tensor", axis=0, tiled=True)
        size = value.shape[0]
        whole = jnp.zeros((size * tensor_count,) + value.shape[1:], value.dtype)
        whole = lax.dynamic_update_slice_in_dim(whole, value, z * size, 0)
        for step in range(1, tensor_count):
            perm = [(i, (i + step) % tensor_count) for i in range(tensor_count)]
            got = lax.ppermute(value, "tensor", perm)
            source = lax.rem(z - step + tensor_count, tensor_count)
            whole = lax.dynamic_update_slice_in_dim(whole, got, source * size, 0)
        return whole

    def scatter_z(value):
        if tensor_count > 4:
            return lax.psum_scatter(value, "tensor", scatter_dimension=0, tiled=False)
        total = lax.dynamic_index_in_dim(value, z, 0, keepdims=False)
        for step in range(1, tensor_count):
            target_z = lax.rem(z + step, tensor_count)
            piece = lax.dynamic_index_in_dim(value, target_z, 0, keepdims=False)
            perm = [(i, (i + step) % tensor_count) for i in range(tensor_count)]
            total += lax.ppermute(piece.astype(BF16), "tensor", perm).astype(F32)
        return total

    def columns(value, start, width):
        return lax.dynamic_slice_in_dim(value, start, width, 1)

    def after(value, *others):
        return lax.optimization_barrier((value,) + others)[0]

    def pair_z(value):
        perm = [(i, i ^ 1) for i in range(tensor_count)]
        got = lax.ppermute(value, "tensor", perm)
        odd = lax.rem(z, 2) == 1
        return jnp.concatenate(
            [jnp.where(odd, got, value), jnp.where(odd, value, got)], axis=0
        )

    if part % BLK == 0 and part // BLK > 1:
        head = (part // BLK + 1) // 2 * BLK
        chunks = [(0, head), (head, part - head)]
    else:
        chunks = [(0, part)]

    half = rows // 2
    own_half = lax.dynamic_slice_in_dim(tokens, lax.rem(z, 2) * half, half, 0)

    def send_tokens(value, dt, g):
        features = lax.rem(chip - dt + g + chips, chips) * (2 * feat)
        return shift(columns(value, features, 2 * feat), -dt)

    def partial(pair, dp, first, width):
        column = lax.rem(chip + dp, chips) * part
        top, block, bottom = pair
        mine, other = gate_up(top, block, bottom, gate_weight, up_weight, column, first, width)
        return mine, swap(other)

    def send_partials(pair, got, dt):
        sums = []
        for dp in range(1, chips):
            pieces = [partial(pair, dp, *chunk) for chunk in chunks]
            for n, (mine, from_core) in enumerate(pieces):
                both = (mine.astype(F32) + from_core.astype(F32)).astype(BF16)
                got[dt, dp, n] = shift(both, dp)
                sums.append(both)
        return sums

    got, kept, gathered = {}, {}, {}
    local = swap(columns(tokens, (me ^ 1) * feat, feat))
    arrived = {dt: send_tokens(own_half, dt, 0) for dt in range(1, chips)}
    sums = send_partials((tokens, me, local), got, 0)
    if sums:
        local = after(local, *sums)
    kept[0] = partial((tokens, me, local), 0, 0, part)
    late_tokens = after(tokens, kept[0][0])
    neighbour_tokens = swap(late_tokens)
    late_half = after(own_half, *sums) if sums else own_half

    for dt in range(1, chips):
        gathered[dt, 0] = pair_z(after(arrived[dt], *sums))
        whole = gathered[dt, 0]
        top = columns(whole, core * feat, feat)
        bottom = swap(columns(whole, (1 - core) * feat, feat))
        pair = (top, jnp.int32(0), bottom)
        sums = send_partials(pair, got, dt)
        pair = (top, jnp.int32(0), after(bottom, *sums))
        kept[dt] = partial(pair, 0, 0, part)
        for g in range(1, chips):
            gathered[dt, g] = pair_z(after(send_tokens(late_half, dt, g), kept[dt][0]))

    def activate(e, first, width, n):
        terms = [lax.slice_in_dim(term, first, first + width, axis=2) for term in kept[e]]
        terms += [got[(e + dp) % chips, dp, n] for dp in range(1, chips)]
        total = sum(term.astype(F32) for term in terms)
        return (jax.nn.silu(total[0]) * total[1]).astype(BF16)

    totals = {u: None for u in range(chips)}
    for e in list(range(1, chips)) + [0]:
        values = [activate(e, *chunk, n) for n, chunk in enumerate(chunks)]
        spans = list(chunks)
        if e:
            values, spans = [jnp.concatenate(values, axis=1)], [(0, part)]
        sent = [[value] + [shift(value, d) for d in range(1, chips)] for value in values]
        for (first, width), copies in zip(spans, sent):
            for d, mine in enumerate(copies):
                u = (e - d + chips) % chips
                row = lax.rem(chip - d + chips, chips) * part + first
                totals[u] = down_add(totals[u], mine, swap(mine), down_weight, row)

    token_rows = []
    for dt in range(chips):
        if dt == 0:
            token_rows += [tokens, neighbour_tokens]
            continue
        else:
            full = jnp.zeros((rows, model), BF16)
            for g in range(chips):
                features = lax.rem(chip + g, chips) * (2 * feat)
                full = lax.dynamic_update_slice_in_dim(full, gathered[dt, g], features, 1)
        token_rows += [full, swap(full)]
    inputs = jnp.concatenate(token_rows, axis=0)
    count = inputs.shape[0]

    blocks, share, size = right_factor.shape
    ratio = tensor_count // fsdp_count
    turn = []
    for a in range(fsdp_count):
        for b in range(tensor_count):
            turn.append((a * tensor_count + b, (b // ratio) * tensor_count + a * ratio + b % ratio))
    back = [(b, a) for a, b in turn]
    right_rows = gather_z(lax.ppermute(right_factor, ("fsdp", "tensor"), turn)[None])
    right_rows = right_rows.reshape(fsdp_count, ratio, blocks, share, size)
    right_rows = right_rows.transpose(0, 2, 1, 3, 4).reshape(
        fsdp_count * blocks, ratio * share, size
    )
    left_rows = jnp.moveaxis(gather_z(jnp.moveaxis(left_factor, 1, 0)), 0, 1)

    block_input = inputs.reshape(count, fsdp_count * blocks, size)
    mixed = jnp.einsum(
        "nim,ijm->nij", block_input, right_rows, preferred_element_type=F32
    ).astype(BF16)
    student = jnp.einsum("nij,jki->njk", mixed, left_rows, preferred_element_type=F32)
    target = jnp.concatenate([totals[u] for u in range(chips)], axis=0)
    scale = 1.0 / math.sqrt(count)
    out_grad = (student * (1.0 / tensor_count) - target.reshape(student.shape)) * scale
    out_grad = out_grad.astype(BF16)
    grad_left = jnp.einsum("njk,nij->kji", out_grad, mixed, preferred_element_type=F32)
    mixed_grad = jnp.einsum(
        "njk,jki->nij", out_grad, left_rows, preferred_element_type=F32
    ).astype(BF16)
    grad_right = jnp.einsum(
        "nij,nim->ijm", mixed_grad, block_input, preferred_element_type=F32
    )
    grad_left = scatter_z(
        grad_left.reshape((tensor_count, -1) + grad_left.shape[1:])
    )
    grad_left = jnp.moveaxis(grad_left, 0, 1)
    grad_right = grad_right.reshape(fsdp_count, blocks, ratio, share, size)
    grad_right = grad_right.transpose(0, 2, 1, 3, 4).reshape(
        tensor_count, blocks, share, size
    )
    grad_right = lax.ppermute(scatter_z(grad_right), ("fsdp", "tensor"), back)
    return grad_right, grad_left


def cut_kernel(count, idx_ref, *refs):
    for in_ref, out_ref in zip(refs[:count], refs[count:]):
        out_ref[...] = in_ref[...]


def cut_tokens(tokens, row, columns):
    block = (tokens.shape[0] // 2, tokens.shape[1] // 2)
    count = len(columns)
    return pl.pallas_call(
        functools.partial(cut_kernel, count),
        grid_spec=pltpu.PrefetchScalarGridSpec(
            num_scalar_prefetch=1,
            grid=(1,),
            in_specs=[
                pl.BlockSpec(block, lambda n, s, k=k: (s[0], s[1 + k])) for k in range(count)
            ],
            out_specs=[pl.BlockSpec(block, lambda n, s: (0, 0))] * count,
        ),
        out_shape=[jax.ShapeDtypeStruct(block, BF16)] * count,
        cost_estimate=SMALL,
        name="cut_tokens",
    )(jnp.stack([row, *columns]).astype(jnp.int32), *[tokens] * count)


def pack_kernel(left_ref, out_ref):
    share = left_ref.shape[1]
    for pair in range(left_ref.shape[0] // 2):
        both = [left_ref[2 * pair].astype(F32), left_ref[2 * pair + 1].astype(F32)]
        both = jnp.concatenate(both, axis=1)
        out_ref[pair * share : (pair + 1) * share, :] = both.astype(BF16)


def pack_left(left):
    pairs, share, blocks = left.shape
    return pl.pallas_call(
        pack_kernel,
        out_shape=jax.ShapeDtypeStruct((pairs // 2 * share, 2 * blocks), BF16),
        cost_estimate=LARGE,
        name="pack_left",
    )(left)


def products_kernel(sets, idx_ref, *refs):
    pieces, (gate_ref, up_ref, mine_ref, other_ref) = refs[: 4 * sets], refs[4 * sets :]
    lhs = jnp.concatenate([piece[...] for piece in pieces], axis=0)
    rows = mine_ref.shape[2]
    for slot, weight_ref in enumerate((gate_ref, up_ref)):
        product = jnp.dot(lhs, weight_ref[...], preferred_element_type=F32).astype(BF16)
        for u in range(sets):
            mine_ref[u, slot] = product[2 * u * rows : (2 * u + 1) * rows]
            other_ref[u, slot] = product[(2 * u + 1) * rows : (2 * u + 2) * rows]


def products(pieces, scalars, gate, up, first, width):
    feat = gate.shape[0]
    sets = len(pieces) // 4
    half = pieces[0][0].shape[0] // (1 if pieces[0][1] is None else 2)
    start = first // BLK

    def piece_spec(row, column):
        if row is None:
            return pl.BlockSpec((half, feat), lambda n, s: (0, s[column]))
        return pl.BlockSpec((half, feat), lambda n, s: (s[row], s[column]))

    weight_spec = pl.BlockSpec(
        (feat, BLK), lambda n, s: (0, s[4] + start + n)
    )
    out_spec = pl.BlockSpec((sets, 2, 2 * half, BLK), lambda n, s: (0, 0, 0, n))
    shape = jax.ShapeDtypeStruct((sets, 2, 2 * half, width), BF16)
    return pl.pallas_call(
        functools.partial(products_kernel, sets),
        grid_spec=pltpu.PrefetchScalarGridSpec(
            num_scalar_prefetch=1,
            grid=(width // BLK,),
            in_specs=[piece_spec(row, column) for _, row, column in pieces]
            + [weight_spec, weight_spec],
            out_specs=[out_spec, out_spec],
        ),
        out_shape=[shape, shape],
        compiler_params=pltpu.CompilerParams(vmem_limit_bytes=40 * 2**20),
        cost_estimate=LARGE if sets > 1 else SMALL,
        name="gate_up_products",
    )(scalars, *[piece for piece, _, _ in pieces], gate, up)


def fill_rows(lhs, pieces):
    rows = pieces[0].shape[0]
    for place, which in enumerate((1, 3, 0, 2)):
        lhs[place * rows : (place + 1) * rows, :] = pieces[which][...]


def whole_spec(array):
    return pl.BlockSpec(array.shape, lambda n, s: (0,) * len(array.shape))


def target_kernel(sign, idx_ref, mine_ref, near_ref, weight_ref, *refs):
    terms, out_ref = refs[:-1], refs[-1]
    lhs = jnp.concatenate([mine_ref[...], near_ref[...]], axis=0)
    product = jnp.dot(lhs, weight_ref[...], preferred_element_type=F32)
    out_ref[...] = sum((ref[...] for ref in terms), sign * product)


def target_part(sign, terms, mine, near, weight, chip):
    rows, width = mine.shape
    outs = weight.shape[1]
    wide = 2 * BLK if outs % (2 * BLK) == 0 else BLK
    block = pl.BlockSpec((2 * rows, wide), lambda n, s: (0, n))
    return pl.pallas_call(
        functools.partial(target_kernel, sign),
        grid_spec=pltpu.PrefetchScalarGridSpec(
            num_scalar_prefetch=1,
            grid=(outs // wide,),
            in_specs=[whole_spec(mine), whole_spec(near)]
            + [pl.BlockSpec((width, wide), lambda n, s: (s[0], n))]
            + [block] * len(terms),
            out_specs=block,
        ),
        out_shape=jax.ShapeDtypeStruct((2 * rows, outs), F32),
        compiler_params=pltpu.CompilerParams(vmem_limit_bytes=40 * 2**20),
        cost_estimate=SMALL,
        name="target_part",
    )(jnp.reshape(chip, (1,)).astype(jnp.int32), mine, near, weight, *terms)


TN = (((0,), (0,)), ((), ()))
NT = (((1,), (1,)), ((), ()))
WIDE = 8


def natural(step, chip, per_chip):
    return lax.rem(chip + step // per_chip, 2) * per_chip + lax.rem(step, per_chip)


def spread_left(z, rows_ref, out_ref, scratch):
    groups = out_ref.shape[0]
    parts, _, size = rows_ref.shape
    blocks = size // 2
    share = blocks // parts
    fold = BLK // blocks
    begin = rows_ref.shape[1] - groups * fold // 2 * share
    scratch[...] = jnp.zeros_like(scratch)
    low = lax.broadcasted_iota(jnp.int32, (blocks, size), 1) < blocks
    for g in range(groups):
        for pair in range(fold // 2):
            row = begin + (g * (fold // 2) + pair) * share
            picked = [
                rows_ref[place(z, owner), row : row + share, :] for owner in range(parts)
            ]
            turned = jnp.concatenate(picked + picked, axis=0).astype(F32).T
            for a in range(2):
                value = turned[a * blocks : (a + 1) * blocks]
                value = jnp.where(low if a == 0 else ~low, value, 0.0)
                lanes = slice(pair * size, (pair + 1) * size)
                for c in range(blocks // WIDE):
                    row = (c * fold + 2 * pair + a) * WIDE
                    scratch[row : row + WIDE, lanes] = value[c * WIDE : (c + 1) * WIDE]
        out_ref[g] = scratch[...].astype(BF16)


def student_kernel(steps, late, tensor_count, idx_ref, *refs):
    tokens, refs = refs[: 8 if late else 4], refs[8 if late else 4 :]
    rights, left_ref, refs = refs[:2], refs[2], refs[3:]
    step = pl.program_id(0)
    if late:
        target_ref, mixed_ref, student_ref, spread = refs
    else:
        mixed_ref, student_ref, diag_ref, spread, scratch = refs
        rows_ref, left_ref = left_ref, diag_ref
        pl.when(step == 0)(lambda: spread_left(idx_ref[3], rows_ref, diag_ref, scratch))
    pair = natural(step, idx_ref[2], steps // 2)
    groups = left_ref.shape[0]
    size = spread.shape[2]
    pairs = spread.shape[1] // WIDE
    share = BLK // groups

    @pl.when(step == 0)
    def _():
        spread[...] = jnp.zeros_like(spread)

    def mix(pieces):
        for half, right_ref in enumerate(rights):
            for t in range(WIDE):
                value = right_ref[0, t * pairs : (t + 1) * pairs, :].astype(F32)
                spread[t, pl.ds(t, pairs, stride=WIDE), :] = value
            factor = jnp.concatenate([spread[t] for t in range(WIDE)], axis=1).astype(BF16)
            lanes = slice(half * WIDE * size, (half + 1) * WIDE * size)
            rows = jnp.concatenate([piece[:, lanes] for piece in pieces], axis=0)
            part = lax.dot_general(factor, rows, NT, preferred_element_type=F32).astype(BF16)
            start = pl.multiple_of((2 * pair + half) * share, share)
            for g in range(groups):
                mixed_ref[g, pl.ds(start, share), :] = part[g * share : (g + 1) * share]

    if late:
        pl.when(step < steps // 2)(lambda: mix(tokens[:4]))
        pl.when(step >= steps // 2)(lambda: mix(tokens[4:]))
    else:
        mix(tokens)

    @pl.when(step == steps - 1)
    def _():
        for g in range(groups):
            span = slice(g * BLK, (g + 1) * BLK)
            student = lax.dot_general(
                mixed_ref[g], left_ref[g], TN, preferred_element_type=F32
            )
            student = student * (1.0 / tensor_count)
            student_ref[:, span] = student - target_ref[:, span] if late else student


def token_specs(half, width, chunk, late):
    if not late:
        return [
            pl.BlockSpec((half, width), lambda n, s, p=p: (s[p % 2], chunk(n, s)))
            for p in range(4)
        ]
    inner = pl.BlockSpec((half, width), lambda n, s: (0, lax.rem(chunk(n, s), 2)))
    return [inner] * 8


def student_part(tokens, scalars, factors, pairs, tensor_count, late=()):
    size = factors.shape[2]
    half = tokens[0].shape[0] // (1 if late else 2)
    blocks = size // 2
    groups = pairs * blocks // BLK
    steps = blocks // (2 * WIDE)

    def chunk(n, s):
        return natural(n, s[2], steps // 2)

    def right_spec(half):
        return pl.BlockSpec(
            (1, WIDE * pairs, size), lambda n, s: (place(s[3], chunk(n, s)), half, 0)
        )

    diag = (groups, BLK, BLK)
    shapes = [
        jax.ShapeDtypeStruct((groups, BLK, 4 * half), BF16),
        jax.ShapeDtypeStruct((4 * half, groups * BLK), F32),
    ]
    scratch = [pltpu.VMEM((WIDE, pairs * WIDE, size), F32)]
    extra = list(late)
    if not late:
        shapes.append(jax.ShapeDtypeStruct(diag, BF16))
        scratch.append(pltpu.VMEM((BLK, BLK), F32))
        extra = [factors]
    return pl.pallas_call(
        functools.partial(student_kernel, steps, bool(late), tensor_count),
        grid_spec=pltpu.PrefetchScalarGridSpec(
            num_scalar_prefetch=1,
            grid=(steps,),
            in_specs=token_specs(half, 2 * WIDE * size, chunk, bool(late))
            + [right_spec(0), right_spec(1)]
            + [whole_spec(array) for array in extra],
            out_specs=[whole_spec(shape) for shape in shapes],
            scratch_shapes=scratch,
        ),
        out_shape=shapes,
        compiler_params=pltpu.CompilerParams(vmem_limit_bytes=40 * 2**20),
        cost_estimate=LARGE,
        name="student_part",
    )(scalars, *tokens, factors, factors, *extra)


def place(z, owner):
    bits = z ^ owner
    return lax.rem(bits, 2) * 2 + bits // 2


def left_kernel(chunks, scale, idx_ref, *refs):
    hidden, refs = refs[:4], refs[4:]
    weight_ref, rest0, rest1, mixed0, mixed1, left_ref, out_ref, back_ref, lhs = refs
    step = pl.program_id(0)
    parts, size = out_ref.shape[0], out_ref.shape[2]
    blocks = chunks * WIDE
    share = BLK // chunks
    fold = BLK // blocks
    pl.when(step == 0)(lambda: fill_rows(lhs, hidden))
    target = jnp.dot(lhs[...], weight_ref[...], preferred_element_type=F32)
    rest = jnp.concatenate([rest0[...], rest1[...]], axis=0)
    out_grad = ((rest - target) * scale).astype(BF16)
    mixed = jnp.concatenate([mixed0[0], mixed1[0]], axis=1)
    left = jnp.dot(mixed, out_grad, preferred_element_type=F32)
    value = lax.dot_general(left_ref[0], out_grad, NT, preferred_element_type=F32)
    value = value.astype(BF16)
    for c in range(chunks):
        back_ref[c] = value[c * share : (c + 1) * share]
    low = lax.broadcasted_iota(jnp.int32, (blocks, size), 1) < blocks
    rows = blocks // parts
    for pair in range(fold // 2):
        lanes = slice(pair * size, (pair + 1) * size)
        picked = []
        for a in (2 * pair, 2 * pair + 1):
            for c in range(chunks):
                begin = (c * fold + a) * WIDE
                picked.append(left[begin : begin + WIDE, lanes])
        turned = jnp.concatenate(picked, axis=0).T
        both = jnp.where(low, turned[:blocks], turned[blocks:]).astype(BF16)
        begin = pl.multiple_of((step * (fold // 2) + pair) * rows, rows)
        for owner in range(parts):
            out_ref[place(idx_ref[3], owner), pl.ds(begin, rows), :] = both[
                owner * rows : (owner + 1) * rows
            ]


def left_grads(hidden, weight, rest, mixed, left_diag, scalars, parts, pairs, size, scale):
    groups, count = left_diag.shape[0], 2 * rest[0].shape[0]
    width = hidden[0].shape[1]
    blocks = groups * BLK // pairs
    chunks = blocks // WIDE
    share = BLK // chunks
    column = pl.BlockSpec((count // 2, BLK), lambda n, s: (0, n))
    slab = pl.BlockSpec((1, BLK, count // 2), lambda n, s: (n, 0, 0))
    out_rows = pairs * blocks * blocks // size // parts
    return pl.pallas_call(
        functools.partial(left_kernel, chunks, scale),
        grid_spec=pltpu.PrefetchScalarGridSpec(
            num_scalar_prefetch=1,
            grid=(groups,),
            in_specs=[whole_spec(piece) for piece in hidden]
            + [pl.BlockSpec((width, BLK), lambda n, s: (1 - s[2], n))]
            + [column, column, slab, slab]
            + [pl.BlockSpec((1, BLK, BLK), lambda n, s: (n, 0, 0))],
            out_specs=[
                pl.BlockSpec((parts, out_rows, size), lambda n, s: (0, 0, 0)),
                pl.BlockSpec((chunks, share, count), lambda n, s: (0, n, 0)),
            ],
            scratch_shapes=[pltpu.VMEM((count, width), BF16)],
        ),
        out_shape=[
            jax.ShapeDtypeStruct((parts, out_rows, size), BF16),
            jax.ShapeDtypeStruct((chunks, groups * share, count), BF16),
        ],
        compiler_params=pltpu.CompilerParams(vmem_limit_bytes=40 * 2**20),
        cost_estimate=SMALL,
        name="left_grads",
    )(scalars, *hidden, weight, *rest, *mixed, left_diag)


def right_kernel(pairs, bit, idx_ref, *refs):
    own, near, far, (back_ref, out_ref, wide) = refs[:4], refs[4:8], refs[8:12], refs[12:]
    size = out_ref.shape[2]
    owner = idx_ref[3] ^ (2 * pl.program_id(0) + bit)

    def right(later):
        for half in range(2):
            lanes = slice(half * WIDE * size, (half + 1) * WIDE * size)
            rows = jnp.concatenate([piece[:, lanes] for piece in own + later], axis=0)
            value = jnp.dot(back_ref[half], rows, preferred_element_type=F32)
            for t in range(WIDE):
                wide[t] = value[:, t * size : (t + 1) * size]
            for t in range(WIDE):
                begin = (half * WIDE + t) * pairs
                out_ref[0, begin : begin + pairs, :] = wide[
                    t, pl.ds(t, pairs, stride=WIDE), :
                ].astype(BF16)

    pl.when(owner // 2 == idx_ref[2])(lambda: right(near))
    pl.when(owner // 2 != idx_ref[2])(lambda: right(far))


def right_grads(back, own, late, scalars, pairs, bit, size, cost):
    half = late[0].shape[0]
    rows, count = back.shape[1:]

    def owner(n, s):
        return s[3] ^ (2 * n + bit)

    return pl.pallas_call(
        functools.partial(right_kernel, pairs, bit),
        grid_spec=pltpu.PrefetchScalarGridSpec(
            num_scalar_prefetch=1,
            grid=(2,),
            in_specs=token_specs(half, 2 * WIDE * size, owner, False)
            + token_specs(half, 2 * WIDE * size, owner, True)
            + [pl.BlockSpec((2, rows, count), lambda n, s: (owner(n, s), 0, 0))],
            out_specs=pl.BlockSpec((1, 2 * WIDE * pairs, size), lambda n, s: (n, 0, 0)),
            scratch_shapes=[pltpu.VMEM((WIDE, pairs * WIDE, size), F32)],
        ),
        out_shape=jax.ShapeDtypeStruct((2, 2 * WIDE * pairs, size), BF16),
        compiler_params=pltpu.CompilerParams(vmem_limit_bytes=40 * 2**20),
        cost_estimate=cost,
        name="right_grads",
    )(scalars, *own, *late, back)


def tiled_body(tokens, gate_weight, up_weight, down_weight, right_factor, left_factor):
    fsdp_count = lax.axis_size("fsdp")
    tensor_count = lax.axis_size("tensor")
    rows, model = tokens.shape
    part = gate_weight.shape[1] // 2
    me, z = lax.axis_index("fsdp"), lax.axis_index("tensor")
    chip, core, odd = lax.div(me, 2), lax.rem(me, 2), lax.rem(z, 2)
    both_axes = ("fsdp", "tensor")

    def swap(value):
        return lax.ppermute(value, "fsdp", [(i, i ^ 1) for i in range(fsdp_count)])

    def across(value):
        return lax.ppermute(value, "fsdp", [(i, i ^ 2) for i in range(fsdp_count)])

    def along(value, bit):
        return lax.ppermute(value, "tensor", [(i, i ^ bit) for i in range(tensor_count)])

    def turn(value, bit):
        perm = []
        for f in range(fsdp_count):
            for t in range(tensor_count):
                perm.append((f * tensor_count + t, (t ^ bit) * tensor_count + f))
        return lax.ppermute(value, both_axes, perm)

    def after(value, *others):
        return lax.optimization_barrier((value,) + others)[0]

    def add(*terms):
        return sum(term.astype(F32) for term in terms)

    near_tokens = swap(tokens)
    first, rest = cut_tokens(tokens, odd, [1 - chip, chip])
    arrived = across(first)
    base = jnp.stack([odd, 1 - odd])
    mine_block = lax.div(part, BLK) * chip
    other_block = lax.div(part, BLK) * (1 - chip)

    def scalars(block):
        return jnp.concatenate([base, jnp.stack([me, core, block])]).astype(jnp.int32)

    own_pieces = [(t, row, 2) for t in (tokens, near_tokens) for row in (0, 1)]
    mine, other = products(
        own_pieces, after(scalars(other_block), first), gate_weight, up_weight, 0, part
    )

    pairs, blocks = left_factor.shape[0], left_factor.shape[2]
    turned = turn(after(right_factor, mine), 0)
    left_rows = pack_left(after(left_factor, mine))
    late_first = across(after(rest, mine))
    turned = after(turned, left_rows, late_first)
    factors = jnp.concatenate([turned.reshape(-1, LANES), left_rows], axis=0)[None]
    sums = add(mine[0], after(swap(other[0]), left_rows)).astype(BF16)

    arrived = after(arrived, mine)
    partner = along(arrived, 1)
    near_arrived = swap(arrived)
    partner = after(partner, factors)
    got_early = across(sums)
    order = jnp.concatenate([base, jnp.stack([chip, z])]).astype(jnp.int32)
    own = [tokens, tokens, near_tokens, near_tokens]
    late = [arrived, partner, near_arrived, swap(partner)]
    late_pieces = [(t, None, 3) for t in late]
    late_order = after(scalars(other_block), sums)
    mine, other = products(late_pieces, late_order, gate_weight, up_weight, 0, part)
    near = swap(after(other[0], got_early))
    sums = add(mine[0], near).astype(BF16)
    got = across(sums)
    mine_order = after(scalars(mine_block), sums)
    kept, other = products(
        own_pieces + late_pieces, mine_order, gate_weight, up_weight, 0, part
    )
    near_kept = swap(after(other, got))
    more = along(after(factors, kept), 2)

    def activate(u, term):
        total = add(kept[u], near_kept[u], term)
        return (jax.nn.silu(total[0]) * total[1]).astype(BF16)

    hidden1 = activate(1, got_early)
    got1 = across(hidden1)
    near1 = swap(hidden1)
    hidden0 = activate(0, after(got, hidden1))
    got0 = across(hidden0)
    near0 = swap(hidden0)
    factors = jnp.concatenate([factors, after(more, hidden0)], axis=0)
    more = along(factors, 1)
    late_partner = along(after(late_first, hidden0), 1)
    target1 = target_part(1.0, [], hidden1, after(near1, hidden0), down_weight, chip)
    factors = jnp.concatenate([factors, after(more, target1)], axis=0)
    mixed0, rest0, left_diag = student_part(
        [after(tokens, target1)] + own[1:], order, factors, pairs, tensor_count
    )
    late_partner = after(late_partner, target1)
    late += [late_first, late_partner, swap(after(late_first, target1)), swap(late_partner)]
    mixed1, rest1 = student_part(
        [after(late[0], mixed0)] + late[1:],
        order,
        factors,
        pairs,
        tensor_count,
        (left_diag, target1),
    )
    near0 = after(near0, mixed1)
    rest0 = target_part(-1.0, [rest0], hidden0, near0, down_weight, chip)
    got1, got0 = after(got1, mixed1), after(got0, rest0)
    hidden = [got0, got1, swap(got0), swap(got1)]

    size = right_factor.shape[2]
    left, back = left_grads(
        hidden,
        down_weight,
        (rest0, rest1),
        (mixed0, mixed1),
        left_diag,
        order,
        tensor_count,
        pairs,
        size,
        1.0 / math.sqrt(rows * fsdp_count),
    )
    got_left = along(left[2:], 1)
    sent = right_grads(back, own, late, order, pairs, 1, size, SMALL)
    left = add(left[:2], after(got_left, sent)).astype(BF16)
    got_left = along(left[1], 2)
    got_right = along(sent, 1)
    kept_back = after(back, sent, left)
    right = right_grads(kept_back, own, late, order, pairs, 0, size, LARGE)
    right = add(right, got_right).astype(BF16)
    grad_right = add(turn(right[0], 0), turn(right[1], 2))
    grad_left = add(left[0], got_left)
    grad_left = grad_left.reshape(pairs // 2, -1, 2, blocks).transpose(0, 2, 1, 3)
    return grad_right.reshape(right_factor.shape), grad_left.reshape(left_factor.shape)


def body(*args):
    tokens, gate_weight, _, _, right_factor, left_factor = args
    counts = (lax.axis_size("fsdp"), lax.axis_size("tensor"))
    feat, hid = gate_weight.shape
    per_owner, share, size = right_factor.shape
    blocks = left_factor.shape[2]
    fits = hid % (2 * BLK) == 0
    fits = fits and counts == (4, 4) and tokens.shape[0] == 128
    fits = fits and hid >= 4 * BLK and feat % BLK == 0
    fits = fits and size == 128 and 2 * blocks == size and per_owner % WIDE == 0
    fits = fits and left_factor.shape[0] == share and share % 16 == 0
    return (tiled_body if fits else general_body)(*args)


def solution(mesh):
    return jax.shard_map(
        body,
        mesh=mesh,
        in_specs=(
            P(("groups", "fsdp"), None),
            P("fsdp", "tensor"),
            P("fsdp", "tensor"),
            P("tensor", "fsdp"),
            P("fsdp", "tensor", None),
            P("fsdp", "tensor", None),
        ),
        out_specs=(P(("groups", "fsdp"), "tensor", None), P(("groups", "fsdp"), "tensor", None)),
        check_vma=False,
    )
```

```python
import functools
import math

import jax
import jax.numpy as jnp
from jax import lax
from jax.experimental import pallas as pl
from jax.experimental.pallas import tpu as pltpu
from jax.sharding import PartitionSpec as P

BLK = 256
LANES = 128
SMALL = pl.CostEstimate(flops=1, bytes_accessed=1, transcendentals=0)
LARGE = pl.CostEstimate(flops=10**10, bytes_accessed=10**7, transcendentals=0)
F32 = jnp.float32
BF16 = jnp.bfloat16


def gate_up_kernel(idx_ref, top_ref, bottom_ref, gate_ref, up_ref, mine_ref, other_ref):
    rows = top_ref.shape[0]
    lhs = jnp.concatenate([top_ref[...], bottom_ref[...]], axis=0)
    for slot, weight_ref in enumerate((gate_ref, up_ref)):
        product = jnp.dot(lhs, weight_ref[...], preferred_element_type=F32).astype(BF16)
        mine_ref[slot] = product[:rows]
        other_ref[slot] = product[rows:]


def gate_up(top, top_block, bottom, gate, up, column, first, width):
    rows, feat = bottom.shape
    if width % BLK or gate.shape[1] % BLK or rows % 16 or feat % 128:
        lhs = jnp.concatenate(
            [lax.dynamic_slice_in_dim(top, top_block * feat, feat, 1), bottom], axis=0
        )
        both = [
            jnp.dot(
                lhs,
                lax.dynamic_slice_in_dim(w, column + first, width, 1),
                preferred_element_type=F32,
            ).astype(BF16)
            for w in (gate, up)
        ]
        both = jnp.stack(both)
        return both[:, :rows], both[:, rows:]
    scalars = jnp.stack([top_block, lax.div(column, BLK) + first // BLK]).astype(jnp.int32)
    weight_spec = pl.BlockSpec((feat, BLK), lambda n, s: (0, s[1] + n))
    out_spec = pl.BlockSpec((2, rows, BLK), lambda n, s: (0, 0, n))
    shape = jax.ShapeDtypeStruct((2, rows, width), BF16)
    return pl.pallas_call(
        gate_up_kernel,
        grid_spec=pltpu.PrefetchScalarGridSpec(
            num_scalar_prefetch=1,
            grid=(width // BLK,),
            in_specs=[
                pl.BlockSpec((rows, feat), lambda n, s: (0, s[0])),
                pl.BlockSpec((rows, feat), lambda n, s: (0, 0)),
                weight_spec,
                weight_spec,
            ],
            out_specs=[out_spec, out_spec],
        ),
        out_shape=[shape, shape],
        compiler_params=pltpu.CompilerParams(vmem_limit_bytes=40 * 2**20),
        cost_estimate=pl.CostEstimate(
            flops=2 * 2 * rows * feat * 2 * width,
            bytes_accessed=2 * feat * 2 * width + 2 * 2 * rows * (feat + 2 * width),
            transcendentals=0,
        ),
        name="gate_up",
    )(scalars, top, bottom, gate, up)


def down_kernel(idx_ref, mine_ref, other_ref, weight_ref, *refs):
    out_ref = refs[-1]
    lhs = jnp.concatenate([mine_ref[...], other_ref[...]], axis=0)
    product = jnp.dot(lhs, weight_ref[...], preferred_element_type=F32)

    @pl.when(pl.program_id(0) == 0)
    def _():
        out_ref[...] = refs[0][...] + product if len(refs) > 1 else product

    @pl.when(pl.program_id(0) > 0)
    def _():
        out_ref[...] += product


def down_add(total, mine, other, weight, row):
    rows, width = mine.shape
    outs = weight.shape[1]
    if width % BLK or weight.shape[0] % BLK or rows % 16 or outs % 128:
        lhs = jnp.concatenate([mine, other], axis=0)
        part = lax.dynamic_slice_in_dim(weight, row, width, 0)
        product = jnp.dot(lhs, part, preferred_element_type=F32)
        return product if total is None else total + product
    scalars = jnp.reshape(lax.div(row, BLK), (1,)).astype(jnp.int32)
    hidden_spec = pl.BlockSpec((rows, BLK), lambda k, s: (0, k))
    whole = pl.BlockSpec((2 * rows, outs), lambda k, s: (0, 0))
    totals = [] if total is None else [total]
    return pl.pallas_call(
        down_kernel,
        grid_spec=pltpu.PrefetchScalarGridSpec(
            num_scalar_prefetch=1,
            grid=(width // BLK,),
            in_specs=[
                hidden_spec,
                hidden_spec,
                pl.BlockSpec((BLK, outs), lambda k, s: (s[0] + k, 0)),
            ]
            + [whole] * len(totals),
            out_specs=whole,
        ),
        out_shape=jax.ShapeDtypeStruct((2 * rows, outs), F32),
        compiler_params=pltpu.CompilerParams(vmem_limit_bytes=40 * 2**20),
        cost_estimate=pl.CostEstimate(
            flops=2 * 2 * rows * width * outs,
            bytes_accessed=2 * width * outs + 2 * 2 * rows * width + 16 * rows * outs,
            transcendentals=0,
        ),
        name="down_add",
    )(scalars, mine, other, weight, *totals)


def general_body(tokens, gate_weight, up_weight, down_weight, right_factor, left_factor):
    fsdp_count = lax.axis_size("fsdp")
    tensor_count = lax.axis_size("tensor")
    chips = fsdp_count // 2
    rows, model = tokens.shape
    feat, hid = gate_weight.shape
    part = hid // chips
    me = lax.axis_index("fsdp")
    chip, core = lax.div(me, 2), lax.rem(me, 2)
    z = lax.axis_index("tensor")

    def swap(value):
        return lax.ppermute(value, "fsdp", [(i, i ^ 1) for i in range(fsdp_count)])

    def shift(value, hops):
        perm = [(i, (i + 2 * hops) % fsdp_count) for i in range(fsdp_count)]
        return lax.ppermute(value, "fsdp", perm)

    def gather_z(value):
        if tensor_count > 4:
            return lax.all_gather(value, "tensor", axis=0, tiled=True)
        size = value.shape[0]
        whole = jnp.zeros((size * tensor_count,) + value.shape[1:], value.dtype)
        whole = lax.dynamic_update_slice_in_dim(whole, value, z * size, 0)
        for step in range(1, tensor_count):
            perm = [(i, (i + step) % tensor_count) for i in range(tensor_count)]
            got = lax.ppermute(value, "tensor", perm)
            source = lax.rem(z - step + tensor_count, tensor_count)
            whole = lax.dynamic_update_slice_in_dim(whole, got, source * size, 0)
        return whole

    def scatter_z(value):
        if tensor_count > 4:
            return lax.psum_scatter(value, "tensor", scatter_dimension=0, tiled=False)
        total = lax.dynamic_index_in_dim(value, z, 0, keepdims=False)
        for step in range(1, tensor_count):
            target_z = lax.rem(z + step, tensor_count)
            piece = lax.dynamic_index_in_dim(value, target_z, 0, keepdims=False)
            perm = [(i, (i + step) % tensor_count) for i in range(tensor_count)]
            total += lax.ppermute(piece.astype(BF16), "tensor", perm).astype(F32)
        return total

    def columns(value, start, width):
        return lax.dynamic_slice_in_dim(value, start, width, 1)

    def after(value, *others):
        return lax.optimization_barrier((value,) + others)[0]

    def pair_z(value):
        perm = [(i, i ^ 1) for i in range(tensor_count)]
        got = lax.ppermute(value, "tensor", perm)
        odd = lax.rem(z, 2) == 1
        return jnp.concatenate(
            [jnp.where(odd, got, value), jnp.where(odd, value, got)], axis=0
        )

    if part % BLK == 0 and part // BLK > 1:
        head = (part // BLK + 1) // 2 * BLK
        chunks = [(0, head), (head, part - head)]
    else:
        chunks = [(0, part)]

    half = rows // 2
    own_half = lax.dynamic_slice_in_dim(tokens, lax.rem(z, 2) * half, half, 0)

    def send_tokens(value, dt, g):
        features = lax.rem(chip - dt + g + chips, chips) * (2 * feat)
        return shift(columns(value, features, 2 * feat), -dt)

    def partial(pair, dp, first, width):
        column = lax.rem(chip + dp, chips) * part
        top, block, bottom = pair
        mine, other = gate_up(top, block, bottom, gate_weight, up_weight, column, first, width)
        return mine, swap(other)

    def send_partials(pair, got, dt):
        sums = []
        for dp in range(1, chips):
            pieces = [partial(pair, dp, *chunk) for chunk in chunks]
            for n, (mine, from_core) in enumerate(pieces):
                both = (mine.astype(F32) + from_core.astype(F32)).astype(BF16)
                got[dt, dp, n] = shift(both, dp)
                sums.append(both)
        return sums

    got, kept, gathered = {}, {}, {}
    local = swap(columns(tokens, (me ^ 1) * feat, feat))
    arrived = {dt: send_tokens(own_half, dt, 0) for dt in range(1, chips)}
    sums = send_partials((tokens, me, local), got, 0)
    if sums:
        local = after(local, *sums)
    kept[0] = partial((tokens, me, local), 0, 0, part)
    late_tokens = after(tokens, kept[0][0])
    neighbour_tokens = swap(late_tokens)
    late_half = after(own_half, *sums) if sums else own_half

    for dt in range(1, chips):
        gathered[dt, 0] = pair_z(after(arrived[dt], *sums))
        whole = gathered[dt, 0]
        top = columns(whole, core * feat, feat)
        bottom = swap(columns(whole, (1 - core) * feat, feat))
        pair = (top, jnp.int32(0), bottom)
        sums = send_partials(pair, got, dt)
        pair = (top, jnp.int32(0), after(bottom, *sums))
        kept[dt] = partial(pair, 0, 0, part)
        for g in range(1, chips):
            gathered[dt, g] = pair_z(after(send_tokens(late_half, dt, g), kept[dt][0]))

    def activate(e, first, width, n):
        terms = [lax.slice_in_dim(term, first, first + width, axis=2) for term in kept[e]]
        terms += [got[(e + dp) % chips, dp, n] for dp in range(1, chips)]
        total = sum(term.astype(F32) for term in terms)
        return (jax.nn.silu(total[0]) * total[1]).astype(BF16)

    totals = {u: None for u in range(chips)}
    for e in list(range(1, chips)) + [0]:
        values = [activate(e, *chunk, n) for n, chunk in enumerate(chunks)]
        spans = list(chunks)
        if e:
            values, spans = [jnp.concatenate(values, axis=1)], [(0, part)]
        sent = [[value] + [shift(value, d) for d in range(1, chips)] for value in values]
        for (first, width), copies in zip(spans, sent):
            for d, mine in enumerate(copies):
                u = (e - d + chips) % chips
                row = lax.rem(chip - d + chips, chips) * part + first
                totals[u] = down_add(totals[u], mine, swap(mine), down_weight, row)

    token_rows = []
    for dt in range(chips):
        if dt == 0:
            token_rows += [tokens, neighbour_tokens]
            continue
        else:
            full = jnp.zeros((rows, model), BF16)
            for g in range(chips):
                features = lax.rem(chip + g, chips) * (2 * feat)
                full = lax.dynamic_update_slice_in_dim(full, gathered[dt, g], features, 1)
        token_rows += [full, swap(full)]
    inputs = jnp.concatenate(token_rows, axis=0)
    count = inputs.shape[0]

    blocks, share, size = right_factor.shape
    ratio = tensor_count // fsdp_count
    turn = []
    for a in range(fsdp_count):
        for b in range(tensor_count):
            turn.append((a * tensor_count + b, (b // ratio) * tensor_count + a * ratio + b % ratio))
    back = [(b, a) for a, b in turn]
    right_rows = gather_z(lax.ppermute(right_factor, ("fsdp", "tensor"), turn)[None])
    right_rows = right_rows.reshape(fsdp_count, ratio, blocks, share, size)
    right_rows = right_rows.transpose(0, 2, 1, 3, 4).reshape(
        fsdp_count * blocks, ratio * share, size
    )
    left_rows = jnp.moveaxis(gather_z(jnp.moveaxis(left_factor, 1, 0)), 0, 1)

    block_input = inputs.reshape(count, fsdp_count * blocks, size)
    mixed = jnp.einsum(
        "nim,ijm->nij", block_input, right_rows, preferred_element_type=F32
    ).astype(BF16)
    student = jnp.einsum("nij,jki->njk", mixed, left_rows, preferred_element_type=F32)
    target = jnp.concatenate([totals[u] for u in range(chips)], axis=0)
    scale = 1.0 / math.sqrt(count)
    out_grad = (student * (1.0 / tensor_count) - target.reshape(student.shape)) * scale
    out_grad = out_grad.astype(BF16)
    grad_left = jnp.einsum("njk,nij->kji", out_grad, mixed, preferred_element_type=F32)
    mixed_grad = jnp.einsum(
        "njk,jki->nij", out_grad, left_rows, preferred_element_type=F32
    ).astype(BF16)
    grad_right = jnp.einsum(
        "nij,nim->ijm", mixed_grad, block_input, preferred_element_type=F32
    )
    grad_left = scatter_z(
        grad_left.reshape((tensor_count, -1) + grad_left.shape[1:])
    )
    grad_left = jnp.moveaxis(grad_left, 0, 1)
    grad_right = grad_right.reshape(fsdp_count, blocks, ratio, share, size)
    grad_right = grad_right.transpose(0, 2, 1, 3, 4).reshape(
        tensor_count, blocks, share, size
    )
    grad_right = lax.ppermute(scatter_z(grad_right), ("fsdp", "tensor"), back)
    return grad_right, grad_left


def cut_kernel(count, idx_ref, *refs):
    for in_ref, out_ref in zip(refs[:count], refs[count:]):
        out_ref[...] = in_ref[...]


def cut_tokens(tokens, row, columns):
    block = (tokens.shape[0] // 2, tokens.shape[1] // 2)
    count = len(columns)
    return pl.pallas_call(
        functools.partial(cut_kernel, count),
        grid_spec=pltpu.PrefetchScalarGridSpec(
            num_scalar_prefetch=1,
            grid=(1,),
            in_specs=[
                pl.BlockSpec(block, lambda n, s, k=k: (s[0], s[1 + k])) for k in range(count)
            ],
            out_specs=[pl.BlockSpec(block, lambda n, s: (0, 0))] * count,
        ),
        out_shape=[jax.ShapeDtypeStruct(block, BF16)] * count,
        cost_estimate=SMALL,
        name="cut_tokens",
    )(jnp.stack([row, *columns]).astype(jnp.int32), *[tokens] * count)


def pack_kernel(left_ref, out_ref):
    share = left_ref.shape[1]
    for pair in range(left_ref.shape[0] // 2):
        both = [left_ref[2 * pair].astype(F32), left_ref[2 * pair + 1].astype(F32)]
        both = jnp.concatenate(both, axis=1)
        out_ref[pair * share : (pair + 1) * share, :] = both.astype(BF16)


def pack_left(left):
    pairs, share, blocks = left.shape
    return pl.pallas_call(
        pack_kernel,
        out_shape=jax.ShapeDtypeStruct((pairs // 2 * share, 2 * blocks), BF16),
        cost_estimate=LARGE,
        name="pack_left",
    )(left)


def products_kernel(sets, idx_ref, *refs):
    pieces, (gate_ref, up_ref, mine_ref, other_ref) = refs[: 4 * sets], refs[4 * sets :]
    lhs = jnp.concatenate([piece[...] for piece in pieces], axis=0)
    rows = mine_ref.shape[2]
    for slot, weight_ref in enumerate((gate_ref, up_ref)):
        product = jnp.dot(lhs, weight_ref[...], preferred_element_type=F32).astype(BF16)
        for u in range(sets):
            mine_ref[u, slot] = product[2 * u * rows : (2 * u + 1) * rows]
            other_ref[u, slot] = product[(2 * u + 1) * rows : (2 * u + 2) * rows]


def products(pieces, scalars, gate, up, first, width):
    feat = gate.shape[0]
    sets = len(pieces) // 4
    half = pieces[0][0].shape[0] // (1 if pieces[0][1] is None else 2)
    start = first // BLK

    def piece_spec(row, column):
        if row is None:
            return pl.BlockSpec((half, feat), lambda n, s: (0, s[column]))
        return pl.BlockSpec((half, feat), lambda n, s: (s[row], s[column]))

    weight_spec = pl.BlockSpec(
        (feat, BLK), lambda n, s: (0, s[4] + start + n)
    )
    out_spec = pl.BlockSpec((sets, 2, 2 * half, BLK), lambda n, s: (0, 0, 0, n))
    shape = jax.ShapeDtypeStruct((sets, 2, 2 * half, width), BF16)
    return pl.pallas_call(
        functools.partial(products_kernel, sets),
        grid_spec=pltpu.PrefetchScalarGridSpec(
            num_scalar_prefetch=1,
            grid=(width // BLK,),
            in_specs=[piece_spec(row, column) for _, row, column in pieces]
            + [weight_spec, weight_spec],
            out_specs=[out_spec, out_spec],
        ),
        out_shape=[shape, shape],
        compiler_params=pltpu.CompilerParams(vmem_limit_bytes=40 * 2**20),
        cost_estimate=LARGE if sets > 1 else SMALL,
        name="gate_up_products",
    )(scalars, *[piece for piece, _, _ in pieces], gate, up)


def fill_rows(lhs, pieces):
    rows = pieces[0].shape[0]
    for place, which in enumerate((1, 3, 0, 2)):
        lhs[place * rows : (place + 1) * rows, :] = pieces[which][...]


def whole_spec(array):
    return pl.BlockSpec(array.shape, lambda n, s: (0,) * len(array.shape))


def target_kernel(sign, idx_ref, mine_ref, near_ref, weight_ref, *refs):
    terms, out_ref = refs[:-1], refs[-1]
    lhs = jnp.concatenate([mine_ref[...], near_ref[...]], axis=0)
    product = jnp.dot(lhs, weight_ref[...], preferred_element_type=F32)
    out_ref[...] = sum((ref[...] for ref in terms), sign * product)


def target_part(sign, terms, mine, near, weight, chip):
    rows, width = mine.shape
    outs = weight.shape[1]
    wide = 2 * BLK if outs % (2 * BLK) == 0 else BLK
    block = pl.BlockSpec((2 * rows, wide), lambda n, s: (0, n))
    return pl.pallas_call(
        functools.partial(target_kernel, sign),
        grid_spec=pltpu.PrefetchScalarGridSpec(
            num_scalar_prefetch=1,
            grid=(outs // wide,),
            in_specs=[whole_spec(mine), whole_spec(near)]
            + [pl.BlockSpec((width, wide), lambda n, s: (s[0], n))]
            + [block] * len(terms),
            out_specs=block,
        ),
        out_shape=jax.ShapeDtypeStruct((2 * rows, outs), F32),
        compiler_params=pltpu.CompilerParams(vmem_limit_bytes=40 * 2**20),
        cost_estimate=SMALL,
        name="target_part",
    )(jnp.reshape(chip, (1,)).astype(jnp.int32), mine, near, weight, *terms)


TN = (((0,), (0,)), ((), ()))
NT = (((1,), (1,)), ((), ()))
WIDE = 8


def natural(step, chip, per_chip):
    return lax.rem(chip + step // per_chip, 2) * per_chip + lax.rem(step, per_chip)


def spread_left(z, rows_ref, out_ref, scratch):
    groups = out_ref.shape[0]
    parts, _, size = rows_ref.shape
    blocks = size // 2
    share = blocks // parts
    fold = BLK // blocks
    begin = rows_ref.shape[1] - groups * fold // 2 * share
    scratch[...] = jnp.zeros_like(scratch)
    low = lax.broadcasted_iota(jnp.int32, (blocks, size), 1) < blocks
    for g in range(groups):
        for pair in range(fold // 2):
            row = begin + (g * (fold // 2) + pair) * share
            picked = [
                rows_ref[place(z, owner), row : row + share, :] for owner in range(parts)
            ]
            turned = jnp.concatenate(picked + picked, axis=0).astype(F32).T
            for a in range(2):
                value = turned[a * blocks : (a + 1) * blocks]
                value = jnp.where(low if a == 0 else ~low, value, 0.0)
                lanes = slice(pair * size, (pair + 1) * size)
                for c in range(blocks // WIDE):
                    row = (c * fold + 2 * pair + a) * WIDE
                    scratch[row : row + WIDE, lanes] = value[c * WIDE : (c + 1) * WIDE]
        out_ref[g] = scratch[...].astype(BF16)


def student_kernel(steps, late, tensor_count, idx_ref, *refs):
    tokens, refs = refs[: 8 if late else 4], refs[8 if late else 4 :]
    rights, left_ref, refs = refs[:2], refs[2], refs[3:]
    step = pl.program_id(0)
    if late:
        target_ref, mixed_ref, student_ref, spread = refs
    else:
        mixed_ref, student_ref, diag_ref, spread, scratch = refs
        rows_ref, left_ref = left_ref, diag_ref
        pl.when(step == 0)(lambda: spread_left(idx_ref[3], rows_ref, diag_ref, scratch))
    pair = natural(step, idx_ref[2], steps // 2)
    groups = left_ref.shape[0]
    size = spread.shape[2]
    pairs = spread.shape[1] // WIDE
    share = BLK // groups

    @pl.when(step == 0)
    def _():
        spread[...] = jnp.zeros_like(spread)

    def mix(pieces):
        for half, right_ref in enumerate(rights):
            for t in range(WIDE):
                value = right_ref[0, t * pairs : (t + 1) * pairs, :].astype(F32)
                spread[t, pl.ds(t, pairs, stride=WIDE), :] = value
            factor = jnp.concatenate([spread[t] for t in range(WIDE)], axis=1).astype(BF16)
            lanes = slice(half * WIDE * size, (half + 1) * WIDE * size)
            rows = jnp.concatenate([piece[:, lanes] for piece in pieces], axis=0)
            part = lax.dot_general(factor, rows, NT, preferred_element_type=F32).astype(BF16)
            start = pl.multiple_of((2 * pair + half) * share, share)
            for g in range(groups):
                mixed_ref[g, pl.ds(start, share), :] = part[g * share : (g + 1) * share]

    if late:
        pl.when(step < steps // 2)(lambda: mix(tokens[:4]))
        pl.when(step >= steps // 2)(lambda: mix(tokens[4:]))
    else:
        mix(tokens)

    @pl.when(step == steps - 1)
    def _():
        for g in range(groups):
            span = slice(g * BLK, (g + 1) * BLK)
            student = lax.dot_general(
                mixed_ref[g], left_ref[g], TN, preferred_element_type=F32
            )
            student = student * (1.0 / tensor_count)
            student_ref[:, span] = student - target_ref[:, span] if late else student


def token_specs(half, width, chunk, late):
    if not late:
        return [
            pl.BlockSpec((half, width), lambda n, s, p=p: (s[p % 2], chunk(n, s)))
            for p in range(4)
        ]
    inner = pl.BlockSpec((half, width), lambda n, s: (0, lax.rem(chunk(n, s), 2)))
    return [inner] * 8


def student_part(tokens, scalars, factors, pairs, tensor_count, late=()):
    size = factors.shape[2]
    half = tokens[0].shape[0] // (1 if late else 2)
    blocks = size // 2
    groups = pairs * blocks // BLK
    steps = blocks // (2 * WIDE)

    def chunk(n, s):
        return natural(n, s[2], steps // 2)

    def right_spec(half):
        return pl.BlockSpec(
            (1, WIDE * pairs, size), lambda n, s: (place(s[3], chunk(n, s)), half, 0)
        )

    diag = (groups, BLK, BLK)
    shapes = [
        jax.ShapeDtypeStruct((groups, BLK, 4 * half), BF16),
        jax.ShapeDtypeStruct((4 * half, groups * BLK), F32),
    ]
    scratch = [pltpu.VMEM((WIDE, pairs * WIDE, size), F32)]
    extra = list(late)
    if not late:
        shapes.append(jax.ShapeDtypeStruct(diag, BF16))
        scratch.append(pltpu.VMEM((BLK, BLK), F32))
        extra = [factors]
    return pl.pallas_call(
        functools.partial(student_kernel, steps, bool(late), tensor_count),
        grid_spec=pltpu.PrefetchScalarGridSpec(
            num_scalar_prefetch=1,
            grid=(steps,),
            in_specs=token_specs(half, 2 * WIDE * size, chunk, bool(late))
            + [right_spec(0), right_spec(1)]
            + [whole_spec(array) for array in extra],
            out_specs=[whole_spec(shape) for shape in shapes],
            scratch_shapes=scratch,
        ),
        out_shape=shapes,
        compiler_params=pltpu.CompilerParams(vmem_limit_bytes=40 * 2**20),
        cost_estimate=LARGE,
        name="student_part",
    )(scalars, *tokens, factors, factors, *extra)


def place(z, owner):
    bits = z ^ owner
    return lax.rem(bits, 2) * 2 + bits // 2


def left_kernel(chunks, scale, idx_ref, *refs):
    hidden, refs = refs[:4], refs[4:]
    weight_ref, rest0, rest1, mixed0, mixed1, left_ref, out_ref, back_ref, lhs = refs
    step = pl.program_id(0)
    parts, size = out_ref.shape[0], out_ref.shape[2]
    blocks = chunks * WIDE
    share = BLK // chunks
    fold = BLK // blocks
    pl.when(step == 0)(lambda: fill_rows(lhs, hidden))
    target = jnp.dot(lhs[...], weight_ref[...], preferred_element_type=F32)
    rest = jnp.concatenate([rest0[...], rest1[...]], axis=0)
    out_grad = ((rest - target) * scale).astype(BF16)
    mixed = jnp.concatenate([mixed0[0], mixed1[0]], axis=1)
    left = jnp.dot(mixed, out_grad, preferred_element_type=F32)
    value = lax.dot_general(left_ref[0], out_grad, NT, preferred_element_type=F32)
    value = value.astype(BF16)
    for c in range(chunks):
        back_ref[c] = value[c * share : (c + 1) * share]
    low = lax.broadcasted_iota(jnp.int32, (blocks, size), 1) < blocks
    rows = blocks // parts
    for pair in range(fold // 2):
        lanes = slice(pair * size, (pair + 1) * size)
        picked = []
        for a in (2 * pair, 2 * pair + 1):
            for c in range(chunks):
                begin = (c * fold + a) * WIDE
                picked.append(left[begin : begin + WIDE, lanes])
        turned = jnp.concatenate(picked, axis=0).T
        both = jnp.where(low, turned[:blocks], turned[blocks:]).astype(BF16)
        begin = pl.multiple_of((step * (fold // 2) + pair) * rows, rows)
        for owner in range(parts):
            out_ref[place(idx_ref[3], owner), pl.ds(begin, rows), :] = both[
                owner * rows : (owner + 1) * rows
            ]


def left_grads(hidden, weight, rest, mixed, left_diag, scalars, parts, pairs, size, scale):
    groups, count = left_diag.shape[0], 2 * rest[0].shape[0]
    width = hidden[0].shape[1]
    blocks = groups * BLK // pairs
    chunks = blocks // WIDE
    share = BLK // chunks
    column = pl.BlockSpec((count // 2, BLK), lambda n, s: (0, n))
    slab = pl.BlockSpec((1, BLK, count // 2), lambda n, s: (n, 0, 0))
    out_rows = pairs * blocks * blocks // size // parts
    return pl.pallas_call(
        functools.partial(left_kernel, chunks, scale),
        grid_spec=pltpu.PrefetchScalarGridSpec(
            num_scalar_prefetch=1,
            grid=(groups,),
            in_specs=[whole_spec(piece) for piece in hidden]
            + [pl.BlockSpec((width, BLK), lambda n, s: (1 - s[2], n))]
            + [column, column, slab, slab]
            + [pl.BlockSpec((1, BLK, BLK), lambda n, s: (n, 0, 0))],
            out_specs=[
                pl.BlockSpec((parts, out_rows, size), lambda n, s: (0, 0, 0)),
                pl.BlockSpec((chunks, share, count), lambda n, s: (0, n, 0)),
            ],
            scratch_shapes=[pltpu.VMEM((count, width), BF16)],
        ),
        out_shape=[
            jax.ShapeDtypeStruct((parts, out_rows, size), BF16),
            jax.ShapeDtypeStruct((chunks, groups * share, count), BF16),
        ],
        compiler_params=pltpu.CompilerParams(vmem_limit_bytes=40 * 2**20),
        cost_estimate=SMALL,
        name="left_grads",
    )(scalars, *hidden, weight, *rest, *mixed, left_diag)


def right_kernel(pairs, bit, idx_ref, *refs):
    own, near, far, (back_ref, out_ref, wide) = refs[:4], refs[4:8], refs[8:12], refs[12:]
    size = out_ref.shape[2]
    owner = idx_ref[3] ^ (2 * pl.program_id(0) + bit)

    def right(later):
        for half in range(2):
            lanes = slice(half * WIDE * size, (half + 1) * WIDE * size)
            rows = jnp.concatenate([piece[:, lanes] for piece in own + later], axis=0)
            value = jnp.dot(back_ref[half], rows, preferred_element_type=F32)
            for t in range(WIDE):
                wide[t] = value[:, t * size : (t + 1) * size]
            for t in range(WIDE):
                begin = (half * WIDE + t) * pairs
                out_ref[0, begin : begin + pairs, :] = wide[
                    t, pl.ds(t, pairs, stride=WIDE), :
                ].astype(BF16)

    pl.when(owner // 2 == idx_ref[2])(lambda: right(near))
    pl.when(owner // 2 != idx_ref[2])(lambda: right(far))


def right_grads(back, own, late, scalars, pairs, bit, size, cost):
    half = late[0].shape[0]
    rows, count = back.shape[1:]

    def owner(n, s):
        return s[3] ^ (2 * n + bit)

    return pl.pallas_call(
        functools.partial(right_kernel, pairs, bit),
        grid_spec=pltpu.PrefetchScalarGridSpec(
            num_scalar_prefetch=1,
            grid=(2,),
            in_specs=token_specs(half, 2 * WIDE * size, owner, False)
            + token_specs(half, 2 * WIDE * size, owner, True)
            + [pl.BlockSpec((2, rows, count), lambda n, s: (owner(n, s), 0, 0))],
            out_specs=pl.BlockSpec((1, 2 * WIDE * pairs, size), lambda n, s: (n, 0, 0)),
            scratch_shapes=[pltpu.VMEM((WIDE, pairs * WIDE, size), F32)],
        ),
        out_shape=jax.ShapeDtypeStruct((2, 2 * WIDE * pairs, size), BF16),
        compiler_params=pltpu.CompilerParams(vmem_limit_bytes=40 * 2**20),
        cost_estimate=cost,
        name="right_grads",
    )(scalars, *own, *late, back)


def tiled_body(tokens, gate_weight, up_weight, down_weight, right_factor, left_factor):
    fsdp_count = lax.axis_size("fsdp")
    tensor_count = lax.axis_size("tensor")
    rows, model = tokens.shape
    part = gate_weight.shape[1] // 2
    me, z = lax.axis_index("fsdp"), lax.axis_index("tensor")
    chip, core, odd = lax.div(me, 2), lax.rem(me, 2), lax.rem(z, 2)
    both_axes = ("fsdp", "tensor")

    def swap(value):
        return lax.ppermute(value, "fsdp", [(i, i ^ 1) for i in range(fsdp_count)])

    def across(value):
        return lax.ppermute(value, "fsdp", [(i, i ^ 2) for i in range(fsdp_count)])

    def along(value, bit):
        return lax.ppermute(value, "tensor", [(i, i ^ bit) for i in range(tensor_count)])

    def turn(value, bit):
        perm = []
        for f in range(fsdp_count):
            for t in range(tensor_count):
                perm.append((f * tensor_count + t, (t ^ bit) * tensor_count + f))
        return lax.ppermute(value, both_axes, perm)

    def after(value, *others):
        return lax.optimization_barrier((value,) + others)[0]

    def add(*terms):
        return sum(term.astype(F32) for term in terms)

    near_tokens = swap(tokens)
    first, rest = cut_tokens(tokens, odd, [1 - chip, chip])
    arrived = across(first)
    base = jnp.stack([odd, 1 - odd])
    mine_block = lax.div(part, BLK) * chip
    other_block = lax.div(part, BLK) * (1 - chip)

    def scalars(block):
        return jnp.concatenate([base, jnp.stack([me, core, block])]).astype(jnp.int32)

    own_pieces = [(t, row, 2) for t in (tokens, near_tokens) for row in (0, 1)]
    mine, other = products(
        own_pieces, after(scalars(other_block), first), gate_weight, up_weight, 0, part
    )

    pairs, blocks = left_factor.shape[0], left_factor.shape[2]
    turned = turn(after(right_factor, mine), 0)
    left_rows = pack_left(after(left_factor, mine))
    late_first = across(after(rest, mine))
    turned = after(turned, left_rows, late_first)
    factors = jnp.concatenate([turned.reshape(-1, LANES), left_rows], axis=0)[None]
    sums = add(mine[0], swap(other[0])).astype(BF16)

    arrived = after(arrived, mine)
    partner = along(arrived, 1)
    near_arrived = swap(arrived)
    partner = after(partner, factors)
    got_early = across(sums)
    order = jnp.concatenate([base, jnp.stack([chip, z])]).astype(jnp.int32)
    own = [tokens, tokens, near_tokens, near_tokens]
    late = [arrived, partner, near_arrived, swap(partner)]
    late_pieces = [(t, None, 3) for t in late]
    late_order = after(scalars(other_block), sums)
    mine, other = products(late_pieces, late_order, gate_weight, up_weight, 0, part)
    near = swap(other[0])
    more = along(after(factors, mine), 2)
    late_partner = along(after(late_first, mine), 1)
    mine_order = after(scalars(mine_block), mine)
    kept, other = products(
        own_pieces + late_pieces, mine_order, gate_weight, up_weight, 0, part
    )
    sums = add(mine[0], after(near, kept)).astype(BF16)
    got = across(sums)
    near_kept = swap(after(other, got_early, sums, more, late_partner))
    factors = jnp.concatenate([factors, after(more, kept)], axis=0)
    more = along(factors, 1)

    def activate(u, term):
        total = add(kept[u], near_kept[u], term)
        return (jax.nn.silu(total[0]) * total[1]).astype(BF16)

    hidden1 = activate(1, got_early)
    near1 = swap(hidden1)
    factors = jnp.concatenate([factors, after(more, hidden1)], axis=0)
    mixed0, rest0, left_diag = student_part(
        [after(tokens, hidden1, sums)] + own[1:], order, factors, pairs, tensor_count
    )
    got1 = across(after(hidden1, mixed0))
    target1 = target_part(1.0, [], hidden1, after(near1, mixed0), down_weight, chip)
    hidden0 = activate(0, after(got, target1))
    got0 = across(hidden0)
    near0 = swap(hidden0)
    late_partner = after(late_partner, mixed0)
    late += [late_first, late_partner, swap(after(late_first, mixed0)), swap(late_partner)]
    mixed1, rest1 = student_part(
        [after(late[0], hidden0)] + late[1:],
        order,
        factors,
        pairs,
        tensor_count,
        (left_diag, target1),
    )
    near0 = after(near0, mixed1)
    rest0 = target_part(-1.0, [rest0], hidden0, near0, down_weight, chip)
    got1, got0 = after(got1, mixed1), after(got0, rest0)
    hidden = [got0, got1, swap(got0), swap(got1)]

    size = right_factor.shape[2]
    left, back = left_grads(
        hidden,
        down_weight,
        (rest0, rest1),
        (mixed0, mixed1),
        left_diag,
        order,
        tensor_count,
        pairs,
        size,
        1.0 / math.sqrt(rows * fsdp_count),
    )
    got_left = along(left[2:], 1)
    sent = right_grads(back, own, late, order, pairs, 1, size, SMALL)
    left = add(left[:2], after(got_left, sent)).astype(BF16)
    got_left = along(left[1], 2)
    got_right = along(sent, 1)
    kept_back = after(back, sent, left)
    right = right_grads(kept_back, own, late, order, pairs, 0, size, LARGE)
    right = add(right, got_right).astype(BF16)
    grad_right = add(turn(right[0], 0), turn(right[1], 2))
    grad_left = add(left[0], got_left)
    grad_left = grad_left.reshape(pairs // 2, -1, 2, blocks).transpose(0, 2, 1, 3)
    return grad_right.reshape(right_factor.shape), grad_left.reshape(left_factor.shape)


def body(*args):
    tokens, gate_weight, _, _, right_factor, left_factor = args
    counts = (lax.axis_size("fsdp"), lax.axis_size("tensor"))
    feat, hid = gate_weight.shape
    per_owner, share, size = right_factor.shape
    blocks = left_factor.shape[2]
    fits = hid % (2 * BLK) == 0
    fits = fits and counts == (4, 4) and tokens.shape[0] == 128
    fits = fits and hid >= 4 * BLK and feat % BLK == 0
    fits = fits and size == 128 and 2 * blocks == size and per_owner % WIDE == 0
    fits = fits and left_factor.shape[0] == share and share % 16 == 0
    return (tiled_body if fits else general_body)(*args)


def solution(mesh):
    return jax.shard_map(
        body,
        mesh=mesh,
        in_specs=(
            P(("groups", "fsdp"), None),
            P("fsdp", "tensor"),
            P("fsdp", "tensor"),
            P("tensor", "fsdp"),
            P("fsdp", "tensor", None),
            P("fsdp", "tensor", None),
        ),
        out_specs=(P(("groups", "fsdp"), "tensor", None), P(("groups", "fsdp"), "tensor", None)),
        check_vma=False,
    )
```
